32 devices in a mesh: parts: 2 (over y), tensor: 4 (over z), dp: 2 (over x), pipe: 2 (over core).
Axes of the slice: x: 2, y: 2, z: 4, core: 2. Of those that a mesh axis runs over, the one named last changes fastest.
Arguments:
- tokens: bfloat16 [32, 3, 16384], P(('parts', 'tensor'), None, ('dp', 'pipe')), parts along dimension 0, may hold values from -6 to 6
- w_query: bfloat16 [16384, 8192], P(('dp', 'pipe'), 'tensor'), may hold values from -0.046875 to 0.046875
- w_key: bfloat16 [16384, 512], P(('dp', 'pipe'), 'tensor'), may hold values from -0.046875 to 0.046875
- w_value: bfloat16 [16384, 512], P(('dp', 'pipe'), 'tensor'), may hold values from -0.046875 to 0.046875
- w_out: bfloat16 [8192, 16384], P('tensor', ('dp', 'pipe')), may hold values from -0.0625 to 0.0625
- shrink_qkv: bfloat16 [16, 16384, 96], P('tensor', ('dp', 'pipe')), may hold values from -0.046875 to 0.046875
- grow_query: bfloat16 [16, 32, 8192], P(('dp', 'pipe'), None, 'tensor'), may hold values from -1 to 1
- grow_key: bfloat16 [16, 32, 512], P(('dp', 'pipe'), None, 'tensor'), may hold values from -1 to 1
- grow_value: bfloat16 [16, 32, 512], P(('dp', 'pipe'), None, 'tensor'), may hold values from -1 to 1
- shrink_out: bfloat16 [16, 8192, 32], P(('dp', 'pipe'), 'tensor'), may hold values from -0.0625 to 0.0625
- grow_out: bfloat16 [16, 32, 16384], P('tensor', None, ('dp', 'pipe')), may hold values from -1 to 1
- cache_keys: bfloat16 [32, 4, 512, 128], P(('parts', 'tensor', 'dp', 'pipe')), parts along dimension 0, may hold values from -64 to 64
- cache_values: bfloat16 [32, 4, 512, 128], P(('parts', 'tensor', 'dp', 'pipe')), parts along dimension 0, may hold values from -6 to 6
- cache_lengths: int32 [32], P(('parts', 'tensor', 'dp', 'pipe')), parts along dimension 0, may hold values from 1 to 512, 4096 in all
- adapter_ids: int32 [16], replicated, may hold values from 0 to 15, as said below
- adapter_slots: int32 [16], replicated, may hold values from 0 to 15, as said below
Outputs:
- attended: bfloat16 [32, 3, 16384], P(('parts', 'tensor'), None, ('dp', 'pipe')), parts along dimension 0
The draws below stay inside these ranges and needn't reach their ends.
There are 2 independent parts, one for each index of `parts`. The reference program is written for one: setup_inputs(seed, part) draws one part's arguments, and reference() takes and returns one part's arrays. A program takes and returns all parts, laid end to end along the dimension named above; an argument that names none is the same for every part. Nothing has to cross between parts.
Inputs may be any that keep to these rules, and one draw needn't show every extreme that they name: `adapter_ids`: take the blocks of requests r with the same r // 4, and those with the same r % 4. The owner of adapter a is adapter_slots[a] // 4. In every block at most 2 requests name adapters of one owner, and in every block some owner is named by exactly 2 requests. `adapter_slots`: A permutation of the pool slots.
All inputs are finite; a program needn't handle non-finite values. No bound on the sum of `cache_lengths` on one device may be relied on, other than what follows from the above.
Results may differ from the reference program's by a relative error of at most 0.03.
Values may be sent and summed in bfloat16 or wider, within the bound.
No kernel may reach another device: no remote copies, remote signals or barrier semaphores. Data moves between devices by JAX's collectives and lax.ppermute only.
A program may use at most 128 MiB of HBM per device.

```python
import math
import jax
import jax.numpy as jnp
import numpy as np
from jax import lax

D = 16384
HQ = 64
KVH = 4
HD = 128
RANK = 32
ADAPT_OWN = 4
CACHE = 512
DRAFT = 3
ADAPTERS = 16
ROWS = 16
N_TENSOR = 4
N_DP = 2
N_PIPE = 2


def adapter_layout(key):
    owner_count = ADAPTERS // ADAPT_OWN
    group_count = ROWS // owner_count
    key_place, key_order, key_flip, key_within = jax.random.split(key, 4)
    placement = jax.random.permutation(key_place, ADAPTERS)
    owner_order = jax.random.permutation(key_order, owner_count)
    tensor_row = jnp.arange(ROWS) // group_count
    group_row = jnp.arange(ROWS) % group_count
    diagonal = (tensor_row + group_row) % owner_count
    flip_bits = jax.random.randint(key_flip, (ROWS,), 0, 2)
    flip_bits = jnp.where(diagonal == 0, 1, jnp.where(diagonal == 1, 0, flip_bits))
    owner_pick = owner_order[(diagonal + flip_bits) % owner_count]
    within = jax.random.randint(key_within, (ROWS,), 0, ADAPT_OWN)
    slot_index = owner_pick * ADAPT_OWN + within
    inverse = jnp.argsort(placement, stable=True)
    chosen_ids = inverse[slot_index]
    return (placement.astype(jnp.int32), chosen_ids.astype(jnp.int32))


def draw_adapter_slots(key, part):
    placement, chosen_ids = adapter_layout(key)
    return placement


def draw_adapter_ids(key, part):
    placement, chosen_ids = adapter_layout(key)
    return chosen_ids


def draw_cache_keys(key, part):
    key = jax.random.fold_in(key, 7)
    key_base = jax.random.fold_in(key, 0)
    array_shape = (ROWS, KVH, CACHE, HD)
    values_base = jnp.clip(jax.random.normal(key_base, array_shape, jnp.float32), -6.0, 6.0)
    return values_base.astype(jnp.bfloat16)


def block_levels(key, extent, shards, low, high):
    def one(position, parts):
        steps = jax.random.uniform(jax.random.fold_in(jax.random.fold_in(key, 6), position), (parts,), jnp.float32, low / len(shards), high / len(shards))
        return jnp.repeat(jnp.exp(steps), extent[position] // parts).reshape((-1,) + (1,) * (len(extent) - position - 1))

    loudness = one(*shards[0])
    for cut in shards[1:]:
        loudness = loudness * one(*cut)
    return loudness


def length_profile(amount, total, limit, skew):
    portions = [(1 << 20) // math.isqrt(standing ** skew) + 1 for standing in range(2, amount + 1)]
    rest, given = total - limit - (amount - 1), [1] * (amount - 1)
    while rest > 0:
        candidates = [i for i in range(amount - 1) if given[i] < limit]
        whole, left = sum([portions[i] for i in candidates]), rest
        for i in candidates:
            more = min(limit - given[i], max(1, left * portions[i] // whole), rest)
            given[i] = given[i] + more
            rest = rest - more
    return np.array([limit] + given)


def ragged(stream_key, number_of, total, most, skew):
    if number_of == 2:
        one = jax.random.randint(stream_key, (), max(1, total - most), min(most, total - 1) + 1)
        return jnp.stack([one, total - one])
    lengths = jnp.asarray(length_profile(number_of, total, most, skew), jnp.int32)
    twos = (number_of - 1) // 2
    donor, taker = lengths[1:1 + 2 * twos:2], lengths[2:2 + 2 * twos:2]
    margin = jnp.minimum(donor - 1, most - taker)
    moved = jax.random.randint(jax.random.fold_in(stream_key, 1), (twos,), 0, 1 << 20) % (margin + 1)
    lengths = lengths.at[1:1 + 2 * twos:2].set(donor - moved).at[2:2 + 2 * twos:2].set(taker + moved)
    return lengths[jax.random.permutation(jax.random.fold_in(stream_key, 2), number_of)]


def normal_values(stream_key, extent, scale, reach, pieces=(), kind=jnp.bfloat16):
    loudness = block_levels(stream_key, extent, pieces, -0.22, 0.18) if pieces else 1.0
    result = jax.random.normal(stream_key, extent, jnp.float32) * scale * loudness
    return jnp.minimum(jnp.maximum(result, -reach), reach).astype(kind)


def setup_inputs(seed: int = 0, part: int = 0) -> dict:
    key_of = jax.random.split(jax.random.key(seed), 17)
    part_keys = jax.random.split(jax.random.fold_in(key_of[16], part), 17)
    return {
        "tokens": normal_values(part_keys[0], (ROWS, DRAFT, D), 1.0, 6.0, ((0, 4), (2, 4))),
        "w_query": normal_values(key_of[1], (D, HQ * HD), D ** -0.5, 0.046875, ((0, 4), (1, 4))),
        "w_key": normal_values(key_of[2], (D, KVH * HD), D ** -0.5, 0.046875, ((0, 4), (1, 4))),
        "w_value": normal_values(key_of[3], (D, KVH * HD), D ** -0.5, 0.046875, ((0, 4), (1, 4))),
        "w_out": normal_values(key_of[4], (HQ * HD, D), (HQ * HD) ** -0.5, 0.0625, ((0, 4), (1, 4))),
        "shrink_qkv": normal_values(key_of[5], (ADAPTERS, D, 3 * RANK), D ** -0.5, 0.046875, ((0, 4), (1, 4))),
        "grow_query": normal_values(key_of[6], (ADAPTERS, RANK, HQ * HD), RANK ** -0.5, 1.0, ((0, 4), (2, 4))),
        "grow_key": normal_values(key_of[7], (ADAPTERS, RANK, KVH * HD), RANK ** -0.5, 1.0, ((0, 4), (2, 4))),
        "grow_value": normal_values(key_of[8], (ADAPTERS, RANK, KVH * HD), RANK ** -0.5, 1.0, ((0, 4), (2, 4))),
        "shrink_out": normal_values(key_of[9], (ADAPTERS, HQ * HD, RANK), (HQ * HD) ** -0.5, 0.0625, ((0, 4), (1, 4))),
        "grow_out": normal_values(key_of[10], (ADAPTERS, RANK, D), RANK ** -0.5, 1.0, ((0, 4), (2, 4))),
        "cache_keys": draw_cache_keys(jax.random.fold_in(jax.random.fold_in(key_of[16], part), 71), part),
        "cache_values": normal_values(part_keys[12], (ROWS, KVH, CACHE, HD), 1.0, 6.0, ((0, 16),)),
        "cache_lengths": ragged(part_keys[13], ROWS, ROWS * CACHE // 2, CACHE, 2).astype(jnp.int32),
        "adapter_ids": draw_adapter_ids(jax.random.fold_in(key_of[16], 71), part),
        "adapter_slots": draw_adapter_slots(jax.random.fold_in(key_of[16], 71), part),
    }


rope_base = 500000.0

def rotate(vectors, positions):
    half_size = vectors.shape[-1] // 2
    frequency = rope_base ** (-2.0 * jnp.arange(half_size, dtype=jnp.float32) / vectors.shape[-1])
    angles = positions[:, None, None] * frequency
    cosine = jnp.cos(angles)
    sine_value = jnp.sin(angles)
    first_half = vectors[..., :half_size]
    second = vectors[..., half_size:]
    return jnp.concatenate([first_half * cosine - second * sine_value, second * cosine + first_half * sine_value], -1)

def block_sum(left_matrix, right_matrix, blocks):
    block_size = left_matrix.shape[1] // blocks

    def add_block(block_index, running):
        row_start = jnp.asarray(block_index * block_size).astype(jnp.int32)
        left_part = lax.dynamic_slice_in_dim(left_matrix, row_start, block_size, 1)
        right_part = lax.dynamic_slice_in_dim(right_matrix, row_start, block_size, 0)
        product = jnp.dot(left_part, right_part, preferred_element_type=jnp.float32)
        rounded = lax.optimization_barrier(product.astype(jnp.bfloat16))
        return running + rounded.astype(jnp.float32)
    initial = jnp.zeros((left_matrix.shape[0], right_matrix.shape[1]), jnp.float32)
    return lax.fori_loop(0, blocks, add_block, initial)

def reference(tokens, w_query, w_key, w_value, w_out, shrink_qkv, grow_query, grow_key, grow_value, shrink_out, grow_out, cache_keys, cache_values, cache_lengths, adapter_ids, adapter_slots):
    highest = lax.Precision.HIGHEST
    query_width = HQ * HD
    key_width = KVH * HD
    row_slots = adapter_slots[adapter_ids].astype(jnp.int32)
    weights_in = jnp.concatenate([w_query, w_key, w_value], 1)
    base_sum = block_sum(tokens.reshape(ROWS * DRAFT, D), weights_in, N_DP * N_PIPE).reshape(ROWS, DRAFT, -1)

    def row_ranks(inputs):
        row_tokens, slot_index = inputs
        rank_values = jnp.dot(row_tokens, shrink_qkv[slot_index], preferred_element_type=jnp.float32)
        query_part = jnp.dot(rank_values[:, :RANK], grow_query[slot_index].astype(jnp.float32), precision=highest)
        key_part = jnp.dot(rank_values[:, RANK:2 * RANK], grow_key[slot_index].astype(jnp.float32), precision=highest)
        value_part = jnp.dot(rank_values[:, 2 * RANK:], grow_value[slot_index].astype(jnp.float32), precision=highest)
        return jnp.concatenate([query_part, key_part, value_part], 1)
    deltas = lax.map(row_ranks, (tokens, row_slots))
    joined_rows = (base_sum + deltas).astype(jnp.bfloat16)
    query_heads = joined_rows[:, :, :query_width]
    key_new = joined_rows[:, :, query_width:query_width + key_width]
    value_new = joined_rows[:, :, query_width + key_width:]
    score_scale = 1.0 / math.sqrt(HD)

    def attend(inputs):
        row_query, row_key, row_value, past_keys, past_values, length = inputs
        positions = (length + jnp.arange(DRAFT, dtype=jnp.int32)).astype(jnp.float32)
        query_rot = rotate(row_query.astype(jnp.float32).reshape(DRAFT, HQ, HD), positions).astype(jnp.bfloat16)
        key_rot = rotate(row_key.astype(jnp.float32).reshape(DRAFT, KVH, HD), positions).astype(jnp.bfloat16)
        values_now = row_value.reshape(DRAFT, KVH, HD).astype(jnp.float32)
        grouped = query_rot.astype(jnp.float32).reshape(DRAFT, KVH, HQ // KVH, HD)
        cached = jnp.einsum('skgd,kld->skgl', grouped, past_keys.astype(jnp.float32), precision=highest) * score_scale
        fresh_scores = jnp.einsum('skgd,tkd->skgt', grouped, key_rot.astype(jnp.float32), precision=highest) * score_scale
        cache_mask = jnp.arange(CACHE, dtype=jnp.int32) < length
        draft_mask = jnp.arange(DRAFT)[None, :] <= jnp.arange(DRAFT)[:, None]
        cached = jnp.where(cache_mask[None, None, None, :], cached, -jnp.inf)
        fresh_scores = jnp.where(draft_mask[:, None, None, :], fresh_scores, -jnp.inf)
        row_peak = jnp.maximum(lax.optimization_barrier(jnp.max(cached, -1)), lax.optimization_barrier(jnp.max(fresh_scores, -1)))
        cached_exp = jnp.exp(cached - row_peak[..., None])
        fresh_exp = jnp.exp(fresh_scores - row_peak[..., None])
        denominator = lax.optimization_barrier(jnp.sum(cached_exp, -1)) + lax.optimization_barrier(jnp.sum(fresh_exp, -1))
        cached_prob = (cached_exp / denominator[..., None]).astype(jnp.bfloat16).astype(jnp.float32)
        fresh_prob = (fresh_exp / denominator[..., None]).astype(jnp.bfloat16).astype(jnp.float32)
        mixed = jnp.einsum('skgl,kld->skgd', cached_prob, past_values.astype(jnp.float32), precision=highest)
        mixed = mixed + jnp.einsum('skgt,tkd->skgd', fresh_prob, values_now, precision=highest)
        return mixed.astype(jnp.bfloat16).reshape(DRAFT, HQ * HD)
    mixed_all = lax.map(attend, (query_heads, key_new, value_new, cache_keys, cache_values, cache_lengths))
    out_base = block_sum(mixed_all.reshape(ROWS * DRAFT, HQ * HD), w_out, N_TENSOR).reshape(ROWS, DRAFT, D)

    def out_delta(inputs):
        row_mixed, slot_index = inputs
        out_rank = jnp.dot(row_mixed, shrink_out[slot_index], preferred_element_type=jnp.float32)
        return jnp.dot(out_rank, grow_out[slot_index].astype(jnp.float32), precision=highest)
    deltas_out = lax.map(out_delta, (mixed_all, row_slots))
    return (out_base + deltas_out).astype(jnp.bfloat16)
```

```python
import math

import jax
import jax.numpy as jnp
from jax import lax
from jax.sharding import PartitionSpec as P

rope_base = 500000.0
EVERY = ("tensor", "dp", "pipe")


def rotate(vectors, positions):
    half_size = vectors.shape[-1] // 2
    frequency = rope_base ** (-2.0 * jnp.arange(half_size, dtype=jnp.float32) / vectors.shape[-1])
    angles = positions[:, None, None] * frequency
    cosine = jnp.cos(angles)
    sine_value = jnp.sin(angles)
    first_half = vectors[..., :half_size]
    second = vectors[..., half_size:]
    return jnp.concatenate(
        [first_half * cosine - second * sine_value, second * cosine + first_half * sine_value], -1
    )


def slot_table(adapter_ids, adapter_slots):
    matches = adapter_ids[:, None] == jnp.arange(adapter_slots.shape[0], dtype=jnp.int32)[None, :]
    return jnp.sum(jnp.where(matches, adapter_slots[None, :], 0), axis=1)


def attend(query_heads, key_new, value_new, cache_keys, cache_values, length):
    drafts, head_count, head_size = query_heads.shape
    kv_heads, cache_size, _ = cache_keys.shape
    positions = (length + jnp.arange(drafts, dtype=jnp.int32)).astype(jnp.float32)
    query_rot = rotate(query_heads.astype(jnp.float32), positions).astype(jnp.bfloat16)
    key_rot = rotate(key_new.astype(jnp.float32), positions).astype(jnp.bfloat16)
    grouped = query_rot.reshape(drafts, kv_heads, head_count // kv_heads, head_size)
    score_scale = 1.0 / math.sqrt(head_size)
    cached = (
        jnp.einsum("skgd,kld->skgl", grouped, cache_keys, preferred_element_type=jnp.float32)
        * score_scale
    )
    fresh_scores = (
        jnp.einsum("skgd,tkd->skgt", grouped, key_rot, preferred_element_type=jnp.float32)
        * score_scale
    )
    cache_mask = jnp.arange(cache_size, dtype=jnp.int32) < length
    draft_mask = jnp.arange(drafts)[None, :] <= jnp.arange(drafts)[:, None]
    cached = jnp.where(cache_mask[None, None, None, :], cached, -jnp.inf)
    fresh_scores = jnp.where(draft_mask[:, None, None, :], fresh_scores, -jnp.inf)
    row_peak = jnp.maximum(jnp.max(cached, -1), jnp.max(fresh_scores, -1))
    cached_exp = jnp.exp(cached - row_peak[..., None])
    fresh_exp = jnp.exp(fresh_scores - row_peak[..., None])
    denominator = jnp.sum(cached_exp, -1) + jnp.sum(fresh_exp, -1)
    cached_prob = (cached_exp / denominator[..., None]).astype(jnp.bfloat16)
    fresh_prob = (fresh_exp / denominator[..., None]).astype(jnp.bfloat16)
    mixed = jnp.einsum(
        "skgl,kld->skgd", cached_prob, cache_values, preferred_element_type=jnp.float32
    )
    mixed = mixed + jnp.einsum(
        "skgt,tkd->skgd", fresh_prob, value_new, preferred_element_type=jnp.float32
    )
    return mixed.astype(jnp.bfloat16)


def local(
    tokens,
    w_query,
    w_key,
    w_value,
    w_out,
    shrink_qkv,
    grow_query,
    grow_key,
    grow_value,
    shrink_out,
    grow_out,
    cache_keys,
    cache_values,
    cache_lengths,
    adapter_ids,
    adapter_slots,
):
    splits = lax.axis_size("tensor")
    groups = lax.axis_size(("dp", "pipe"))
    tensor_index = lax.axis_index("tensor")
    group_index = lax.axis_index(("dp", "pipe"))
    local_rows, drafts, feature_width = tokens.shape
    per_owner = shrink_qkv.shape[0]
    rank_size = grow_out.shape[1]
    query_cols = w_query.shape[1]
    key_cols = w_key.shape[1]
    kv_heads = cache_keys.shape[1]
    head_size = cache_keys.shape[3]
    rows = splits * groups
    row_slots = jnp.repeat(slot_table(adapter_ids, adapter_slots), drafts)
    within = jnp.arange(per_owner, dtype=jnp.int32)[None, :]
    width_hot = (row_slots[:, None] == within + tensor_index * per_owner)[:, :, None]
    column_hot = (row_slots[:, None] == within + group_index * per_owner)[:, :, None]

    def spread_ranks(ranks, hot):
        return jnp.where(hot, ranks[:, None, :], 0.0).reshape(rows * drafts, -1).astype(jnp.bfloat16)

    flat_tokens = lax.all_gather(tokens, "tensor", axis=0, tiled=True).reshape(
        rows * drafts, feature_width
    )
    rank_part = jnp.einsum(
        "nd,adr->nar", flat_tokens, shrink_qkv, preferred_element_type=jnp.float32
    )
    rank_part = jnp.sum(jnp.where(width_hot, rank_part, 0.0), 1)
    rank_all = lax.psum(rank_part, EVERY)

    def grown(index, grow):
        ranks = spread_ranks(rank_all[:, index * rank_size : (index + 1) * rank_size], column_hot)
        return jnp.dot(
            ranks, grow.reshape(per_owner * rank_size, -1), preferred_element_type=jnp.float32
        )

    def product(index, weight, grow):
        base = jnp.dot(flat_tokens, weight, preferred_element_type=jnp.float32)
        return (base + grown(index, grow)).astype(jnp.bfloat16).reshape(rows, drafts, -1)

    partial = jnp.concatenate(
        [
            product(0, w_query, grow_query),
            product(1, w_key, grow_key),
            product(2, w_value, grow_value),
        ],
        2,
    )
    arrived = lax.all_to_all(partial, EVERY, split_axis=0, concat_axis=0, tiled=True)
    joined = jnp.sum(
        arrived.reshape(splits, groups, drafts, -1).astype(jnp.float32), 1
    ).astype(jnp.bfloat16)
    joined = jnp.transpose(joined, (1, 0, 2))
    query_heads = joined[:, :, :query_cols].reshape(drafts, -1, head_size)
    key_new = joined[:, :, query_cols : query_cols + key_cols].reshape(drafts, kv_heads, head_size)
    value_new = joined[:, :, query_cols + key_cols :].reshape(drafts, kv_heads, head_size)
    mixed = attend(
        query_heads, key_new, value_new, cache_keys[0], cache_values[0], cache_lengths[0]
    )
    mixed = jnp.transpose(mixed.reshape(drafts, splits, -1), (1, 0, 2))
    outgoing = jnp.repeat(mixed, groups, axis=0)
    flat_heads = lax.all_to_all(
        outgoing, EVERY, split_axis=0, concat_axis=0, tiled=True
    ).reshape(rows * drafts, -1)
    out_part = jnp.einsum(
        "nw,awr->nar", flat_heads, shrink_out, preferred_element_type=jnp.float32
    )
    out_part = jnp.sum(jnp.where(column_hot, out_part, 0.0), 1)
    out_rank = lax.psum(out_part, EVERY)
    out = jnp.dot(flat_heads, w_out, preferred_element_type=jnp.float32)
    out = out + jnp.dot(
        spread_ranks(out_rank, width_hot),
        grow_out.reshape(per_owner * rank_size, -1),
        preferred_element_type=jnp.float32,
    )
    blocks = lax.all_to_all(
        out.astype(jnp.bfloat16).reshape(splits, local_rows, drafts, feature_width),
        "tensor",
        split_axis=0,
        concat_axis=0,
        tiled=True,
    )
    return jnp.sum(blocks.astype(jnp.float32), 0).astype(jnp.bfloat16)


def solution(mesh):
    placed = (
        P(("parts", "tensor"), None, ("dp", "pipe")),
        P(("dp", "pipe"), "tensor"),
        P(("dp", "pipe"), "tensor"),
        P(("dp", "pipe"), "tensor"),
        P("tensor", ("dp", "pipe")),
        P("tensor", ("dp", "pipe"), None),
        P(("dp", "pipe"), None, "tensor"),
        P(("dp", "pipe"), None, "tensor"),
        P(("dp", "pipe"), None, "tensor"),
        P(("dp", "pipe"), "tensor", None),
        P("tensor", None, ("dp", "pipe")),
        P(("parts", "tensor", "dp", "pipe"), None, None, None),
        P(("parts", "tensor", "dp", "pipe"), None, None, None),
        P(("parts", "tensor", "dp", "pipe")),
        P(),
        P(),
    )
    return jax.shard_map(
        local,
        mesh=mesh,
        in_specs=placed,
        out_specs=P(("parts", "tensor"), None, ("dp", "pipe")),
        check_vma=False,
    )
```

```python
import math

import jax
import jax.numpy as jnp
from jax import lax
from jax.sharding import PartitionSpec as P

rope_base = 500000.0
EVERY = ("tensor", "dp", "pipe")


def rotate(vectors, positions):
    half_size = vectors.shape[-1] // 2
    frequency = rope_base ** (-2.0 * jnp.arange(half_size, dtype=jnp.float32) / vectors.shape[-1])
    angles = positions[:, None, None] * frequency
    cosine = jnp.cos(angles)
    sine_value = jnp.sin(angles)
    first_half = vectors[..., :half_size]
    second = vectors[..., half_size:]
    return jnp.concatenate(
        [first_half * cosine - second * sine_value, second * cosine + first_half * sine_value], -1
    )


def to_growers(partial, splits):
    total = None
    for shift in range(splits):
        route = [
            (t * splits + g, ((g + shift) % splits) * splits + t)
            for t in range(splits)
            for g in range(splits)
        ]
        got = lax.ppermute(partial, EVERY, route).astype(jnp.float32)
        total = got if total is None else total + got
    return total


def to_out_growers(partial, splits):
    total = None
    for shift in range(splits):
        route = [
            (t * splits + g, g * splits + (t + shift) % splits)
            for t in range(splits)
            for g in range(splits)
        ]
        got = lax.ppermute(partial, EVERY, route).astype(jnp.float32)
        total = got if total is None else total + got
    return total


def slot_table(adapter_ids, adapter_slots):
    matches = adapter_ids[:, None] == jnp.arange(adapter_slots.shape[0], dtype=jnp.int32)[None, :]
    return jnp.sum(jnp.where(matches, adapter_slots[None, :], 0), axis=1)


def attend(query_heads, key_new, value_new, cache_keys, cache_values, length):
    drafts, head_count, head_size = query_heads.shape
    kv_heads, cache_size, _ = cache_keys.shape
    positions = (length + jnp.arange(drafts, dtype=jnp.int32)).astype(jnp.float32)
    query_rot = rotate(query_heads.astype(jnp.float32), positions).astype(jnp.bfloat16)
    key_rot = rotate(key_new.astype(jnp.float32), positions).astype(jnp.bfloat16)
    grouped = query_rot.reshape(drafts, kv_heads, head_count // kv_heads, head_size)
    score_scale = 1.0 / math.sqrt(head_size)
    cached = (
        jnp.einsum("skgd,kld->skgl", grouped, cache_keys, preferred_element_type=jnp.float32)
        * score_scale
    )
    fresh_scores = (
        jnp.einsum("skgd,tkd->skgt", grouped, key_rot, preferred_element_type=jnp.float32)
        * score_scale
    )
    cache_mask = jnp.arange(cache_size, dtype=jnp.int32) < length
    draft_mask = jnp.arange(drafts)[None, :] <= jnp.arange(drafts)[:, None]
    cached = jnp.where(cache_mask[None, None, None, :], cached, -jnp.inf)
    fresh_scores = jnp.where(draft_mask[:, None, None, :], fresh_scores, -jnp.inf)
    row_peak = jnp.maximum(jnp.max(cached, -1), jnp.max(fresh_scores, -1))
    cached_exp = jnp.exp(cached - row_peak[..., None])
    fresh_exp = jnp.exp(fresh_scores - row_peak[..., None])
    denominator = jnp.sum(cached_exp, -1) + jnp.sum(fresh_exp, -1)
    cached_prob = (cached_exp / denominator[..., None]).astype(jnp.bfloat16)
    fresh_prob = (fresh_exp / denominator[..., None]).astype(jnp.bfloat16)
    mixed = jnp.einsum(
        "skgl,kld->skgd", cached_prob, cache_values, preferred_element_type=jnp.float32
    )
    mixed = mixed + jnp.einsum(
        "skgt,tkd->skgd", fresh_prob, value_new, preferred_element_type=jnp.float32
    )
    return mixed.astype(jnp.bfloat16)


def local(
    tokens,
    w_query,
    w_key,
    w_value,
    w_out,
    shrink_qkv,
    grow_query,
    grow_key,
    grow_value,
    shrink_out,
    grow_out,
    cache_keys,
    cache_values,
    cache_lengths,
    adapter_ids,
    adapter_slots,
):
    splits = lax.axis_size("tensor")
    groups = lax.axis_size(("dp", "pipe"))
    tensor_index = lax.axis_index("tensor")
    group_index = lax.axis_index(("dp", "pipe"))
    local_rows, drafts, feature_width = tokens.shape
    per_owner = shrink_qkv.shape[0]
    rank_size = grow_out.shape[1]
    query_cols = w_query.shape[1]
    key_cols = w_key.shape[1]
    kv_heads = cache_keys.shape[1]
    head_size = cache_keys.shape[3]
    rows = splits * groups
    row_slots = jnp.repeat(slot_table(adapter_ids, adapter_slots), drafts)
    within = jnp.arange(per_owner, dtype=jnp.int32)[None, :]
    width_hot = (row_slots[:, None] == within + tensor_index * per_owner)[:, :, None]
    column_hot = (row_slots[:, None] == within + group_index * per_owner)[:, :, None]

    def spread_ranks(ranks, hot):
        return jnp.where(hot, ranks[:, None, :], 0.0).reshape(rows * drafts, -1).astype(jnp.bfloat16)

    flat_tokens = lax.all_gather(tokens, "tensor", axis=0, tiled=True).reshape(
        rows * drafts, feature_width
    )
    rank_part = jnp.einsum(
        "nd,adr->nar", flat_tokens, shrink_qkv, preferred_element_type=jnp.float32
    )
    rank_part = jnp.sum(jnp.where(width_hot, rank_part, 0.0), 1)
    rank_all = to_growers(rank_part.astype(jnp.bfloat16), splits)

    def grown(index, grow):
        ranks = spread_ranks(rank_all[:, index * rank_size : (index + 1) * rank_size], column_hot)
        return jnp.dot(
            ranks, grow.reshape(per_owner * rank_size, -1), preferred_element_type=jnp.float32
        )

    bases = [
        jnp.dot(flat_tokens, weight, preferred_element_type=jnp.float32)
        for weight in (w_query, w_key, w_value)
    ]

    def product(index, grow):
        return (bases[index] + grown(index, grow)).astype(jnp.bfloat16).reshape(rows, drafts, -1)

    partial = jnp.concatenate(
        [
            product(0, grow_query),
            product(1, grow_key),
            product(2, grow_value),
        ],
        2,
    )
    arrived = lax.all_to_all(partial, EVERY, split_axis=0, concat_axis=0, tiled=True)
    joined = jnp.sum(
        arrived.reshape(splits, groups, drafts, -1).astype(jnp.float32), 1
    ).astype(jnp.bfloat16)
    joined = jnp.transpose(joined, (1, 0, 2))
    query_heads = joined[:, :, :query_cols].reshape(drafts, -1, head_size)
    key_new = joined[:, :, query_cols : query_cols + key_cols].reshape(drafts, kv_heads, head_size)
    value_new = joined[:, :, query_cols + key_cols :].reshape(drafts, kv_heads, head_size)
    mixed = attend(
        query_heads, key_new, value_new, cache_keys[0], cache_values[0], cache_lengths[0]
    )
    mixed = jnp.transpose(mixed.reshape(drafts, splits, -1), (1, 0, 2))
    outgoing = jnp.repeat(mixed, groups, axis=0)
    flat_heads = lax.all_to_all(
        outgoing, EVERY, split_axis=0, concat_axis=0, tiled=True
    ).reshape(rows * drafts, -1)
    out_part = jnp.einsum(
        "nw,awr->nar", flat_heads, shrink_out, preferred_element_type=jnp.float32
    )
    out_part = jnp.sum(jnp.where(column_hot, out_part, 0.0), 1)
    out_rank = to_out_growers(out_part.astype(jnp.bfloat16), splits)
    out = jnp.dot(flat_heads, w_out, preferred_element_type=jnp.float32)
    out = out + jnp.dot(
        spread_ranks(out_rank, width_hot),
        grow_out.reshape(per_owner * rank_size, -1),
        preferred_element_type=jnp.float32,
    )
    blocks = lax.all_to_all(
        out.astype(jnp.bfloat16).reshape(splits, local_rows, drafts, feature_width),
        "tensor",
        split_axis=0,
        concat_axis=0,
        tiled=True,
    )
    return jnp.sum(blocks.astype(jnp.float32), 0).astype(jnp.bfloat16)


def solution(mesh):
    placed = (
        P(("parts", "tensor"), None, ("dp", "pipe")),
        P(("dp", "pipe"), "tensor"),
        P(("dp", "pipe"), "tensor"),
        P(("dp", "pipe"), "tensor"),
        P("tensor", ("dp", "pipe")),
        P("tensor", ("dp", "pipe"), None),
        P(("dp", "pipe"), None, "tensor"),
        P(("dp", "pipe"), None, "tensor"),
        P(("dp", "pipe"), None, "tensor"),
        P(("dp", "pipe"), "tensor", None),
        P("tensor", None, ("dp", "pipe")),
        P(("parts", "tensor", "dp", "pipe"), None, None, None),
        P(("parts", "tensor", "dp", "pipe"), None, None, None),
        P(("parts", "tensor", "dp", "pipe")),
        P(),
        P(),
    )
    return jax.shard_map(
        local,
        mesh=mesh,
        in_specs=placed,
        out_specs=P(("parts", "tensor"), None, ("dp", "pipe")),
        check_vma=False,
    )
```

```python
import functools
import math

import jax
import jax.numpy as jnp
from jax import lax
from jax.experimental import pallas as pl
from jax.experimental.pallas import tpu as pltpu
from jax.sharding import PartitionSpec as P

rope_base = 500000.0
EVERY = ("tensor", "dp", "pipe")
GROUP = ("dp", "pipe")
VMEM = pl.BlockSpec(memory_space=pltpu.VMEM)
HBM = pl.BlockSpec(memory_space=pltpu.HBM)
MIB = 1 << 20


def dot(left, right):
    return jnp.dot(left, right, preferred_element_type=jnp.float32)


def dot_nt(left, right):
    return lax.dot_general(
        left, right, (((1,), (1,)), ((), ())), preferred_element_type=jnp.float32
    )


def iota(shape, axis):
    return lax.broadcasted_iota(jnp.int32, shape, axis)


def call(kernel, outs, ins, scratch=(), flops=0, moved=0, limit=24 * MIB):
    return pl.pallas_call(
        kernel,
        out_shape=outs,
        in_specs=ins,
        out_specs=jax.tree.map(lambda _: VMEM, outs),
        scratch_shapes=list(scratch),
        cost_estimate=pl.CostEstimate(flops=flops, bytes_accessed=moved, transcendentals=0),
        compiler_params=pltpu.CompilerParams(vmem_limit_bytes=limit),
    )


def shape(dims, kind=jnp.bfloat16):
    return jax.ShapeDtypeStruct(tuple(dims), kind)


def over(value, size):
    return value >> (size.bit_length() - 1) if size & (size - 1) == 0 else lax.div(value, size)


def rest_of(value, size):
    return value & (size - 1) if size & (size - 1) == 0 else lax.rem(value, size)


def block_first(sizes, group, block, draft):
    groups, blocks, drafts = sizes
    return (block * drafts + draft) * groups + group


def group_first(sizes, group, block, draft):
    groups, blocks, drafts = sizes
    return (group * blocks + block) * drafts + draft


def parts_of(order, sizes, index):
    groups, blocks, drafts = sizes
    if order is block_first:
        return (
            rest_of(index, groups),
            over(index, groups * drafts),
            rest_of(over(index, groups), drafts),
        )
    return over(index, blocks * drafts), rest_of(over(index, drafts), blocks), rest_of(index, drafts)


def reorder(sizes, after, before, turn_block, turn_group=0):
    groups, blocks, drafts = sizes
    rows = groups * blocks * drafts
    group, block, draft = parts_of(after, sizes, iota((rows, rows), 0))
    wanted = before(
        sizes, rest_of(group + turn_group, groups), rest_of(block + turn_block, blocks), draft
    )
    return jnp.where(wanted == iota((rows, rows), 1), 1.0, 0.0).astype(jnp.bfloat16)


def rank_kernel(blocks, drafts, groups, *refs):
    pieces = refs[:blocks]
    shrink_ref, place_ref, rows_ref, rank_ref, wide = refs[blocks:]
    for block in range(blocks):
        for draft in range(drafts):
            start = (block * drafts + draft) * groups
            wide[start : start + groups, :] = pieces[block][draft].astype(jnp.float32)
    rows = wide[...].astype(jnp.bfloat16)
    rows_ref[...] = rows
    rank_ref[...] = owned_ranks(rows, shrink_ref[...], place_ref[...], rank_ref.shape[1])


def owned_ranks(rows, shrink, place, width):
    ranks = dot_nt(rows, shrink)
    columns = iota(ranks.shape, 1)
    kept = jnp.where(over(columns, width) == place, ranks, 0.0).astype(jnp.bfloat16)
    fold = rest_of(iota((ranks.shape[1], width), 0), width) == iota((ranks.shape[1], width), 1)
    return dot(kept, jnp.where(fold, 1.0, 0.0).astype(jnp.bfloat16)).astype(jnp.bfloat16)


def spread_ranks(ranks, place, width, owned):
    parts = ranks.shape[1] // width
    span = owned * width
    row = iota((ranks.shape[1], parts * span), 0)
    column = iota((ranks.shape[1], parts * span), 1)
    tile = (over(row, width) == over(column, span)) & (
        rest_of(row, width) == rest_of(column, width)
    )
    wide = dot(ranks, jnp.where(tile, 1.0, 0.0).astype(jnp.bfloat16))
    slot = over(rest_of(iota(wide.shape, 1), span), width)
    return jnp.where(slot == place, wide, 0.0).astype(jnp.bfloat16)


def stream_kernel(weights, chunks, rows_ref, *refs):
    sources = refs[:weights]
    total_ref, buffer, sems = refs[weights:]
    depth = rows_ref.shape[1] // chunks

    def copy(chunk, index):
        part = pl.ds(chunk * depth, depth)
        start = sum(source.shape[1] for source in sources[:index])
        return pltpu.make_async_copy(
            sources[index].at[part],
            buffer.at[part, pl.ds(start, sources[index].shape[1])],
            sems.at[chunk, index],
        )

    for chunk in range(chunks):
        for index in range(weights):
            copy(chunk, index).start()
    for chunk in range(chunks):
        for index in range(weights):
            copy(chunk, index).wait()
        product = dot(
            rows_ref[:, chunk * depth : (chunk + 1) * depth],
            buffer[chunk * depth : (chunk + 1) * depth, :],
        )
        if chunk == 0:
            total_ref[...] = product
        else:
            total_ref[...] += product


def stream(rows, weights, chunks):
    width = sum(w.shape[1] for w in weights)
    return call(
        functools.partial(stream_kernel, len(weights), chunks),
        shape((rows.shape[0], width), jnp.float32),
        [VMEM] + [HBM] * len(weights),
        [
            pltpu.VMEM((rows.shape[1], width), jnp.bfloat16),
            pltpu.SemaphoreType.DMA((chunks, len(weights))),
        ],
        2 * rows.shape[0] * rows.shape[1] * width,
        2 * rows.shape[1] * width,
        40 * MIB,
    )(rows, *weights)


def pack_kernel(blocks, keys_ref, values_ref, extra_ref, *refs):
    outs = refs[:blocks]
    sems = refs[blocks]
    size = keys_ref.shape[2]
    me = lax.axis_index("tensor")
    copies = []
    for shift in range(blocks):
        head = lax.rem(me + shift, blocks)
        copies += [
            pltpu.make_async_copy(
                keys_ref.at[0, head], outs[shift].at[pl.ds(0, size)], sems.at[shift, 0]
            ),
            pltpu.make_async_copy(
                values_ref.at[0, head], outs[shift].at[pl.ds(size, size)], sems.at[shift, 1]
            ),
            pltpu.make_async_copy(
                extra_ref,
                outs[shift].at[pl.ds(2 * size, extra_ref.shape[0])],
                sems.at[shift, 2],
            ),
        ]
    for copy in copies:
        copy.start()
    for copy in copies:
        copy.wait()


def pack(blocks, keys, values, extra):
    rows = 2 * keys.shape[2] + extra.shape[0]
    outs = [shape((rows, keys.shape[3]))] * blocks
    return pl.pallas_call(
        functools.partial(pack_kernel, blocks),
        out_shape=outs,
        in_specs=[HBM, HBM, VMEM],
        out_specs=[HBM] * blocks,
        scratch_shapes=[pltpu.SemaphoreType.DMA((blocks, 3))],
        cost_estimate=pl.CostEstimate(flops=0, bytes_accessed=8 * keys.size, transcendentals=0),
        compiler_params=pltpu.CompilerParams(vmem_limit_bytes=24 * MIB),
    )(keys, values, extra)


def grow_kernel(blocks, drafts, groups, width, *refs):
    total_ref, place_ref, turn_ref, *rest = refs
    ranks_in = rest[:blocks]
    grows = rest[blocks : blocks + 3]
    outs = rest[blocks + 3 :]
    sizes = (groups, blocks, drafts)
    ranks = ranks_in[0][...].astype(jnp.float32)
    for other in ranks_in[1:]:
        ranks = ranks + other[...].astype(jnp.float32)
    ranks = dot(
        reorder(sizes, block_first, block_first, turn_ref[0]), ranks.astype(jnp.bfloat16)
    )
    wide = spread_ranks(
        ranks.astype(jnp.bfloat16), place_ref[...], width, grows[0].shape[0] // width
    )
    by_group = reorder(sizes, group_first, block_first, 0, turn_ref[1])
    start = 0
    for index, grow in enumerate(grows):
        deep, cols = grow.shape
        full = total_ref[:, start : start + cols] + dot(
            wide[:, index * deep : (index + 1) * deep], grow[...]
        )
        full = dot(by_group, full.astype(jnp.bfloat16)).astype(jnp.bfloat16)
        for step in range(groups):
            for block in range(blocks):
                row = (step * blocks + block) * drafts
                outs[step][block, :, start : start + cols] = full[row : row + drafts]
        start += cols


def attend_kernel(blocks, drafts, groups, cache_size, *refs):
    parts = refs[:groups]
    caches = refs[groups : groups + blocks]
    mixed_ref, query_s, fresh_s, out_s = refs[groups + blocks :]
    head_size = caches[0].shape[1]
    cols = parts[0].shape[2]
    heads = cols // head_size - 2
    count = heads * drafts
    scale = 1.0 / math.sqrt(head_size)
    fresh_s[...] = jnp.zeros(fresh_s.shape, jnp.float32)
    pad = fresh_s.shape[1]
    for block in range(blocks):
        joined = parts[0][block].astype(jnp.float32)
        for other in parts[1:]:
            joined = joined + other[block].astype(jnp.float32)
        joined = joined.astype(jnp.bfloat16).astype(jnp.float32)
        extra = caches[block][2 * cache_size :, :].astype(jnp.float32)
        cosine = extra[0:drafts] + extra[drafts : 2 * drafts]
        sine = extra[2 * drafts : 3 * drafts] + extra[3 * drafts : 4 * drafts]
        length = extra[4 * drafts : 4 * drafts + 1, 0:1] * 16.0 + extra[
            4 * drafts + 1 : 4 * drafts + 2, 0:1
        ]

        def rotated(head):
            value = joined[:, head * head_size : (head + 1) * head_size]
            return value * cosine + pltpu.roll(value, head_size // 2, 1) * sine

        for head in range(heads):
            query_s[block, head * drafts : (head + 1) * drafts, :] = rotated(head)
        fresh_s[2 * block, 0:drafts, :] = rotated(heads)
        fresh_s[2 * block + 1, 0:drafts, :] = joined[:, (heads + 1) * head_size :]
        query = query_s[block].astype(jnp.bfloat16)
        old = dot_nt(query, caches[block][0:cache_size, :]) * scale
        new = dot_nt(query, fresh_s[2 * block].astype(jnp.bfloat16)) * scale
        old_seen = iota(old.shape, 1).astype(jnp.float32) < length
        new_seen = iota(new.shape, 1) <= lax.rem(iota(new.shape, 0), drafts)
        old = jnp.where(old_seen, old, -jnp.inf)
        new = jnp.where(new_seen, new, -jnp.inf)
        peak = jnp.maximum(
            jnp.max(old, 1, keepdims=True), jnp.max(new, 1, keepdims=True)
        )
        old = jnp.exp(old - peak)
        new = jnp.exp(new - peak)
        below = jnp.sum(old, 1, keepdims=True) + jnp.sum(new, 1, keepdims=True)
        mixed = dot(
            (old / below).astype(jnp.bfloat16), caches[block][cache_size : 2 * cache_size, :]
        ) + dot((new / below).astype(jnp.bfloat16), fresh_s[2 * block + 1].astype(jnp.bfloat16))
        for head in range(heads):
            out_s[
                block * drafts : (block + 1) * drafts, head * head_size : (head + 1) * head_size
            ] = mixed[head * drafts : (head + 1) * drafts]
    mixed_ref[...] = out_s[...].astype(jnp.bfloat16)


def out_rank_kernel(span, got_ref, shrink_ref, place_ref, rows_ref, rank_ref, wide):
    for group in range(got_ref.shape[0]):
        wide[group * span : (group + 1) * span, :] = got_ref[group].astype(jnp.float32)
    rows = wide[...].astype(jnp.bfloat16)
    rows_ref[...] = rows
    rank_ref[...] = owned_ranks(rows, shrink_ref[...], place_ref[...], rank_ref.shape[1])


def out_grow_kernel(blocks, drafts, groups, *refs):
    total_ref, place_ref, turn_ref, *rest = refs
    ranks_in = rest[:blocks]
    grow_ref = rest[blocks]
    outs = rest[blocks + 1 :]
    sizes = (groups, blocks, drafts)
    width = ranks_in[0].shape[1]
    ranks = None
    for index, part in enumerate(ranks_in):
        moved = dot(reorder(sizes, group_first, group_first, turn_ref[index]), part[...])
        ranks = moved if ranks is None else ranks + moved
    wide = spread_ranks(
        ranks.astype(jnp.bfloat16), place_ref[...], width, grow_ref.shape[0] // width
    )
    full = (total_ref[...] + dot(wide, grow_ref[...])).astype(jnp.bfloat16)
    full = dot(reorder(sizes, block_first, group_first, 0), full).astype(jnp.bfloat16)
    for block in range(blocks):
        for draft in range(drafts):
            start = (block * drafts + draft) * groups
            outs[block][draft] = full[start : start + groups]


def halves(value):
    high = value.astype(jnp.bfloat16)
    return high, (value - high.astype(jnp.float32)).astype(jnp.bfloat16)


def by_head(
    tokens,
    w_query,
    w_key,
    w_value,
    w_out,
    shrink_qkv,
    grow_query,
    grow_key,
    grow_value,
    shrink_out,
    grow_out,
    cache_keys,
    cache_values,
    cache_lengths,
    adapter_ids,
    adapter_slots,
):
    blocks = lax.axis_size("tensor")
    groups = lax.axis_size(GROUP)
    tensor_index = lax.axis_index("tensor")
    group_index = lax.axis_index(GROUP)
    _, drafts, features = tokens.shape
    owned = shrink_qkv.shape[0]
    width = grow_out.shape[1]
    cache_size, head_size = cache_keys.shape[2:]
    span = blocks * drafts
    count = groups * span

    def over_tensor(value, shift):
        route = [(t, (t + shift) % blocks) for t in range(blocks)]
        return lax.ppermute(value, "tensor", route)

    def over_group(value, shift):
        route = [(g, (g + shift) % groups) for g in range(groups)]
        return lax.ppermute(value, GROUP, route)

    def to_growers(value, shift):
        route = [
            (t * groups + g, ((g + shift) % blocks) * groups + t)
            for t in range(blocks)
            for g in range(groups)
        ]
        return lax.ppermute(value, EVERY, route)

    def to_out_growers(value, shift):
        route = [
            (t * groups + g, g * groups + (t + shift) % groups)
            for t in range(blocks)
            for g in range(groups)
        ]
        return lax.ppermute(value, EVERY, route)

    mine = jnp.transpose(tokens, (1, 0, 2))
    pieces = [mine] + [over_tensor(mine, shift) for shift in range(1, blocks)]

    length = cache_lengths[0]
    positions = (length + jnp.arange(drafts, dtype=jnp.int32)).astype(jnp.float32)
    half_size = head_size // 2
    frequency = rope_base ** (-2.0 * jnp.arange(half_size, dtype=jnp.float32) / head_size)
    angles = positions[:, None] * frequency
    cosine = jnp.cos(angles)
    sine = jnp.sin(angles)
    cos_high, cos_low = halves(jnp.concatenate([cosine, cosine], 1))
    sin_high, sin_low = halves(jnp.concatenate([-sine, sine], 1))
    spell = jnp.stack([length // 16, length % 16]).astype(jnp.bfloat16)
    used = 4 * drafts + 2
    extra = jnp.concatenate(
        [
            cos_high,
            cos_low,
            sin_high,
            sin_low,
            jnp.broadcast_to(spell[:, None], (2, head_size)),
            jnp.zeros((-used % 16, head_size), jnp.bfloat16),
        ],
        0,
    )

    messages = pack(blocks, cache_keys, cache_values, extra)
    caches = [messages[0]] + [over_tensor(messages[shift], shift) for shift in range(1, blocks)]

    matches = adapter_ids[:, None] == jnp.arange(adapter_slots.shape[0], dtype=jnp.int32)[None, :]
    row_slots = jnp.sum(jnp.where(matches, adapter_slots[None, :], 0), axis=1)
    turned = (tensor_index - jnp.arange(blocks, dtype=jnp.int32)) % blocks
    places = turned[None, :] * groups + jnp.arange(groups, dtype=jnp.int32)[:, None]
    slots = jnp.sum(
        jnp.where(
            places[:, :, None] == jnp.arange(blocks * groups, dtype=jnp.int32), row_slots, 0
        ),
        -1,
    )
    group_slots = jnp.broadcast_to(slots[:, :, None], (groups, blocks, drafts)).reshape(count, 1)
    block_slots = jnp.broadcast_to(slots.T[:, None, :], (blocks, drafts, groups)).reshape(count, 1)
    first_width = block_slots - tensor_index * owned
    first_column = block_slots - group_index * owned
    last_width = group_slots - tensor_index * owned
    last_column = group_slots - group_index * owned

    shrink_in = jnp.transpose(shrink_qkv, (0, 2, 1)).reshape(-1, features)
    rows, rank_part = call(
        functools.partial(rank_kernel, blocks, drafts, groups),
        [shape((count, features)), shape((count, shrink_qkv.shape[2]))],
        [VMEM] * (blocks + 2),
        [pltpu.VMEM((count, features), jnp.float32)],
        2 * count * shrink_qkv.size,
        2 * shrink_qkv.size + 4 * count * features,
    )(*pieces, shrink_in, first_width)
    ranks = [to_growers(rank_part, shift) for shift in range(blocks)]
    weights_in = (w_query, w_key, w_value)
    total = stream(rows, weights_in, 8)
    cols = total.shape[1]
    turn = jnp.stack([(group_index - tensor_index) % blocks, group_index]).astype(jnp.int32)
    sent = call(
        functools.partial(grow_kernel, blocks, drafts, groups, width),
        [shape((blocks, drafts, cols))] * groups,
        [VMEM, VMEM, pl.BlockSpec(memory_space=pltpu.SMEM)] + [VMEM] * (blocks + 3),
        [],
        2 * count * owned * width * cols,
        8 * count * cols + 2 * owned * width * cols,
    )(
        total,
        first_column,
        turn,
        *ranks,
        *[grow.reshape(owned * width, -1) for grow in (grow_query, grow_key, grow_value)],
    )
    parts = [sent[0]] + [over_group(sent[shift], shift) for shift in range(1, groups)]
    head_cols = cols - 2 * head_size
    mixed = call(
        functools.partial(attend_kernel, blocks, drafts, groups, cache_size),
        shape((span, head_cols)),
        [VMEM] * (groups + blocks),
        [
            pltpu.VMEM((blocks, head_cols // head_size * drafts, head_size), jnp.float32),
            pltpu.VMEM((2 * blocks, 128, head_size), jnp.float32),
            pltpu.VMEM((span, head_cols), jnp.float32),
        ],
        4 * span * head_cols * cache_size,
        4 * blocks * cache_size * head_size,
    )(*parts, *caches)
    gathered = lax.all_gather(mixed, GROUP, axis=0, tiled=False)
    out_rows, out_part = call(
        functools.partial(out_rank_kernel, span),
        [shape((count, head_cols)), shape((count, width))],
        [VMEM] * 3,
        [pltpu.VMEM((count, head_cols), jnp.float32)],
        2 * count * shrink_out.size,
        2 * shrink_out.size + 4 * count * head_cols,
    )(gathered, jnp.transpose(shrink_out, (0, 2, 1)).reshape(-1, head_cols), last_column)
    out_ranks = [to_out_growers(out_part, shift) for shift in range(groups)]
    out_total = stream(out_rows, (w_out,), 8)
    out_cols = out_total.shape[1]
    out_turn = (
        (group_index - tensor_index - jnp.arange(groups, dtype=jnp.int32)) % blocks
    ).astype(jnp.int32)
    leaving = call(
        functools.partial(out_grow_kernel, blocks, drafts, groups),
        [shape((drafts, groups, out_cols))] * blocks,
        [VMEM, VMEM, pl.BlockSpec(memory_space=pltpu.SMEM)] + [VMEM] * (groups + 1),
        [],
        2 * count * owned * width * out_cols,
        8 * count * out_cols + 2 * owned * width * out_cols,
    )(out_total, last_width, out_turn, *out_ranks, grow_out.reshape(owned * width, -1))
    result = leaving[0].astype(jnp.float32)
    for shift in range(1, blocks):
        result = result + over_tensor(leaving[shift], -shift).astype(jnp.float32)
    return jnp.transpose(result.astype(jnp.bfloat16), (1, 0, 2))


def rotate(vectors, positions):
    half_size = vectors.shape[-1] // 2
    frequency = rope_base ** (-2.0 * jnp.arange(half_size, dtype=jnp.float32) / vectors.shape[-1])
    angles = positions[:, None, None] * frequency
    cosine = jnp.cos(angles)
    sine_value = jnp.sin(angles)
    first_half = vectors[..., :half_size]
    second = vectors[..., half_size:]
    return jnp.concatenate(
        [first_half * cosine - second * sine_value, second * cosine + first_half * sine_value], -1
    )


def to_growers(partial, splits):
    total = None
    for shift in range(splits):
        route = [
            (t * splits + g, ((g + shift) % splits) * splits + t)
            for t in range(splits)
            for g in range(splits)
        ]
        got = lax.ppermute(partial, EVERY, route).astype(jnp.float32)
        total = got if total is None else total + got
    return total


def to_out_growers(partial, splits):
    total = None
    for shift in range(splits):
        route = [
            (t * splits + g, g * splits + (t + shift) % splits)
            for t in range(splits)
            for g in range(splits)
        ]
        got = lax.ppermute(partial, EVERY, route).astype(jnp.float32)
        total = got if total is None else total + got
    return total


def slot_table(adapter_ids, adapter_slots):
    matches = adapter_ids[:, None] == jnp.arange(adapter_slots.shape[0], dtype=jnp.int32)[None, :]
    return jnp.sum(jnp.where(matches, adapter_slots[None, :], 0), axis=1)


def attend(query_heads, key_new, value_new, cache_keys, cache_values, length):
    drafts, head_count, head_size = query_heads.shape
    kv_heads, cache_size, _ = cache_keys.shape
    positions = (length + jnp.arange(drafts, dtype=jnp.int32)).astype(jnp.float32)
    query_rot = rotate(query_heads.astype(jnp.float32), positions).astype(jnp.bfloat16)
    key_rot = rotate(key_new.astype(jnp.float32), positions).astype(jnp.bfloat16)
    grouped = query_rot.reshape(drafts, kv_heads, head_count // kv_heads, head_size)
    score_scale = 1.0 / math.sqrt(head_size)
    cached = (
        jnp.einsum("skgd,kld->skgl", grouped, cache_keys, preferred_element_type=jnp.float32)
        * score_scale
    )
    fresh_scores = (
        jnp.einsum("skgd,tkd->skgt", grouped, key_rot, preferred_element_type=jnp.float32)
        * score_scale
    )
    cache_mask = jnp.arange(cache_size, dtype=jnp.int32) < length
    draft_mask = jnp.arange(drafts)[None, :] <= jnp.arange(drafts)[:, None]
    cached = jnp.where(cache_mask[None, None, None, :], cached, -jnp.inf)
    fresh_scores = jnp.where(draft_mask[:, None, None, :], fresh_scores, -jnp.inf)
    row_peak = jnp.maximum(jnp.max(cached, -1), jnp.max(fresh_scores, -1))
    cached_exp = jnp.exp(cached - row_peak[..., None])
    fresh_exp = jnp.exp(fresh_scores - row_peak[..., None])
    denominator = jnp.sum(cached_exp, -1) + jnp.sum(fresh_exp, -1)
    cached_prob = (cached_exp / denominator[..., None]).astype(jnp.bfloat16)
    fresh_prob = (fresh_exp / denominator[..., None]).astype(jnp.bfloat16)
    mixed = jnp.einsum(
        "skgl,kld->skgd", cached_prob, cache_values, preferred_element_type=jnp.float32
    )
    mixed = mixed + jnp.einsum(
        "skgt,tkd->skgd", fresh_prob, value_new, preferred_element_type=jnp.float32
    )
    return mixed.astype(jnp.bfloat16)


def by_row(
    tokens,
    w_query,
    w_key,
    w_value,
    w_out,
    shrink_qkv,
    grow_query,
    grow_key,
    grow_value,
    shrink_out,
    grow_out,
    cache_keys,
    cache_values,
    cache_lengths,
    adapter_ids,
    adapter_slots,
):
    splits = lax.axis_size("tensor")
    groups = lax.axis_size(("dp", "pipe"))
    tensor_index = lax.axis_index("tensor")
    group_index = lax.axis_index(("dp", "pipe"))
    local_rows, drafts, feature_width = tokens.shape
    per_owner = shrink_qkv.shape[0]
    rank_size = grow_out.shape[1]
    query_cols = w_query.shape[1]
    key_cols = w_key.shape[1]
    kv_heads = cache_keys.shape[1]
    head_size = cache_keys.shape[3]
    rows = splits * groups
    row_slots = jnp.repeat(slot_table(adapter_ids, adapter_slots), drafts)
    within = jnp.arange(per_owner, dtype=jnp.int32)[None, :]
    width_hot = (row_slots[:, None] == within + tensor_index * per_owner)[:, :, None]
    column_hot = (row_slots[:, None] == within + group_index * per_owner)[:, :, None]

    def spread_ranks(ranks, hot):
        return jnp.where(hot, ranks[:, None, :], 0.0).reshape(rows * drafts, -1).astype(jnp.bfloat16)

    flat_tokens = lax.all_gather(tokens, "tensor", axis=0, tiled=True).reshape(
        rows * drafts, feature_width
    )
    rank_part = jnp.einsum(
        "nd,adr->nar", flat_tokens, shrink_qkv, preferred_element_type=jnp.float32
    )
    rank_part = jnp.sum(jnp.where(width_hot, rank_part, 0.0), 1)
    rank_all = to_growers(rank_part.astype(jnp.bfloat16), splits)

    def grown(index, grow):
        ranks = spread_ranks(rank_all[:, index * rank_size : (index + 1) * rank_size], column_hot)
        return jnp.dot(
            ranks, grow.reshape(per_owner * rank_size, -1), preferred_element_type=jnp.float32
        )

    bases = [
        jnp.dot(flat_tokens, weight, preferred_element_type=jnp.float32)
        for weight in (w_query, w_key, w_value)
    ]

    def product(index, grow):
        return (bases[index] + grown(index, grow)).astype(jnp.bfloat16).reshape(rows, drafts, -1)

    partial = jnp.concatenate(
        [
            product(0, grow_query),
            product(1, grow_key),
            product(2, grow_value),
        ],
        2,
    )
    arrived = lax.all_to_all(partial, EVERY, split_axis=0, concat_axis=0, tiled=True)
    joined = jnp.sum(
        arrived.reshape(splits, groups, drafts, -1).astype(jnp.float32), 1
    ).astype(jnp.bfloat16)
    joined = jnp.transpose(joined, (1, 0, 2))
    query_heads = joined[:, :, :query_cols].reshape(drafts, -1, head_size)
    key_new = joined[:, :, query_cols : query_cols + key_cols].reshape(drafts, kv_heads, head_size)
    value_new = joined[:, :, query_cols + key_cols :].reshape(drafts, kv_heads, head_size)
    mixed = attend(
        query_heads, key_new, value_new, cache_keys[0], cache_values[0], cache_lengths[0]
    )
    mixed = jnp.transpose(mixed.reshape(drafts, splits, -1), (1, 0, 2))
    outgoing = jnp.repeat(mixed, groups, axis=0)
    flat_heads = lax.all_to_all(
        outgoing, EVERY, split_axis=0, concat_axis=0, tiled=True
    ).reshape(rows * drafts, -1)
    out_part = jnp.einsum(
        "nw,awr->nar", flat_heads, shrink_out, preferred_element_type=jnp.float32
    )
    out_part = jnp.sum(jnp.where(column_hot, out_part, 0.0), 1)
    out_rank = to_out_growers(out_part.astype(jnp.bfloat16), splits)
    out = jnp.dot(flat_heads, w_out, preferred_element_type=jnp.float32)
    out = out + jnp.dot(
        spread_ranks(out_rank, width_hot),
        grow_out.reshape(per_owner * rank_size, -1),
        preferred_element_type=jnp.float32,
    )
    blocks = lax.all_to_all(
        out.astype(jnp.bfloat16).reshape(splits, local_rows, drafts, feature_width),
        "tensor",
        split_axis=0,
        concat_axis=0,
        tiled=True,
    )
    return jnp.sum(blocks.astype(jnp.float32), 0).astype(jnp.bfloat16)


def local(*arrays):
    heads = arrays[11].shape[1]
    if heads == lax.axis_size("tensor") == lax.axis_size(GROUP):
        return by_head(*arrays)
    return by_row(*arrays)


def solution(mesh):
    placed = (
        P(("parts", "tensor"), None, ("dp", "pipe")),
        P(("dp", "pipe"), "tensor"),
        P(("dp", "pipe"), "tensor"),
        P(("dp", "pipe"), "tensor"),
        P("tensor", ("dp", "pipe")),
        P("tensor", ("dp", "pipe"), None),
        P(("dp", "pipe"), None, "tensor"),
        P(("dp", "pipe"), None, "tensor"),
        P(("dp", "pipe"), None, "tensor"),
        P(("dp", "pipe"), "tensor", None),
        P("tensor", None, ("dp", "pipe")),
        P(("parts", "tensor", "dp", "pipe"), None, None, None),
        P(("parts", "tensor", "dp", "pipe"), None, None, None),
        P(("parts", "tensor", "dp", "pipe")),
        P(),
        P(),
    )
    return jax.shard_map(
        local,
        mesh=mesh,
        in_specs=placed,
        out_specs=P(("parts", "tensor"), None, ("dp", "pipe")),
        check_vma=False,
    )
```

```python
import functools
import math

import jax
import jax.numpy as jnp
import numpy as np
from jax import lax
from jax.experimental import pallas as pl
from jax.experimental.pallas import tpu as pltpu
from jax.sharding import PartitionSpec as P

rope_base = 500000.0
EVERY = ("tensor", "dp", "pipe")
GROUP = ("dp", "pipe")
VMEM = pl.BlockSpec(memory_space=pltpu.VMEM)
HBM = pl.BlockSpec(memory_space=pltpu.HBM)
MIB = 1 << 20


def dot(left, right):
    return jnp.dot(left, right, preferred_element_type=jnp.float32)


def dot_nt(left, right):
    return lax.dot_general(
        left, right, (((1,), (1,)), ((), ())), preferred_element_type=jnp.float32
    )


def iota(shape, axis):
    return lax.broadcasted_iota(jnp.int32, shape, axis)


def call(kernel, outs, ins, scratch=(), flops=0, moved=0, limit=24 * MIB):
    return pl.pallas_call(
        kernel,
        out_shape=outs,
        in_specs=ins,
        out_specs=jax.tree.map(lambda _: VMEM, outs),
        scratch_shapes=list(scratch),
        cost_estimate=pl.CostEstimate(flops=flops, bytes_accessed=moved, transcendentals=0),
        compiler_params=pltpu.CompilerParams(vmem_limit_bytes=limit),
    )


def shape(dims, kind=jnp.bfloat16):
    return jax.ShapeDtypeStruct(tuple(dims), kind)


def over(value, size):
    return value >> (size.bit_length() - 1) if size & (size - 1) == 0 else lax.div(value, size)


def rest_of(value, size):
    return value & (size - 1) if size & (size - 1) == 0 else lax.rem(value, size)


def block_first(sizes, group, block, draft):
    groups, blocks, drafts = sizes
    return (block * drafts + draft) * groups + group


def group_first(sizes, group, block, draft):
    groups, blocks, drafts = sizes
    return (group * blocks + block) * drafts + draft


def parts_of(order, sizes, index):
    groups, blocks, drafts = sizes
    if order is block_first:
        return (
            rest_of(index, groups),
            over(index, groups * drafts),
            rest_of(over(index, groups), drafts),
        )
    return over(index, blocks * drafts), rest_of(over(index, drafts), blocks), rest_of(index, drafts)


def reorder(sizes, after, before, turn_block, turn_group=0):
    groups, blocks, drafts = sizes
    rows = groups * blocks * drafts
    group, block, draft = parts_of(after, sizes, iota((rows, rows), 0))
    wanted = before(
        sizes, rest_of(group + turn_group, groups), rest_of(block + turn_block, blocks), draft
    )
    return jnp.where(wanted == iota((rows, rows), 1), 1.0, 0.0).astype(jnp.bfloat16)


def group_of():
    return lax.axis_index("dp") * lax.axis_size("pipe") + lax.axis_index("pipe")


def rank_kernel(sizes, owned, *refs):
    groups, blocks, drafts = sizes
    pieces = refs[:blocks]
    shrink_ref, slots_ref, rows_ref, rank_ref, wide = refs[blocks:]
    for block in range(blocks):
        for draft in range(drafts):
            start = (block * drafts + draft) * groups
            wide[start : start + groups, :] = pieces[block][draft].astype(jnp.float32)
    rows = wide[...].astype(jnp.bfloat16)
    rows_ref[...] = rows
    place = slots_ref[:, 0:1] - lax.axis_index("tensor") * owned
    ranks = owned_ranks(
        rows, shrink_ref[...], place, shrink_ref.shape[0] // owned, rank_ref.shape[2]
    )
    for target in range(rank_ref.shape[0]):
        rank_ref[target] = ranks


def owned_ranks(rows, shrink, place, width, lanes):
    ranks = dot_nt(rows, shrink)
    kept = jnp.where(over(iota(ranks.shape, 1), width) == place, ranks, 0.0).astype(jnp.bfloat16)
    fold = (ranks.shape[1], lanes)
    fold = rest_of(iota(fold, 0), width) == iota(fold, 1)
    return dot(kept, jnp.where(fold, 1.0, 0.0).astype(jnp.bfloat16)).astype(jnp.bfloat16)


def spread_ranks(ranks, place, width, owned, parts):
    span = owned * width
    row = iota((ranks.shape[1], parts * span), 0)
    column = iota((ranks.shape[1], parts * span), 1)
    tile = (over(row, width) == over(column, span)) & (
        rest_of(row, width) == rest_of(column, width)
    )
    wide = dot(ranks, jnp.where(tile, 1.0, 0.0).astype(jnp.bfloat16))
    slot = over(rest_of(iota(wide.shape, 1), span), width)
    return jnp.where(slot == place, wide, 0.0).astype(jnp.bfloat16)


def stream_kernel(first, chunks, depth, rows_ref, weight_ref, *refs):
    *sums, total_ref, buffer, sems = refs

    def copy(chunk):
        return pltpu.make_async_copy(
            weight_ref.at[pl.ds(first + chunk * depth, depth)],
            buffer.at[pl.ds(chunk * depth, depth)],
            sems.at[chunk],
        )

    for chunk in range(chunks):
        copy(chunk).start()
    for chunk in range(chunks):
        start = first + chunk * depth
        copy(chunk).wait()
        product = dot(
            rows_ref[:, start : start + depth], buffer[chunk * depth : (chunk + 1) * depth, :]
        )
        if chunk:
            total_ref[...] += product
        elif sums:
            total_ref[...] = sums[0][...] + product
        else:
            total_ref[...] = product


def stream(rows, weight, chunks, first, size, *sums):
    width = weight.shape[1]
    return call(
        functools.partial(stream_kernel, first, chunks, size // chunks),
        shape((rows.shape[0], width), jnp.float32),
        [VMEM, HBM] + [VMEM] * len(sums),
        [pltpu.VMEM((size, width), jnp.bfloat16), pltpu.SemaphoreType.DMA((chunks,))],
        2 * rows.shape[0] * size * width,
        2 * size * width,
        40 * MIB,
    )(rows, weight, *sums)


def pack_kernel(sizes, ids_ref, pool_ref, length_ref, keys_ref, values_ref, turns_ref, *refs):
    groups, blocks, drafts = sizes
    outs = refs[:blocks]
    slots_ref, extra_f32, extra_ref, sems = refs[blocks:]
    size, head_size = keys_ref.shape[2:]
    me = lax.axis_index("tensor")
    length = length_ref[0]
    positions = (iota((drafts, head_size), 0) + length).astype(jnp.float32)
    angles = positions * turns_ref[0:1, :]
    extra_f32[...] = jnp.zeros(extra_f32.shape, jnp.float32)
    for index, value in enumerate((jnp.cos(angles), jnp.sin(angles) * turns_ref[1:2, :])):
        high = value.astype(jnp.bfloat16).astype(jnp.float32)
        start = 2 * index * drafts
        extra_f32[start : start + drafts, :] = high
        extra_f32[start + drafts : start + 2 * drafts, :] = value - high
    ones = jnp.ones((1, head_size), jnp.float32)
    extra_f32[4 * drafts : 4 * drafts + 1, :] = ones * (length >> 4).astype(jnp.float32)
    extra_f32[4 * drafts + 1 : 4 * drafts + 2, :] = ones * (length & 15).astype(jnp.float32)
    extra_ref[...] = extra_f32[...].astype(jnp.bfloat16)
    copies = []
    for shift in range(blocks):
        head = lax.rem(me + shift, blocks)
        copies += [
            pltpu.make_async_copy(
                keys_ref.at[0, head], outs[shift].at[pl.ds(0, size)], sems.at[shift, 0]
            ),
            pltpu.make_async_copy(
                values_ref.at[0, head], outs[shift].at[pl.ds(size, size)], sems.at[shift, 1]
            ),
            pltpu.make_async_copy(
                extra_ref,
                outs[shift].at[pl.ds(2 * size, extra_ref.shape[0])],
                sems.at[shift, 2],
            ),
        ]
    for copy in copies:
        copy.start()
    index = iota(slots_ref.shape, 0)
    column = iota(slots_ref.shape, 1)
    near = parts_of(block_first, sizes, index)
    far = parts_of(group_first, sizes, index)
    row_group = jnp.where(column == 0, near[0], far[0])
    row_block = jnp.where(column == 0, near[1], far[1])
    place = row_block * groups + row_group
    slots = jnp.zeros(slots_ref.shape, jnp.int32)
    for block in range(blocks):
        for group in range(groups):
            row = lax.rem(me - block + blocks, blocks) * groups + group
            slots = jnp.where(place == block * groups + group, pool_ref[ids_ref[row]], slots)
    slots_ref[...] = slots
    for copy in copies:
        copy.wait()


def pack(sizes, ids, pool, lengths, keys, values):
    groups, blocks, drafts = sizes
    head_size = keys.shape[3]
    half = np.arange(head_size // 2)
    frequency = (rope_base ** (-2.0 * half / head_size)).astype(np.float32)
    signs = np.ones(half.size, np.float32)
    turns = np.stack([np.tile(frequency, 2), np.concatenate([-signs, signs])])
    used = -(-(4 * drafts + 2) // 16) * 16
    outs = [shape((2 * keys.shape[2] + used, head_size))] * blocks
    smem = pl.BlockSpec(memory_space=pltpu.SMEM)
    return pl.pallas_call(
        functools.partial(pack_kernel, sizes),
        out_shape=outs + [shape((groups * blocks * drafts, 128), jnp.int32)],
        in_specs=[smem, smem, smem, VMEM, VMEM, VMEM],
        out_specs=[HBM] * blocks + [VMEM],
        scratch_shapes=[
            pltpu.VMEM((used, head_size), jnp.float32),
            pltpu.VMEM((used, head_size), jnp.bfloat16),
            pltpu.SemaphoreType.DMA((blocks, 3)),
        ],
        cost_estimate=pl.CostEstimate(flops=0, bytes_accessed=8 * keys.size, transcendentals=0),
        compiler_params=pltpu.CompilerParams(vmem_limit_bytes=24 * MIB),
    )(ids, pool, lengths, keys, values, jnp.asarray(turns))


def grow_kernel(sizes, width, total_ref, rows_ref, key_ref, value_ref, slots_ref, ranks_ref, *rest):
    groups, blocks, drafts = sizes
    grows = rest[:3]
    outs = rest[3:]
    group = group_of()
    owned = grows[0].shape[0] // width
    ranks = ranks_ref[group * groups].astype(jnp.float32)
    for other in range(1, groups):
        ranks = ranks + ranks_ref[group * groups + other].astype(jnp.float32)
    turn = rest_of(group - lax.axis_index("tensor") + blocks, blocks)
    ranks = dot(reorder(sizes, block_first, block_first, turn), ranks.astype(jnp.bfloat16))
    place = slots_ref[:, 0:1] - group * owned
    wide = spread_ranks(ranks.astype(jnp.bfloat16), place, width, owned, len(grows))
    by_group = reorder(sizes, group_first, block_first, 0, group)
    start = 0
    for index, grow in enumerate(grows):
        deep, cols = grow.shape
        base = total_ref[...] if index == 0 else dot(rows_ref[...], (key_ref, value_ref)[index - 1][...])
        full = base + dot(wide[:, index * deep : (index + 1) * deep], grow[...])
        full = dot(by_group, full.astype(jnp.bfloat16)).astype(jnp.bfloat16)
        for step in range(groups):
            for block in range(blocks):
                row = (step * blocks + block) * drafts
                outs[step][block, :, start : start + cols] = full[row : row + drafts]
        start += cols


def attend_kernel(blocks, drafts, groups, cache_size, *refs):
    parts = refs[:groups]
    caches = refs[groups : groups + blocks]
    mixed_ref, query_s, fresh_s, out_s = refs[groups + blocks :]
    head_size = caches[0].shape[1]
    cols = parts[0].shape[2]
    heads = cols // head_size - 2
    count = heads * drafts
    scale = 1.0 / math.sqrt(head_size)
    fresh_s[...] = jnp.zeros(fresh_s.shape, jnp.float32)
    pad = fresh_s.shape[1]
    for block in range(blocks):
        joined = parts[0][block].astype(jnp.float32)
        for other in parts[1:]:
            joined = joined + other[block].astype(jnp.float32)
        joined = joined.astype(jnp.bfloat16).astype(jnp.float32)
        extra = caches[block][2 * cache_size :, :].astype(jnp.float32)
        cosine = extra[0:drafts] + extra[drafts : 2 * drafts]
        sine = extra[2 * drafts : 3 * drafts] + extra[3 * drafts : 4 * drafts]
        length = extra[4 * drafts : 4 * drafts + 1, 0:1] * 16.0 + extra[
            4 * drafts + 1 : 4 * drafts + 2, 0:1
        ]

        def rotated(head):
            value = joined[:, head * head_size : (head + 1) * head_size]
            return value * cosine + pltpu.roll(value, head_size // 2, 1) * sine

        for head in range(heads):
            query_s[block, head * drafts : (head + 1) * drafts, :] = rotated(head)
        fresh_s[2 * block, 0:drafts, :] = rotated(heads)
        fresh_s[2 * block + 1, 0:drafts, :] = joined[:, (heads + 1) * head_size :]
        query = query_s[block].astype(jnp.bfloat16)
        old = dot_nt(query, caches[block][0:cache_size, :]) * scale
        new = dot_nt(query, fresh_s[2 * block].astype(jnp.bfloat16)) * scale
        old_seen = iota(old.shape, 1).astype(jnp.float32) < length
        new_seen = iota(new.shape, 1) <= lax.rem(iota(new.shape, 0), drafts)
        old = jnp.where(old_seen, old, -jnp.inf)
        new = jnp.where(new_seen, new, -jnp.inf)
        peak = jnp.maximum(
            jnp.max(old, 1, keepdims=True), jnp.max(new, 1, keepdims=True)
        )
        old = jnp.exp(old - peak)
        new = jnp.exp(new - peak)
        below = jnp.sum(old, 1, keepdims=True) + jnp.sum(new, 1, keepdims=True)
        mixed = dot(
            (old / below).astype(jnp.bfloat16), caches[block][cache_size : 2 * cache_size, :]
        ) + dot((new / below).astype(jnp.bfloat16), fresh_s[2 * block + 1].astype(jnp.bfloat16))
        for head in range(heads):
            out_s[
                block * drafts : (block + 1) * drafts, head * head_size : (head + 1) * head_size
            ] = mixed[head * drafts : (head + 1) * drafts]
    mixed_ref[...] = out_s[...].astype(jnp.bfloat16)


def out_rank_kernel(owned, got_ref, shrink_ref, slots_ref, rows_ref, rank_ref, wide):
    span = got_ref.shape[1]
    for group in range(got_ref.shape[0]):
        wide[group * span : (group + 1) * span, :] = got_ref[group].astype(jnp.float32)
    rows = wide[...].astype(jnp.bfloat16)
    rows_ref[...] = rows
    place = slots_ref[:, 1:2] - group_of() * owned
    ranks = owned_ranks(
        rows, shrink_ref[...], place, shrink_ref.shape[0] // owned, rank_ref.shape[2]
    )
    for target in range(rank_ref.shape[0]):
        rank_ref[target] = ranks


def out_grow_kernel(sizes, width, total_ref, slots_ref, ranks_ref, grow_ref, *outs):
    groups, blocks, drafts = sizes
    owned = grow_ref.shape[0] // width
    me = lax.axis_index("tensor")
    ranks = None
    for source in range(blocks):
        turn = rest_of(source - me + blocks, blocks)
        moved = dot(
            reorder(sizes, group_first, group_first, turn), ranks_ref[source * groups + me]
        )
        ranks = moved if ranks is None else ranks + moved
    place = slots_ref[:, 1:2] - me * owned
    wide = spread_ranks(ranks.astype(jnp.bfloat16), place, width, owned, 1)
    full = (total_ref[...] + dot(wide, grow_ref[...])).astype(jnp.bfloat16)
    full = dot(reorder(sizes, block_first, group_first, 0), full).astype(jnp.bfloat16)
    for block in range(blocks):
        for draft in range(drafts):
            start = (block * drafts + draft) * groups
            outs[block][draft] = full[start : start + groups]


def by_head(
    tokens,
    w_query,
    w_key,
    w_value,
    w_out,
    shrink_qkv,
    grow_query,
    grow_key,
    grow_value,
    shrink_out,
    grow_out,
    cache_keys,
    cache_values,
    cache_lengths,
    adapter_ids,
    adapter_slots,
):
    blocks = lax.axis_size("tensor")
    groups = lax.axis_size(GROUP)
    _, drafts, features = tokens.shape
    sizes = (groups, blocks, drafts)
    owned = shrink_qkv.shape[0]
    width = grow_out.shape[1]
    cache_size, head_size = cache_keys.shape[2:]
    span = blocks * drafts
    count = groups * span
    lanes = -(-shrink_qkv.shape[2] // 128) * 128

    def over_tensor(value, shift):
        route = [(t, (t + shift) % blocks) for t in range(blocks)]
        return lax.ppermute(value, "tensor", route)

    def over_group(value, shift):
        route = [(g, (g + shift) % groups) for g in range(groups)]
        return lax.ppermute(value, GROUP, route)

    def exchange(value):
        return lax.all_to_all(value, EVERY, split_axis=0, concat_axis=0, tiled=True)

    mine = jnp.transpose(tokens, (1, 0, 2))
    pieces = [mine] + [over_tensor(mine, shift) for shift in range(1, blocks)]

    *messages, slots = pack(
        sizes, adapter_ids, adapter_slots, cache_lengths, cache_keys, cache_values
    )
    caches = {shift: over_tensor(messages[shift], shift) for shift in range(1, blocks) if shift != 2}

    shrink_in = jnp.transpose(shrink_qkv, (0, 2, 1)).reshape(-1, features)
    rows, rank_part = call(
        functools.partial(rank_kernel, sizes, owned),
        [shape((count, features)), shape((blocks * groups, count, lanes))],
        [VMEM] * (blocks + 2),
        [pltpu.VMEM((count, features), jnp.float32)],
        2 * count * shrink_qkv.size,
        2 * shrink_qkv.size + 4 * count * features,
    )(*pieces, shrink_in, slots)
    ranks = exchange(rank_part)
    half = features // 2
    total = stream(rows, w_query, 4, 0, half)
    total, *late = lax.optimization_barrier((total, *messages[2:3]))
    for message in late:
        caches[2] = over_tensor(message, 2)
    total = stream(rows, w_query, 4, half, features - half, total)
    caches = [messages[0]] + [caches[shift] for shift in range(1, blocks)]
    cols = total.shape[1] + w_key.shape[1] + w_value.shape[1]
    sent = call(
        functools.partial(grow_kernel, sizes, width),
        [shape((blocks, drafts, cols))] * groups,
        [VMEM] * 9,
        [],
        2 * count * owned * width * cols,
        8 * count * cols + 2 * owned * width * cols,
    )(
        total,
        rows,
        w_key,
        w_value,
        slots,
        ranks,
        *[grow.reshape(owned * width, -1) for grow in (grow_query, grow_key, grow_value)],
    )
    parts = [sent[0]] + [over_group(sent[shift], shift) for shift in range(1, groups)]
    head_cols = cols - 2 * head_size
    mixed = call(
        functools.partial(attend_kernel, blocks, drafts, groups, cache_size),
        shape((span, head_cols)),
        [VMEM] * (groups + blocks),
        [
            pltpu.VMEM((blocks, head_cols // head_size * drafts, head_size), jnp.float32),
            pltpu.VMEM((2 * blocks, 128, head_size), jnp.float32),
            pltpu.VMEM((span, head_cols), jnp.float32),
        ],
        4 * span * head_cols * cache_size,
        4 * blocks * cache_size * head_size,
    )(*parts, *caches)
    gathered = lax.all_gather(mixed, GROUP, axis=0, tiled=False)
    out_rows, out_part = call(
        functools.partial(out_rank_kernel, owned),
        [shape((count, head_cols)), shape((blocks * groups, count, lanes))],
        [VMEM] * 3,
        [pltpu.VMEM((count, head_cols), jnp.float32)],
        2 * count * shrink_out.size,
        2 * shrink_out.size + 4 * count * head_cols,
    )(gathered, jnp.transpose(shrink_out, (0, 2, 1)).reshape(-1, head_cols), slots)
    out_ranks = exchange(out_part)
    out_total = stream(out_rows, w_out, 8, 0, head_cols)
    out_cols = out_total.shape[1]
    leaving = call(
        functools.partial(out_grow_kernel, sizes, width),
        [shape((drafts, groups, out_cols))] * blocks,
        [VMEM] * 4,
        [],
        2 * count * owned * width * out_cols,
        8 * count * out_cols + 2 * owned * width * out_cols,
    )(out_total, slots, out_ranks, grow_out.reshape(owned * width, -1))
    result = leaving[0].astype(jnp.float32)
    for shift in range(1, blocks):
        result = result + over_tensor(leaving[shift], -shift).astype(jnp.float32)
    return jnp.transpose(result.astype(jnp.bfloat16), (1, 0, 2))


def rotate(vectors, positions):
    half_size = vectors.shape[-1] // 2
    frequency = rope_base ** (-2.0 * jnp.arange(half_size, dtype=jnp.float32) / vectors.shape[-1])
    angles = positions[:, None, None] * frequency
    cosine = jnp.cos(angles)
    sine_value = jnp.sin(angles)
    first_half = vectors[..., :half_size]
    second = vectors[..., half_size:]
    return jnp.concatenate(
        [first_half * cosine - second * sine_value, second * cosine + first_half * sine_value], -1
    )


def to_growers(partial, splits):
    total = None
    for shift in range(splits):
        route = [
            (t * splits + g, ((g + shift) % splits) * splits + t)
            for t in range(splits)
            for g in range(splits)
        ]
        got = lax.ppermute(partial, EVERY, route).astype(jnp.float32)
        total = got if total is None else total + got
    return total


def to_out_growers(partial, splits):
    total = None
    for shift in range(splits):
        route = [
            (t * splits + g, g * splits + (t + shift) % splits)
            for t in range(splits)
            for g in range(splits)
        ]
        got = lax.ppermute(partial, EVERY, route).astype(jnp.float32)
        total = got if total is None else total + got
    return total


def slot_table(adapter_ids, adapter_slots):
    matches = adapter_ids[:, None] == jnp.arange(adapter_slots.shape[0], dtype=jnp.int32)[None, :]
    return jnp.sum(jnp.where(matches, adapter_slots[None, :], 0), axis=1)


def attend(query_heads, key_new, value_new, cache_keys, cache_values, length):
    drafts, head_count, head_size = query_heads.shape
    kv_heads, cache_size, _ = cache_keys.shape
    positions = (length + jnp.arange(drafts, dtype=jnp.int32)).astype(jnp.float32)
    query_rot = rotate(query_heads.astype(jnp.float32), positions).astype(jnp.bfloat16)
    key_rot = rotate(key_new.astype(jnp.float32), positions).astype(jnp.bfloat16)
    grouped = query_rot.reshape(drafts, kv_heads, head_count // kv_heads, head_size)
    score_scale = 1.0 / math.sqrt(head_size)
    cached = (
        jnp.einsum("skgd,kld->skgl", grouped, cache_keys, preferred_element_type=jnp.float32)
        * score_scale
    )
    fresh_scores = (
        jnp.einsum("skgd,tkd->skgt", grouped, key_rot, preferred_element_type=jnp.float32)
        * score_scale
    )
    cache_mask = jnp.arange(cache_size, dtype=jnp.int32) < length
    draft_mask = jnp.arange(drafts)[None, :] <= jnp.arange(drafts)[:, None]
    cached = jnp.where(cache_mask[None, None, None, :], cached, -jnp.inf)
    fresh_scores = jnp.where(draft_mask[:, None, None, :], fresh_scores, -jnp.inf)
    row_peak = jnp.maximum(jnp.max(cached, -1), jnp.max(fresh_scores, -1))
    cached_exp = jnp.exp(cached - row_peak[..., None])
    fresh_exp = jnp.exp(fresh_scores - row_peak[..., None])
    denominator = jnp.sum(cached_exp, -1) + jnp.sum(fresh_exp, -1)
    cached_prob = (cached_exp / denominator[..., None]).astype(jnp.bfloat16)
    fresh_prob = (fresh_exp / denominator[..., None]).astype(jnp.bfloat16)
    mixed = jnp.einsum(
        "skgl,kld->skgd", cached_prob, cache_values, preferred_element_type=jnp.float32
    )
    mixed = mixed + jnp.einsum(
        "skgt,tkd->skgd", fresh_prob, value_new, preferred_element_type=jnp.float32
    )
    return mixed.astype(jnp.bfloat16)


def by_row(
    tokens,
    w_query,
    w_key,
    w_value,
    w_out,
    shrink_qkv,
    grow_query,
    grow_key,
    grow_value,
    shrink_out,
    grow_out,
    cache_keys,
    cache_values,
    cache_lengths,
    adapter_ids,
    adapter_slots,
):
    splits = lax.axis_size("tensor")
    groups = lax.axis_size(("dp", "pipe"))
    tensor_index = lax.axis_index("tensor")
    group_index = lax.axis_index(("dp", "pipe"))
    local_rows, drafts, feature_width = tokens.shape
    per_owner = shrink_qkv.shape[0]
    rank_size = grow_out.shape[1]
    query_cols = w_query.shape[1]
    key_cols = w_key.shape[1]
    kv_heads = cache_keys.shape[1]
    head_size = cache_keys.shape[3]
    rows = splits * groups
    row_slots = jnp.repeat(slot_table(adapter_ids, adapter_slots), drafts)
    within = jnp.arange(per_owner, dtype=jnp.int32)[None, :]
    width_hot = (row_slots[:, None] == within + tensor_index * per_owner)[:, :, None]
    column_hot = (row_slots[:, None] == within + group_index * per_owner)[:, :, None]

    def spread_ranks(ranks, hot):
        return jnp.where(hot, ranks[:, None, :], 0.0).reshape(rows * drafts, -1).astype(jnp.bfloat16)

    flat_tokens = lax.all_gather(tokens, "tensor", axis=0, tiled=True).reshape(
        rows * drafts, feature_width
    )
    rank_part = jnp.einsum(
        "nd,adr->nar", flat_tokens, shrink_qkv, preferred_element_type=jnp.float32
    )
    rank_part = jnp.sum(jnp.where(width_hot, rank_part, 0.0), 1)
    rank_all = to_growers(rank_part.astype(jnp.bfloat16), splits)

    def grown(index, grow):
        ranks = spread_ranks(rank_all[:, index * rank_size : (index + 1) * rank_size], column_hot)
        return jnp.dot(
            ranks, grow.reshape(per_owner * rank_size, -1), preferred_element_type=jnp.float32
        )

    bases = [
        jnp.dot(flat_tokens, weight, preferred_element_type=jnp.float32)
        for weight in (w_query, w_key, w_value)
    ]

    def product(index, grow):
        return (bases[index] + grown(index, grow)).astype(jnp.bfloat16).reshape(rows, drafts, -1)

    partial = jnp.concatenate(
        [
            product(0, grow_query),
            product(1, grow_key),
            product(2, grow_value),
        ],
        2,
    )
    arrived = lax.all_to_all(partial, EVERY, split_axis=0, concat_axis=0, tiled=True)
    joined = jnp.sum(
        arrived.reshape(splits, groups, drafts, -1).astype(jnp.float32), 1
    ).astype(jnp.bfloat16)
    joined = jnp.transpose(joined, (1, 0, 2))
    query_heads = joined[:, :, :query_cols].reshape(drafts, -1, head_size)
    key_new = joined[:, :, query_cols : query_cols + key_cols].reshape(drafts, kv_heads, head_size)
    value_new = joined[:, :, query_cols + key_cols :].reshape(drafts, kv_heads, head_size)
    mixed = attend(
        query_heads, key_new, value_new, cache_keys[0], cache_values[0], cache_lengths[0]
    )
    mixed = jnp.transpose(mixed.reshape(drafts, splits, -1), (1, 0, 2))
    outgoing = jnp.repeat(mixed, groups, axis=0)
    flat_heads = lax.all_to_all(
        outgoing, EVERY, split_axis=0, concat_axis=0, tiled=True
    ).reshape(rows * drafts, -1)
    out_part = jnp.einsum(
        "nw,awr->nar", flat_heads, shrink_out, preferred_element_type=jnp.float32
    )
    out_part = jnp.sum(jnp.where(column_hot, out_part, 0.0), 1)
    out_rank = to_out_growers(out_part.astype(jnp.bfloat16), splits)
    out = jnp.dot(flat_heads, w_out, preferred_element_type=jnp.float32)
    out = out + jnp.dot(
        spread_ranks(out_rank, width_hot),
        grow_out.reshape(per_owner * rank_size, -1),
        preferred_element_type=jnp.float32,
    )
    blocks = lax.all_to_all(
        out.astype(jnp.bfloat16).reshape(splits, local_rows, drafts, feature_width),
        "tensor",
        split_axis=0,
        concat_axis=0,
        tiled=True,
    )
    return jnp.sum(blocks.astype(jnp.float32), 0).astype(jnp.bfloat16)


def local(*arrays):
    heads = arrays[11].shape[1]
    if heads == lax.axis_size("tensor") == lax.axis_size(GROUP):
        return by_head(*arrays)
    return by_row(*arrays)


def solution(mesh):
    placed = (
        P(("parts", "tensor"), None, ("dp", "pipe")),
        P(("dp", "pipe"), "tensor"),
        P(("dp", "pipe"), "tensor"),
        P(("dp", "pipe"), "tensor"),
        P("tensor", ("dp", "pipe")),
        P("tensor", ("dp", "pipe"), None),
        P(("dp", "pipe"), None, "tensor"),
        P(("dp", "pipe"), None, "tensor"),
        P(("dp", "pipe"), None, "tensor"),
        P(("dp", "pipe"), "tensor", None),
        P("tensor", None, ("dp", "pipe")),
        P(("parts", "tensor", "dp", "pipe"), None, None, None),
        P(("parts", "tensor", "dp", "pipe"), None, None, None),
        P(("parts", "tensor", "dp", "pipe")),
        P(),
        P(),
    )
    return jax.shard_map(
        local,
        mesh=mesh,
        in_specs=placed,
        out_specs=P(("parts", "tensor"), None, ("dp", "pipe")),
        check_vma=False,
    )
```

```python
import functools
import math

import jax
import jax.numpy as jnp
from jax import lax
from jax.experimental import pallas as pl
from jax.experimental.pallas import tpu as pltpu
from jax.sharding import PartitionSpec as P

rope_base = 500000.0
EVERY = ("tensor", "dp", "pipe")
GROUP = ("dp", "pipe")
VMEM = pl.BlockSpec(memory_space=pltpu.VMEM)
HBM = pl.BlockSpec(memory_space=pltpu.HBM)
MIB = 1 << 20


def dot(left, right):
    return jnp.dot(left, right, preferred_element_type=jnp.float32)


def dot_nt(left, right):
    return lax.dot_general(
        left, right, (((1,), (1,)), ((), ())), preferred_element_type=jnp.float32
    )


def iota(shape, axis):
    return lax.broadcasted_iota(jnp.int32, shape, axis)


def call(kernel, outs, ins, scratch=(), flops=0, moved=0, limit=24 * MIB):
    return pl.pallas_call(
        kernel,
        out_shape=outs,
        in_specs=ins,
        out_specs=jax.tree.map(lambda _: VMEM, outs),
        scratch_shapes=list(scratch),
        cost_estimate=pl.CostEstimate(flops=flops, bytes_accessed=moved, transcendentals=0),
        compiler_params=pltpu.CompilerParams(vmem_limit_bytes=limit),
    )


def shape(dims, kind=jnp.bfloat16):
    return jax.ShapeDtypeStruct(tuple(dims), kind)


def over(value, size):
    return value >> (size.bit_length() - 1) if size & (size - 1) == 0 else lax.div(value, size)


def rest_of(value, size):
    return value & (size - 1) if size & (size - 1) == 0 else lax.rem(value, size)


def block_first(sizes, group, block, draft):
    groups, blocks, drafts = sizes
    return (block * drafts + draft) * groups + group


def group_first(sizes, group, block, draft):
    groups, blocks, drafts = sizes
    return (group * blocks + block) * drafts + draft


def parts_of(order, sizes, index):
    groups, blocks, drafts = sizes
    if order is block_first:
        return (
            rest_of(index, groups),
            over(index, groups * drafts),
            rest_of(over(index, groups), drafts),
        )
    return over(index, blocks * drafts), rest_of(over(index, drafts), blocks), rest_of(index, drafts)


def reorder(sizes, after, before, turn_block, turn_group=0):
    groups, blocks, drafts = sizes
    rows = groups * blocks * drafts
    group, block, draft = parts_of(after, sizes, iota((rows, rows), 0))
    wanted = before(
        sizes, rest_of(group + turn_group, groups), rest_of(block + turn_block, blocks), draft
    )
    return jnp.where(wanted == iota((rows, rows), 1), 1.0, 0.0).astype(jnp.bfloat16)


def group_of():
    return lax.axis_index("dp") * lax.axis_size("pipe") + lax.axis_index("pipe")


def rank_kernel(sizes, owned, *refs):
    groups, blocks, drafts = sizes
    pieces = refs[:blocks]
    shrink_ref, slots_ref, rows_ref, rank_ref, wide = refs[blocks:]
    for block in range(blocks):
        for draft in range(drafts):
            start = (block * drafts + draft) * groups
            wide[start : start + groups, :] = pieces[block][draft].astype(jnp.float32)
    rows = wide[...].astype(jnp.bfloat16)
    rows_ref[...] = rows
    place = slots_ref[:, 0:1] - lax.axis_index("tensor") * owned
    ranks = owned_ranks(
        rows, shrink_ref[...], place, shrink_ref.shape[0] // owned, rank_ref.shape[2]
    )
    for target in range(rank_ref.shape[0]):
        rank_ref[target] = ranks


def owned_ranks(rows, shrink, place, width, lanes):
    ranks = dot_nt(rows, shrink)
    kept = jnp.where(over(iota(ranks.shape, 1), width) == place, ranks, 0.0).astype(jnp.bfloat16)
    fold = (ranks.shape[1], lanes)
    fold = rest_of(iota(fold, 0), width) == iota(fold, 1)
    return dot(kept, jnp.where(fold, 1.0, 0.0).astype(jnp.bfloat16)).astype(jnp.bfloat16)


def spread_ranks(ranks, place, width, owned, parts):
    span = owned * width
    row = iota((ranks.shape[1], parts * span), 0)
    column = iota((ranks.shape[1], parts * span), 1)
    tile = (over(row, width) == over(column, span)) & (
        rest_of(row, width) == rest_of(column, width)
    )
    wide = dot(ranks, jnp.where(tile, 1.0, 0.0).astype(jnp.bfloat16))
    slot = over(rest_of(iota(wide.shape, 1), span), width)
    return jnp.where(slot == place, wide, 0.0).astype(jnp.bfloat16)


def stream_kernel(first, chunks, depth, rows_ref, weight_ref, *refs):
    *sums, total_ref, buffer, sems = refs

    def copy(chunk):
        return pltpu.make_async_copy(
            weight_ref.at[pl.ds(first + chunk * depth, depth)],
            buffer.at[pl.ds(chunk * depth, depth)],
            sems.at[chunk],
        )

    for chunk in range(chunks):
        copy(chunk).start()
    for chunk in range(chunks):
        start = first + chunk * depth
        copy(chunk).wait()
        product = dot(
            rows_ref[:, start : start + depth], buffer[chunk * depth : (chunk + 1) * depth, :]
        )
        if chunk:
            total_ref[...] += product
        elif sums:
            total_ref[...] = sums[0][...] + product
        else:
            total_ref[...] = product


def stream(rows, weight, chunks, first, size, *sums):
    width = weight.shape[1]
    return call(
        functools.partial(stream_kernel, first, chunks, size // chunks),
        shape((rows.shape[0], width), jnp.float32),
        [VMEM, HBM] + [VMEM] * len(sums),
        [pltpu.VMEM((size, width), jnp.bfloat16), pltpu.SemaphoreType.DMA((chunks,))],
        limit=50 * MIB,
    )(rows, weight, *sums)


def product_kernel(rows_ref, weight_ref, total_ref):
    width = total_ref.shape[1]
    step = width if width % 1024 else 1024
    for start in range(0, width, step):
        total_ref[:, start : start + step] = dot(
            rows_ref[...], weight_ref[:, start : start + step]
        )


def product(rows, weight):
    return call(
        product_kernel, shape((rows.shape[0], weight.shape[1]), jnp.float32), [VMEM] * 2
    )(rows, weight)


def pack_kernel(sizes, ids_ref, pool_ref, length_ref, keys_ref, values_ref, *refs):
    groups, blocks, drafts = sizes
    outs = refs[:blocks]
    slots_ref, extra_f32, extra_ref, sems = refs[blocks:]
    size, head_size = keys_ref.shape[2:]
    me = lax.axis_index("tensor")
    length = length_ref[0]
    positions = (iota((drafts, head_size), 0) + length).astype(jnp.float32)
    lane = iota((drafts, head_size), 1)
    half = (lane & (head_size // 2 - 1)).astype(jnp.float32)
    angles = positions * jnp.exp(half * (-2.0 * math.log(rope_base) / head_size))
    signs = jnp.where(lane < head_size // 2, -1.0, 1.0)
    extra_f32[...] = jnp.zeros(extra_f32.shape, jnp.float32)
    for index, value in enumerate((jnp.cos(angles), jnp.sin(angles) * signs)):
        high = value.astype(jnp.bfloat16).astype(jnp.float32)
        start = 2 * index * drafts
        extra_f32[start : start + drafts, :] = high
        extra_f32[start + drafts : start + 2 * drafts, :] = value - high
    ones = jnp.ones((1, head_size), jnp.float32)
    extra_f32[4 * drafts : 4 * drafts + 1, :] = ones * (length >> 4).astype(jnp.float32)
    extra_f32[4 * drafts + 1 : 4 * drafts + 2, :] = ones * (length & 15).astype(jnp.float32)
    extra_ref[...] = extra_f32[...].astype(jnp.bfloat16)
    copies = []
    for shift in range(blocks):
        head = lax.rem(me + shift, blocks)
        copies += [
            pltpu.make_async_copy(
                keys_ref.at[0, head], outs[shift].at[pl.ds(0, size)], sems.at[shift, 0]
            ),
            pltpu.make_async_copy(
                values_ref.at[0, head], outs[shift].at[pl.ds(size, size)], sems.at[shift, 1]
            ),
            pltpu.make_async_copy(
                extra_ref,
                outs[shift].at[pl.ds(2 * size, extra_ref.shape[0])],
                sems.at[shift, 2],
            ),
        ]
    for copy in copies:
        copy.start()
    index = iota(slots_ref.shape, 0)
    column = iota(slots_ref.shape, 1)
    near = parts_of(block_first, sizes, index)
    far = parts_of(group_first, sizes, index)
    row_group = jnp.where(column == 0, near[0], far[0])
    row_block = jnp.where(column == 0, near[1], far[1])
    place = row_block * groups + row_group
    slots = jnp.zeros(slots_ref.shape, jnp.int32)
    for block in range(blocks):
        for group in range(groups):
            row = lax.rem(me - block + blocks, blocks) * groups + group
            slots = jnp.where(place == block * groups + group, pool_ref[ids_ref[row]], slots)
    slots_ref[...] = slots
    for copy in copies:
        copy.wait()


def pack(sizes, ids, pool, lengths, keys, values):
    groups, blocks, drafts = sizes
    head_size = keys.shape[3]
    used = -(-(4 * drafts + 2) // 16) * 16
    outs = [shape((2 * keys.shape[2] + used, head_size))] * blocks
    smem = pl.BlockSpec(memory_space=pltpu.SMEM)
    return pl.pallas_call(
        functools.partial(pack_kernel, sizes),
        out_shape=outs + [shape((groups * blocks * drafts, 128), jnp.int32)],
        in_specs=[smem, smem, smem, VMEM, VMEM],
        out_specs=[HBM] * blocks + [VMEM],
        scratch_shapes=[
            pltpu.VMEM((used, head_size), jnp.float32),
            pltpu.VMEM((used, head_size), jnp.bfloat16),
            pltpu.SemaphoreType.DMA((blocks, 3)),
        ],
        cost_estimate=pl.CostEstimate(flops=0, bytes_accessed=320 * keys.size, transcendentals=0),
        compiler_params=pltpu.CompilerParams(vmem_limit_bytes=24 * MIB),
    )(ids, pool, lengths, keys, values)


def grow_kernel(sizes, width, total_ref, rows_ref, key_ref, value_ref, slots_ref, ranks_ref, *rest):
    groups, blocks, drafts = sizes
    grows = rest[:3]
    outs = rest[3:]
    group = group_of()
    owned = grows[0].shape[0] // width
    ranks = ranks_ref[group * groups].astype(jnp.float32)
    for other in range(1, groups):
        ranks = ranks + ranks_ref[group * groups + other].astype(jnp.float32)
    turn = rest_of(group - lax.axis_index("tensor") + blocks, blocks)
    ranks = dot(reorder(sizes, block_first, block_first, turn), ranks.astype(jnp.bfloat16))
    place = slots_ref[:, 0:1] - group * owned
    wide = spread_ranks(ranks.astype(jnp.bfloat16), place, width, owned, len(grows))
    by_group = reorder(sizes, group_first, block_first, 0, group)
    start = 0
    for index, grow in enumerate(grows):
        deep, cols = grow.shape
        base = total_ref[...] if index == 0 else dot(rows_ref[...], (key_ref, value_ref)[index - 1][...])
        full = base + dot(wide[:, index * deep : (index + 1) * deep], grow[...])
        full = dot(by_group, full.astype(jnp.bfloat16)).astype(jnp.bfloat16)
        for step in range(groups):
            for block in range(blocks):
                row = (step * blocks + block) * drafts
                outs[step][block, :, start : start + cols] = full[row : row + drafts]
        start += cols


def attend_kernel(blocks, drafts, groups, cache_size, *refs):
    parts = refs[:groups]
    caches = refs[groups : groups + blocks]
    mixed_ref, query_s, fresh_s, out_s = refs[groups + blocks :]
    head_size = caches[0].shape[1]
    cols = parts[0].shape[2]
    heads = cols // head_size - 2
    count = heads * drafts
    scale = 1.0 / math.sqrt(head_size)
    fresh_s[...] = jnp.zeros(fresh_s.shape, jnp.float32)
    pad = fresh_s.shape[1]
    for block in range(blocks):
        joined = parts[0][block].astype(jnp.float32)
        for other in parts[1:]:
            joined = joined + other[block].astype(jnp.float32)
        joined = joined.astype(jnp.bfloat16).astype(jnp.float32)
        extra = caches[block][2 * cache_size :, :].astype(jnp.float32)
        cosine = extra[0:drafts] + extra[drafts : 2 * drafts]
        sine = extra[2 * drafts : 3 * drafts] + extra[3 * drafts : 4 * drafts]
        length = extra[4 * drafts : 4 * drafts + 1, 0:1] * 16.0 + extra[
            4 * drafts + 1 : 4 * drafts + 2, 0:1
        ]

        def rotated(head):
            value = joined[:, head * head_size : (head + 1) * head_size]
            return value * cosine + pltpu.roll(value, head_size // 2, 1) * sine

        for head in range(heads):
            query_s[block, head * drafts : (head + 1) * drafts, :] = rotated(head)
        fresh_s[2 * block, 0:drafts, :] = rotated(heads)
        fresh_s[2 * block + 1, 0:drafts, :] = joined[:, (heads + 1) * head_size :]
        query = query_s[block].astype(jnp.bfloat16)
        old = dot_nt(query, caches[block][0:cache_size, :]) * scale
        new = dot_nt(query, fresh_s[2 * block].astype(jnp.bfloat16)) * scale
        old_seen = iota(old.shape, 1).astype(jnp.float32) < length
        new_seen = iota(new.shape, 1) <= lax.rem(iota(new.shape, 0), drafts)
        old = jnp.where(old_seen, old, -jnp.inf)
        new = jnp.where(new_seen, new, -jnp.inf)
        peak = jnp.maximum(
            jnp.max(old, 1, keepdims=True), jnp.max(new, 1, keepdims=True)
        )
        old = jnp.exp(old - peak)
        new = jnp.exp(new - peak)
        below = jnp.sum(old, 1, keepdims=True) + jnp.sum(new, 1, keepdims=True)
        mixed = dot(
            (old / below).astype(jnp.bfloat16), caches[block][cache_size : 2 * cache_size, :]
        ) + dot((new / below).astype(jnp.bfloat16), fresh_s[2 * block + 1].astype(jnp.bfloat16))
        for head in range(heads):
            out_s[
                block * drafts : (block + 1) * drafts, head * head_size : (head + 1) * head_size
            ] = mixed[head * drafts : (head + 1) * drafts]
    mixed_ref[...] = out_s[...].astype(jnp.bfloat16)


def out_rank_kernel(owned, got_ref, shrink_ref, slots_ref, rows_ref, rank_ref, wide):
    span = got_ref.shape[1]
    for group in range(got_ref.shape[0]):
        wide[group * span : (group + 1) * span, :] = got_ref[group].astype(jnp.float32)
    rows = wide[...].astype(jnp.bfloat16)
    rows_ref[...] = rows
    place = slots_ref[:, 1:2] - group_of() * owned
    ranks = owned_ranks(
        rows, shrink_ref[...], place, shrink_ref.shape[0] // owned, rank_ref.shape[2]
    )
    for target in range(rank_ref.shape[0]):
        rank_ref[target] = ranks


def out_grow_kernel(sizes, width, total_ref, slots_ref, ranks_ref, grow_ref, *outs):
    groups, blocks, drafts = sizes
    owned = grow_ref.shape[0] // width
    me = lax.axis_index("tensor")
    ranks = None
    for source in range(blocks):
        turn = rest_of(source - me + blocks, blocks)
        moved = dot(
            reorder(sizes, group_first, group_first, turn), ranks_ref[source * groups + me]
        )
        ranks = moved if ranks is None else ranks + moved
    place = slots_ref[:, 1:2] - me * owned
    wide = spread_ranks(ranks.astype(jnp.bfloat16), place, width, owned, 1)
    full = (total_ref[...] + dot(wide, grow_ref[...])).astype(jnp.bfloat16)
    full = dot(reorder(sizes, block_first, group_first, 0), full).astype(jnp.bfloat16)
    for block in range(blocks):
        for draft in range(drafts):
            start = (block * drafts + draft) * groups
            outs[block][draft] = full[start : start + groups]


def by_head(
    tokens,
    w_query,
    w_key,
    w_value,
    w_out,
    shrink_qkv,
    grow_query,
    grow_key,
    grow_value,
    shrink_out,
    grow_out,
    cache_keys,
    cache_values,
    cache_lengths,
    adapter_ids,
    adapter_slots,
):
    blocks = lax.axis_size("tensor")
    groups = lax.axis_size(GROUP)
    _, drafts, features = tokens.shape
    sizes = (groups, blocks, drafts)
    owned = shrink_qkv.shape[0]
    width = grow_out.shape[1]
    cache_size, head_size = cache_keys.shape[2:]
    span = blocks * drafts
    count = groups * span
    lanes = -(-shrink_qkv.shape[2] // 128) * 128

    def over_tensor(value, shift):
        route = [(t, (t + shift) % blocks) for t in range(blocks)]
        return lax.ppermute(value, "tensor", route)

    def over_group(value, shift):
        route = [(g, (g + shift) % groups) for g in range(groups)]
        return lax.ppermute(value, GROUP, route)

    def exchange(value):
        return lax.all_to_all(value, EVERY, split_axis=0, concat_axis=0, tiled=True)

    mine = jnp.transpose(tokens, (1, 0, 2))
    pieces = [mine] + [over_tensor(mine, shift) for shift in range(1, blocks)]

    *messages, slots = pack(
        sizes, adapter_ids, adapter_slots, cache_lengths, cache_keys, cache_values
    )
    caches = {shift: over_tensor(messages[shift], shift) for shift in range(1, blocks) if shift != 2}

    shrink_in = jnp.transpose(shrink_qkv, (0, 2, 1)).reshape(-1, features)
    rows, rank_part = call(
        functools.partial(rank_kernel, sizes, owned),
        [shape((count, features)), shape((blocks * groups, count, lanes))],
        [VMEM] * (blocks + 2),
        [pltpu.VMEM((count, features), jnp.float32)],
    )(*pieces, shrink_in, slots)
    ranks = exchange(rank_part)
    half = features // 2
    total = stream(rows, w_query, 4, 0, half)
    total, *late = lax.optimization_barrier((total, *messages[2:3]))
    for message in late:
        caches[2] = over_tensor(message, 2)
    total = stream(rows, w_query, 4, half, features - half, total)
    caches = [messages[0]] + [caches[shift] for shift in range(1, blocks)]
    cols = total.shape[1] + w_key.shape[1] + w_value.shape[1]
    sent = call(
        functools.partial(grow_kernel, sizes, width),
        [shape((blocks, drafts, cols))] * groups,
        [VMEM] * 9,
        [],
    )(
        total,
        rows,
        w_key,
        w_value,
        slots,
        ranks,
        *[grow.reshape(owned * width, -1) for grow in (grow_query, grow_key, grow_value)],
    )
    parts = [sent[0]] + [over_group(sent[shift], shift) for shift in range(1, groups)]
    head_cols = cols - 2 * head_size
    mixed = call(
        functools.partial(attend_kernel, blocks, drafts, groups, cache_size),
        shape((span, head_cols)),
        [VMEM] * (groups + blocks),
        [
            pltpu.VMEM((blocks, head_cols // head_size * drafts, head_size), jnp.float32),
            pltpu.VMEM((2 * blocks, 128, head_size), jnp.float32),
            pltpu.VMEM((span, head_cols), jnp.float32),
        ],
        4 * span * head_cols * cache_size,
        320 * blocks * cache_size * head_size,
    )(*parts, *caches)
    gathered = lax.all_gather(mixed, GROUP, axis=0, tiled=False)
    out_rows, out_part = call(
        functools.partial(out_rank_kernel, owned),
        [shape((count, head_cols)), shape((blocks * groups, count, lanes))],
        [VMEM] * 3,
        [pltpu.VMEM((count, head_cols), jnp.float32)],
        2 * count * shrink_out.size,
        2 * shrink_out.size + 4 * count * head_cols,
    )(gathered, jnp.transpose(shrink_out, (0, 2, 1)).reshape(-1, head_cols), slots)
    out_ranks = exchange(out_part)
    out_cols = w_out.shape[1]
    out_total = product(out_rows, w_out)
    leaving = call(
        functools.partial(out_grow_kernel, sizes, width),
        [shape((drafts, groups, out_cols))] * blocks,
        [VMEM] * 4,
        [],
        2 * count * owned * width * out_cols,
        8 * count * out_cols + 2 * owned * width * out_cols,
    )(out_total, slots, out_ranks, grow_out.reshape(owned * width, -1))
    result = leaving[0].astype(jnp.float32)
    for shift in range(1, blocks):
        result = result + over_tensor(leaving[shift], -shift).astype(jnp.float32)
    return jnp.transpose(result.astype(jnp.bfloat16), (1, 0, 2))


def rotate(vectors, positions):
    half_size = vectors.shape[-1] // 2
    frequency = rope_base ** (-2.0 * jnp.arange(half_size, dtype=jnp.float32) / vectors.shape[-1])
    angles = positions[:, None, None] * frequency
    cosine = jnp.cos(angles)
    sine_value = jnp.sin(angles)
    first_half = vectors[..., :half_size]
    second = vectors[..., half_size:]
    return jnp.concatenate(
        [first_half * cosine - second * sine_value, second * cosine + first_half * sine_value], -1
    )


def to_growers(partial, splits):
    total = None
    for shift in range(splits):
        route = [
            (t * splits + g, ((g + shift) % splits) * splits + t)
            for t in range(splits)
            for g in range(splits)
        ]
        got = lax.ppermute(partial, EVERY, route).astype(jnp.float32)
        total = got if total is None else total + got
    return total


def to_out_growers(partial, splits):
    total = None
    for shift in range(splits):
        route = [
            (t * splits + g, g * splits + (t + shift) % splits)
            for t in range(splits)
            for g in range(splits)
        ]
        got = lax.ppermute(partial, EVERY, route).astype(jnp.float32)
        total = got if total is None else total + got
    return total


def slot_table(adapter_ids, adapter_slots):
    matches = adapter_ids[:, None] == jnp.arange(adapter_slots.shape[0], dtype=jnp.int32)[None, :]
    return jnp.sum(jnp.where(matches, adapter_slots[None, :], 0), axis=1)


def attend(query_heads, key_new, value_new, cache_keys, cache_values, length):
    drafts, head_count, head_size = query_heads.shape
    kv_heads, cache_size, _ = cache_keys.shape
    positions = (length + jnp.arange(drafts, dtype=jnp.int32)).astype(jnp.float32)
    query_rot = rotate(query_heads.astype(jnp.float32), positions).astype(jnp.bfloat16)
    key_rot = rotate(key_new.astype(jnp.float32), positions).astype(jnp.bfloat16)
    grouped = query_rot.reshape(drafts, kv_heads, head_count // kv_heads, head_size)
    score_scale = 1.0 / math.sqrt(head_size)
    cached = (
        jnp.einsum("skgd,kld->skgl", grouped, cache_keys, preferred_element_type=jnp.float32)
        * score_scale
    )
    fresh_scores = (
        jnp.einsum("skgd,tkd->skgt", grouped, key_rot, preferred_element_type=jnp.float32)
        * score_scale
    )
    cache_mask = jnp.arange(cache_size, dtype=jnp.int32) < length
    draft_mask = jnp.arange(drafts)[None, :] <= jnp.arange(drafts)[:, None]
    cached = jnp.where(cache_mask[None, None, None, :], cached, -jnp.inf)
    fresh_scores = jnp.where(draft_mask[:, None, None, :], fresh_scores, -jnp.inf)
    row_peak = jnp.maximum(jnp.max(cached, -1), jnp.max(fresh_scores, -1))
    cached_exp = jnp.exp(cached - row_peak[..., None])
    fresh_exp = jnp.exp(fresh_scores - row_peak[..., None])
    denominator = jnp.sum(cached_exp, -1) + jnp.sum(fresh_exp, -1)
    cached_prob = (cached_exp / denominator[..., None]).astype(jnp.bfloat16)
    fresh_prob = (fresh_exp / denominator[..., None]).astype(jnp.bfloat16)
    mixed = jnp.einsum(
        "skgl,kld->skgd", cached_prob, cache_values, preferred_element_type=jnp.float32
    )
    mixed = mixed + jnp.einsum(
        "skgt,tkd->skgd", fresh_prob, value_new, preferred_element_type=jnp.float32
    )
    return mixed.astype(jnp.bfloat16)


def by_row(
    tokens,
    w_query,
    w_key,
    w_value,
    w_out,
    shrink_qkv,
    grow_query,
    grow_key,
    grow_value,
    shrink_out,
    grow_out,
    cache_keys,
    cache_values,
    cache_lengths,
    adapter_ids,
    adapter_slots,
):
    splits = lax.axis_size("tensor")
    groups = lax.axis_size(("dp", "pipe"))
    tensor_index = lax.axis_index("tensor")
    group_index = lax.axis_index(("dp", "pipe"))
    local_rows, drafts, feature_width = tokens.shape
    per_owner = shrink_qkv.shape[0]
    rank_size = grow_out.shape[1]
    query_cols = w_query.shape[1]
    key_cols = w_key.shape[1]
    kv_heads = cache_keys.shape[1]
    head_size = cache_keys.shape[3]
    rows = splits * groups
    row_slots = jnp.repeat(slot_table(adapter_ids, adapter_slots), drafts)
    within = jnp.arange(per_owner, dtype=jnp.int32)[None, :]
    width_hot = (row_slots[:, None] == within + tensor_index * per_owner)[:, :, None]
    column_hot = (row_slots[:, None] == within + group_index * per_owner)[:, :, None]

    def spread_ranks(ranks, hot):
        return jnp.where(hot, ranks[:, None, :], 0.0).reshape(rows * drafts, -1).astype(jnp.bfloat16)

    flat_tokens = lax.all_gather(tokens, "tensor", axis=0, tiled=True).reshape(
        rows * drafts, feature_width
    )
    rank_part = jnp.einsum(
        "nd,adr->nar", flat_tokens, shrink_qkv, preferred_element_type=jnp.float32
    )
    rank_part = jnp.sum(jnp.where(width_hot, rank_part, 0.0), 1)
    rank_all = to_growers(rank_part.astype(jnp.bfloat16), splits)

    def grown(index, grow):
        ranks = spread_ranks(rank_all[:, index * rank_size : (index + 1) * rank_size], column_hot)
        return jnp.dot(
            ranks, grow.reshape(per_owner * rank_size, -1), preferred_element_type=jnp.float32
        )

    bases = [
        jnp.dot(flat_tokens, weight, preferred_element_type=jnp.float32)
        for weight in (w_query, w_key, w_value)
    ]

    def product(index, grow):
        return (bases[index] + grown(index, grow)).astype(jnp.bfloat16).reshape(rows, drafts, -1)

    partial = jnp.concatenate(
        [
            product(0, grow_query),
            product(1, grow_key),
            product(2, grow_value),
        ],
        2,
    )
    arrived = lax.all_to_all(partial, EVERY, split_axis=0, concat_axis=0, tiled=True)
    joined = jnp.sum(
        arrived.reshape(splits, groups, drafts, -1).astype(jnp.float32), 1
    ).astype(jnp.bfloat16)
    joined = jnp.transpose(joined, (1, 0, 2))
    query_heads = joined[:, :, :query_cols].reshape(drafts, -1, head_size)
    key_new = joined[:, :, query_cols : query_cols + key_cols].reshape(drafts, kv_heads, head_size)
    value_new = joined[:, :, query_cols + key_cols :].reshape(drafts, kv_heads, head_size)
    mixed = attend(
        query_heads, key_new, value_new, cache_keys[0], cache_values[0], cache_lengths[0]
    )
    mixed = jnp.transpose(mixed.reshape(drafts, splits, -1), (1, 0, 2))
    outgoing = jnp.repeat(mixed, groups, axis=0)
    flat_heads = lax.all_to_all(
        outgoing, EVERY, split_axis=0, concat_axis=0, tiled=True
    ).reshape(rows * drafts, -1)
    out_part = jnp.einsum(
        "nw,awr->nar", flat_heads, shrink_out, preferred_element_type=jnp.float32
    )
    out_part = jnp.sum(jnp.where(column_hot, out_part, 0.0), 1)
    out_rank = to_out_growers(out_part.astype(jnp.bfloat16), splits)
    out = jnp.dot(flat_heads, w_out, preferred_element_type=jnp.float32)
    out = out + jnp.dot(
        spread_ranks(out_rank, width_hot),
        grow_out.reshape(per_owner * rank_size, -1),
        preferred_element_type=jnp.float32,
    )
    blocks = lax.all_to_all(
        out.astype(jnp.bfloat16).reshape(splits, local_rows, drafts, feature_width),
        "tensor",
        split_axis=0,
        concat_axis=0,
        tiled=True,
    )
    return jnp.sum(blocks.astype(jnp.float32), 0).astype(jnp.bfloat16)


def local(*arrays):
    heads = arrays[11].shape[1]
    if heads == lax.axis_size("tensor") == lax.axis_size(GROUP):
        return by_head(*arrays)
    return by_row(*arrays)


def solution(mesh):
    placed = (
        P(("parts", "tensor"), None, ("dp", "pipe")),
        P(("dp", "pipe"), "tensor"),
        P(("dp", "pipe"), "tensor"),
        P(("dp", "pipe"), "tensor"),
        P("tensor", ("dp", "pipe")),
        P("tensor", ("dp", "pipe"), None),
        P(("dp", "pipe"), None, "tensor"),
        P(("dp", "pipe"), None, "tensor"),
        P(("dp", "pipe"), None, "tensor"),
        P(("dp", "pipe"), "tensor", None),
        P("tensor", None, ("dp", "pipe")),
        P(("parts", "tensor", "dp", "pipe"), None, None, None),
        P(("parts", "tensor", "dp", "pipe"), None, None, None),
        P(("parts", "tensor", "dp", "pipe")),
        P(),
        P(),
    )
    return jax.shard_map(
        local,
        mesh=mesh,
        in_specs=placed,
        out_specs=P(("parts", "tensor"), None, ("dp", "pipe")),
        check_vma=False,
    )
```

```python
import functools
import math

import jax
import jax.numpy as jnp
from jax import lax
from jax.experimental import pallas as pl
from jax.experimental.pallas import tpu as pltpu
from jax.sharding import PartitionSpec as P

rope_base = 500000.0
EVERY = ("tensor", "dp", "pipe")
GROUP = ("dp", "pipe")
VMEM = pl.BlockSpec(memory_space=pltpu.VMEM)
HBM = pl.BlockSpec(memory_space=pltpu.HBM)
MIB = 1 << 20


def dot(left, right):
    return jnp.dot(left, right, preferred_element_type=jnp.float32)


def dot_nt(left, right):
    return lax.dot_general(
        left, right, (((1,), (1,)), ((), ())), preferred_element_type=jnp.float32
    )


def iota(shape, axis):
    return lax.broadcasted_iota(jnp.int32, shape, axis)


def call(kernel, outs, ins, scratch=(), flops=0, moved=0, limit=24 * MIB):
    return pl.pallas_call(
        kernel,
        out_shape=outs,
        in_specs=ins,
        out_specs=jax.tree.map(lambda _: VMEM, outs),
        scratch_shapes=list(scratch),
        cost_estimate=pl.CostEstimate(flops=flops, bytes_accessed=moved, transcendentals=0),
        compiler_params=pltpu.CompilerParams(vmem_limit_bytes=limit),
    )


def shape(dims, kind=jnp.bfloat16):
    return jax.ShapeDtypeStruct(tuple(dims), kind)


def over(value, size):
    return value >> (size.bit_length() - 1) if size & (size - 1) == 0 else lax.div(value, size)


def rest_of(value, size):
    return value & (size - 1) if size & (size - 1) == 0 else lax.rem(value, size)


def block_first(sizes, group, block, draft):
    groups, blocks, drafts = sizes
    return (block * drafts + draft) * groups + group


def group_first(sizes, group, block, draft):
    groups, blocks, drafts = sizes
    return (group * blocks + block) * drafts + draft


def parts_of(order, sizes, index):
    groups, blocks, drafts = sizes
    if order is block_first:
        return (
            rest_of(index, groups),
            over(index, groups * drafts),
            rest_of(over(index, groups), drafts),
        )
    return over(index, blocks * drafts), rest_of(over(index, drafts), blocks), rest_of(index, drafts)


def reorder(sizes, after, before, turn_block, turn_group=0):
    groups, blocks, drafts = sizes
    rows = groups * blocks * drafts
    group, block, draft = parts_of(after, sizes, iota((rows, rows), 0))
    wanted = before(
        sizes, rest_of(group + turn_group, groups), rest_of(block + turn_block, blocks), draft
    )
    return jnp.where(wanted == iota((rows, rows), 1), 1.0, 0.0).astype(jnp.bfloat16)


def group_of():
    return lax.axis_index("dp") * lax.axis_size("pipe") + lax.axis_index("pipe")


def rank_kernel(sizes, owned, *refs):
    groups, blocks, drafts = sizes
    pieces = refs[:blocks]
    shrink_ref, slots_ref, rows_ref, rank_ref, wide = refs[blocks:]
    for block in range(blocks):
        for draft in range(drafts):
            start = (block * drafts + draft) * groups
            wide[start : start + groups, :] = pieces[block][draft].astype(jnp.float32)
    rows = wide[...].astype(jnp.bfloat16)
    rows_ref[...] = rows
    place = slots_ref[:, 0:1] - lax.axis_index("tensor") * owned
    ranks = owned_ranks(
        rows, shrink_ref[...], place, shrink_ref.shape[0] // owned, rank_ref.shape[2]
    )
    for target in range(rank_ref.shape[0]):
        rank_ref[target] = ranks


def owned_ranks(rows, shrink, place, width, lanes):
    ranks = dot_nt(rows, shrink)
    kept = jnp.where(over(iota(ranks.shape, 1), width) == place, ranks, 0.0).astype(jnp.bfloat16)
    fold = (ranks.shape[1], lanes)
    fold = rest_of(iota(fold, 0), width) == iota(fold, 1)
    return dot(kept, jnp.where(fold, 1.0, 0.0).astype(jnp.bfloat16)).astype(jnp.bfloat16)


def spread_ranks(ranks, place, width, owned, parts):
    span = owned * width
    row = iota((ranks.shape[1], parts * span), 0)
    column = iota((ranks.shape[1], parts * span), 1)
    tile = (over(row, width) == over(column, span)) & (
        rest_of(row, width) == rest_of(column, width)
    )
    wide = dot(ranks, jnp.where(tile, 1.0, 0.0).astype(jnp.bfloat16))
    slot = over(rest_of(iota(wide.shape, 1), span), width)
    return jnp.where(slot == place, wide, 0.0).astype(jnp.bfloat16)


def product_kernel(first, depth, rows_ref, weight_ref, *refs):
    *sums, total_ref = refs
    width = total_ref.shape[1]
    step = width if width % 1024 else 1024
    for start in range(0, width, step):
        part = dot(
            rows_ref[:, first : first + depth],
            weight_ref[first : first + depth, start : start + step],
        )
        if sums:
            part = sums[0][:, start : start + step] + part
        total_ref[:, start : start + step] = part


def product(rows, weight, first, depth, *sums):
    width = weight.shape[1]
    return call(
        functools.partial(product_kernel, first, depth),
        shape((rows.shape[0], width), jnp.float32),
        [VMEM] * (2 + len(sums)),
    )(rows, weight, *sums)


def pack_kernel(sizes, ids_ref, pool_ref, length_ref, keys_ref, values_ref, *refs):
    refs = refs[2:]
    groups, blocks, drafts = sizes
    outs = refs[:blocks]
    slots_ref, extra_f32, extra_ref, sems = refs[blocks:]
    size, head_size = keys_ref.shape[2:]
    me = lax.axis_index("tensor")
    length = length_ref[0]
    positions = (iota((drafts, head_size), 0) + length).astype(jnp.float32)
    lane = iota((drafts, head_size), 1)
    half = (lane & (head_size // 2 - 1)).astype(jnp.float32)
    angles = positions * jnp.exp(half * (-2.0 * math.log(rope_base) / head_size))
    signs = jnp.where(lane < head_size // 2, -1.0, 1.0)
    extra_f32[...] = jnp.zeros(extra_f32.shape, jnp.float32)
    for index, value in enumerate((jnp.cos(angles), jnp.sin(angles) * signs)):
        high = value.astype(jnp.bfloat16).astype(jnp.float32)
        start = 2 * index * drafts
        extra_f32[start : start + drafts, :] = high
        extra_f32[start + drafts : start + 2 * drafts, :] = value - high
    ones = jnp.ones((1, head_size), jnp.float32)
    extra_f32[4 * drafts : 4 * drafts + 1, :] = ones * (length >> 4).astype(jnp.float32)
    extra_f32[4 * drafts + 1 : 4 * drafts + 2, :] = ones * (length & 15).astype(jnp.float32)
    extra_ref[...] = extra_f32[...].astype(jnp.bfloat16)
    copies = []
    for shift in range(blocks):
        head = lax.rem(me + shift, blocks)
        copies += [
            pltpu.make_async_copy(
                keys_ref.at[0, head], outs[shift].at[pl.ds(0, size)], sems.at[shift, 0]
            ),
            pltpu.make_async_copy(
                values_ref.at[0, head], outs[shift].at[pl.ds(size, size)], sems.at[shift, 1]
            ),
            pltpu.make_async_copy(
                extra_ref,
                outs[shift].at[pl.ds(2 * size, extra_ref.shape[0])],
                sems.at[shift, 2],
            ),
        ]
    for copy in copies:
        copy.start()
    index = iota(slots_ref.shape, 0)
    column = iota(slots_ref.shape, 1)
    near = parts_of(block_first, sizes, index)
    far = parts_of(group_first, sizes, index)
    row_group = jnp.where(column == 0, near[0], far[0])
    row_block = jnp.where(column == 0, near[1], far[1])
    place = row_block * groups + row_group
    slots = jnp.zeros(slots_ref.shape, jnp.int32)
    for block in range(blocks):
        for group in range(groups):
            row = lax.rem(me - block + blocks, blocks) * groups + group
            slots = jnp.where(place == block * groups + group, pool_ref[ids_ref[row]], slots)
    slots_ref[...] = slots
    for copy in copies:
        copy.wait()


def pack(sizes, ids, pool, lengths, keys, values, later):
    groups, blocks, drafts = sizes
    head_size = keys.shape[3]
    used = -(-(4 * drafts + 2) // 16) * 16
    outs = [shape((2 * keys.shape[2] + used, head_size))] * blocks
    smem = pl.BlockSpec(memory_space=pltpu.SMEM)
    return pl.pallas_call(
        functools.partial(pack_kernel, sizes),
        out_shape=outs + [shape((groups * blocks * drafts, 128), jnp.int32)],
        in_specs=[smem, smem, smem, VMEM, VMEM] + [HBM] * 2,
        out_specs=[HBM] * blocks + [VMEM],
        scratch_shapes=[
            pltpu.VMEM((used, head_size), jnp.float32),
            pltpu.VMEM((used, head_size), jnp.bfloat16),
            pltpu.SemaphoreType.DMA((blocks, 3)),
        ],
        cost_estimate=pl.CostEstimate(flops=0, bytes_accessed=320 * keys.size, transcendentals=0),
        compiler_params=pltpu.CompilerParams(vmem_limit_bytes=40 * MIB),
    )(ids, pool, lengths, keys, values, *[later] * 2)


def grow_kernel(sizes, width, total_ref, rows_ref, key_ref, value_ref, slots_ref, ranks_ref, *rest):
    groups, blocks, drafts = sizes
    grows = rest[:3]
    outs = rest[3:]
    group = group_of()
    owned = grows[0].shape[0] // width
    ranks = ranks_ref[group * groups].astype(jnp.float32)
    for other in range(1, groups):
        ranks = ranks + ranks_ref[group * groups + other].astype(jnp.float32)
    turn = rest_of(group - lax.axis_index("tensor") + blocks, blocks)
    ranks = dot(reorder(sizes, block_first, block_first, turn), ranks.astype(jnp.bfloat16))
    place = slots_ref[:, 0:1] - group * owned
    wide = spread_ranks(ranks.astype(jnp.bfloat16), place, width, owned, len(grows))
    by_group = reorder(sizes, group_first, block_first, 0, group)
    start = 0
    for index, grow in enumerate(grows):
        deep, cols = grow.shape
        base = total_ref[...] if index == 0 else dot(rows_ref[...], (key_ref, value_ref)[index - 1][...])
        full = base + dot(wide[:, index * deep : (index + 1) * deep], grow[...])
        full = dot(by_group, full.astype(jnp.bfloat16)).astype(jnp.bfloat16)
        for step in range(groups):
            for block in range(blocks):
                row = (step * blocks + block) * drafts
                outs[step][block, :, start : start + cols] = full[row : row + drafts]
        start += cols


def attend_kernel(blocks, drafts, groups, cache_size, *refs):
    parts = refs[:groups]
    caches = refs[groups : groups + blocks]
    _, mixed_ref, query_s, fresh_s, out_s = refs[groups + blocks :]
    head_size = caches[0].shape[1]
    cols = parts[0].shape[2]
    heads = cols // head_size - 2
    count = heads * drafts
    scale = 1.0 / math.sqrt(head_size)
    fresh_s[...] = jnp.zeros(fresh_s.shape, jnp.float32)
    pad = fresh_s.shape[1]
    for block in range(blocks):
        joined = parts[0][block].astype(jnp.float32)
        for other in parts[1:]:
            joined = joined + other[block].astype(jnp.float32)
        joined = joined.astype(jnp.bfloat16).astype(jnp.float32)
        extra = caches[block][2 * cache_size :, :].astype(jnp.float32)
        cosine = extra[0:drafts] + extra[drafts : 2 * drafts]
        sine = extra[2 * drafts : 3 * drafts] + extra[3 * drafts : 4 * drafts]
        length = extra[4 * drafts : 4 * drafts + 1, 0:1] * 16.0 + extra[
            4 * drafts + 1 : 4 * drafts + 2, 0:1
        ]

        def rotated(head):
            value = joined[:, head * head_size : (head + 1) * head_size]
            return value * cosine + pltpu.roll(value, head_size // 2, 1) * sine

        for head in range(heads):
            query_s[block, head * drafts : (head + 1) * drafts, :] = rotated(head)
        fresh_s[2 * block, 0:drafts, :] = rotated(heads)
        fresh_s[2 * block + 1, 0:drafts, :] = joined[:, (heads + 1) * head_size :]
        query = query_s[block].astype(jnp.bfloat16)
        old = dot_nt(query, caches[block][0:cache_size, :]) * scale
        new = dot_nt(query, fresh_s[2 * block].astype(jnp.bfloat16)) * scale
        old_seen = iota(old.shape, 1).astype(jnp.float32) < length
        new_seen = iota(new.shape, 1) <= lax.rem(iota(new.shape, 0), drafts)
        old = jnp.where(old_seen, old, -jnp.inf)
        new = jnp.where(new_seen, new, -jnp.inf)
        peak = jnp.maximum(
            jnp.max(old, 1, keepdims=True), jnp.max(new, 1, keepdims=True)
        )
        old = jnp.exp(old - peak)
        new = jnp.exp(new - peak)
        below = jnp.sum(old, 1, keepdims=True) + jnp.sum(new, 1, keepdims=True)
        mixed = dot(
            (old / below).astype(jnp.bfloat16), caches[block][cache_size : 2 * cache_size, :]
        ) + dot((new / below).astype(jnp.bfloat16), fresh_s[2 * block + 1].astype(jnp.bfloat16))
        for head in range(heads):
            out_s[
                block * drafts : (block + 1) * drafts, head * head_size : (head + 1) * head_size
            ] = mixed[head * drafts : (head + 1) * drafts]
    mixed_ref[...] = out_s[...].astype(jnp.bfloat16)


def out_rank_kernel(owned, got_ref, shrink_ref, slots_ref, rows_ref, rank_ref, wide):
    span = got_ref.shape[1]
    for group in range(got_ref.shape[0]):
        wide[group * span : (group + 1) * span, :] = got_ref[group].astype(jnp.float32)
    rows = wide[...].astype(jnp.bfloat16)
    rows_ref[...] = rows
    place = slots_ref[:, 1:2] - group_of() * owned
    ranks = owned_ranks(
        rows, shrink_ref[...], place, shrink_ref.shape[0] // owned, rank_ref.shape[2]
    )
    for target in range(rank_ref.shape[0]):
        rank_ref[target] = ranks


def out_grow_kernel(sizes, width, total_ref, slots_ref, ranks_ref, grow_ref, *outs):
    groups, blocks, drafts = sizes
    owned = grow_ref.shape[0] // width
    me = lax.axis_index("tensor")
    ranks = None
    for source in range(blocks):
        turn = rest_of(source - me + blocks, blocks)
        moved = dot(
            reorder(sizes, group_first, group_first, turn), ranks_ref[source * groups + me]
        )
        ranks = moved if ranks is None else ranks + moved
    place = slots_ref[:, 1:2] - me * owned
    wide = spread_ranks(ranks.astype(jnp.bfloat16), place, width, owned, 1)
    full = (total_ref[...] + dot(wide, grow_ref[...])).astype(jnp.bfloat16)
    full = dot(reorder(sizes, block_first, group_first, 0), full).astype(jnp.bfloat16)
    for block in range(blocks):
        for draft in range(drafts):
            start = (block * drafts + draft) * groups
            outs[block][draft] = full[start : start + groups]


def by_head(
    tokens,
    w_query,
    w_key,
    w_value,
    w_out,
    shrink_qkv,
    grow_query,
    grow_key,
    grow_value,
    shrink_out,
    grow_out,
    cache_keys,
    cache_values,
    cache_lengths,
    adapter_ids,
    adapter_slots,
):
    blocks = lax.axis_size("tensor")
    groups = lax.axis_size(GROUP)
    _, drafts, features = tokens.shape
    sizes = (groups, blocks, drafts)
    owned = shrink_qkv.shape[0]
    width = grow_out.shape[1]
    cache_size, head_size = cache_keys.shape[2:]
    span = blocks * drafts
    count = groups * span
    lanes = -(-shrink_qkv.shape[2] // 128) * 128

    def over_tensor(value, shift):
        route = [(t, (t + shift) % blocks) for t in range(blocks)]
        return lax.ppermute(value, "tensor", route)

    def over_group(value, shift):
        route = [(g, (g + shift) % groups) for g in range(groups)]
        return lax.ppermute(value, GROUP, route)

    def exchange(value):
        return lax.all_to_all(value, EVERY, split_axis=0, concat_axis=0, tiled=True)

    mine = jnp.transpose(tokens, (1, 0, 2))
    pieces = [mine] + [over_tensor(mine, shift) for shift in range(1, blocks)]

    *messages, slots = pack(
        sizes, adapter_ids, adapter_slots, cache_lengths, cache_keys, cache_values, w_out
    )
    caches = {shift: over_tensor(messages[shift], shift) for shift in range(1, blocks) if shift != 2}

    shrink_in = jnp.transpose(shrink_qkv, (0, 2, 1)).reshape(-1, features)
    rows, rank_part = call(
        functools.partial(rank_kernel, sizes, owned),
        [shape((count, features)), shape((blocks * groups, count, lanes))],
        [VMEM] * (blocks + 2),
        [pltpu.VMEM((count, features), jnp.float32)],
    )(*pieces, shrink_in, slots)
    ranks = exchange(rank_part)
    half = features // 2
    total = product(rows, w_query, 0, half)
    total, *late = lax.optimization_barrier((total, *messages[2:3]))
    for message in late:
        caches[2] = over_tensor(message, 2)
    total = product(rows, w_query, half, features - half, total)
    caches = [messages[0]] + [caches[shift] for shift in range(1, blocks)]
    cols = total.shape[1] + w_key.shape[1] + w_value.shape[1]
    sent = call(
        functools.partial(grow_kernel, sizes, width),
        [shape((blocks, drafts, cols))] * groups,
        [VMEM] * 9,
        [],
    )(
        total,
        rows,
        w_key,
        w_value,
        slots,
        ranks,
        *[grow.reshape(owned * width, -1) for grow in (grow_query, grow_key, grow_value)],
    )
    parts = [sent[0]] + [over_group(sent[shift], shift) for shift in range(1, groups)]
    head_cols = cols - 2 * head_size
    mixed = call(
        functools.partial(attend_kernel, blocks, drafts, groups, cache_size),
        shape((span, head_cols)),
        [VMEM] * (groups + blocks) + [HBM],
        [
            pltpu.VMEM((blocks, head_cols // head_size * drafts, head_size), jnp.float32),
            pltpu.VMEM((2 * blocks, 128, head_size), jnp.float32),
            pltpu.VMEM((span, head_cols), jnp.float32),
        ],
        4 * span * head_cols * cache_size,
        320 * blocks * cache_size * head_size,
        40 * MIB,
    )(*parts, *caches, w_query)
    gathered = lax.all_gather(mixed, GROUP, axis=0, tiled=False)
    out_rows, out_part = call(
        functools.partial(out_rank_kernel, owned),
        [shape((count, head_cols)), shape((blocks * groups, count, lanes))],
        [VMEM] * 3,
        [pltpu.VMEM((count, head_cols), jnp.float32)],
        2 * count * shrink_out.size,
        2 * shrink_out.size + 4 * count * head_cols,
    )(gathered, jnp.transpose(shrink_out, (0, 2, 1)).reshape(-1, head_cols), slots)
    out_ranks = exchange(out_part)
    out_cols = w_out.shape[1]
    out_total = product(out_rows, w_out, 0, head_cols)
    leaving = call(
        functools.partial(out_grow_kernel, sizes, width),
        [shape((drafts, groups, out_cols))] * blocks,
        [VMEM] * 4,
        [],
        2 * count * owned * width * out_cols,
        8 * count * out_cols + 2 * owned * width * out_cols,
    )(out_total, slots, out_ranks, grow_out.reshape(owned * width, -1))
    result = leaving[0].astype(jnp.float32)
    for shift in range(1, blocks):
        result = result + over_tensor(leaving[shift], -shift).astype(jnp.float32)
    return jnp.transpose(result.astype(jnp.bfloat16), (1, 0, 2))


def rotate(vectors, positions):
    half_size = vectors.shape[-1] // 2
    frequency = rope_base ** (-2.0 * jnp.arange(half_size, dtype=jnp.float32) / vectors.shape[-1])
    angles = positions[:, None, None] * frequency
    cosine = jnp.cos(angles)
    sine_value = jnp.sin(angles)
    first_half = vectors[..., :half_size]
    second = vectors[..., half_size:]
    return jnp.concatenate(
        [first_half * cosine - second * sine_value, second * cosine + first_half * sine_value], -1
    )


def to_growers(partial, splits):
    total = None
    for shift in range(splits):
        route = [
            (t * splits + g, ((g + shift) % splits) * splits + t)
            for t in range(splits)
            for g in range(splits)
        ]
        got = lax.ppermute(partial, EVERY, route).astype(jnp.float32)
        total = got if total is None else total + got
    return total


def to_out_growers(partial, splits):
    total = None
    for shift in range(splits):
        route = [
            (t * splits + g, g * splits + (t + shift) % splits)
            for t in range(splits)
            for g in range(splits)
        ]
        got = lax.ppermute(partial, EVERY, route).astype(jnp.float32)
        total = got if total is None else total + got
    return total


def slot_table(adapter_ids, adapter_slots):
    matches = adapter_ids[:, None] == jnp.arange(adapter_slots.shape[0], dtype=jnp.int32)[None, :]
    return jnp.sum(jnp.where(matches, adapter_slots[None, :], 0), axis=1)


def attend(query_heads, key_new, value_new, cache_keys, cache_values, length):
    drafts, head_count, head_size = query_heads.shape
    kv_heads, cache_size, _ = cache_keys.shape
    positions = (length + jnp.arange(drafts, dtype=jnp.int32)).astype(jnp.float32)
    query_rot = rotate(query_heads.astype(jnp.float32), positions).astype(jnp.bfloat16)
    key_rot = rotate(key_new.astype(jnp.float32), positions).astype(jnp.bfloat16)
    grouped = query_rot.reshape(drafts, kv_heads, head_count // kv_heads, head_size)
    score_scale = 1.0 / math.sqrt(head_size)
    cached = (
        jnp.einsum("skgd,kld->skgl", grouped, cache_keys, preferred_element_type=jnp.float32)
        * score_scale
    )
    fresh_scores = (
        jnp.einsum("skgd,tkd->skgt", grouped, key_rot, preferred_element_type=jnp.float32)
        * score_scale
    )
    cache_mask = jnp.arange(cache_size, dtype=jnp.int32) < length
    draft_mask = jnp.arange(drafts)[None, :] <= jnp.arange(drafts)[:, None]
    cached = jnp.where(cache_mask[None, None, None, :], cached, -jnp.inf)
    fresh_scores = jnp.where(draft_mask[:, None, None, :], fresh_scores, -jnp.inf)
    row_peak = jnp.maximum(jnp.max(cached, -1), jnp.max(fresh_scores, -1))
    cached_exp = jnp.exp(cached - row_peak[..., None])
    fresh_exp = jnp.exp(fresh_scores - row_peak[..., None])
    denominator = jnp.sum(cached_exp, -1) + jnp.sum(fresh_exp, -1)
    cached_prob = (cached_exp / denominator[..., None]).astype(jnp.bfloat16)
    fresh_prob = (fresh_exp / denominator[..., None]).astype(jnp.bfloat16)
    mixed = jnp.einsum(
        "skgl,kld->skgd", cached_prob, cache_values, preferred_element_type=jnp.float32
    )
    mixed = mixed + jnp.einsum(
        "skgt,tkd->skgd", fresh_prob, value_new, preferred_element_type=jnp.float32
    )
    return mixed.astype(jnp.bfloat16)


def by_row(
    tokens,
    w_query,
    w_key,
    w_value,
    w_out,
    shrink_qkv,
    grow_query,
    grow_key,
    grow_value,
    shrink_out,
    grow_out,
    cache_keys,
    cache_values,
    cache_lengths,
    adapter_ids,
    adapter_slots,
):
    splits = lax.axis_size("tensor")
    groups = lax.axis_size(("dp", "pipe"))
    tensor_index = lax.axis_index("tensor")
    group_index = lax.axis_index(("dp", "pipe"))
    local_rows, drafts, feature_width = tokens.shape
    per_owner = shrink_qkv.shape[0]
    rank_size = grow_out.shape[1]
    query_cols = w_query.shape[1]
    key_cols = w_key.shape[1]
    kv_heads = cache_keys.shape[1]
    head_size = cache_keys.shape[3]
    rows = splits * groups
    row_slots = jnp.repeat(slot_table(adapter_ids, adapter_slots), drafts)
    within = jnp.arange(per_owner, dtype=jnp.int32)[None, :]
    width_hot = (row_slots[:, None] == within + tensor_index * per_owner)[:, :, None]
    column_hot = (row_slots[:, None] == within + group_index * per_owner)[:, :, None]

    def spread_ranks(ranks, hot):
        return jnp.where(hot, ranks[:, None, :], 0.0).reshape(rows * drafts, -1).astype(jnp.bfloat16)

    flat_tokens = lax.all_gather(tokens, "tensor", axis=0, tiled=True).reshape(
        rows * drafts, feature_width
    )
    rank_part = jnp.einsum(
        "nd,adr->nar", flat_tokens, shrink_qkv, preferred_element_type=jnp.float32
    )
    rank_part = jnp.sum(jnp.where(width_hot, rank_part, 0.0), 1)
    rank_all = to_growers(rank_part.astype(jnp.bfloat16), splits)

    def grown(index, grow):
        ranks = spread_ranks(rank_all[:, index * rank_size : (index + 1) * rank_size], column_hot)
        return jnp.dot(
            ranks, grow.reshape(per_owner * rank_size, -1), preferred_element_type=jnp.float32
        )

    bases = [
        jnp.dot(flat_tokens, weight, preferred_element_type=jnp.float32)
        for weight in (w_query, w_key, w_value)
    ]

    def product(index, grow):
        return (bases[index] + grown(index, grow)).astype(jnp.bfloat16).reshape(rows, drafts, -1)

    partial = jnp.concatenate(
        [
            product(0, grow_query),
            product(1, grow_key),
            product(2, grow_value),
        ],
        2,
    )
    arrived = lax.all_to_all(partial, EVERY, split_axis=0, concat_axis=0, tiled=True)
    joined = jnp.sum(
        arrived.reshape(splits, groups, drafts, -1).astype(jnp.float32), 1
    ).astype(jnp.bfloat16)
    joined = jnp.transpose(joined, (1, 0, 2))
    query_heads = joined[:, :, :query_cols].reshape(drafts, -1, head_size)
    key_new = joined[:, :, query_cols : query_cols + key_cols].reshape(drafts, kv_heads, head_size)
    value_new = joined[:, :, query_cols + key_cols :].reshape(drafts, kv_heads, head_size)
    mixed = attend(
        query_heads, key_new, value_new, cache_keys[0], cache_values[0], cache_lengths[0]
    )
    mixed = jnp.transpose(mixed.reshape(drafts, splits, -1), (1, 0, 2))
    outgoing = jnp.repeat(mixed, groups, axis=0)
    flat_heads = lax.all_to_all(
        outgoing, EVERY, split_axis=0, concat_axis=0, tiled=True
    ).reshape(rows * drafts, -1)
    out_part = jnp.einsum(
        "nw,awr->nar", flat_heads, shrink_out, preferred_element_type=jnp.float32
    )
    out_part = jnp.sum(jnp.where(column_hot, out_part, 0.0), 1)
    out_rank = to_out_growers(out_part.astype(jnp.bfloat16), splits)
    out = jnp.dot(flat_heads, w_out, preferred_element_type=jnp.float32)
    out = out + jnp.dot(
        spread_ranks(out_rank, width_hot),
        grow_out.reshape(per_owner * rank_size, -1),
        preferred_element_type=jnp.float32,
    )
    blocks = lax.all_to_all(
        out.astype(jnp.bfloat16).reshape(splits, local_rows, drafts, feature_width),
        "tensor",
        split_axis=0,
        concat_axis=0,
        tiled=True,
    )
    return jnp.sum(blocks.astype(jnp.float32), 0).astype(jnp.bfloat16)


def local(*arrays):
    heads = arrays[11].shape[1]
    if heads == lax.axis_size("tensor") == lax.axis_size(GROUP):
        return by_head(*arrays)
    return by_row(*arrays)


def solution(mesh):
    placed = (
        P(("parts", "tensor"), None, ("dp", "pipe")),
        P(("dp", "pipe"), "tensor"),
        P(("dp", "pipe"), "tensor"),
        P(("dp", "pipe"), "tensor"),
        P("tensor", ("dp", "pipe")),
        P("tensor", ("dp", "pipe"), None),
        P(("dp", "pipe"), None, "tensor"),
        P(("dp", "pipe"), None, "tensor"),
        P(("dp", "pipe"), None, "tensor"),
        P(("dp", "pipe"), "tensor", None),
        P("tensor", None, ("dp", "pipe")),
        P(("parts", "tensor", "dp", "pipe"), None, None, None),
        P(("parts", "tensor", "dp", "pipe"), None, None, None),
        P(("parts", "tensor", "dp", "pipe")),
        P(),
        P(),
    )
    return jax.shard_map(
        local,
        mesh=mesh,
        in_specs=placed,
        out_specs=P(("parts", "tensor"), None, ("dp", "pipe")),
        check_vma=False,
    )
```

```python
import functools
import math

import jax
import jax.numpy as jnp
from jax import lax
from jax.experimental import pallas as pl
from jax.experimental.pallas import tpu as pltpu
from jax.sharding import PartitionSpec as P

rope_base = 500000.0
EVERY = ("tensor", "dp", "pipe")
GROUP = ("dp", "pipe")
VMEM = pl.BlockSpec(memory_space=pltpu.VMEM)
HBM = pl.BlockSpec(memory_space=pltpu.HBM)
MIB = 1 << 20


def dot(left, right):
    return jnp.dot(left, right, preferred_element_type=jnp.float32)


def dot_nt(left, right):
    return lax.dot_general(
        left, right, (((1,), (1,)), ((), ())), preferred_element_type=jnp.float32
    )


def iota(shape, axis):
    return lax.broadcasted_iota(jnp.int32, shape, axis)


def call(kernel, outs, ins, scratch=(), flops=0, moved=0, limit=24 * MIB):
    return pl.pallas_call(
        kernel,
        out_shape=outs,
        in_specs=ins,
        out_specs=jax.tree.map(lambda _: VMEM, outs),
        scratch_shapes=list(scratch),
        cost_estimate=pl.CostEstimate(flops=flops, bytes_accessed=moved, transcendentals=0),
        compiler_params=pltpu.CompilerParams(vmem_limit_bytes=limit),
    )


def shape(dims, kind=jnp.bfloat16):
    return jax.ShapeDtypeStruct(tuple(dims), kind)


def over(value, size):
    return value >> (size.bit_length() - 1) if size & (size - 1) == 0 else lax.div(value, size)


def rest_of(value, size):
    return value & (size - 1) if size & (size - 1) == 0 else lax.rem(value, size)


def block_first(sizes, group, block, draft):
    groups, blocks, drafts = sizes
    return (block * drafts + draft) * groups + group


def group_first(sizes, group, block, draft):
    groups, blocks, drafts = sizes
    return (group * blocks + block) * drafts + draft


def parts_of(order, sizes, index):
    groups, blocks, drafts = sizes
    if order is block_first:
        return (
            rest_of(index, groups),
            over(index, groups * drafts),
            rest_of(over(index, groups), drafts),
        )
    return over(index, blocks * drafts), rest_of(over(index, drafts), blocks), rest_of(index, drafts)


def reorder(sizes, after, before, turn_block, turn_group=0):
    groups, blocks, drafts = sizes
    rows = groups * blocks * drafts
    group, block, draft = parts_of(after, sizes, iota((rows, rows), 0))
    wanted = before(
        sizes, rest_of(group + turn_group, groups), rest_of(block + turn_block, blocks), draft
    )
    return jnp.where(wanted == iota((rows, rows), 1), 1.0, 0.0).astype(jnp.bfloat16)


def group_of():
    return lax.axis_index("dp") * lax.axis_size("pipe") + lax.axis_index("pipe")


def rank_kernel(sizes, owned, *refs):
    groups, blocks, drafts = sizes
    pieces = refs[:blocks]
    shrink_ref, slots_ref, rows_ref, rank_ref, wide = refs[blocks:]
    for block in range(blocks):
        for draft in range(drafts):
            start = (block * drafts + draft) * groups
            wide[start : start + groups, :] = pieces[block][draft].astype(jnp.float32)
    rows = wide[...].astype(jnp.bfloat16)
    rows_ref[...] = rows
    place = slots_ref[:, 0:1] - lax.axis_index("tensor") * owned
    ranks = owned_ranks(
        rows, shrink_ref[...], place, shrink_ref.shape[0] // owned, rank_ref.shape[2]
    )
    for target in range(rank_ref.shape[0]):
        rank_ref[target] = ranks


def owned_ranks(rows, shrink, place, width, lanes):
    ranks = dot_nt(rows, shrink)
    kept = jnp.where(over(iota(ranks.shape, 1), width) == place, ranks, 0.0).astype(jnp.bfloat16)
    fold = (ranks.shape[1], lanes)
    fold = rest_of(iota(fold, 0), width) == iota(fold, 1)
    return dot(kept, jnp.where(fold, 1.0, 0.0).astype(jnp.bfloat16)).astype(jnp.bfloat16)


def spread_ranks(ranks, place, width, owned, parts):
    span = owned * width
    row = iota((ranks.shape[1], parts * span), 0)
    column = iota((ranks.shape[1], parts * span), 1)
    tile = (over(row, width) == over(column, span)) & (
        rest_of(row, width) == rest_of(column, width)
    )
    wide = dot(ranks, jnp.where(tile, 1.0, 0.0).astype(jnp.bfloat16))
    slot = over(rest_of(iota(wide.shape, 1), span), width)
    return jnp.where(slot == place, wide, 0.0).astype(jnp.bfloat16)


def product_kernel(first, depth, added, rows_ref, weight_ref, *refs):
    sums, total_ref = refs[:added], refs[-1]
    width = total_ref.shape[1]
    step = width if width % 1024 else 1024
    for start in range(0, width, step):
        part = dot(
            rows_ref[:, first : first + depth],
            weight_ref[first : first + depth, start : start + step],
        )
        if sums:
            part = sums[0][:, start : start + step] + part
        total_ref[:, start : start + step] = part


def product(rows, weight, first, depth, sums=(), after=()):
    width = weight.shape[1]
    return call(
        functools.partial(product_kernel, first, depth, len(sums)),
        shape((rows.shape[0], width), jnp.float32),
        [VMEM] * (2 + len(sums)) + [HBM] * len(after),
    )(rows, weight, *sums, *after)


def pack_kernel(sizes, ids_ref, pool_ref, length_ref, keys_ref, values_ref, *refs):
    refs = refs[6:]
    groups, blocks, drafts = sizes
    outs = refs[:blocks]
    slots_ref, extra_f32, extra_ref, sems = refs[blocks:]
    size, head_size = keys_ref.shape[2:]
    me = lax.axis_index("tensor")
    length = length_ref[0]
    positions = (iota((drafts, head_size), 0) + length).astype(jnp.float32)
    lane = iota((drafts, head_size), 1)
    half = (lane & (head_size // 2 - 1)).astype(jnp.float32)
    angles = positions * jnp.exp(half * (-2.0 * math.log(rope_base) / head_size))
    signs = jnp.where(lane < head_size // 2, -1.0, 1.0)
    extra_f32[...] = jnp.zeros(extra_f32.shape, jnp.float32)
    for index, value in enumerate((jnp.cos(angles), jnp.sin(angles) * signs)):
        high = value.astype(jnp.bfloat16).astype(jnp.float32)
        start = 2 * index * drafts
        extra_f32[start : start + drafts, :] = high
        extra_f32[start + drafts : start + 2 * drafts, :] = value - high
    ones = jnp.ones((1, head_size), jnp.float32)
    extra_f32[4 * drafts : 4 * drafts + 1, :] = ones * (length >> 4).astype(jnp.float32)
    extra_f32[4 * drafts + 1 : 4 * drafts + 2, :] = ones * (length & 15).astype(jnp.float32)
    extra_ref[...] = extra_f32[...].astype(jnp.bfloat16)
    copies = []
    for shift in range(blocks):
        head = lax.rem(me + shift, blocks)
        copies += [
            pltpu.make_async_copy(
                keys_ref.at[0, head], outs[shift].at[pl.ds(0, size)], sems.at[shift, 0]
            ),
            pltpu.make_async_copy(
                values_ref.at[0, head], outs[shift].at[pl.ds(size, size)], sems.at[shift, 1]
            ),
            pltpu.make_async_copy(
                extra_ref,
                outs[shift].at[pl.ds(2 * size, extra_ref.shape[0])],
                sems.at[shift, 2],
            ),
        ]
    for copy in copies:
        copy.start()
    index = iota(slots_ref.shape, 0)
    column = iota(slots_ref.shape, 1)
    near = parts_of(block_first, sizes, index)
    far = parts_of(group_first, sizes, index)
    row_group = jnp.where(column == 0, near[0], far[0])
    row_block = jnp.where(column == 0, near[1], far[1])
    place = row_block * groups + row_group
    slots = jnp.zeros(slots_ref.shape, jnp.int32)
    for block in range(blocks):
        for group in range(groups):
            row = lax.rem(me - block + blocks, blocks) * groups + group
            slots = jnp.where(place == block * groups + group, pool_ref[ids_ref[row]], slots)
    slots_ref[...] = slots
    for copy in copies:
        copy.wait()


def pack(sizes, ids, pool, lengths, keys, values, later):
    groups, blocks, drafts = sizes
    head_size = keys.shape[3]
    used = -(-(4 * drafts + 2) // 16) * 16
    outs = [shape((2 * keys.shape[2] + used, head_size))] * blocks
    smem = pl.BlockSpec(memory_space=pltpu.SMEM)
    return pl.pallas_call(
        functools.partial(pack_kernel, sizes),
        out_shape=outs + [shape((groups * blocks * drafts, 128), jnp.int32)],
        in_specs=[smem, smem, smem, VMEM, VMEM] + [HBM] * 6,
        out_specs=[HBM] * blocks + [VMEM],
        scratch_shapes=[
            pltpu.VMEM((used, head_size), jnp.float32),
            pltpu.VMEM((used, head_size), jnp.bfloat16),
            pltpu.SemaphoreType.DMA((blocks, 3)),
        ],
        cost_estimate=pl.CostEstimate(flops=0, bytes_accessed=320 * keys.size, transcendentals=0),
        compiler_params=pltpu.CompilerParams(vmem_limit_bytes=40 * MIB),
    )(ids, pool, lengths, keys, values, *[later] * 6)


def grow_kernel(sizes, width, total_ref, rows_ref, key_ref, value_ref, slots_ref, ranks_ref, *rest):
    groups, blocks, drafts = sizes
    grows = rest[:3]
    outs = rest[3:]
    group = group_of()
    owned = grows[0].shape[0] // width
    ranks = ranks_ref[group * groups].astype(jnp.float32)
    for other in range(1, groups):
        ranks = ranks + ranks_ref[group * groups + other].astype(jnp.float32)
    turn = rest_of(group - lax.axis_index("tensor") + blocks, blocks)
    ranks = dot(reorder(sizes, block_first, block_first, turn), ranks.astype(jnp.bfloat16))
    place = slots_ref[:, 0:1] - group * owned
    wide = spread_ranks(ranks.astype(jnp.bfloat16), place, width, owned, len(grows))
    by_group = reorder(sizes, group_first, block_first, 0, group)
    start = 0
    for index, grow in enumerate(grows):
        deep, cols = grow.shape
        base = total_ref[...] if index == 0 else dot(rows_ref[...], (key_ref, value_ref)[index - 1][...])
        full = base + dot(wide[:, index * deep : (index + 1) * deep], grow[...])
        full = dot(by_group, full.astype(jnp.bfloat16)).astype(jnp.bfloat16)
        for step in range(groups):
            for block in range(blocks):
                row = (step * blocks + block) * drafts
                outs[step][block, :, start : start + cols] = full[row : row + drafts]
        start += cols


def attend_kernel(blocks, drafts, groups, cache_size, *refs):
    parts = refs[:groups]
    caches = refs[groups : groups + blocks]
    mixed_ref, query_s, fresh_s, out_s = refs[-4:]
    head_size = caches[0].shape[1]
    cols = parts[0].shape[2]
    heads = cols // head_size - 2
    count = heads * drafts
    scale = 1.0 / math.sqrt(head_size)
    fresh_s[...] = jnp.zeros(fresh_s.shape, jnp.float32)
    pad = fresh_s.shape[1]
    for block in range(blocks):
        joined = parts[0][block].astype(jnp.float32)
        for other in parts[1:]:
            joined = joined + other[block].astype(jnp.float32)
        joined = joined.astype(jnp.bfloat16).astype(jnp.float32)
        extra = caches[block][2 * cache_size :, :].astype(jnp.float32)
        cosine = extra[0:drafts] + extra[drafts : 2 * drafts]
        sine = extra[2 * drafts : 3 * drafts] + extra[3 * drafts : 4 * drafts]
        length = extra[4 * drafts : 4 * drafts + 1, 0:1] * 16.0 + extra[
            4 * drafts + 1 : 4 * drafts + 2, 0:1
        ]

        def rotated(head):
            value = joined[:, head * head_size : (head + 1) * head_size]
            return value * cosine + pltpu.roll(value, head_size // 2, 1) * sine

        for head in range(heads):
            query_s[block, head * drafts : (head + 1) * drafts, :] = rotated(head)
        fresh_s[2 * block, 0:drafts, :] = rotated(heads)
        fresh_s[2 * block + 1, 0:drafts, :] = joined[:, (heads + 1) * head_size :]
        query = query_s[block].astype(jnp.bfloat16)
        old = dot_nt(query, caches[block][0:cache_size, :]) * scale
        new = dot_nt(query, fresh_s[2 * block].astype(jnp.bfloat16)) * scale
        old_seen = iota(old.shape, 1).astype(jnp.float32) < length
        new_seen = iota(new.shape, 1) <= lax.rem(iota(new.shape, 0), drafts)
        old = jnp.where(old_seen, old, -jnp.inf)
        new = jnp.where(new_seen, new, -jnp.inf)
        peak = jnp.maximum(
            jnp.max(old, 1, keepdims=True), jnp.max(new, 1, keepdims=True)
        )
        old = jnp.exp(old - peak)
        new = jnp.exp(new - peak)
        below = jnp.sum(old, 1, keepdims=True) + jnp.sum(new, 1, keepdims=True)
        mixed = dot(
            (old / below).astype(jnp.bfloat16), caches[block][cache_size : 2 * cache_size, :]
        ) + dot((new / below).astype(jnp.bfloat16), fresh_s[2 * block + 1].astype(jnp.bfloat16))
        for head in range(heads):
            out_s[
                block * drafts : (block + 1) * drafts, head * head_size : (head + 1) * head_size
            ] = mixed[head * drafts : (head + 1) * drafts]
    mixed_ref[...] = out_s[...].astype(jnp.bfloat16)


def out_rank_kernel(owned, got_ref, shrink_ref, slots_ref, rows_ref, rank_ref, wide):
    span = got_ref.shape[1]
    for group in range(got_ref.shape[0]):
        wide[group * span : (group + 1) * span, :] = got_ref[group].astype(jnp.float32)
    rows = wide[...].astype(jnp.bfloat16)
    rows_ref[...] = rows
    place = slots_ref[:, 1:2] - group_of() * owned
    ranks = owned_ranks(
        rows, shrink_ref[...], place, shrink_ref.shape[0] // owned, rank_ref.shape[2]
    )
    for target in range(rank_ref.shape[0]):
        rank_ref[target] = ranks


def out_grow_kernel(sizes, width, total_ref, slots_ref, ranks_ref, grow_ref, *outs):
    groups, blocks, drafts = sizes
    owned = grow_ref.shape[0] // width
    me = lax.axis_index("tensor")
    ranks = None
    for source in range(blocks):
        turn = rest_of(source - me + blocks, blocks)
        moved = dot(
            reorder(sizes, group_first, group_first, turn), ranks_ref[source * groups + me]
        )
        ranks = moved if ranks is None else ranks + moved
    place = slots_ref[:, 1:2] - me * owned
    wide = spread_ranks(ranks.astype(jnp.bfloat16), place, width, owned, 1)
    full = (total_ref[...] + dot(wide, grow_ref[...])).astype(jnp.bfloat16)
    full = dot(reorder(sizes, block_first, group_first, 0), full).astype(jnp.bfloat16)
    for block in range(blocks):
        for draft in range(drafts):
            start = (block * drafts + draft) * groups
            outs[block][draft] = full[start : start + groups]


def by_head(
    tokens,
    w_query,
    w_key,
    w_value,
    w_out,
    shrink_qkv,
    grow_query,
    grow_key,
    grow_value,
    shrink_out,
    grow_out,
    cache_keys,
    cache_values,
    cache_lengths,
    adapter_ids,
    adapter_slots,
):
    blocks = lax.axis_size("tensor")
    groups = lax.axis_size(GROUP)
    _, drafts, features = tokens.shape
    sizes = (groups, blocks, drafts)
    owned = shrink_qkv.shape[0]
    width = grow_out.shape[1]
    cache_size, head_size = cache_keys.shape[2:]
    span = blocks * drafts
    count = groups * span
    lanes = -(-shrink_qkv.shape[2] // 128) * 128

    def over_tensor(value, shift):
        route = [(t, (t + shift) % blocks) for t in range(blocks)]
        return lax.ppermute(value, "tensor", route)

    def over_group(value, shift):
        route = [(g, (g + shift) % groups) for g in range(groups)]
        return lax.ppermute(value, GROUP, route)

    def exchange(value):
        return lax.all_to_all(value, EVERY, split_axis=0, concat_axis=0, tiled=True)

    mine = jnp.transpose(tokens, (1, 0, 2))
    pieces = [mine] + [over_tensor(mine, shift) for shift in range(1, blocks)]

    *messages, slots = pack(
        sizes, adapter_ids, adapter_slots, cache_lengths, cache_keys, cache_values, w_out
    )
    caches = {shift: over_tensor(messages[shift], shift) for shift in range(1, blocks) if shift != 2}

    shrink_in = jnp.transpose(shrink_qkv, (0, 2, 1)).reshape(-1, features)
    rows, rank_part = call(
        functools.partial(rank_kernel, sizes, owned),
        [shape((count, features)), shape((blocks * groups, count, lanes))],
        [VMEM] * (blocks + 2),
        [pltpu.VMEM((count, features), jnp.float32)],
    )(*pieces, shrink_in, slots)
    ranks = exchange(rank_part)
    half = features // 2
    early = [caches[shift] for shift in sorted(caches)]
    total = product(rows, w_query, 0, half)
    total, *late = lax.optimization_barrier((total, *messages[2:3]))
    for message in late:
        caches[2] = over_tensor(message, 2)
    total = product(rows, w_query, half, features - half, [total], early)
    caches = [messages[0]] + [caches[shift] for shift in range(1, blocks)]
    cols = total.shape[1] + w_key.shape[1] + w_value.shape[1]
    sent = call(
        functools.partial(grow_kernel, sizes, width),
        [shape((blocks, drafts, cols))] * groups,
        [VMEM] * 9,
        [],
    )(
        total,
        rows,
        w_key,
        w_value,
        slots,
        ranks,
        *[grow.reshape(owned * width, -1) for grow in (grow_query, grow_key, grow_value)],
    )
    parts = [sent[0]] + [over_group(sent[shift], shift) for shift in range(1, groups)]
    head_cols = cols - 2 * head_size
    mixed = call(
        functools.partial(attend_kernel, blocks, drafts, groups, cache_size),
        shape((span, head_cols)),
        [VMEM] * (groups + blocks) + [HBM] * 5,
        [
            pltpu.VMEM((blocks, head_cols // head_size * drafts, head_size), jnp.float32),
            pltpu.VMEM((2 * blocks, 128, head_size), jnp.float32),
            pltpu.VMEM((span, head_cols), jnp.float32),
        ],
        4 * span * head_cols * cache_size,
        320 * blocks * cache_size * head_size,
        40 * MIB,
    )(*parts, *caches, *[w_query] * 5)
    gathered = lax.all_gather(mixed, GROUP, axis=0, tiled=False)
    out_rows, out_part = call(
        functools.partial(out_rank_kernel, owned),
        [shape((count, head_cols)), shape((blocks * groups, count, lanes))],
        [VMEM] * 3,
        [pltpu.VMEM((count, head_cols), jnp.float32)],
        2 * count * shrink_out.size,
        2 * shrink_out.size + 4 * count * head_cols,
    )(gathered, jnp.transpose(shrink_out, (0, 2, 1)).reshape(-1, head_cols), slots)
    out_ranks = exchange(out_part)
    out_cols = w_out.shape[1]
    out_total = product(out_rows, w_out, 0, head_cols)
    leaving = call(
        functools.partial(out_grow_kernel, sizes, width),
        [shape((drafts, groups, out_cols))] * blocks,
        [VMEM] * 4,
        [],
        2 * count * owned * width * out_cols,
        8 * count * out_cols + 2 * owned * width * out_cols,
    )(out_total, slots, out_ranks, grow_out.reshape(owned * width, -1))
    result = leaving[0].astype(jnp.float32)
    for shift in range(1, blocks):
        result = result + over_tensor(leaving[shift], -shift).astype(jnp.float32)
    return jnp.transpose(result.astype(jnp.bfloat16), (1, 0, 2))


def rotate(vectors, positions):
    half_size = vectors.shape[-1] // 2
    frequency = rope_base ** (-2.0 * jnp.arange(half_size, dtype=jnp.float32) / vectors.shape[-1])
    angles = positions[:, None, None] * frequency
    cosine = jnp.cos(angles)
    sine_value = jnp.sin(angles)
    first_half = vectors[..., :half_size]
    second = vectors[..., half_size:]
    return jnp.concatenate(
        [first_half * cosine - second * sine_value, second * cosine + first_half * sine_value], -1
    )


def to_growers(partial, splits):
    total = None
    for shift in range(splits):
        route = [
            (t * splits + g, ((g + shift) % splits) * splits + t)
            for t in range(splits)
            for g in range(splits)
        ]
        got = lax.ppermute(partial, EVERY, route).astype(jnp.float32)
        total = got if total is None else total + got
    return total


def to_out_growers(partial, splits):
    total = None
    for shift in range(splits):
        route = [
            (t * splits + g, g * splits + (t + shift) % splits)
            for t in range(splits)
            for g in range(splits)
        ]
        got = lax.ppermute(partial, EVERY, route).astype(jnp.float32)
        total = got if total is None else total + got
    return total


def slot_table(adapter_ids, adapter_slots):
    matches = adapter_ids[:, None] == jnp.arange(adapter_slots.shape[0], dtype=jnp.int32)[None, :]
    return jnp.sum(jnp.where(matches, adapter_slots[None, :], 0), axis=1)


def attend(query_heads, key_new, value_new, cache_keys, cache_values, length):
    drafts, head_count, head_size = query_heads.shape
    kv_heads, cache_size, _ = cache_keys.shape
    positions = (length + jnp.arange(drafts, dtype=jnp.int32)).astype(jnp.float32)
    query_rot = rotate(query_heads.astype(jnp.float32), positions).astype(jnp.bfloat16)
    key_rot = rotate(key_new.astype(jnp.float32), positions).astype(jnp.bfloat16)
    grouped = query_rot.reshape(drafts, kv_heads, head_count // kv_heads, head_size)
    score_scale = 1.0 / math.sqrt(head_size)
    cached = (
        jnp.einsum("skgd,kld->skgl", grouped, cache_keys, preferred_element_type=jnp.float32)
        * score_scale
    )
    fresh_scores = (
        jnp.einsum("skgd,tkd->skgt", grouped, key_rot, preferred_element_type=jnp.float32)
        * score_scale
    )
    cache_mask = jnp.arange(cache_size, dtype=jnp.int32) < length
    draft_mask = jnp.arange(drafts)[None, :] <= jnp.arange(drafts)[:, None]
    cached = jnp.where(cache_mask[None, None, None, :], cached, -jnp.inf)
    fresh_scores = jnp.where(draft_mask[:, None, None, :], fresh_scores, -jnp.inf)
    row_peak = jnp.maximum(jnp.max(cached, -1), jnp.max(fresh_scores, -1))
    cached_exp = jnp.exp(cached - row_peak[..., None])
    fresh_exp = jnp.exp(fresh_scores - row_peak[..., None])
    denominator = jnp.sum(cached_exp, -1) + jnp.sum(fresh_exp, -1)
    cached_prob = (cached_exp / denominator[..., None]).astype(jnp.bfloat16)
    fresh_prob = (fresh_exp / denominator[..., None]).astype(jnp.bfloat16)
    mixed = jnp.einsum(
        "skgl,kld->skgd", cached_prob, cache_values, preferred_element_type=jnp.float32
    )
    mixed = mixed + jnp.einsum(
        "skgt,tkd->skgd", fresh_prob, value_new, preferred_element_type=jnp.float32
    )
    return mixed.astype(jnp.bfloat16)


def by_row(
    tokens,
    w_query,
    w_key,
    w_value,
    w_out,
    shrink_qkv,
    grow_query,
    grow_key,
    grow_value,
    shrink_out,
    grow_out,
    cache_keys,
    cache_values,
    cache_lengths,
    adapter_ids,
    adapter_slots,
):
    splits = lax.axis_size("tensor")
    groups = lax.axis_size(("dp", "pipe"))
    tensor_index = lax.axis_index("tensor")
    group_index = lax.axis_index(("dp", "pipe"))
    local_rows, drafts, feature_width = tokens.shape
    per_owner = shrink_qkv.shape[0]
    rank_size = grow_out.shape[1]
    query_cols = w_query.shape[1]
    key_cols = w_key.shape[1]
    kv_heads = cache_keys.shape[1]
    head_size = cache_keys.shape[3]
    rows = splits * groups
    row_slots = jnp.repeat(slot_table(adapter_ids, adapter_slots), drafts)
    within = jnp.arange(per_owner, dtype=jnp.int32)[None, :]
    width_hot = (row_slots[:, None] == within + tensor_index * per_owner)[:, :, None]
    column_hot = (row_slots[:, None] == within + group_index * per_owner)[:, :, None]

    def spread_ranks(ranks, hot):
        return jnp.where(hot, ranks[:, None, :], 0.0).reshape(rows * drafts, -1).astype(jnp.bfloat16)

    flat_tokens = lax.all_gather(tokens, "tensor", axis=0, tiled=True).reshape(
        rows * drafts, feature_width
    )
    rank_part = jnp.einsum(
        "nd,adr->nar", flat_tokens, shrink_qkv, preferred_element_type=jnp.float32
    )
    rank_part = jnp.sum(jnp.where(width_hot, rank_part, 0.0), 1)
    rank_all = to_growers(rank_part.astype(jnp.bfloat16), splits)

    def grown(index, grow):
        ranks = spread_ranks(rank_all[:, index * rank_size : (index + 1) * rank_size], column_hot)
        return jnp.dot(
            ranks, grow.reshape(per_owner * rank_size, -1), preferred_element_type=jnp.float32
        )

    bases = [
        jnp.dot(flat_tokens, weight, preferred_element_type=jnp.float32)
        for weight in (w_query, w_key, w_value)
    ]

    def product(index, grow):
        return (bases[index] + grown(index, grow)).astype(jnp.bfloat16).reshape(rows, drafts, -1)

    partial = jnp.concatenate(
        [
            product(0, grow_query),
            product(1, grow_key),
            product(2, grow_value),
        ],
        2,
    )
    arrived = lax.all_to_all(partial, EVERY, split_axis=0, concat_axis=0, tiled=True)
    joined = jnp.sum(
        arrived.reshape(splits, groups, drafts, -1).astype(jnp.float32), 1
    ).astype(jnp.bfloat16)
    joined = jnp.transpose(joined, (1, 0, 2))
    query_heads = joined[:, :, :query_cols].reshape(drafts, -1, head_size)
    key_new = joined[:, :, query_cols : query_cols + key_cols].reshape(drafts, kv_heads, head_size)
    value_new = joined[:, :, query_cols + key_cols :].reshape(drafts, kv_heads, head_size)
    mixed = attend(
        query_heads, key_new, value_new, cache_keys[0], cache_values[0], cache_lengths[0]
    )
    mixed = jnp.transpose(mixed.reshape(drafts, splits, -1), (1, 0, 2))
    outgoing = jnp.repeat(mixed, groups, axis=0)
    flat_heads = lax.all_to_all(
        outgoing, EVERY, split_axis=0, concat_axis=0, tiled=True
    ).reshape(rows * drafts, -1)
    out_part = jnp.einsum(
        "nw,awr->nar", flat_heads, shrink_out, preferred_element_type=jnp.float32
    )
    out_part = jnp.sum(jnp.where(column_hot, out_part, 0.0), 1)
    out_rank = to_out_growers(out_part.astype(jnp.bfloat16), splits)
    out = jnp.dot(flat_heads, w_out, preferred_element_type=jnp.float32)
    out = out + jnp.dot(
        spread_ranks(out_rank, width_hot),
        grow_out.reshape(per_owner * rank_size, -1),
        preferred_element_type=jnp.float32,
    )
    blocks = lax.all_to_all(
        out.astype(jnp.bfloat16).reshape(splits, local_rows, drafts, feature_width),
        "tensor",
        split_axis=0,
        concat_axis=0,
        tiled=True,
    )
    return jnp.sum(blocks.astype(jnp.float32), 0).astype(jnp.bfloat16)


def local(*arrays):
    heads = arrays[11].shape[1]
    if heads == lax.axis_size("tensor") == lax.axis_size(GROUP):
        return by_head(*arrays)
    return by_row(*arrays)


def solution(mesh):
    placed = (
        P(("parts", "tensor"), None, ("dp", "pipe")),
        P(("dp", "pipe"), "tensor"),
        P(("dp", "pipe"), "tensor"),
        P(("dp", "pipe"), "tensor"),
        P("tensor", ("dp", "pipe")),
        P("tensor", ("dp", "pipe"), None),
        P(("dp", "pipe"), None, "tensor"),
        P(("dp", "pipe"), None, "tensor"),
        P(("dp", "pipe"), None, "tensor"),
        P(("dp", "pipe"), "tensor", None),
        P("tensor", None, ("dp", "pipe")),
        P(("parts", "tensor", "dp", "pipe"), None, None, None),
        P(("parts", "tensor", "dp", "pipe"), None, None, None),
        P(("parts", "tensor", "dp", "pipe")),
        P(),
        P(),
    )
    return jax.shard_map(
        local,
        mesh=mesh,
        in_specs=placed,
        out_specs=P(("parts", "tensor"), None, ("dp", "pipe")),
        check_vma=False,
    )
```

```python
import functools
import math

import jax
import jax.numpy as jnp
import numpy as np
from jax import lax
from jax.experimental import pallas as pl
from jax.experimental.pallas import tpu as pltpu
from jax.sharding import PartitionSpec as P

rope_base = 500000.0
EVERY = ("tensor", "dp", "pipe")
GROUP = ("dp", "pipe")
VMEM = pl.BlockSpec(memory_space=pltpu.VMEM)
HBM = pl.BlockSpec(memory_space=pltpu.HBM)
MIB = 1 << 20


def dot(left, right):
    return jnp.dot(left, right, preferred_element_type=jnp.float32)


def dot_nt(left, right):
    return lax.dot_general(
        left, right, (((1,), (1,)), ((), ())), preferred_element_type=jnp.float32
    )


def iota(shape, axis):
    return lax.broadcasted_iota(jnp.int32, shape, axis)


def call(kernel, outs, ins, scratch=(), flops=0, moved=0, limit=24 * MIB):
    return pl.pallas_call(
        kernel,
        out_shape=outs,
        in_specs=ins,
        out_specs=jax.tree.map(lambda _: VMEM, outs),
        scratch_shapes=list(scratch),
        cost_estimate=pl.CostEstimate(flops=flops, bytes_accessed=moved, transcendentals=0),
        compiler_params=pltpu.CompilerParams(vmem_limit_bytes=limit),
    )


def shape(dims, kind=jnp.bfloat16):
    return jax.ShapeDtypeStruct(tuple(dims), kind)


def over(value, size):
    return value >> (size.bit_length() - 1) if size & (size - 1) == 0 else lax.div(value, size)


def rest_of(value, size):
    return value & (size - 1) if size & (size - 1) == 0 else lax.rem(value, size)


def as_gathered(sizes, group, block, draft):
    groups, blocks, drafts = sizes
    return (block * drafts + draft) * groups + group


def by_request(sizes, group, block, draft):
    groups, blocks, drafts = sizes
    return (block * groups + group) * drafts + draft


def parts_of(order, sizes, index):
    groups, blocks, drafts = sizes
    block = over(index, groups * drafts)
    if order is as_gathered:
        return rest_of(index, groups), block, rest_of(over(index, groups), drafts)
    return rest_of(over(index, drafts), groups), block, rest_of(index, drafts)


def turned(block, blocks):
    return rest_of(lax.axis_index("tensor") - block + blocks, blocks)


def reorder(sizes, after, before):
    groups, blocks, drafts = sizes
    rows = groups * blocks * drafts
    group, block, draft = parts_of(after, sizes, iota((rows, rows), 0))
    wanted = before(sizes, group, turned(block, blocks), draft)
    return jnp.where(wanted == iota((rows, rows), 1), 1.0, 0.0).astype(jnp.bfloat16)


def group_of():
    return lax.axis_index("dp") * lax.axis_size("pipe") + lax.axis_index("pipe")


def rank_kernel(sizes, owned, *refs):
    groups, blocks, drafts = sizes
    pieces = refs[:blocks]
    shrink_ref, slots_ref, rows_ref, rank_ref, wide = refs[blocks:]
    for block in range(blocks):
        for draft in range(drafts):
            start = (block * drafts + draft) * groups
            wide[start : start + groups, :] = pieces[block][draft].astype(jnp.float32)
    rows = wide[...].astype(jnp.bfloat16)
    rows_ref[...] = rows
    place = slots_ref[:, 0:1] - lax.axis_index("tensor") * owned
    ranks = owned_ranks(
        rows, shrink_ref[...], place, shrink_ref.shape[0] // owned, rank_ref.shape[2]
    )
    ranks = dot(reorder(sizes, by_request, as_gathered), ranks).astype(jnp.bfloat16)
    for target in range(rank_ref.shape[0]):
        rank_ref[target] = ranks


def owned_ranks(rows, shrink, place, width, lanes):
    ranks = dot_nt(rows, shrink)
    kept = jnp.where(over(iota(ranks.shape, 1), width) == place, ranks, 0.0).astype(jnp.bfloat16)
    fold = (ranks.shape[1], lanes)
    fold = rest_of(iota(fold, 0), width) == iota(fold, 1)
    return dot(kept, jnp.where(fold, 1.0, 0.0).astype(jnp.bfloat16)).astype(jnp.bfloat16)


def spread_ranks(ranks, place, width, owned, parts):
    span = owned * width
    row = iota((ranks.shape[1], parts * span), 0)
    column = iota((ranks.shape[1], parts * span), 1)
    tile = (over(row, width) == over(column, span)) & (
        rest_of(row, width) == rest_of(column, width)
    )
    wide = dot(ranks, jnp.where(tile, 1.0, 0.0).astype(jnp.bfloat16))
    slot = over(rest_of(iota(wide.shape, 1), span), width)
    return jnp.where(slot == place, wide, 0.0).astype(jnp.bfloat16)


def stream_kernel(chunks, rows_ref, weight_ref, total_ref, buffer, sems):
    depth = rows_ref.shape[1] // chunks

    def copy(chunk):
        part = pl.ds(chunk * depth, depth)
        return pltpu.make_async_copy(weight_ref.at[part], buffer.at[part], sems.at[chunk])

    for chunk in range(chunks):
        copy(chunk).start()
    for chunk in range(chunks):
        copy(chunk).wait()
        product = dot(
            rows_ref[:, chunk * depth : (chunk + 1) * depth],
            buffer[chunk * depth : (chunk + 1) * depth, :],
        )
        if chunk:
            total_ref[...] += product
        else:
            total_ref[...] = product


def stream(rows, weight, chunks):
    return call(
        functools.partial(stream_kernel, chunks),
        shape((rows.shape[0], weight.shape[1]), jnp.float32),
        [VMEM, HBM],
        [pltpu.VMEM(weight.shape, weight.dtype), pltpu.SemaphoreType.DMA((chunks,))],
        2 * rows.shape[0] * weight.size,
        2 * weight.size,
        40 * MIB,
    )(rows, weight)


def prepare_kernel(sizes, ids_ref, pool_ref, length_ref, _, slots_ref, cosine_ref, sine_ref):
    groups, blocks, drafts = sizes
    width = cosine_ref.shape[1]
    lane = iota(cosine_ref.shape, 1)
    half = (lane & (width // 2 - 1)).astype(jnp.float32)
    positions = (iota(cosine_ref.shape, 0) + length_ref[0]).astype(jnp.float32)
    angles = positions * jnp.exp(half * (-2.0 * math.log(rope_base) / width))
    cosine_ref[...] = jnp.cos(angles)
    sine_ref[...] = jnp.sin(angles) * jnp.where(lane < width // 2, -1.0, 1.0)
    index = iota(slots_ref.shape, 0)
    column = iota(slots_ref.shape, 1)
    near = parts_of(as_gathered, sizes, index)
    far = parts_of(by_request, sizes, index)
    row_group = jnp.where(column == 0, near[0], far[0])
    row_block = jnp.where(column == 0, turned(near[1], blocks), far[1])
    place = row_block * groups + row_group
    slots = jnp.zeros(slots_ref.shape, jnp.int32)
    for row in range(blocks * groups):
        slots = jnp.where(place == row, pool_ref[ids_ref[row]], slots)
    slots_ref[...] = slots


def prepare(sizes, ids, pool, lengths, head_size, later):
    groups, blocks, drafts = sizes
    smem = pl.BlockSpec(memory_space=pltpu.SMEM)
    table = shape((8 * -(-drafts // 8), head_size), jnp.float32)
    return call(
        functools.partial(prepare_kernel, sizes),
        [shape((groups * blocks * drafts, 128), jnp.int32), table, table],
        [smem, smem, smem, HBM],
        limit=40 * MIB,
    )(ids, pool, lengths, later)


def grow_kernel(
    sizes, width, total_ref, rows_ref, key_ref, value_ref, slots_ref, ranks_ref, *refs
):
    groups, blocks, drafts = sizes
    *grows, out_ref = refs
    group = group_of()
    owned = grows[0].shape[0] // width
    ranks = ranks_ref[group * groups].astype(jnp.float32)
    for other in range(1, groups):
        ranks = ranks + ranks_ref[group * groups + other].astype(jnp.float32)
    ranks = dot(reorder(sizes, as_gathered, by_request), ranks.astype(jnp.bfloat16))
    place = slots_ref[:, 0:1] - group * owned
    wide = spread_ranks(ranks.astype(jnp.bfloat16), place, width, owned, len(grows))
    arranged = reorder(sizes, by_request, as_gathered)
    start = 0
    for index, grow in enumerate(grows):
        deep, cols = grow.shape
        if index == 0:
            full = total_ref[...]
        else:
            full = dot(rows_ref[...], (key_ref, value_ref)[index - 1][...])
        full = full + dot(wide[:, index * deep : (index + 1) * deep], grow[...])
        full = dot(arranged, full.astype(jnp.bfloat16)).astype(jnp.bfloat16)
        for row in range(groups * blocks):
            out_ref[row, :, start : start + cols] = full[row * drafts : (row + 1) * drafts]
        start += cols


def attend_kernel(
    sizes, arrived_ref, keys_ref, values_ref, length_ref, cosine_ref, sine_ref, out_ref, *scratch
):
    groups, blocks, drafts = sizes
    query_s, fresh_s, out_s = scratch
    cache_size, head_size = keys_ref.shape[2:]
    heads = arrived_ref.shape[2] // head_size - 2
    scale = 1.0 / math.sqrt(head_size)
    fresh_s[...] = jnp.zeros(fresh_s.shape, jnp.float32)
    cosine = cosine_ref[0:drafts, :]
    sine = sine_ref[0:drafts, :]
    for block in range(blocks):
        joined = arrived_ref[block * groups].astype(jnp.float32)
        for other in range(1, groups):
            joined = joined + arrived_ref[block * groups + other].astype(jnp.float32)
        joined = joined.astype(jnp.bfloat16).astype(jnp.float32)

        def rotated(head):
            value = joined[:, head * head_size : (head + 1) * head_size]
            return value * cosine + pltpu.roll(value, head_size // 2, 1) * sine

        for head in range(heads):
            query_s[block, head * drafts : (head + 1) * drafts, :] = rotated(head)
        fresh_s[2 * block, 0:drafts, :] = rotated(heads)
        fresh_s[2 * block + 1, 0:drafts, :] = joined[:, (heads + 1) * head_size :]
        query = query_s[block].astype(jnp.bfloat16)
        old = dot_nt(query, keys_ref[0, block]) * scale
        new = dot_nt(query, fresh_s[2 * block].astype(jnp.bfloat16)) * scale
        old = jnp.where(iota(old.shape, 1) < length_ref[0], old, -jnp.inf)
        seen = iota(new.shape, 1) <= lax.rem(iota(new.shape, 0), drafts)
        new = jnp.where(seen, new, -jnp.inf)
        peak = jnp.maximum(jnp.max(old, 1, keepdims=True), jnp.max(new, 1, keepdims=True))
        old = jnp.exp(old - peak)
        new = jnp.exp(new - peak)
        below = jnp.sum(old, 1, keepdims=True) + jnp.sum(new, 1, keepdims=True)
        mixed = dot((old / below).astype(jnp.bfloat16), values_ref[0, block]) + dot(
            (new / below).astype(jnp.bfloat16), fresh_s[2 * block + 1].astype(jnp.bfloat16)
        )
        for head in range(heads):
            out_s[block, 0:drafts, head * head_size : (head + 1) * head_size] = mixed[
                head * drafts : (head + 1) * drafts
            ]
        result = out_s[block, 0:drafts, :].astype(jnp.bfloat16)
        for target in range(groups):
            out_ref[block * groups + target] = result


def out_rank_kernel(owned, got_ref, shrink_ref, slots_ref, rows_ref, rank_ref, wide):
    drafts = got_ref.shape[1]
    for row in range(got_ref.shape[0]):
        wide[row * drafts : (row + 1) * drafts, :] = got_ref[row].astype(jnp.float32)
    rows = wide[...].astype(jnp.bfloat16)
    rows_ref[...] = rows
    place = slots_ref[:, 1:2] - group_of() * owned
    ranks = owned_ranks(
        rows, shrink_ref[...], place, shrink_ref.shape[0] // owned, rank_ref.shape[2]
    )
    for target in range(rank_ref.shape[0]):
        rank_ref[target] = ranks


def out_grow_kernel(sizes, width, total_ref, slots_ref, ranks_ref, grow_ref, *outs):
    groups, blocks, drafts = sizes
    owned = grow_ref.shape[0] // width
    me = lax.axis_index("tensor")
    ranks = ranks_ref[me].astype(jnp.float32)
    for source in range(1, blocks):
        ranks = ranks + ranks_ref[source * groups + me].astype(jnp.float32)
    place = slots_ref[:, 1:2] - me * owned
    wide = spread_ranks(ranks.astype(jnp.bfloat16), place, width, owned, 1)
    full = (total_ref[...] + dot(wide, grow_ref[...])).astype(jnp.bfloat16)
    full = dot(reorder(sizes, as_gathered, by_request), full).astype(jnp.bfloat16)
    for block in range(blocks):
        for draft in range(drafts):
            start = (block * drafts + draft) * groups
            outs[block][draft] = full[start : start + groups]


def by_kernels(
    tokens,
    w_query,
    w_key,
    w_value,
    w_out,
    shrink_qkv,
    grow_query,
    grow_key,
    grow_value,
    shrink_out,
    grow_out,
    cache_keys,
    cache_values,
    cache_lengths,
    adapter_ids,
    adapter_slots,
):
    blocks = lax.axis_size("tensor")
    groups = lax.axis_size(GROUP)
    _, drafts, features = tokens.shape
    sizes = (groups, blocks, drafts)
    owned = shrink_qkv.shape[0]
    width = grow_out.shape[1]
    head_size = cache_keys.shape[3]
    span = blocks * drafts
    count = groups * span
    lanes = -(-shrink_qkv.shape[2] // 128) * 128

    def over_tensor(value, shift):
        route = [(t, (t + shift) % blocks) for t in range(blocks)]
        return lax.ppermute(value, "tensor", route)

    def exchange(value):
        return lax.all_to_all(value, EVERY, split_axis=0, concat_axis=0, tiled=True)

    mine = jnp.transpose(tokens, (1, 0, 2))
    pieces = [mine] + [over_tensor(mine, shift) for shift in range(1, blocks)]

    slots, cosine, sine = prepare(
        sizes, adapter_ids, adapter_slots, cache_lengths, head_size, w_out
    )
    shrink_in = jnp.transpose(shrink_qkv, (0, 2, 1)).reshape(-1, features)
    rows, rank_part = call(
        functools.partial(rank_kernel, sizes, owned),
        [shape((count, features)), shape((blocks * groups, count, lanes))],
        [VMEM] * (blocks + 2),
        [pltpu.VMEM((count, features), jnp.float32)],
        2 * count * shrink_qkv.size,
        2 * shrink_qkv.size + 4 * count * features,
    )(*pieces, shrink_in, slots)
    ranks = exchange(rank_part)
    total = stream(rows, w_query, 8)
    cols = total.shape[1] + w_key.shape[1] + w_value.shape[1]
    sent = call(
        functools.partial(grow_kernel, sizes, width),
        shape((blocks * groups, drafts, cols)),
        [VMEM] * 9,
        [],
        2 * count * owned * width * cols,
        8 * count * cols + 2 * owned * width * cols,
    )(
        total,
        rows,
        w_key,
        w_value,
        slots,
        ranks,
        *[grow.reshape(owned * width, -1) for grow in (grow_query, grow_key, grow_value)],
    )
    head_cols = cols - 2 * head_size
    heads = head_cols // head_size
    mixed = call(
        functools.partial(attend_kernel, sizes),
        shape((blocks * groups, drafts, head_cols)),
        [VMEM] * 3 + [pl.BlockSpec(memory_space=pltpu.SMEM)] + [VMEM] * 2,
        [
            pltpu.VMEM((blocks, heads * drafts, head_size), jnp.float32),
            pltpu.VMEM((2 * blocks, 128, head_size), jnp.float32),
            pltpu.VMEM((blocks, drafts, head_cols), jnp.float32),
        ],
    )(exchange(sent), cache_keys, cache_values, cache_lengths, cosine, sine)
    gathered = exchange(mixed)
    out_rows, out_part = call(
        functools.partial(out_rank_kernel, owned),
        [shape((count, head_cols)), shape((blocks * groups, count, lanes))],
        [VMEM] * 3,
        [pltpu.VMEM((count, head_cols), jnp.float32)],
    )(gathered, jnp.transpose(shrink_out, (0, 2, 1)).reshape(-1, head_cols), slots)
    out_ranks = exchange(out_part)
    out_total = stream(out_rows, w_out, 8)
    out_cols = out_total.shape[1]
    leaving = call(
        functools.partial(out_grow_kernel, sizes, width),
        [shape((drafts, groups, out_cols))] * blocks,
        [VMEM] * 4,
        [],
        2 * count * owned * width * out_cols,
        8 * count * out_cols + 2 * owned * width * out_cols,
    )(out_total, slots, out_ranks, grow_out.reshape(owned * width, -1))
    result = leaving[0].astype(jnp.float32)
    for shift in range(1, blocks):
        result = result + over_tensor(leaving[shift], -shift).astype(jnp.float32)
    return jnp.transpose(result.astype(jnp.bfloat16), (1, 0, 2))


def rotate(vectors, positions):
    half_size = vectors.shape[-1] // 2
    frequency = rope_base ** (-2.0 * jnp.arange(half_size, dtype=jnp.float32) / vectors.shape[-1])
    angles = positions[:, None, None] * frequency
    cosine = jnp.cos(angles)
    sine_value = jnp.sin(angles)
    first_half = vectors[..., :half_size]
    second = vectors[..., half_size:]
    return jnp.concatenate(
        [first_half * cosine - second * sine_value, second * cosine + first_half * sine_value], -1
    )


def to_growers(partial, splits):
    total = None
    for shift in range(splits):
        route = [
            (t * splits + g, ((g + shift) % splits) * splits + t)
            for t in range(splits)
            for g in range(splits)
        ]
        got = lax.ppermute(partial, EVERY, route).astype(jnp.float32)
        total = got if total is None else total + got
    return total


def to_out_growers(partial, splits):
    total = None
    for shift in range(splits):
        route = [
            (t * splits + g, g * splits + (t + shift) % splits)
            for t in range(splits)
            for g in range(splits)
        ]
        got = lax.ppermute(partial, EVERY, route).astype(jnp.float32)
        total = got if total is None else total + got
    return total


def slot_table(adapter_ids, adapter_slots):
    matches = adapter_ids[:, None] == jnp.arange(adapter_slots.shape[0], dtype=jnp.int32)[None, :]
    return jnp.sum(jnp.where(matches, adapter_slots[None, :], 0), axis=1)


def attend(query_heads, key_new, value_new, cache_keys, cache_values, length):
    drafts, head_count, head_size = query_heads.shape
    kv_heads, cache_size, _ = cache_keys.shape
    positions = (length + jnp.arange(drafts, dtype=jnp.int32)).astype(jnp.float32)
    query_rot = rotate(query_heads.astype(jnp.float32), positions).astype(jnp.bfloat16)
    key_rot = rotate(key_new.astype(jnp.float32), positions).astype(jnp.bfloat16)
    grouped = query_rot.reshape(drafts, kv_heads, head_count // kv_heads, head_size)
    score_scale = 1.0 / math.sqrt(head_size)
    cached = (
        jnp.einsum("skgd,kld->skgl", grouped, cache_keys, preferred_element_type=jnp.float32)
        * score_scale
    )
    fresh_scores = (
        jnp.einsum("skgd,tkd->skgt", grouped, key_rot, preferred_element_type=jnp.float32)
        * score_scale
    )
    cache_mask = jnp.arange(cache_size, dtype=jnp.int32) < length
    draft_mask = jnp.arange(drafts)[None, :] <= jnp.arange(drafts)[:, None]
    cached = jnp.where(cache_mask[None, None, None, :], cached, -jnp.inf)
    fresh_scores = jnp.where(draft_mask[:, None, None, :], fresh_scores, -jnp.inf)
    row_peak = jnp.maximum(jnp.max(cached, -1), jnp.max(fresh_scores, -1))
    cached_exp = jnp.exp(cached - row_peak[..., None])
    fresh_exp = jnp.exp(fresh_scores - row_peak[..., None])
    denominator = jnp.sum(cached_exp, -1) + jnp.sum(fresh_exp, -1)
    cached_prob = (cached_exp / denominator[..., None]).astype(jnp.bfloat16)
    fresh_prob = (fresh_exp / denominator[..., None]).astype(jnp.bfloat16)
    mixed = jnp.einsum(
        "skgl,kld->skgd", cached_prob, cache_values, preferred_element_type=jnp.float32
    )
    mixed = mixed + jnp.einsum(
        "skgt,tkd->skgd", fresh_prob, value_new, preferred_element_type=jnp.float32
    )
    return mixed.astype(jnp.bfloat16)


def by_row(
    tokens,
    w_query,
    w_key,
    w_value,
    w_out,
    shrink_qkv,
    grow_query,
    grow_key,
    grow_value,
    shrink_out,
    grow_out,
    cache_keys,
    cache_values,
    cache_lengths,
    adapter_ids,
    adapter_slots,
):
    splits = lax.axis_size("tensor")
    groups = lax.axis_size(("dp", "pipe"))
    tensor_index = lax.axis_index("tensor")
    group_index = lax.axis_index(("dp", "pipe"))
    local_rows, drafts, feature_width = tokens.shape
    per_owner = shrink_qkv.shape[0]
    rank_size = grow_out.shape[1]
    query_cols = w_query.shape[1]
    key_cols = w_key.shape[1]
    kv_heads = cache_keys.shape[1]
    head_size = cache_keys.shape[3]
    rows = splits * groups
    row_slots = jnp.repeat(slot_table(adapter_ids, adapter_slots), drafts)
    within = jnp.arange(per_owner, dtype=jnp.int32)[None, :]
    width_hot = (row_slots[:, None] == within + tensor_index * per_owner)[:, :, None]
    column_hot = (row_slots[:, None] == within + group_index * per_owner)[:, :, None]

    def spread_ranks(ranks, hot):
        return jnp.where(hot, ranks[:, None, :], 0.0).reshape(rows * drafts, -1).astype(jnp.bfloat16)

    flat_tokens = lax.all_gather(tokens, "tensor", axis=0, tiled=True).reshape(
        rows * drafts, feature_width
    )
    rank_part = jnp.einsum(
        "nd,adr->nar", flat_tokens, shrink_qkv, preferred_element_type=jnp.float32
    )
    rank_part = jnp.sum(jnp.where(width_hot, rank_part, 0.0), 1)
    rank_all = to_growers(rank_part.astype(jnp.bfloat16), splits)

    def grown(index, grow):
        ranks = spread_ranks(rank_all[:, index * rank_size : (index + 1) * rank_size], column_hot)
        return jnp.dot(
            ranks, grow.reshape(per_owner * rank_size, -1), preferred_element_type=jnp.float32
        )

    bases = [
        jnp.dot(flat_tokens, weight, preferred_element_type=jnp.float32)
        for weight in (w_query, w_key, w_value)
    ]

    def product(index, grow):
        return (bases[index] + grown(index, grow)).astype(jnp.bfloat16).reshape(rows, drafts, -1)

    partial = jnp.concatenate(
        [
            product(0, grow_query),
            product(1, grow_key),
            product(2, grow_value),
        ],
        2,
    )
    arrived = lax.all_to_all(partial, EVERY, split_axis=0, concat_axis=0, tiled=True)
    joined = jnp.sum(
        arrived.reshape(splits, groups, drafts, -1).astype(jnp.float32), 1
    ).astype(jnp.bfloat16)
    joined = jnp.transpose(joined, (1, 0, 2))
    query_heads = joined[:, :, :query_cols].reshape(drafts, -1, head_size)
    key_new = joined[:, :, query_cols : query_cols + key_cols].reshape(drafts, kv_heads, head_size)
    value_new = joined[:, :, query_cols + key_cols :].reshape(drafts, kv_heads, head_size)
    mixed = attend(
        query_heads, key_new, value_new, cache_keys[0], cache_values[0], cache_lengths[0]
    )
    mixed = jnp.transpose(mixed.reshape(drafts, splits, -1), (1, 0, 2))
    outgoing = jnp.repeat(mixed, groups, axis=0)
    flat_heads = lax.all_to_all(
        outgoing, EVERY, split_axis=0, concat_axis=0, tiled=True
    ).reshape(rows * drafts, -1)
    out_part = jnp.einsum(
        "nw,awr->nar", flat_heads, shrink_out, preferred_element_type=jnp.float32
    )
    out_part = jnp.sum(jnp.where(column_hot, out_part, 0.0), 1)
    out_rank = to_out_growers(out_part.astype(jnp.bfloat16), splits)
    out = jnp.dot(flat_heads, w_out, preferred_element_type=jnp.float32)
    out = out + jnp.dot(
        spread_ranks(out_rank, width_hot),
        grow_out.reshape(per_owner * rank_size, -1),
        preferred_element_type=jnp.float32,
    )
    blocks = lax.all_to_all(
        out.astype(jnp.bfloat16).reshape(splits, local_rows, drafts, feature_width),
        "tensor",
        split_axis=0,
        concat_axis=0,
        tiled=True,
    )
    return jnp.sum(blocks.astype(jnp.float32), 0).astype(jnp.bfloat16)


def local(*arrays):
    heads = arrays[11].shape[1]
    if heads == lax.axis_size("tensor") == lax.axis_size(GROUP):
        return by_kernels(*arrays)
    return by_row(*arrays)


def solution(mesh):
    placed = (
        P(("parts", "tensor"), None, ("dp", "pipe")),
        P(("dp", "pipe"), "tensor"),
        P(("dp", "pipe"), "tensor"),
        P(("dp", "pipe"), "tensor"),
        P("tensor", ("dp", "pipe")),
        P("tensor", ("dp", "pipe"), None),
        P(("dp", "pipe"), None, "tensor"),
        P(("dp", "pipe"), None, "tensor"),
        P(("dp", "pipe"), None, "tensor"),
        P(("dp", "pipe"), "tensor", None),
        P("tensor", None, ("dp", "pipe")),
        P(("parts", "tensor", "dp", "pipe"), None, None, None),
        P(("parts", "tensor", "dp", "pipe"), None, None, None),
        P(("parts", "tensor", "dp", "pipe")),
        P(),
        P(),
    )
    return jax.shard_map(
        local,
        mesh=mesh,
        in_specs=placed,
        out_specs=P(("parts", "tensor"), None, ("dp", "pipe")),
        check_vma=False,
    )
```

```python
import functools
import math

import jax
import jax.numpy as jnp
import numpy as np
from jax import lax
from jax.experimental import pallas as pl
from jax.experimental.pallas import tpu as pltpu
from jax.sharding import PartitionSpec as P

rope_base = 500000.0
EVERY = ("tensor", "dp", "pipe")
GROUP = ("dp", "pipe")
VMEM = pl.BlockSpec(memory_space=pltpu.VMEM)
HBM = pl.BlockSpec(memory_space=pltpu.HBM)
MIB = 1 << 20


def dot(left, right):
    return jnp.dot(left, right, preferred_element_type=jnp.float32)


def dot_nt(left, right):
    return lax.dot_general(
        left, right, (((1,), (1,)), ((), ())), preferred_element_type=jnp.float32
    )


def iota(shape, axis):
    return lax.broadcasted_iota(jnp.int32, shape, axis)


def call(kernel, outs, ins, scratch=(), flops=0, moved=0, limit=24 * MIB):
    return pl.pallas_call(
        kernel,
        out_shape=outs,
        in_specs=ins,
        out_specs=jax.tree.map(lambda _: VMEM, outs),
        scratch_shapes=list(scratch),
        cost_estimate=pl.CostEstimate(flops=flops, bytes_accessed=moved, transcendentals=0),
        compiler_params=pltpu.CompilerParams(vmem_limit_bytes=limit),
    )


def shape(dims, kind=jnp.bfloat16):
    return jax.ShapeDtypeStruct(tuple(dims), kind)


def over(value, size):
    return value >> (size.bit_length() - 1) if size & (size - 1) == 0 else lax.div(value, size)


def rest_of(value, size):
    return value & (size - 1) if size & (size - 1) == 0 else lax.rem(value, size)


def as_gathered(sizes, group, block, draft):
    groups, blocks, drafts = sizes
    return (block * drafts + draft) * groups + group


def by_draft(sizes, group, block, draft):
    groups, blocks, drafts = sizes
    return (draft * blocks + block) * groups + group


def parts_of(order, sizes, index):
    groups, blocks, drafts = sizes
    group, left = rest_of(index, groups), over(index, groups)
    if order is as_gathered:
        return group, over(left, drafts), rest_of(left, drafts)
    return group, rest_of(left, blocks), over(left, blocks)


def turned(block, blocks):
    return rest_of(lax.axis_index("tensor") - block + blocks, blocks)


def reorder(sizes, after, before):
    groups, blocks, drafts = sizes
    rows = groups * blocks * drafts
    group, block, draft = parts_of(after, sizes, iota((rows, rows), 0))
    wanted = before(sizes, group, turned(block, blocks), draft)
    return jnp.where(wanted == iota((rows, rows), 1), 1.0, 0.0).astype(jnp.bfloat16)


def group_of():
    return lax.axis_index("dp") * lax.axis_size("pipe") + lax.axis_index("pipe")


def rank_kernel(sizes, owned, *refs):
    groups, blocks, drafts = sizes
    pieces = refs[:blocks]
    shrink_ref, slots_ref, rows_ref, rank_ref, wide = refs[blocks:]
    for block in range(blocks):
        for draft in range(drafts):
            start = (block * drafts + draft) * groups
            wide[start : start + groups, :] = pieces[block][draft].astype(jnp.float32)
    rows = wide[...].astype(jnp.bfloat16)
    rows_ref[...] = rows
    place = slots_ref[:, 0:1] - lax.axis_index("tensor") * owned
    ranks = owned_ranks(
        rows, shrink_ref[...], place, shrink_ref.shape[0] // owned, rank_ref.shape[2]
    )
    ranks = dot(reorder(sizes, by_draft, as_gathered), ranks).astype(jnp.bfloat16)
    for target in range(rank_ref.shape[0]):
        rank_ref[target] = ranks


def owned_ranks(rows, shrink, place, width, lanes):
    ranks = dot_nt(rows, shrink)
    kept = jnp.where(over(iota(ranks.shape, 1), width) == place, ranks, 0.0).astype(jnp.bfloat16)
    fold = (ranks.shape[1], lanes)
    fold = rest_of(iota(fold, 0), width) == iota(fold, 1)
    return dot(kept, jnp.where(fold, 1.0, 0.0).astype(jnp.bfloat16)).astype(jnp.bfloat16)


def spread_ranks(ranks, place, width, owned, parts):
    span = owned * width
    row = iota((ranks.shape[1], parts * span), 0)
    column = iota((ranks.shape[1], parts * span), 1)
    tile = (over(row, width) == over(column, span)) & (
        rest_of(row, width) == rest_of(column, width)
    )
    wide = dot(ranks, jnp.where(tile, 1.0, 0.0).astype(jnp.bfloat16))
    slot = over(rest_of(iota(wide.shape, 1), span), width)
    return jnp.where(slot == place, wide, 0.0).astype(jnp.bfloat16)


def stream_kernel(chunks, rows_ref, weight_ref, *refs):
    total_ref, buffer, sems = refs[-3:]
    depth = rows_ref.shape[1] // chunks

    def copy(chunk):
        part = pl.ds(chunk * depth, depth)
        return pltpu.make_async_copy(weight_ref.at[part], buffer.at[part], sems.at[chunk])

    for chunk in range(chunks):
        copy(chunk).start()
    for chunk in range(chunks):
        copy(chunk).wait()
        product = dot(
            rows_ref[:, chunk * depth : (chunk + 1) * depth],
            buffer[chunk * depth : (chunk + 1) * depth, :],
        )
        if chunk:
            total_ref[...] += product
        else:
            total_ref[...] = product


def stream(rows, weight, chunks, later=()):
    return call(
        functools.partial(stream_kernel, chunks),
        shape((rows.shape[0], weight.shape[1]), jnp.float32),
        [VMEM, HBM] + [HBM] * len(later),
        [pltpu.VMEM(weight.shape, weight.dtype), pltpu.SemaphoreType.DMA((chunks,))],
        2 * rows.shape[0] * weight.size,
        2 * weight.size,
        40 * MIB,
    )(rows, weight, *later)


def prepare_kernel(sizes, ids_ref, pool_ref, length_ref, _, slots_ref, cosine_ref, sine_ref):
    groups, blocks, drafts = sizes
    width = cosine_ref.shape[1]
    lane = iota(cosine_ref.shape, 1)
    half = (lane & (width // 2 - 1)).astype(jnp.float32)
    positions = (lax.rem(iota(cosine_ref.shape, 0), drafts) + length_ref[0]).astype(jnp.float32)
    angles = positions * jnp.exp(half * (-2.0 * math.log(rope_base) / width))
    cosine_ref[...] = jnp.cos(angles)
    sine_ref[...] = jnp.sin(angles) * jnp.where(lane < width // 2, -1.0, 1.0)
    index = iota(slots_ref.shape, 0)
    column = iota(slots_ref.shape, 1)
    near = parts_of(as_gathered, sizes, index)
    far = parts_of(by_draft, sizes, index)
    row_group = jnp.where(column == 0, near[0], far[0])
    row_block = jnp.where(column == 0, turned(near[1], blocks), far[1])
    place = row_block * groups + row_group
    slots = jnp.zeros(slots_ref.shape, jnp.int32)
    for row in range(blocks * groups):
        slots = jnp.where(place == row, pool_ref[ids_ref[row]], slots)
    slots_ref[...] = slots


def prepare(sizes, ids, pool, lengths, table, later):
    groups, blocks, drafts = sizes
    smem = pl.BlockSpec(memory_space=pltpu.SMEM)
    table = shape(table, jnp.float32)
    return call(
        functools.partial(prepare_kernel, sizes),
        [shape((groups * blocks * drafts, 128), jnp.int32), table, table],
        [smem, smem, smem, HBM],
        limit=40 * MIB,
    )(ids, pool, lengths, later)


def grow_kernel(
    sizes, width, total_ref, rows_ref, key_ref, value_ref, slots_ref, ranks_ref, *refs
):
    groups, blocks, drafts = sizes
    *grows, out_ref, held = refs
    group = group_of()
    requests = groups * blocks
    lines = out_ref.shape[1]
    held[...] = jnp.zeros(held.shape, jnp.float32)
    owned = grows[0].shape[0] // width
    ranks = ranks_ref[group * groups].astype(jnp.float32)
    for other in range(1, groups):
        ranks = ranks + ranks_ref[group * groups + other].astype(jnp.float32)
    ranks = dot(reorder(sizes, as_gathered, by_draft), ranks.astype(jnp.bfloat16))
    place = slots_ref[:, 0:1] - group * owned
    wide = spread_ranks(ranks.astype(jnp.bfloat16), place, width, owned, len(grows))
    arranged = reorder(sizes, by_draft, as_gathered)
    start = 0
    for index, grow in enumerate(grows):
        deep, cols = grow.shape
        if index == 0:
            full = total_ref[...]
        else:
            full = dot(rows_ref[...], (key_ref, value_ref)[index - 1][...])
        full = full + dot(wide[:, index * deep : (index + 1) * deep], grow[...])
        full = dot(arranged, full.astype(jnp.bfloat16))
        for head in range(cols // 128):
            for draft in range(drafts):
                held[pl.ds(start + draft, requests, stride=lines), :] = full[
                    draft * requests : (draft + 1) * requests, head * 128 : (head + 1) * 128
                ]
            start += drafts
    for row in range(requests):
        out_ref[row] = held[row * lines : (row + 1) * lines, :].astype(jnp.bfloat16)


def attend_kernel(
    sizes, arrived_ref, keys_ref, values_ref, length_ref, cosine_ref, sine_ref, out_ref, *scratch
):
    groups, blocks, drafts = sizes
    (fresh_s,) = scratch
    cache_size, head_size = keys_ref.shape[2:]
    count = out_ref.shape[1]
    scale = 1.0 / math.sqrt(head_size)
    fresh_s[...] = jnp.zeros(fresh_s.shape, jnp.float32)
    for block in range(blocks):
        joined = arrived_ref[block * groups].astype(jnp.float32)
        for other in range(1, groups):
            joined = joined + arrived_ref[block * groups + other].astype(jnp.float32)
        joined = joined.astype(jnp.bfloat16).astype(jnp.float32)
        rotated = joined * cosine_ref[...] + pltpu.roll(joined, head_size // 2, 1) * sine_ref[...]
        fresh_s[2 * block, 0:drafts, :] = rotated[count : count + drafts]
        fresh_s[2 * block + 1, 0:drafts, :] = joined[count + drafts : count + 2 * drafts]
        query = rotated[0:count].astype(jnp.bfloat16)
        old = dot_nt(query, keys_ref[0, block]) * scale
        new = dot_nt(query, fresh_s[2 * block].astype(jnp.bfloat16)) * scale
        old = jnp.where(iota(old.shape, 1) < length_ref[0], old, -jnp.inf)
        seen = iota(new.shape, 1) <= lax.rem(iota(new.shape, 0), drafts)
        new = jnp.where(seen, new, -jnp.inf)
        peak = jnp.maximum(jnp.max(old, 1, keepdims=True), jnp.max(new, 1, keepdims=True))
        old = jnp.exp(old - peak)
        new = jnp.exp(new - peak)
        below = jnp.sum(old, 1, keepdims=True) + jnp.sum(new, 1, keepdims=True)
        mixed = dot((old / below).astype(jnp.bfloat16), values_ref[0, block]) + dot(
            (new / below).astype(jnp.bfloat16), fresh_s[2 * block + 1].astype(jnp.bfloat16)
        )
        mixed = mixed.astype(jnp.bfloat16)
        for target in range(groups):
            out_ref[block * groups + target] = mixed


def packing(rows, width, lanes):
    parts = lanes // width
    return parts, rows // parts


def out_rank_kernel(sizes, owned, got_ref, shrink_ref, slots_ref, rows_ref, rank_ref, wide):
    drafts = sizes[2]
    requests, lines, head_size = got_ref.shape
    for row in range(requests):
        wide[row * lines : (row + 1) * lines, :] = got_ref[row].astype(jnp.float32)
    for head in range(lines // drafts):
        for draft in range(drafts):
            rows_ref[
                draft * requests : (draft + 1) * requests,
                head * head_size : (head + 1) * head_size,
            ] = wide[pl.ds(head * drafts + draft, requests, stride=lines), :].astype(jnp.bfloat16)
    rows = rows_ref[...]
    place = slots_ref[:, 1:2] - group_of() * owned
    width = shrink_ref.shape[0] // owned
    _, held, lanes = rank_ref.shape
    parts, span = packing(rows.shape[0], width, lanes)
    ranks = dot_nt(rows, shrink_ref[...])
    kept = jnp.where(over(iota(ranks.shape, 1), width) == place, ranks, 0.0).astype(jnp.bfloat16)
    fold = (ranks.shape[1], lanes)
    fold = rest_of(iota(fold, 0), width) == rest_of(iota(fold, 1), width)
    ranks = dot(kept, jnp.where(fold, 1.0, 0.0).astype(jnp.bfloat16))
    mine = over(iota(ranks.shape, 1), width) == over(iota(ranks.shape, 0), span)
    ranks = jnp.where(mine, ranks, 0.0).astype(jnp.bfloat16)
    put = (held, rows.shape[0])
    put = iota(put, 0) == rest_of(iota(put, 1), span)
    ranks = dot(jnp.where(put, 1.0, 0.0).astype(jnp.bfloat16), ranks).astype(jnp.bfloat16)
    for target in range(rank_ref.shape[0]):
        rank_ref[target] = ranks


def out_grow_kernel(sizes, width, total_ref, slots_ref, ranks_ref, grow_ref, *outs):
    groups, blocks, drafts = sizes
    owned = grow_ref.shape[0] // width
    me = lax.axis_index("tensor")
    ranks = ranks_ref[me].astype(jnp.float32)
    for source in range(1, blocks):
        ranks = ranks + ranks_ref[source * groups + me].astype(jnp.float32)
    count = total_ref.shape[0]
    held, lanes = ranks.shape
    parts, span = packing(count, width, lanes)
    put = rest_of(iota((count, held), 0), span) == iota((count, held), 1)
    ranks = dot(jnp.where(put, 1.0, 0.0).astype(jnp.bfloat16), ranks.astype(jnp.bfloat16))
    mine = over(iota(ranks.shape, 1), width) == over(iota(ranks.shape, 0), span)
    ranks = jnp.where(mine, ranks, 0.0).astype(jnp.bfloat16)
    tile = (lanes, owned * width)
    tile = rest_of(iota(tile, 0), width) == rest_of(iota(tile, 1), width)
    ranks = dot(ranks, jnp.where(tile, 1.0, 0.0).astype(jnp.bfloat16))
    place = slots_ref[:, 1:2] - me * owned
    wide = jnp.where(over(iota(ranks.shape, 1), width) == place, ranks, 0.0).astype(jnp.bfloat16)
    full = (total_ref[...] + dot(wide, grow_ref[...])).astype(jnp.bfloat16)
    full = dot(reorder(sizes, as_gathered, by_draft), full).astype(jnp.bfloat16)
    for block in range(blocks):
        for draft in range(drafts):
            start = (block * drafts + draft) * groups
            outs[block][draft] = full[start : start + groups]


def by_kernels(
    tokens,
    w_query,
    w_key,
    w_value,
    w_out,
    shrink_qkv,
    grow_query,
    grow_key,
    grow_value,
    shrink_out,
    grow_out,
    cache_keys,
    cache_values,
    cache_lengths,
    adapter_ids,
    adapter_slots,
):
    blocks = lax.axis_size("tensor")
    groups = lax.axis_size(GROUP)
    _, drafts, features = tokens.shape
    sizes = (groups, blocks, drafts)
    owned = shrink_qkv.shape[0]
    width = grow_out.shape[1]
    head_size = cache_keys.shape[3]
    span = blocks * drafts
    count = groups * span
    lanes = -(-shrink_qkv.shape[2] // 128) * 128

    def over_tensor(value, shift):
        route = [(t, (t + shift) % blocks) for t in range(blocks)]
        return lax.ppermute(value, "tensor", route)

    def exchange(value):
        return lax.all_to_all(value, EVERY, split_axis=0, concat_axis=0, tiled=True)

    mine = jnp.transpose(tokens, (1, 0, 2))
    pieces = [mine] + [over_tensor(mine, shift) for shift in range(1, blocks)]

    lines = (w_query.shape[1] // head_size + 2) * drafts
    lines = -(-lines // 8) * 8
    slots, cosine, sine = prepare(
        sizes, adapter_ids, adapter_slots, cache_lengths, (lines, head_size), w_out
    )
    shrink_in = jnp.transpose(shrink_qkv, (0, 2, 1)).reshape(-1, features)
    rows, rank_part = call(
        functools.partial(rank_kernel, sizes, owned),
        [shape((count, features)), shape((blocks * groups, count, lanes))],
        [VMEM] * (blocks + 2),
        [pltpu.VMEM((count, features), jnp.float32)],
        2 * count * shrink_qkv.size,
        2 * shrink_qkv.size + 4 * count * features,
    )(*pieces, shrink_in, slots)
    ranks = exchange(rank_part)
    total = stream(rows, w_query, 8, [w_out] * 3)
    cols = total.shape[1] + w_key.shape[1] + w_value.shape[1]
    head_cols = total.shape[1]
    query_lines = head_cols // head_size * drafts
    sent = call(
        functools.partial(grow_kernel, sizes, width),
        shape((blocks * groups, lines, head_size)),
        [VMEM] * 9,
        [pltpu.VMEM((blocks * groups * lines, head_size), jnp.float32)],
        2 * count * owned * width * cols,
        8 * count * cols + 2 * owned * width * cols,
    )(
        total,
        rows,
        w_key,
        w_value,
        slots,
        ranks,
        *[grow.reshape(owned * width, -1) for grow in (grow_query, grow_key, grow_value)],
    )
    mixed = call(
        functools.partial(attend_kernel, sizes),
        shape((blocks * groups, query_lines, head_size)),
        [VMEM] * 3 + [pl.BlockSpec(memory_space=pltpu.SMEM)] + [VMEM] * 2,
        [pltpu.VMEM((2 * blocks, 128, head_size), jnp.float32)],
    )(exchange(sent), cache_keys, cache_values, cache_lengths, cosine, sine)
    gathered = exchange(mixed)
    held = -(-packing(count, width, 128)[1] // 16) * 16
    out_rows, out_part = call(
        functools.partial(out_rank_kernel, sizes, owned),
        [shape((count, head_cols)), shape((blocks * groups, held, 128))],
        [VMEM] * 3,
        [pltpu.VMEM((blocks * groups * query_lines, head_size), jnp.float32)],
    )(gathered, jnp.transpose(shrink_out, (0, 2, 1)).reshape(-1, head_cols), slots)
    out_ranks = exchange(out_part)
    out_total = stream(out_rows, w_out, 8)
    out_cols = out_total.shape[1]
    leaving = call(
        functools.partial(out_grow_kernel, sizes, width),
        [shape((drafts, groups, out_cols))] * blocks,
        [VMEM] * 4,
        [],
        2 * count * owned * width * out_cols,
        8 * count * out_cols + 2 * owned * width * out_cols,
    )(out_total, slots, out_ranks, grow_out.reshape(owned * width, -1))
    result = leaving[0].astype(jnp.float32)
    for shift in range(1, blocks):
        result = result + over_tensor(leaving[shift], -shift).astype(jnp.float32)
    return jnp.transpose(result.astype(jnp.bfloat16), (1, 0, 2))


def rotate(vectors, positions):
    half_size = vectors.shape[-1] // 2
    frequency = rope_base ** (-2.0 * jnp.arange(half_size, dtype=jnp.float32) / vectors.shape[-1])
    angles = positions[:, None, None] * frequency
    cosine = jnp.cos(angles)
    sine_value = jnp.sin(angles)
    first_half = vectors[..., :half_size]
    second = vectors[..., half_size:]
    return jnp.concatenate(
        [first_half * cosine - second * sine_value, second * cosine + first_half * sine_value], -1
    )


def to_growers(partial, splits):
    total = None
    for shift in range(splits):
        route = [
            (t * splits + g, ((g + shift) % splits) * splits + t)
            for t in range(splits)
            for g in range(splits)
        ]
        got = lax.ppermute(partial, EVERY, route).astype(jnp.float32)
        total = got if total is None else total + got
    return total


def to_out_growers(partial, splits):
    total = None
    for shift in range(splits):
        route = [
            (t * splits + g, g * splits + (t + shift) % splits)
            for t in range(splits)
            for g in range(splits)
        ]
        got = lax.ppermute(partial, EVERY, route).astype(jnp.float32)
        total = got if total is None else total + got
    return total


def slot_table(adapter_ids, adapter_slots):
    matches = adapter_ids[:, None] == jnp.arange(adapter_slots.shape[0], dtype=jnp.int32)[None, :]
    return jnp.sum(jnp.where(matches, adapter_slots[None, :], 0), axis=1)


def attend(query_heads, key_new, value_new, cache_keys, cache_values, length):
    drafts, head_count, head_size = query_heads.shape
    kv_heads, cache_size, _ = cache_keys.shape
    positions = (length + jnp.arange(drafts, dtype=jnp.int32)).astype(jnp.float32)
    query_rot = rotate(query_heads.astype(jnp.float32), positions).astype(jnp.bfloat16)
    key_rot = rotate(key_new.astype(jnp.float32), positions).astype(jnp.bfloat16)
    grouped = query_rot.reshape(drafts, kv_heads, head_count // kv_heads, head_size)
    score_scale = 1.0 / math.sqrt(head_size)
    cached = (
        jnp.einsum("skgd,kld->skgl", grouped, cache_keys, preferred_element_type=jnp.float32)
        * score_scale
    )
    fresh_scores = (
        jnp.einsum("skgd,tkd->skgt", grouped, key_rot, preferred_element_type=jnp.float32)
        * score_scale
    )
    cache_mask = jnp.arange(cache_size, dtype=jnp.int32) < length
    draft_mask = jnp.arange(drafts)[None, :] <= jnp.arange(drafts)[:, None]
    cached = jnp.where(cache_mask[None, None, None, :], cached, -jnp.inf)
    fresh_scores = jnp.where(draft_mask[:, None, None, :], fresh_scores, -jnp.inf)
    row_peak = jnp.maximum(jnp.max(cached, -1), jnp.max(fresh_scores, -1))
    cached_exp = jnp.exp(cached - row_peak[..., None])
    fresh_exp = jnp.exp(fresh_scores - row_peak[..., None])
    denominator = jnp.sum(cached_exp, -1) + jnp.sum(fresh_exp, -1)
    cached_prob = (cached_exp / denominator[..., None]).astype(jnp.bfloat16)
    fresh_prob = (fresh_exp / denominator[..., None]).astype(jnp.bfloat16)
    mixed = jnp.einsum(
        "skgl,kld->skgd", cached_prob, cache_values, preferred_element_type=jnp.float32
    )
    mixed = mixed + jnp.einsum(
        "skgt,tkd->skgd", fresh_prob, value_new, preferred_element_type=jnp.float32
    )
    return mixed.astype(jnp.bfloat16)


def by_row(
    tokens,
    w_query,
    w_key,
    w_value,
    w_out,
    shrink_qkv,
    grow_query,
    grow_key,
    grow_value,
    shrink_out,
    grow_out,
    cache_keys,
    cache_values,
    cache_lengths,
    adapter_ids,
    adapter_slots,
):
    splits = lax.axis_size("tensor")
    groups = lax.axis_size(("dp", "pipe"))
    tensor_index = lax.axis_index("tensor")
    group_index = lax.axis_index(("dp", "pipe"))
    local_rows, drafts, feature_width = tokens.shape
    per_owner = shrink_qkv.shape[0]
    rank_size = grow_out.shape[1]
    query_cols = w_query.shape[1]
    key_cols = w_key.shape[1]
    kv_heads = cache_keys.shape[1]
    head_size = cache_keys.shape[3]
    rows = splits * groups
    row_slots = jnp.repeat(slot_table(adapter_ids, adapter_slots), drafts)
    within = jnp.arange(per_owner, dtype=jnp.int32)[None, :]
    width_hot = (row_slots[:, None] == within + tensor_index * per_owner)[:, :, None]
    column_hot = (row_slots[:, None] == within + group_index * per_owner)[:, :, None]

    def spread_ranks(ranks, hot):
        return jnp.where(hot, ranks[:, None, :], 0.0).reshape(rows * drafts, -1).astype(jnp.bfloat16)

    flat_tokens = lax.all_gather(tokens, "tensor", axis=0, tiled=True).reshape(
        rows * drafts, feature_width
    )
    rank_part = jnp.einsum(
        "nd,adr->nar", flat_tokens, shrink_qkv, preferred_element_type=jnp.float32
    )
    rank_part = jnp.sum(jnp.where(width_hot, rank_part, 0.0), 1)
    rank_all = to_growers(rank_part.astype(jnp.bfloat16), splits)

    def grown(index, grow):
        ranks = spread_ranks(rank_all[:, index * rank_size : (index + 1) * rank_size], column_hot)
        return jnp.dot(
            ranks, grow.reshape(per_owner * rank_size, -1), preferred_element_type=jnp.float32
        )

    bases = [
        jnp.dot(flat_tokens, weight, preferred_element_type=jnp.float32)
        for weight in (w_query, w_key, w_value)
    ]

    def product(index, grow):
        return (bases[index] + grown(index, grow)).astype(jnp.bfloat16).reshape(rows, drafts, -1)

    partial = jnp.concatenate(
        [
            product(0, grow_query),
            product(1, grow_key),
            product(2, grow_value),
        ],
        2,
    )
    arrived = lax.all_to_all(partial, EVERY, split_axis=0, concat_axis=0, tiled=True)
    joined = jnp.sum(
        arrived.reshape(splits, groups, drafts, -1).astype(jnp.float32), 1
    ).astype(jnp.bfloat16)
    joined = jnp.transpose(joined, (1, 0, 2))
    query_heads = joined[:, :, :query_cols].reshape(drafts, -1, head_size)
    key_new = joined[:, :, query_cols : query_cols + key_cols].reshape(drafts, kv_heads, head_size)
    value_new = joined[:, :, query_cols + key_cols :].reshape(drafts, kv_heads, head_size)
    mixed = attend(
        query_heads, key_new, value_new, cache_keys[0], cache_values[0], cache_lengths[0]
    )
    mixed = jnp.transpose(mixed.reshape(drafts, splits, -1), (1, 0, 2))
    outgoing = jnp.repeat(mixed, groups, axis=0)
    flat_heads = lax.all_to_all(
        outgoing, EVERY, split_axis=0, concat_axis=0, tiled=True
    ).reshape(rows * drafts, -1)
    out_part = jnp.einsum(
        "nw,awr->nar", flat_heads, shrink_out, preferred_element_type=jnp.float32
    )
    out_part = jnp.sum(jnp.where(column_hot, out_part, 0.0), 1)
    out_rank = to_out_growers(out_part.astype(jnp.bfloat16), splits)
    out = jnp.dot(flat_heads, w_out, preferred_element_type=jnp.float32)
    out = out + jnp.dot(
        spread_ranks(out_rank, width_hot),
        grow_out.reshape(per_owner * rank_size, -1),
        preferred_element_type=jnp.float32,
    )
    blocks = lax.all_to_all(
        out.astype(jnp.bfloat16).reshape(splits, local_rows, drafts, feature_width),
        "tensor",
        split_axis=0,
        concat_axis=0,
        tiled=True,
    )
    return jnp.sum(blocks.astype(jnp.float32), 0).astype(jnp.bfloat16)


def local(*arrays):
    heads = arrays[11].shape[1]
    if heads == lax.axis_size("tensor") == lax.axis_size(GROUP):
        return by_kernels(*arrays)
    return by_row(*arrays)


def solution(mesh):
    placed = (
        P(("parts", "tensor"), None, ("dp", "pipe")),
        P(("dp", "pipe"), "tensor"),
        P(("dp", "pipe"), "tensor"),
        P(("dp", "pipe"), "tensor"),
        P("tensor", ("dp", "pipe")),
        P("tensor", ("dp", "pipe"), None),
        P(("dp", "pipe"), None, "tensor"),
        P(("dp", "pipe"), None, "tensor"),
        P(("dp", "pipe"), None, "tensor"),
        P(("dp", "pipe"), "tensor", None),
        P("tensor", None, ("dp", "pipe")),
        P(("parts", "tensor", "dp", "pipe"), None, None, None),
        P(("parts", "tensor", "dp", "pipe"), None, None, None),
        P(("parts", "tensor", "dp", "pipe")),
        P(),
        P(),
    )
    return jax.shard_map(
        local,
        mesh=mesh,
        in_specs=placed,
        out_specs=P(("parts", "tensor"), None, ("dp", "pipe")),
        check_vma=False,
    )
```

```python
import functools
import math

import jax
import jax.numpy as jnp
import numpy as np
from jax import lax
from jax.experimental import pallas as pl
from jax.experimental.pallas import tpu as pltpu
from jax.sharding import PartitionSpec as P

rope_base = 500000.0
EVERY = ("tensor", "dp", "pipe")
GROUP = ("dp", "pipe")
VMEM = pl.BlockSpec(memory_space=pltpu.VMEM)
HBM = pl.BlockSpec(memory_space=pltpu.HBM)
MIB = 1 << 20


def dot(left, right):
    return jnp.dot(left, right, preferred_element_type=jnp.float32)


def dot_nt(left, right):
    return lax.dot_general(
        left, right, (((1,), (1,)), ((), ())), preferred_element_type=jnp.float32
    )


def iota(shape, axis):
    return lax.broadcasted_iota(jnp.int32, shape, axis)


def call(kernel, outs, ins, scratch=(), flops=0, moved=0, limit=24 * MIB):
    return pl.pallas_call(
        kernel,
        out_shape=outs,
        in_specs=ins,
        out_specs=jax.tree.map(lambda _: VMEM, outs),
        scratch_shapes=list(scratch),
        cost_estimate=pl.CostEstimate(flops=flops, bytes_accessed=moved, transcendentals=0),
        compiler_params=pltpu.CompilerParams(vmem_limit_bytes=limit),
    )


def shape(dims, kind=jnp.bfloat16):
    return jax.ShapeDtypeStruct(tuple(dims), kind)


def over(value, size):
    return value >> (size.bit_length() - 1) if size & (size - 1) == 0 else lax.div(value, size)


def rest_of(value, size):
    return value & (size - 1) if size & (size - 1) == 0 else lax.rem(value, size)


def as_gathered(sizes, group, block, draft):
    groups, blocks, drafts = sizes
    return (block * drafts + draft) * groups + group


def by_draft(sizes, group, block, draft):
    groups, blocks, drafts = sizes
    return (draft * blocks + block) * groups + group


def parts_of(order, sizes, index):
    groups, blocks, drafts = sizes
    group, left = rest_of(index, groups), over(index, groups)
    if order is as_gathered:
        return group, over(left, drafts), rest_of(left, drafts)
    return group, rest_of(left, blocks), over(left, blocks)


def turned(block, blocks):
    return rest_of(lax.axis_index("tensor") - block + blocks, blocks)


def reorder(sizes, after, before):
    groups, blocks, drafts = sizes
    rows = groups * blocks * drafts
    group, block, draft = parts_of(after, sizes, iota((rows, rows), 0))
    wanted = before(sizes, group, turned(block, blocks), draft)
    return jnp.where(wanted == iota((rows, rows), 1), 1.0, 0.0).astype(jnp.bfloat16)


def group_of():
    return lax.axis_index("dp") * lax.axis_size("pipe") + lax.axis_index("pipe")


def rank_kernel(sizes, owned, *refs):
    groups, blocks, drafts = sizes
    pieces = refs[:blocks]
    shrink_ref, slots_ref = refs[blocks : blocks + 2]
    rows_ref, rank_ref, wide = refs[-3:]
    for block in range(blocks):
        for draft in range(drafts):
            start = (block * drafts + draft) * groups
            wide[start : start + groups, :] = pieces[block][draft].astype(jnp.float32)
    rows = wide[...].astype(jnp.bfloat16)
    rows_ref[...] = rows
    place = slots_ref[:, 0:1] - lax.axis_index("tensor") * owned
    ranks = owned_ranks(
        rows, shrink_ref[...], place, shrink_ref.shape[0] // owned, rank_ref.shape[2]
    )
    put = (rank_ref.shape[1], rows.shape[0])
    draft = parts_of(as_gathered, sizes, iota((rows.shape[0], put[0]), 0))[2]
    line = slots_ref[:, 2:3] * drafts + draft
    put = jnp.where(line == iota((rows.shape[0], put[0]), 1), 1.0, 0.0).astype(jnp.bfloat16)
    ranks = lax.dot_general(
        put, ranks, (((0,), (0,)), ((), ())), preferred_element_type=jnp.float32
    ).astype(jnp.bfloat16)
    for target in range(rank_ref.shape[0]):
        rank_ref[target] = ranks


def owned_ranks(rows, shrink, place, width, lanes):
    ranks = dot_nt(rows, shrink)
    kept = jnp.where(over(iota(ranks.shape, 1), width) == place, ranks, 0.0).astype(jnp.bfloat16)
    fold = (ranks.shape[1], lanes)
    fold = rest_of(iota(fold, 0), width) == iota(fold, 1)
    return dot(kept, jnp.where(fold, 1.0, 0.0).astype(jnp.bfloat16)).astype(jnp.bfloat16)


def spread_ranks(ranks, place, width, owned, parts):
    span = owned * width
    row = iota((ranks.shape[1], parts * span), 0)
    column = iota((ranks.shape[1], parts * span), 1)
    tile = (over(row, width) == over(column, span)) & (
        rest_of(row, width) == rest_of(column, width)
    )
    wide = dot(ranks, jnp.where(tile, 1.0, 0.0).astype(jnp.bfloat16))
    slot = over(rest_of(iota(wide.shape, 1), span), width)
    return jnp.where(slot == place, wide, 0.0).astype(jnp.bfloat16)


def stream_kernel(chunks, rows_ref, weight_ref, *refs):
    total_ref, buffer, sems = refs[-3:]
    depth = rows_ref.shape[1] // chunks

    def copy(chunk):
        part = pl.ds(chunk * depth, depth)
        return pltpu.make_async_copy(weight_ref.at[part], buffer.at[part], sems.at[chunk])

    for chunk in range(chunks):
        copy(chunk).start()
    for chunk in range(chunks):
        copy(chunk).wait()
        product = dot(
            rows_ref[:, chunk * depth : (chunk + 1) * depth],
            buffer[chunk * depth : (chunk + 1) * depth, :],
        )
        if chunk:
            total_ref[...] += product
        else:
            total_ref[...] = product


def stream(rows, weight, chunks, later=()):
    return call(
        functools.partial(stream_kernel, chunks),
        shape((rows.shape[0], weight.shape[1]), jnp.float32),
        [VMEM, HBM] + [HBM] * len(later),
        [pltpu.VMEM(weight.shape, weight.dtype), pltpu.SemaphoreType.DMA((chunks,))],
        limit=40 * MIB,
    )(rows, weight, *later)


def prepare_kernel(sizes, owned, ids_ref, pool_ref, length_ref, _, *outs):
    slots_ref, cosine_ref, sine_ref = outs
    groups, blocks, drafts = sizes
    width = cosine_ref.shape[1]
    lane = iota(cosine_ref.shape, 1)
    half = (lane & (width // 2 - 1)).astype(jnp.float32)
    positions = (lax.rem(iota(cosine_ref.shape, 0), drafts) + length_ref[0]).astype(jnp.float32)
    angles = positions * jnp.exp(half * (-2.0 * math.log(rope_base) / width))
    cosine_ref[...] = jnp.cos(angles)
    sine_ref[...] = jnp.sin(angles) * jnp.where(lane < width // 2, -1.0, 1.0)
    index = iota(slots_ref.shape, 0)
    column = iota(slots_ref.shape, 1)
    near = parts_of(as_gathered, sizes, index)
    far = parts_of(by_draft, sizes, index)
    row_group = jnp.where(column == 1, far[0], near[0])
    row_block = jnp.where(column == 1, far[1], turned(near[1], blocks))
    place = row_block * groups + row_group
    slots = jnp.zeros(slots_ref.shape, jnp.int32)
    sent, taken = 0, 0
    for row in range(blocks * groups):
        slot = pool_ref[ids_ref[row]]
        owner = over(slot, owned)
        sends = jnp.where(owner == lax.axis_index("tensor"), 1, 0)
        takes = jnp.where(owner == group_of(), 1, 0)
        line = jnp.where(column == 2, sent - 64 * (1 - sends), taken - 64 * (1 - takes))
        slots = jnp.where(place == row, jnp.where(column < 2, slot, line), slots)
        sent, taken = sent + sends, taken + takes
    slots_ref[...] = slots


def prepare(sizes, owned, ids, pool, lengths, table, later):
    groups, blocks, drafts = sizes
    smem = pl.BlockSpec(memory_space=pltpu.SMEM)
    table = shape(table, jnp.float32)
    return call(
        functools.partial(prepare_kernel, sizes, owned),
        [shape((groups * blocks * drafts, 128), jnp.int32), table, table],
        [smem, smem, smem, HBM],
        limit=40 * MIB,
    )(ids, pool, lengths, later)


def grow_kernel(
    sizes, width, total_ref, rows_ref, key_ref, value_ref, slots_ref, ranks_ref, *refs
):
    groups, blocks, drafts = sizes
    grows, (out_ref, held) = refs[:3], refs[-2:]
    group = group_of()
    requests = groups * blocks
    lines = out_ref.shape[1]
    held[...] = jnp.zeros(held.shape, jnp.float32)
    owned = grows[0].shape[0] // width
    ranks = ranks_ref[group * groups].astype(jnp.float32)
    for other in range(1, groups):
        ranks = ranks + ranks_ref[group * groups + other].astype(jnp.float32)
    get = (rows_ref.shape[0], ranks.shape[0])
    draft = parts_of(as_gathered, sizes, iota(get, 0))[2]
    get = slots_ref[:, 3:4] * drafts + draft == iota(get, 1)
    ranks = dot(jnp.where(get, 1.0, 0.0).astype(jnp.bfloat16), ranks.astype(jnp.bfloat16))
    place = slots_ref[:, 0:1] - group * owned
    wide = spread_ranks(ranks.astype(jnp.bfloat16), place, width, owned, len(grows))
    arranged = reorder(sizes, by_draft, as_gathered)
    start = 0
    for index, grow in enumerate(grows):
        deep, cols = grow.shape
        if index == 0:
            full = total_ref[...]
        else:
            full = dot(rows_ref[...], (key_ref, value_ref)[index - 1][...])
        full = full + dot(wide[:, index * deep : (index + 1) * deep], grow[...])
        full = dot(arranged, full.astype(jnp.bfloat16))
        for head in range(cols // 128):
            for draft in range(drafts):
                held[pl.ds(start + draft, requests, stride=lines), :] = full[
                    draft * requests : (draft + 1) * requests, head * 128 : (head + 1) * 128
                ]
            start += drafts
    for row in range(requests):
        out_ref[row] = held[row * lines : (row + 1) * lines, :].astype(jnp.bfloat16)


def attend_kernel(
    sizes, arrived_ref, keys_ref, values_ref, length_ref, cosine_ref, sine_ref, out_ref, *scratch
):
    groups, blocks, drafts = sizes
    (fresh_s,) = scratch
    cache_size, head_size = keys_ref.shape[2:]
    count = out_ref.shape[1]
    scale = 1.0 / math.sqrt(head_size)
    fresh_s[...] = jnp.zeros(fresh_s.shape, jnp.float32)
    for block in range(blocks):
        joined = arrived_ref[block * groups].astype(jnp.float32)
        for other in range(1, groups):
            joined = joined + arrived_ref[block * groups + other].astype(jnp.float32)
        joined = joined.astype(jnp.bfloat16).astype(jnp.float32)
        rotated = joined * cosine_ref[...] + pltpu.roll(joined, head_size // 2, 1) * sine_ref[...]
        fresh_s[2 * block, 0:drafts, :] = rotated[count : count + drafts]
        fresh_s[2 * block + 1, 0:drafts, :] = joined[count + drafts : count + 2 * drafts]
        query = rotated[0:count].astype(jnp.bfloat16)
        old = dot_nt(query, keys_ref[0, block]) * scale
        new = dot_nt(query, fresh_s[2 * block].astype(jnp.bfloat16)) * scale
        old = jnp.where(iota(old.shape, 1) < length_ref[0], old, -jnp.inf)
        seen = iota(new.shape, 1) <= lax.rem(iota(new.shape, 0), drafts)
        new = jnp.where(seen, new, -jnp.inf)
        peak = jnp.maximum(jnp.max(old, 1, keepdims=True), jnp.max(new, 1, keepdims=True))
        old = jnp.exp(old - peak)
        new = jnp.exp(new - peak)
        below = jnp.sum(old, 1, keepdims=True) + jnp.sum(new, 1, keepdims=True)
        mixed = dot((old / below).astype(jnp.bfloat16), values_ref[0, block]) + dot(
            (new / below).astype(jnp.bfloat16), fresh_s[2 * block + 1].astype(jnp.bfloat16)
        )
        mixed = mixed.astype(jnp.bfloat16)
        for target in range(groups):
            out_ref[block * groups + target] = mixed


def packing(rows, width, lanes):
    parts = lanes // width
    return parts, rows // parts


def out_rank_kernel(sizes, owned, got_ref, shrink_ref, slots_ref, rows_ref, rank_ref, wide):
    drafts = sizes[2]
    requests, lines, head_size = got_ref.shape
    for row in range(requests):
        wide[row * lines : (row + 1) * lines, :] = got_ref[row].astype(jnp.float32)
    for head in range(lines // drafts):
        for draft in range(drafts):
            rows_ref[
                draft * requests : (draft + 1) * requests,
                head * head_size : (head + 1) * head_size,
            ] = wide[pl.ds(head * drafts + draft, requests, stride=lines), :].astype(jnp.bfloat16)
    rows = rows_ref[...]
    place = slots_ref[:, 1:2] - group_of() * owned
    width = shrink_ref.shape[0] // owned
    _, held, lanes = rank_ref.shape
    parts, span = packing(rows.shape[0], width, lanes)
    ranks = dot_nt(rows, shrink_ref[...])
    kept = jnp.where(over(iota(ranks.shape, 1), width) == place, ranks, 0.0).astype(jnp.bfloat16)
    fold = (ranks.shape[1], lanes)
    fold = rest_of(iota(fold, 0), width) == rest_of(iota(fold, 1), width)
    ranks = dot(kept, jnp.where(fold, 1.0, 0.0).astype(jnp.bfloat16))
    mine = over(iota(ranks.shape, 1), width) == over(iota(ranks.shape, 0), span)
    ranks = jnp.where(mine, ranks, 0.0).astype(jnp.bfloat16)
    put = (held, rows.shape[0])
    put = iota(put, 0) == rest_of(iota(put, 1), span)
    ranks = dot(jnp.where(put, 1.0, 0.0).astype(jnp.bfloat16), ranks).astype(jnp.bfloat16)
    for target in range(rank_ref.shape[0]):
        rank_ref[target] = ranks


def out_grow_kernel(sizes, width, total_ref, slots_ref, ranks_ref, grow_ref, *outs):
    groups, blocks, drafts = sizes
    owned = grow_ref.shape[0] // width
    me = lax.axis_index("tensor")
    ranks = ranks_ref[me].astype(jnp.float32)
    for source in range(1, blocks):
        ranks = ranks + ranks_ref[source * groups + me].astype(jnp.float32)
    count = total_ref.shape[0]
    held, lanes = ranks.shape
    parts, span = packing(count, width, lanes)
    put = rest_of(iota((count, held), 0), span) == iota((count, held), 1)
    ranks = dot(jnp.where(put, 1.0, 0.0).astype(jnp.bfloat16), ranks.astype(jnp.bfloat16))
    mine = over(iota(ranks.shape, 1), width) == over(iota(ranks.shape, 0), span)
    ranks = jnp.where(mine, ranks, 0.0).astype(jnp.bfloat16)
    tile = (lanes, owned * width)
    tile = rest_of(iota(tile, 0), width) == rest_of(iota(tile, 1), width)
    ranks = dot(ranks, jnp.where(tile, 1.0, 0.0).astype(jnp.bfloat16))
    place = slots_ref[:, 1:2] - me * owned
    wide = jnp.where(over(iota(ranks.shape, 1), width) == place, ranks, 0.0).astype(jnp.bfloat16)
    full = (total_ref[...] + dot(wide, grow_ref[...])).astype(jnp.bfloat16)
    full = dot(reorder(sizes, as_gathered, by_draft), full).astype(jnp.bfloat16)
    for block in range(blocks):
        for draft in range(drafts):
            start = (block * drafts + draft) * groups
            outs[block][draft] = full[start : start + groups]


def by_kernels(
    tokens,
    w_query,
    w_key,
    w_value,
    w_out,
    shrink_qkv,
    grow_query,
    grow_key,
    grow_value,
    shrink_out,
    grow_out,
    cache_keys,
    cache_values,
    cache_lengths,
    adapter_ids,
    adapter_slots,
):
    blocks = lax.axis_size("tensor")
    groups = lax.axis_size(GROUP)
    _, drafts, features = tokens.shape
    sizes = (groups, blocks, drafts)
    owned = shrink_qkv.shape[0]
    width = grow_out.shape[1]
    head_size = cache_keys.shape[3]
    span = blocks * drafts
    count = groups * span
    lanes = -(-shrink_qkv.shape[2] // 128) * 128

    def over_tensor(value, shift):
        route = [(t, (t + shift) % blocks) for t in range(blocks)]
        return lax.ppermute(value, "tensor", route)

    def exchange(value):
        return lax.all_to_all(value, EVERY, split_axis=0, concat_axis=0, tiled=True)

    mine = jnp.transpose(tokens, (1, 0, 2))
    pieces = [mine] + [over_tensor(mine, shift) for shift in range(1, blocks)]

    lines = (w_query.shape[1] // head_size + 2) * drafts
    lines = -(-lines // 8) * 8
    slots, cosine, sine = prepare(
        sizes, owned, adapter_ids, adapter_slots, cache_lengths, (lines, head_size), w_out
    )
    packed = -(-2 * blocks * drafts // 16) * 16
    shrink_in = jnp.transpose(shrink_qkv, (0, 2, 1)).reshape(-1, features)
    rows, rank_part = call(
        functools.partial(rank_kernel, sizes, owned),
        [shape((count, features)), shape((blocks * groups, packed, lanes))],
        [VMEM] * (blocks + 2),
        [pltpu.VMEM((count, features), jnp.float32)],
        2 * count * shrink_qkv.size,
        2 * shrink_qkv.size + 4 * count * features,
    )(*pieces, shrink_in, slots)
    ranks = exchange(rank_part)
    total = stream(rows, w_query, 8, [w_out] * 3)
    cols = total.shape[1] + w_key.shape[1] + w_value.shape[1]
    head_cols = total.shape[1]
    query_lines = head_cols // head_size * drafts
    sent = call(
        functools.partial(grow_kernel, sizes, width),
        shape((blocks * groups, lines, head_size)),
        [VMEM] * 9 + [HBM] * 2,
        [pltpu.VMEM((blocks * groups * lines, head_size), jnp.float32)],
        limit=40 * MIB,
    )(
        total,
        rows,
        w_key,
        w_value,
        slots,
        ranks,
        *[grow.reshape(owned * width, -1) for grow in (grow_query, grow_key, grow_value)],
        *[w_out] * 2,
    )
    mixed = call(
        functools.partial(attend_kernel, sizes),
        shape((blocks * groups, query_lines, head_size)),
        [VMEM] * 3 + [pl.BlockSpec(memory_space=pltpu.SMEM)] + [VMEM] * 2,
        [pltpu.VMEM((2 * blocks, 128, head_size), jnp.float32)],
    )(exchange(sent), cache_keys, cache_values, cache_lengths, cosine, sine)
    gathered = exchange(mixed)
    held = -(-packing(count, width, 128)[1] // 16) * 16
    out_rows, out_part = call(
        functools.partial(out_rank_kernel, sizes, owned),
        [shape((count, head_cols)), shape((blocks * groups, held, 128))],
        [VMEM] * 3,
        [pltpu.VMEM((blocks * groups * query_lines, head_size), jnp.float32)],
    )(gathered, jnp.transpose(shrink_out, (0, 2, 1)).reshape(-1, head_cols), slots)
    out_ranks = exchange(out_part)
    out_total = stream(out_rows, w_out, 8)
    out_cols = out_total.shape[1]
    leaving = call(
        functools.partial(out_grow_kernel, sizes, width),
        [shape((drafts, groups, out_cols))] * blocks,
        [VMEM] * 4,
        [],
        2 * count * owned * width * out_cols,
        8 * count * out_cols + 2 * owned * width * out_cols,
    )(out_total, slots, out_ranks, grow_out.reshape(owned * width, -1))
    result = leaving[0].astype(jnp.float32)
    for shift in range(1, blocks):
        result = result + over_tensor(leaving[shift], -shift).astype(jnp.float32)
    return jnp.transpose(result.astype(jnp.bfloat16), (1, 0, 2))


def rotate(vectors, positions):
    half_size = vectors.shape[-1] // 2
    frequency = rope_base ** (-2.0 * jnp.arange(half_size, dtype=jnp.float32) / vectors.shape[-1])
    angles = positions[:, None, None] * frequency
    cosine = jnp.cos(angles)
    sine_value = jnp.sin(angles)
    first_half = vectors[..., :half_size]
    second = vectors[..., half_size:]
    return jnp.concatenate(
        [first_half * cosine - second * sine_value, second * cosine + first_half * sine_value], -1
    )


def to_growers(partial, splits):
    total = None
    for shift in range(splits):
        route = [
            (t * splits + g, ((g + shift) % splits) * splits + t)
            for t in range(splits)
            for g in range(splits)
        ]
        got = lax.ppermute(partial, EVERY, route).astype(jnp.float32)
        total = got if total is None else total + got
    return total


def to_out_growers(partial, splits):
    total = None
    for shift in range(splits):
        route = [
            (t * splits + g, g * splits + (t + shift) % splits)
            for t in range(splits)
            for g in range(splits)
        ]
        got = lax.ppermute(partial, EVERY, route).astype(jnp.float32)
        total = got if total is None else total + got
    return total


def slot_table(adapter_ids, adapter_slots):
    matches = adapter_ids[:, None] == jnp.arange(adapter_slots.shape[0], dtype=jnp.int32)[None, :]
    return jnp.sum(jnp.where(matches, adapter_slots[None, :], 0), axis=1)


def attend(query_heads, key_new, value_new, cache_keys, cache_values, length):
    drafts, head_count, head_size = query_heads.shape
    kv_heads, cache_size, _ = cache_keys.shape
    positions = (length + jnp.arange(drafts, dtype=jnp.int32)).astype(jnp.float32)
    query_rot = rotate(query_heads.astype(jnp.float32), positions).astype(jnp.bfloat16)
    key_rot = rotate(key_new.astype(jnp.float32), positions).astype(jnp.bfloat16)
    grouped = query_rot.reshape(drafts, kv_heads, head_count // kv_heads, head_size)
    score_scale = 1.0 / math.sqrt(head_size)
    cached = (
        jnp.einsum("skgd,kld->skgl", grouped, cache_keys, preferred_element_type=jnp.float32)
        * score_scale
    )
    fresh_scores = (
        jnp.einsum("skgd,tkd->skgt", grouped, key_rot, preferred_element_type=jnp.float32)
        * score_scale
    )
    cache_mask = jnp.arange(cache_size, dtype=jnp.int32) < length
    draft_mask = jnp.arange(drafts)[None, :] <= jnp.arange(drafts)[:, None]
    cached = jnp.where(cache_mask[None, None, None, :], cached, -jnp.inf)
    fresh_scores = jnp.where(draft_mask[:, None, None, :], fresh_scores, -jnp.inf)
    row_peak = jnp.maximum(jnp.max(cached, -1), jnp.max(fresh_scores, -1))
    cached_exp = jnp.exp(cached - row_peak[..., None])
    fresh_exp = jnp.exp(fresh_scores - row_peak[..., None])
    denominator = jnp.sum(cached_exp, -1) + jnp.sum(fresh_exp, -1)
    cached_prob = (cached_exp / denominator[..., None]).astype(jnp.bfloat16)
    fresh_prob = (fresh_exp / denominator[..., None]).astype(jnp.bfloat16)
    mixed = jnp.einsum(
        "skgl,kld->skgd", cached_prob, cache_values, preferred_element_type=jnp.float32
    )
    mixed = mixed + jnp.einsum(
        "skgt,tkd->skgd", fresh_prob, value_new, preferred_element_type=jnp.float32
    )
    return mixed.astype(jnp.bfloat16)


def by_row(
    tokens,
    w_query,
    w_key,
    w_value,
    w_out,
    shrink_qkv,
    grow_query,
    grow_key,
    grow_value,
    shrink_out,
    grow_out,
    cache_keys,
    cache_values,
    cache_lengths,
    adapter_ids,
    adapter_slots,
):
    splits = lax.axis_size("tensor")
    groups = lax.axis_size(("dp", "pipe"))
    tensor_index = lax.axis_index("tensor")
    group_index = lax.axis_index(("dp", "pipe"))
    local_rows, drafts, feature_width = tokens.shape
    per_owner = shrink_qkv.shape[0]
    rank_size = grow_out.shape[1]
    query_cols = w_query.shape[1]
    key_cols = w_key.shape[1]
    kv_heads = cache_keys.shape[1]
    head_size = cache_keys.shape[3]
    rows = splits * groups
    row_slots = jnp.repeat(slot_table(adapter_ids, adapter_slots), drafts)
    within = jnp.arange(per_owner, dtype=jnp.int32)[None, :]
    width_hot = (row_slots[:, None] == within + tensor_index * per_owner)[:, :, None]
    column_hot = (row_slots[:, None] == within + group_index * per_owner)[:, :, None]

    def spread_ranks(ranks, hot):
        return jnp.where(hot, ranks[:, None, :], 0.0).reshape(rows * drafts, -1).astype(jnp.bfloat16)

    flat_tokens = lax.all_gather(tokens, "tensor", axis=0, tiled=True).reshape(
        rows * drafts, feature_width
    )
    rank_part = jnp.einsum(
        "nd,adr->nar", flat_tokens, shrink_qkv, preferred_element_type=jnp.float32
    )
    rank_part = jnp.sum(jnp.where(width_hot, rank_part, 0.0), 1)
    rank_all = to_growers(rank_part.astype(jnp.bfloat16), splits)

    def grown(index, grow):
        ranks = spread_ranks(rank_all[:, index * rank_size : (index + 1) * rank_size], column_hot)
        return jnp.dot(
            ranks, grow.reshape(per_owner * rank_size, -1), preferred_element_type=jnp.float32
        )

    bases = [
        jnp.dot(flat_tokens, weight, preferred_element_type=jnp.float32)
        for weight in (w_query, w_key, w_value)
    ]

    def product(index, grow):
        return (bases[index] + grown(index, grow)).astype(jnp.bfloat16).reshape(rows, drafts, -1)

    partial = jnp.concatenate(
        [
            product(0, grow_query),
            product(1, grow_key),
            product(2, grow_value),
        ],
        2,
    )
    arrived = lax.all_to_all(partial, EVERY, split_axis=0, concat_axis=0, tiled=True)
    joined = jnp.sum(
        arrived.reshape(splits, groups, drafts, -1).astype(jnp.float32), 1
    ).astype(jnp.bfloat16)
    joined = jnp.transpose(joined, (1, 0, 2))
    query_heads = joined[:, :, :query_cols].reshape(drafts, -1, head_size)
    key_new = joined[:, :, query_cols : query_cols + key_cols].reshape(drafts, kv_heads, head_size)
    value_new = joined[:, :, query_cols + key_cols :].reshape(drafts, kv_heads, head_size)
    mixed = attend(
        query_heads, key_new, value_new, cache_keys[0], cache_values[0], cache_lengths[0]
    )
    mixed = jnp.transpose(mixed.reshape(drafts, splits, -1), (1, 0, 2))
    outgoing = jnp.repeat(mixed, groups, axis=0)
    flat_heads = lax.all_to_all(
        outgoing, EVERY, split_axis=0, concat_axis=0, tiled=True
    ).reshape(rows * drafts, -1)
    out_part = jnp.einsum(
        "nw,awr->nar", flat_heads, shrink_out, preferred_element_type=jnp.float32
    )
    out_part = jnp.sum(jnp.where(column_hot, out_part, 0.0), 1)
    out_rank = to_out_growers(out_part.astype(jnp.bfloat16), splits)
    out = jnp.dot(flat_heads, w_out, preferred_element_type=jnp.float32)
    out = out + jnp.dot(
        spread_ranks(out_rank, width_hot),
        grow_out.reshape(per_owner * rank_size, -1),
        preferred_element_type=jnp.float32,
    )
    blocks = lax.all_to_all(
        out.astype(jnp.bfloat16).reshape(splits, local_rows, drafts, feature_width),
        "tensor",
        split_axis=0,
        concat_axis=0,
        tiled=True,
    )
    return jnp.sum(blocks.astype(jnp.float32), 0).astype(jnp.bfloat16)


def local(*arrays):
    heads = arrays[11].shape[1]
    if heads == lax.axis_size("tensor") == lax.axis_size(GROUP):
        return by_kernels(*arrays)
    return by_row(*arrays)


def solution(mesh):
    placed = (
        P(("parts", "tensor"), None, ("dp", "pipe")),
        P(("dp", "pipe"), "tensor"),
        P(("dp", "pipe"), "tensor"),
        P(("dp", "pipe"), "tensor"),
        P("tensor", ("dp", "pipe")),
        P("tensor", ("dp", "pipe"), None),
        P(("dp", "pipe"), None, "tensor"),
        P(("dp", "pipe"), None, "tensor"),
        P(("dp", "pipe"), None, "tensor"),
        P(("dp", "pipe"), "tensor", None),
        P("tensor", None, ("dp", "pipe")),
        P(("parts", "tensor", "dp", "pipe"), None, None, None),
        P(("parts", "tensor", "dp", "pipe"), None, None, None),
        P(("parts", "tensor", "dp", "pipe")),
        P(),
        P(),
    )
    return jax.shard_map(
        local,
        mesh=mesh,
        in_specs=placed,
        out_specs=P(("parts", "tensor"), None, ("dp", "pipe")),
        check_vma=False,
    )
```

```python
import functools
import math

import jax
import jax.numpy as jnp
import numpy as np
from jax import lax
from jax.experimental import pallas as pl
from jax.experimental.pallas import tpu as pltpu
from jax.sharding import PartitionSpec as P

rope_base = 500000.0
EVERY = ("tensor", "dp", "pipe")
GROUP = ("dp", "pipe")
VMEM = pl.BlockSpec(memory_space=pltpu.VMEM)
HBM = pl.BlockSpec(memory_space=pltpu.HBM)
MIB = 1 << 20


def dot(left, right):
    return jnp.dot(left, right, preferred_element_type=jnp.float32)


def dot_nt(left, right):
    return lax.dot_general(
        left, right, (((1,), (1,)), ((), ())), preferred_element_type=jnp.float32
    )


def iota(shape, axis):
    return lax.broadcasted_iota(jnp.int32, shape, axis)


def call(kernel, outs, ins, scratch=(), flops=0, moved=0, limit=24 * MIB):
    return pl.pallas_call(
        kernel,
        out_shape=outs,
        in_specs=ins,
        out_specs=jax.tree.map(lambda _: VMEM, outs),
        scratch_shapes=list(scratch),
        cost_estimate=pl.CostEstimate(flops=flops, bytes_accessed=moved, transcendentals=0),
        compiler_params=pltpu.CompilerParams(vmem_limit_bytes=limit),
    )


def shape(dims, kind=jnp.bfloat16):
    return jax.ShapeDtypeStruct(tuple(dims), kind)


def over(value, size):
    return value >> (size.bit_length() - 1) if size & (size - 1) == 0 else lax.div(value, size)


def rest_of(value, size):
    return value & (size - 1) if size & (size - 1) == 0 else lax.rem(value, size)


def as_gathered(sizes, group, block, draft):
    groups, blocks, drafts = sizes
    return (block * drafts + draft) * groups + group


def by_draft(sizes, group, block, draft):
    groups, blocks, drafts = sizes
    return (draft * blocks + block) * groups + group


def parts_of(order, sizes, index):
    groups, blocks, drafts = sizes
    group, left = rest_of(index, groups), over(index, groups)
    if order is as_gathered:
        return group, over(left, drafts), rest_of(left, drafts)
    return group, rest_of(left, blocks), over(left, blocks)


def turned(block, blocks):
    return rest_of(lax.axis_index("tensor") - block + blocks, blocks)


def reorder(sizes, after, before):
    groups, blocks, drafts = sizes
    rows = groups * blocks * drafts
    group, block, draft = parts_of(after, sizes, iota((rows, rows), 0))
    wanted = before(sizes, group, turned(block, blocks), draft)
    return jnp.where(wanted == iota((rows, rows), 1), 1.0, 0.0).astype(jnp.bfloat16)


def group_of():
    return lax.axis_index("dp") * lax.axis_size("pipe") + lax.axis_index("pipe")


def rank_kernel(sizes, owned, *refs):
    groups, blocks, drafts = sizes
    pieces = refs[:blocks]
    shrink_ref, slots_ref = refs[blocks : blocks + 2]
    rows_ref, rank_ref, wide = refs[-3:]
    for block in range(blocks):
        for draft in range(drafts):
            start = (block * drafts + draft) * groups
            wide[start : start + groups, :] = pieces[block][draft].astype(jnp.float32)
    rows = wide[...].astype(jnp.bfloat16)
    rows_ref[...] = rows
    place = slots_ref[:, 0:1] - lax.axis_index("tensor") * owned
    ranks = owned_ranks(
        rows, shrink_ref[...], place, shrink_ref.shape[0] // owned, rank_ref.shape[2]
    )
    put = (rank_ref.shape[1], rows.shape[0])
    draft = parts_of(as_gathered, sizes, iota((rows.shape[0], put[0]), 0))[2]
    line = slots_ref[:, 2:3] * drafts + draft
    put = jnp.where(line == iota((rows.shape[0], put[0]), 1), 1.0, 0.0).astype(jnp.bfloat16)
    ranks = lax.dot_general(
        put, ranks, (((0,), (0,)), ((), ())), preferred_element_type=jnp.float32
    ).astype(jnp.bfloat16)
    for target in range(rank_ref.shape[0]):
        rank_ref[target] = ranks


def owned_ranks(rows, shrink, place, width, lanes):
    ranks = dot_nt(rows, shrink)
    kept = jnp.where(over(iota(ranks.shape, 1), width) == place, ranks, 0.0).astype(jnp.bfloat16)
    fold = (ranks.shape[1], lanes)
    fold = rest_of(iota(fold, 0), width) == iota(fold, 1)
    return dot(kept, jnp.where(fold, 1.0, 0.0).astype(jnp.bfloat16)).astype(jnp.bfloat16)


def spread_ranks(ranks, place, width, owned, parts):
    span = owned * width
    row = iota((ranks.shape[1], parts * span), 0)
    column = iota((ranks.shape[1], parts * span), 1)
    tile = (over(row, width) == over(column, span)) & (
        rest_of(row, width) == rest_of(column, width)
    )
    wide = dot(ranks, jnp.where(tile, 1.0, 0.0).astype(jnp.bfloat16))
    slot = over(rest_of(iota(wide.shape, 1), span), width)
    return jnp.where(slot == place, wide, 0.0).astype(jnp.bfloat16)


def stream_kernel(chunks, small, rows_ref, weight_ref, *refs):
    total_ref, buffer, sems = refs[-3:]
    depth = rows_ref.shape[1] // chunks
    width = weight_ref.shape[1]

    def copy(chunk):
        part = pl.ds(chunk * depth, depth)
        return pltpu.make_async_copy(weight_ref.at[part], buffer.at[part], sems.at[chunk])

    for chunk in range(chunks):
        copy(chunk).start()
    start = width
    for other in refs[:small]:
        total_ref[:, start : start + other.shape[1]] = dot(rows_ref[...], other[...])
        start += other.shape[1]
    for chunk in range(chunks):
        copy(chunk).wait()
        product = dot(
            rows_ref[:, chunk * depth : (chunk + 1) * depth],
            buffer[chunk * depth : (chunk + 1) * depth, :],
        )
        if chunk:
            total_ref[:, 0:width] += product
        else:
            total_ref[:, 0:width] = product


def stream(rows, weight, chunks, small=(), later=()):
    width = weight.shape[1] + sum(other.shape[1] for other in small)
    return call(
        functools.partial(stream_kernel, chunks, len(small)),
        shape((rows.shape[0], width), jnp.float32),
        [VMEM, HBM] + [VMEM] * len(small) + [HBM] * len(later),
        [pltpu.VMEM(weight.shape, weight.dtype), pltpu.SemaphoreType.DMA((chunks,))],
        limit=40 * MIB,
    )(rows, weight, *small, *later)


def prepare_kernel(sizes, owned, ids_ref, pool_ref, length_ref, _, *outs):
    slots_ref, cosine_ref, sine_ref = outs
    groups, blocks, drafts = sizes
    width = cosine_ref.shape[1]
    lane = iota(cosine_ref.shape, 1)
    half = (lane & (width // 2 - 1)).astype(jnp.float32)
    positions = (lax.rem(iota(cosine_ref.shape, 0), drafts) + length_ref[0]).astype(jnp.float32)
    angles = positions * jnp.exp(half * (-2.0 * math.log(rope_base) / width))
    cosine_ref[...] = jnp.cos(angles)
    sine_ref[...] = jnp.sin(angles) * jnp.where(lane < width // 2, -1.0, 1.0)
    index = iota(slots_ref.shape, 0)
    column = iota(slots_ref.shape, 1)
    near = parts_of(as_gathered, sizes, index)
    far = parts_of(by_draft, sizes, index)
    row_group = jnp.where(column == 1, far[0], near[0])
    row_block = jnp.where(column == 1, far[1], turned(near[1], blocks))
    place = row_block * groups + row_group
    slots = jnp.zeros(slots_ref.shape, jnp.int32)
    sent, taken = 0, 0
    for row in range(blocks * groups):
        slot = pool_ref[ids_ref[row]]
        owner = over(slot, owned)
        sends = jnp.where(owner == lax.axis_index("tensor"), 1, 0)
        takes = jnp.where(owner == group_of(), 1, 0)
        line = jnp.where(column == 2, sent - 64 * (1 - sends), taken - 64 * (1 - takes))
        slots = jnp.where(place == row, jnp.where(column < 2, slot, line), slots)
        sent, taken = sent + sends, taken + takes
    slots_ref[...] = slots


def prepare(sizes, owned, ids, pool, lengths, table, later):
    groups, blocks, drafts = sizes
    smem = pl.BlockSpec(memory_space=pltpu.SMEM)
    table = shape(table, jnp.float32)
    return call(
        functools.partial(prepare_kernel, sizes, owned),
        [shape((groups * blocks * drafts, 128), jnp.int32), table, table],
        [smem, smem, smem, HBM],
        limit=40 * MIB,
    )(ids, pool, lengths, later)


def grow_kernel(sizes, width, total_ref, slots_ref, ranks_ref, *refs):
    groups, blocks, drafts = sizes
    grows, (out_ref, held) = refs[:3], refs[-2:]
    group = group_of()
    requests = groups * blocks
    lines = out_ref.shape[1]
    held[...] = jnp.zeros(held.shape, jnp.float32)
    owned = grows[0].shape[0] // width
    ranks = ranks_ref[group * groups].astype(jnp.float32)
    for other in range(1, groups):
        ranks = ranks + ranks_ref[group * groups + other].astype(jnp.float32)
    get = (total_ref.shape[0], ranks.shape[0])
    draft = parts_of(as_gathered, sizes, iota(get, 0))[2]
    get = slots_ref[:, 3:4] * drafts + draft == iota(get, 1)
    ranks = dot(jnp.where(get, 1.0, 0.0).astype(jnp.bfloat16), ranks.astype(jnp.bfloat16))
    place = slots_ref[:, 0:1] - group * owned
    wide = spread_ranks(ranks.astype(jnp.bfloat16), place, width, owned, len(grows))
    arranged = reorder(sizes, by_draft, as_gathered)
    start, column = 0, 0
    for index, grow in enumerate(grows):
        deep, cols = grow.shape
        full = total_ref[:, column : column + cols] + dot(
            wide[:, index * deep : (index + 1) * deep], grow[...]
        )
        column += cols
        full = dot(arranged, full.astype(jnp.bfloat16))
        for head in range(cols // 128):
            for draft in range(drafts):
                held[pl.ds(start + draft, requests, stride=lines), :] = full[
                    draft * requests : (draft + 1) * requests, head * 128 : (head + 1) * 128
                ]
            start += drafts
    for row in range(requests):
        out_ref[row] = held[row * lines : (row + 1) * lines, :].astype(jnp.bfloat16)


def attend_kernel(
    sizes, arrived_ref, keys_ref, values_ref, length_ref, cosine_ref, sine_ref, out_ref, *scratch
):
    groups, blocks, drafts = sizes
    (fresh_s,) = scratch
    cache_size, head_size = keys_ref.shape[2:]
    count = out_ref.shape[1]
    scale = 1.0 / math.sqrt(head_size)
    fresh_s[...] = jnp.zeros(fresh_s.shape, jnp.float32)
    for block in range(blocks):
        joined = arrived_ref[block * groups].astype(jnp.float32)
        for other in range(1, groups):
            joined = joined + arrived_ref[block * groups + other].astype(jnp.float32)
        joined = joined.astype(jnp.bfloat16).astype(jnp.float32)
        rotated = joined * cosine_ref[...] + pltpu.roll(joined, head_size // 2, 1) * sine_ref[...]
        fresh_s[2 * block, 0:drafts, :] = rotated[count : count + drafts]
        fresh_s[2 * block + 1, 0:drafts, :] = joined[count + drafts : count + 2 * drafts]
        query = rotated[0:count].astype(jnp.bfloat16)
        old = dot_nt(query, keys_ref[0, block]) * scale
        new = dot_nt(query, fresh_s[2 * block].astype(jnp.bfloat16)) * scale
        old = jnp.where(iota(old.shape, 1) < length_ref[0], old, -jnp.inf)
        seen = iota(new.shape, 1) <= lax.rem(iota(new.shape, 0), drafts)
        new = jnp.where(seen, new, -jnp.inf)
        peak = jnp.maximum(jnp.max(old, 1, keepdims=True), jnp.max(new, 1, keepdims=True))
        old = jnp.exp(old - peak)
        new = jnp.exp(new - peak)
        below = jnp.sum(old, 1, keepdims=True) + jnp.sum(new, 1, keepdims=True)
        mixed = dot((old / below).astype(jnp.bfloat16), values_ref[0, block]) + dot(
            (new / below).astype(jnp.bfloat16), fresh_s[2 * block + 1].astype(jnp.bfloat16)
        )
        mixed = mixed.astype(jnp.bfloat16)
        for target in range(groups):
            out_ref[block * groups + target] = mixed


def packing(rows, width, lanes):
    parts = lanes // width
    return parts, rows // parts


def out_rank_kernel(sizes, owned, got_ref, shrink_ref, slots_ref, rows_ref, rank_ref, wide):
    drafts = sizes[2]
    requests, lines, head_size = got_ref.shape
    for row in range(requests):
        wide[row * lines : (row + 1) * lines, :] = got_ref[row].astype(jnp.float32)
    for head in range(lines // drafts):
        for draft in range(drafts):
            rows_ref[
                draft * requests : (draft + 1) * requests,
                head * head_size : (head + 1) * head_size,
            ] = wide[pl.ds(head * drafts + draft, requests, stride=lines), :].astype(jnp.bfloat16)
    rows = rows_ref[...]
    place = slots_ref[:, 1:2] - group_of() * owned
    width = shrink_ref.shape[0] // owned
    _, held, lanes = rank_ref.shape
    parts, span = packing(rows.shape[0], width, lanes)
    ranks = dot_nt(rows, shrink_ref[...])
    kept = jnp.where(over(iota(ranks.shape, 1), width) == place, ranks, 0.0).astype(jnp.bfloat16)
    fold = (ranks.shape[1], lanes)
    fold = rest_of(iota(fold, 0), width) == rest_of(iota(fold, 1), width)
    ranks = dot(kept, jnp.where(fold, 1.0, 0.0).astype(jnp.bfloat16))
    mine = over(iota(ranks.shape, 1), width) == over(iota(ranks.shape, 0), span)
    ranks = jnp.where(mine, ranks, 0.0).astype(jnp.bfloat16)
    put = (held, rows.shape[0])
    put = iota(put, 0) == rest_of(iota(put, 1), span)
    ranks = dot(jnp.where(put, 1.0, 0.0).astype(jnp.bfloat16), ranks).astype(jnp.bfloat16)
    for target in range(rank_ref.shape[0]):
        rank_ref[target] = ranks


def out_grow_kernel(sizes, width, total_ref, slots_ref, ranks_ref, grow_ref, *outs):
    groups, blocks, drafts = sizes
    owned = grow_ref.shape[0] // width
    me = lax.axis_index("tensor")
    ranks = ranks_ref[me].astype(jnp.float32)
    for source in range(1, blocks):
        ranks = ranks + ranks_ref[source * groups + me].astype(jnp.float32)
    count = total_ref.shape[0]
    held, lanes = ranks.shape
    parts, span = packing(count, width, lanes)
    put = rest_of(iota((count, held), 0), span) == iota((count, held), 1)
    ranks = dot(jnp.where(put, 1.0, 0.0).astype(jnp.bfloat16), ranks.astype(jnp.bfloat16))
    mine = over(iota(ranks.shape, 1), width) == over(iota(ranks.shape, 0), span)
    ranks = jnp.where(mine, ranks, 0.0).astype(jnp.bfloat16)
    tile = (lanes, owned * width)
    tile = rest_of(iota(tile, 0), width) == rest_of(iota(tile, 1), width)
    ranks = dot(ranks, jnp.where(tile, 1.0, 0.0).astype(jnp.bfloat16))
    place = slots_ref[:, 1:2] - me * owned
    wide = jnp.where(over(iota(ranks.shape, 1), width) == place, ranks, 0.0).astype(jnp.bfloat16)
    full = (total_ref[...] + dot(wide, grow_ref[...])).astype(jnp.bfloat16)
    full = dot(reorder(sizes, as_gathered, by_draft), full).astype(jnp.bfloat16)
    for block in range(blocks):
        for draft in range(drafts):
            start = (block * drafts + draft) * groups
            outs[block][draft] = full[start : start + groups]


def by_kernels(
    tokens,
    w_query,
    w_key,
    w_value,
    w_out,
    shrink_qkv,
    grow_query,
    grow_key,
    grow_value,
    shrink_out,
    grow_out,
    cache_keys,
    cache_values,
    cache_lengths,
    adapter_ids,
    adapter_slots,
):
    blocks = lax.axis_size("tensor")
    groups = lax.axis_size(GROUP)
    _, drafts, features = tokens.shape
    sizes = (groups, blocks, drafts)
    owned = shrink_qkv.shape[0]
    width = grow_out.shape[1]
    head_size = cache_keys.shape[3]
    span = blocks * drafts
    count = groups * span
    lanes = -(-shrink_qkv.shape[2] // 128) * 128

    def over_tensor(value, shift):
        route = [(t, (t + shift) % blocks) for t in range(blocks)]
        return lax.ppermute(value, "tensor", route)

    def exchange(value):
        return lax.all_to_all(value, EVERY, split_axis=0, concat_axis=0, tiled=True)

    mine = jnp.transpose(tokens, (1, 0, 2))
    pieces = [mine] + [over_tensor(mine, shift) for shift in range(1, blocks)]

    lines = (w_query.shape[1] // head_size + 2) * drafts
    lines = -(-lines // 8) * 8
    slots, cosine, sine = prepare(
        sizes, owned, adapter_ids, adapter_slots, cache_lengths, (lines, head_size), w_out
    )
    packed = -(-2 * blocks * drafts // 16) * 16
    shrink_in = jnp.transpose(shrink_qkv, (0, 2, 1)).reshape(-1, features)
    rows, rank_part = call(
        functools.partial(rank_kernel, sizes, owned),
        [shape((count, features)), shape((blocks * groups, packed, lanes))],
        [VMEM] * (blocks + 2),
        [pltpu.VMEM((count, features), jnp.float32)],
        2 * count * shrink_qkv.size,
        2 * shrink_qkv.size + 4 * count * features,
    )(*pieces, shrink_in, slots)
    ranks = exchange(rank_part)
    total = stream(rows, w_query, 8, [w_key, w_value], [w_out] * 3)
    cols = total.shape[1]
    head_cols = w_query.shape[1]
    query_lines = head_cols // head_size * drafts
    sent = call(
        functools.partial(grow_kernel, sizes, width),
        shape((blocks * groups, lines, head_size)),
        [VMEM] * 6 + [HBM] * 2,
        [pltpu.VMEM((blocks * groups * lines, head_size), jnp.float32)],
        limit=40 * MIB,
    )(
        total,
        slots,
        ranks,
        *[grow.reshape(owned * width, -1) for grow in (grow_query, grow_key, grow_value)],
        *[w_out] * 2,
    )
    mixed = call(
        functools.partial(attend_kernel, sizes),
        shape((blocks * groups, query_lines, head_size)),
        [VMEM] * 3 + [pl.BlockSpec(memory_space=pltpu.SMEM)] + [VMEM] * 2,
        [pltpu.VMEM((2 * blocks, 128, head_size), jnp.float32)],
    )(exchange(sent), cache_keys, cache_values, cache_lengths, cosine, sine)
    gathered = exchange(mixed)
    held = -(-packing(count, width, 128)[1] // 16) * 16
    out_rows, out_part = call(
        functools.partial(out_rank_kernel, sizes, owned),
        [shape((count, head_cols)), shape((blocks * groups, held, 128))],
        [VMEM] * 3,
        [pltpu.VMEM((blocks * groups * query_lines, head_size), jnp.float32)],
    )(gathered, jnp.transpose(shrink_out, (0, 2, 1)).reshape(-1, head_cols), slots)
    out_ranks = exchange(out_part)
    out_total = stream(out_rows, w_out, 8)
    out_cols = out_total.shape[1]
    leaving = call(
        functools.partial(out_grow_kernel, sizes, width),
        [shape((drafts, groups, out_cols))] * blocks,
        [VMEM] * 4,
        [],
        2 * count * owned * width * out_cols,
        8 * count * out_cols + 2 * owned * width * out_cols,
    )(out_total, slots, out_ranks, grow_out.reshape(owned * width, -1))
    result = leaving[0].astype(jnp.float32)
    for shift in range(1, blocks):
        result = result + over_tensor(leaving[shift], -shift).astype(jnp.float32)
    return jnp.transpose(result.astype(jnp.bfloat16), (1, 0, 2))


def rotate(vectors, positions):
    half_size = vectors.shape[-1] // 2
    frequency = rope_base ** (-2.0 * jnp.arange(half_size, dtype=jnp.float32) / vectors.shape[-1])
    angles = positions[:, None, None] * frequency
    cosine = jnp.cos(angles)
    sine_value = jnp.sin(angles)
    first_half = vectors[..., :half_size]
    second = vectors[..., half_size:]
    return jnp.concatenate(
        [first_half * cosine - second * sine_value, second * cosine + first_half * sine_value], -1
    )


def to_growers(partial, splits):
    total = None
    for shift in range(splits):
        route = [
            (t * splits + g, ((g + shift) % splits) * splits + t)
            for t in range(splits)
            for g in range(splits)
        ]
        got = lax.ppermute(partial, EVERY, route).astype(jnp.float32)
        total = got if total is None else total + got
    return total


def to_out_growers(partial, splits):
    total = None
    for shift in range(splits):
        route = [
            (t * splits + g, g * splits + (t + shift) % splits)
            for t in range(splits)
            for g in range(splits)
        ]
        got = lax.ppermute(partial, EVERY, route).astype(jnp.float32)
        total = got if total is None else total + got
    return total


def slot_table(adapter_ids, adapter_slots):
    matches = adapter_ids[:, None] == jnp.arange(adapter_slots.shape[0], dtype=jnp.int32)[None, :]
    return jnp.sum(jnp.where(matches, adapter_slots[None, :], 0), axis=1)


def attend(query_heads, key_new, value_new, cache_keys, cache_values, length):
    drafts, head_count, head_size = query_heads.shape
    kv_heads, cache_size, _ = cache_keys.shape
    positions = (length + jnp.arange(drafts, dtype=jnp.int32)).astype(jnp.float32)
    query_rot = rotate(query_heads.astype(jnp.float32), positions).astype(jnp.bfloat16)
    key_rot = rotate(key_new.astype(jnp.float32), positions).astype(jnp.bfloat16)
    grouped = query_rot.reshape(drafts, kv_heads, head_count // kv_heads, head_size)
    score_scale = 1.0 / math.sqrt(head_size)
    cached = (
        jnp.einsum("skgd,kld->skgl", grouped, cache_keys, preferred_element_type=jnp.float32)
        * score_scale
    )
    fresh_scores = (
        jnp.einsum("skgd,tkd->skgt", grouped, key_rot, preferred_element_type=jnp.float32)
        * score_scale
    )
    cache_mask = jnp.arange(cache_size, dtype=jnp.int32) < length
    draft_mask = jnp.arange(drafts)[None, :] <= jnp.arange(drafts)[:, None]
    cached = jnp.where(cache_mask[None, None, None, :], cached, -jnp.inf)
    fresh_scores = jnp.where(draft_mask[:, None, None, :], fresh_scores, -jnp.inf)
    row_peak = jnp.maximum(jnp.max(cached, -1), jnp.max(fresh_scores, -1))
    cached_exp = jnp.exp(cached - row_peak[..., None])
    fresh_exp = jnp.exp(fresh_scores - row_peak[..., None])
    denominator = jnp.sum(cached_exp, -1) + jnp.sum(fresh_exp, -1)
    cached_prob = (cached_exp / denominator[..., None]).astype(jnp.bfloat16)
    fresh_prob = (fresh_exp / denominator[..., None]).astype(jnp.bfloat16)
    mixed = jnp.einsum(
        "skgl,kld->skgd", cached_prob, cache_values, preferred_element_type=jnp.float32
    )
    mixed = mixed + jnp.einsum(
        "skgt,tkd->skgd", fresh_prob, value_new, preferred_element_type=jnp.float32
    )
    return mixed.astype(jnp.bfloat16)


def by_row(
    tokens,
    w_query,
    w_key,
    w_value,
    w_out,
    shrink_qkv,
    grow_query,
    grow_key,
    grow_value,
    shrink_out,
    grow_out,
    cache_keys,
    cache_values,
    cache_lengths,
    adapter_ids,
    adapter_slots,
):
    splits = lax.axis_size("tensor")
    groups = lax.axis_size(("dp", "pipe"))
    tensor_index = lax.axis_index("tensor")
    group_index = lax.axis_index(("dp", "pipe"))
    local_rows, drafts, feature_width = tokens.shape
    per_owner = shrink_qkv.shape[0]
    rank_size = grow_out.shape[1]
    query_cols = w_query.shape[1]
    key_cols = w_key.shape[1]
    kv_heads = cache_keys.shape[1]
    head_size = cache_keys.shape[3]
    rows = splits * groups
    row_slots = jnp.repeat(slot_table(adapter_ids, adapter_slots), drafts)
    within = jnp.arange(per_owner, dtype=jnp.int32)[None, :]
    width_hot = (row_slots[:, None] == within + tensor_index * per_owner)[:, :, None]
    column_hot = (row_slots[:, None] == within + group_index * per_owner)[:, :, None]

    def spread_ranks(ranks, hot):
        return jnp.where(hot, ranks[:, None, :], 0.0).reshape(rows * drafts, -1).astype(jnp.bfloat16)

    flat_tokens = lax.all_gather(tokens, "tensor", axis=0, tiled=True).reshape(
        rows * drafts, feature_width
    )
    rank_part = jnp.einsum(
        "nd,adr->nar", flat_tokens, shrink_qkv, preferred_element_type=jnp.float32
    )
    rank_part = jnp.sum(jnp.where(width_hot, rank_part, 0.0), 1)
    rank_all = to_growers(rank_part.astype(jnp.bfloat16), splits)

    def grown(index, grow):
        ranks = spread_ranks(rank_all[:, index * rank_size : (index + 1) * rank_size], column_hot)
        return jnp.dot(
            ranks, grow.reshape(per_owner * rank_size, -1), preferred_element_type=jnp.float32
        )

    bases = [
        jnp.dot(flat_tokens, weight, preferred_element_type=jnp.float32)
        for weight in (w_query, w_key, w_value)
    ]

    def product(index, grow):
        return (bases[index] + grown(index, grow)).astype(jnp.bfloat16).reshape(rows, drafts, -1)

    partial = jnp.concatenate(
        [
            product(0, grow_query),
            product(1, grow_key),
            product(2, grow_value),
        ],
        2,
    )
    arrived = lax.all_to_all(partial, EVERY, split_axis=0, concat_axis=0, tiled=True)
    joined = jnp.sum(
        arrived.reshape(splits, groups, drafts, -1).astype(jnp.float32), 1
    ).astype(jnp.bfloat16)
    joined = jnp.transpose(joined, (1, 0, 2))
    query_heads = joined[:, :, :query_cols].reshape(drafts, -1, head_size)
    key_new = joined[:, :, query_cols : query_cols + key_cols].reshape(drafts, kv_heads, head_size)
    value_new = joined[:, :, query_cols + key_cols :].reshape(drafts, kv_heads, head_size)
    mixed = attend(
        query_heads, key_new, value_new, cache_keys[0], cache_values[0], cache_lengths[0]
    )
    mixed = jnp.transpose(mixed.reshape(drafts, splits, -1), (1, 0, 2))
    outgoing = jnp.repeat(mixed, groups, axis=0)
    flat_heads = lax.all_to_all(
        outgoing, EVERY, split_axis=0, concat_axis=0, tiled=True
    ).reshape(rows * drafts, -1)
    out_part = jnp.einsum(
        "nw,awr->nar", flat_heads, shrink_out, preferred_element_type=jnp.float32
    )
    out_part = jnp.sum(jnp.where(column_hot, out_part, 0.0), 1)
    out_rank = to_out_growers(out_part.astype(jnp.bfloat16), splits)
    out = jnp.dot(flat_heads, w_out, preferred_element_type=jnp.float32)
    out = out + jnp.dot(
        spread_ranks(out_rank, width_hot),
        grow_out.reshape(per_owner * rank_size, -1),
        preferred_element_type=jnp.float32,
    )
    blocks = lax.all_to_all(
        out.astype(jnp.bfloat16).reshape(splits, local_rows, drafts, feature_width),
        "tensor",
        split_axis=0,
        concat_axis=0,
        tiled=True,
    )
    return jnp.sum(blocks.astype(jnp.float32), 0).astype(jnp.bfloat16)


def local(*arrays):
    heads = arrays[11].shape[1]
    if heads == lax.axis_size("tensor") == lax.axis_size(GROUP):
        return by_kernels(*arrays)
    return by_row(*arrays)


def solution(mesh):
    placed = (
        P(("parts", "tensor"), None, ("dp", "pipe")),
        P(("dp", "pipe"), "tensor"),
        P(("dp", "pipe"), "tensor"),
        P(("dp", "pipe"), "tensor"),
        P("tensor", ("dp", "pipe")),
        P("tensor", ("dp", "pipe"), None),
        P(("dp", "pipe"), None, "tensor"),
        P(("dp", "pipe"), None, "tensor"),
        P(("dp", "pipe"), None, "tensor"),
        P(("dp", "pipe"), "tensor", None),
        P("tensor", None, ("dp", "pipe")),
        P(("parts", "tensor", "dp", "pipe"), None, None, None),
        P(("parts", "tensor", "dp", "pipe"), None, None, None),
        P(("parts", "tensor", "dp", "pipe")),
        P(),
        P(),
    )
    return jax.shard_map(
        local,
        mesh=mesh,
        in_specs=placed,
        out_specs=P(("parts", "tensor"), None, ("dp", "pipe")),
        check_vma=False,
    )
```

```python
import functools
import math

import jax
import jax.numpy as jnp
import numpy as np
from jax import lax
from jax.experimental import pallas as pl
from jax.experimental.pallas import tpu as pltpu
from jax.sharding import PartitionSpec as P

rope_base = 500000.0
EVERY = ("tensor", "dp", "pipe")
GROUP = ("dp", "pipe")
VMEM = pl.BlockSpec(memory_space=pltpu.VMEM)
HBM = pl.BlockSpec(memory_space=pltpu.HBM)
MIB = 1 << 20


def dot(left, right):
    return jnp.dot(left, right, preferred_element_type=jnp.float32)


def dot_nt(left, right):
    return lax.dot_general(
        left, right, (((1,), (1,)), ((), ())), preferred_element_type=jnp.float32
    )


def iota(shape, axis):
    return lax.broadcasted_iota(jnp.int32, shape, axis)


def call(kernel, outs, ins, scratch=(), flops=0, moved=0, limit=24 * MIB):
    return pl.pallas_call(
        kernel,
        out_shape=outs,
        in_specs=ins,
        out_specs=jax.tree.map(lambda _: VMEM, outs),
        scratch_shapes=list(scratch),
        cost_estimate=pl.CostEstimate(flops=flops, bytes_accessed=moved, transcendentals=0),
        compiler_params=pltpu.CompilerParams(vmem_limit_bytes=limit),
    )


def shape(dims, kind=jnp.bfloat16):
    return jax.ShapeDtypeStruct(tuple(dims), kind)


def over(value, size):
    return value >> (size.bit_length() - 1) if size & (size - 1) == 0 else lax.div(value, size)


def rest_of(value, size):
    return value & (size - 1) if size & (size - 1) == 0 else lax.rem(value, size)


def as_gathered(sizes, group, block, draft):
    groups, blocks, drafts = sizes
    return (block * drafts + draft) * groups + group


def by_draft(sizes, group, block, draft):
    groups, blocks, drafts = sizes
    return (draft * blocks + block) * groups + group


def parts_of(order, sizes, index):
    groups, blocks, drafts = sizes
    group, left = rest_of(index, groups), over(index, groups)
    if order is as_gathered:
        return group, over(left, drafts), rest_of(left, drafts)
    return group, rest_of(left, blocks), over(left, blocks)


def turned(block, blocks):
    return rest_of(lax.axis_index("tensor") - block + blocks, blocks)


def reorder(sizes, after, before):
    groups, blocks, drafts = sizes
    rows = groups * blocks * drafts
    group, block, draft = parts_of(after, sizes, iota((rows, rows), 0))
    wanted = before(sizes, group, turned(block, blocks), draft)
    return jnp.where(wanted == iota((rows, rows), 1), 1.0, 0.0).astype(jnp.bfloat16)


def group_of():
    return lax.axis_index("dp") * lax.axis_size("pipe") + lax.axis_index("pipe")


def rank_kernel(sizes, owned, *refs):
    groups, blocks, drafts = sizes
    pieces = refs[:blocks]
    shrink_ref, slots_ref = refs[blocks : blocks + 2]
    rows_ref, rank_ref, wide = refs[-3:]
    for block in range(blocks):
        for draft in range(drafts):
            start = (block * drafts + draft) * groups
            wide[start : start + groups, :] = pieces[block][draft].astype(jnp.float32)
    rows = wide[...].astype(jnp.bfloat16)
    rows_ref[...] = rows
    place = slots_ref[:, 0:1] - lax.axis_index("tensor") * owned
    ranks = owned_ranks(
        rows, shrink_ref[...], place, shrink_ref.shape[0] // owned, rank_ref.shape[2]
    )
    put = (rank_ref.shape[1], rows.shape[0])
    draft = parts_of(as_gathered, sizes, iota((rows.shape[0], put[0]), 0))[2]
    line = slots_ref[:, 2:3] * drafts + draft
    put = jnp.where(line == iota((rows.shape[0], put[0]), 1), 1.0, 0.0).astype(jnp.bfloat16)
    ranks = lax.dot_general(
        put, ranks, (((0,), (0,)), ((), ())), preferred_element_type=jnp.float32
    ).astype(jnp.bfloat16)
    for target in range(rank_ref.shape[0]):
        rank_ref[target] = ranks


def owned_ranks(rows, shrink, place, width, lanes):
    ranks = dot_nt(rows, shrink)
    kept = jnp.where(over(iota(ranks.shape, 1), width) == place, ranks, 0.0).astype(jnp.bfloat16)
    fold = (ranks.shape[1], lanes)
    fold = rest_of(iota(fold, 0), width) == iota(fold, 1)
    return dot(kept, jnp.where(fold, 1.0, 0.0).astype(jnp.bfloat16)).astype(jnp.bfloat16)


def spread_ranks(ranks, place, width, owned, parts):
    span = owned * width
    row = iota((ranks.shape[1], parts * span), 0)
    column = iota((ranks.shape[1], parts * span), 1)
    tile = (over(row, width) == over(column, span)) & (
        rest_of(row, width) == rest_of(column, width)
    )
    wide = dot(ranks, jnp.where(tile, 1.0, 0.0).astype(jnp.bfloat16))
    slot = over(rest_of(iota(wide.shape, 1), span), width)
    return jnp.where(slot == place, wide, 0.0).astype(jnp.bfloat16)


def stream_kernel(chunks, small, rows_ref, weight_ref, *refs):
    total_ref, buffer, sems = refs[-3:]
    depth = rows_ref.shape[1] // chunks
    width = weight_ref.shape[1]

    def copy(chunk):
        part = pl.ds(chunk * depth, depth)
        return pltpu.make_async_copy(weight_ref.at[part], buffer.at[part], sems.at[chunk])

    for chunk in range(chunks):
        copy(chunk).start()
    start = width
    for other in refs[:small]:
        total_ref[:, start : start + other.shape[1]] = dot(rows_ref[...], other[...])
        start += other.shape[1]
    for chunk in range(chunks):
        copy(chunk).wait()
        product = dot(
            rows_ref[:, chunk * depth : (chunk + 1) * depth],
            buffer[chunk * depth : (chunk + 1) * depth, :],
        )
        if chunk:
            total_ref[:, 0:width] += product
        else:
            total_ref[:, 0:width] = product


def stream(rows, weight, chunks, small=(), later=()):
    width = weight.shape[1] + sum(other.shape[1] for other in small)
    return call(
        functools.partial(stream_kernel, chunks, len(small)),
        shape((rows.shape[0], width), jnp.float32),
        [VMEM, HBM] + [VMEM] * len(small) + [HBM] * len(later),
        [pltpu.VMEM(weight.shape, weight.dtype), pltpu.SemaphoreType.DMA((chunks,))],
        limit=40 * MIB,
    )(rows, weight, *small, *later)


def prepare_kernel(sizes, owned, ids_ref, pool_ref, length_ref, _, *outs):
    slots_ref, cosine_ref, sine_ref = outs
    groups, blocks, drafts = sizes
    width = cosine_ref.shape[1]
    lane = iota(cosine_ref.shape, 1)
    half = (lane & (width // 2 - 1)).astype(jnp.float32)
    positions = (lax.rem(iota(cosine_ref.shape, 0), drafts) + length_ref[0]).astype(jnp.float32)
    angles = positions * jnp.exp(half * (-2.0 * math.log(rope_base) / width))
    cosine_ref[...] = jnp.cos(angles)
    sine_ref[...] = jnp.sin(angles) * jnp.where(lane < width // 2, -1.0, 1.0)
    index = iota(slots_ref.shape, 0)
    column = iota(slots_ref.shape, 1)
    near = parts_of(as_gathered, sizes, index)
    far = parts_of(by_draft, sizes, index)
    row_group = jnp.where(column == 1, far[0], near[0])
    row_block = jnp.where(column == 1, far[1], turned(near[1], blocks))
    place = row_block * groups + row_group
    slots = jnp.zeros(slots_ref.shape, jnp.int32)
    sent, taken = 0, 0
    for row in range(blocks * groups):
        slot = pool_ref[ids_ref[row]]
        owner = over(slot, owned)
        sends = jnp.where(owner == lax.axis_index("tensor"), 1, 0)
        takes = jnp.where(owner == group_of(), 1, 0)
        line = jnp.where(column == 2, sent - 64 * (1 - sends), taken - 64 * (1 - takes))
        slots = jnp.where(place == row, jnp.where(column < 2, slot, line), slots)
        sent, taken = sent + sends, taken + takes
    slots_ref[...] = slots


def prepare(sizes, owned, ids, pool, lengths, table, later):
    groups, blocks, drafts = sizes
    smem = pl.BlockSpec(memory_space=pltpu.SMEM)
    table = shape(table, jnp.float32)
    return call(
        functools.partial(prepare_kernel, sizes, owned),
        [shape((groups * blocks * drafts, 128), jnp.int32), table, table],
        [smem, smem, smem, HBM],
        limit=40 * MIB,
    )(ids, pool, lengths, later)


def grow_kernel(sizes, width, total_ref, rows_ref, value_ref, slots_ref, ranks_ref, *refs):
    groups, blocks, drafts = sizes
    grows, (out_ref, held) = refs[:3], refs[-2:]
    group = group_of()
    requests = groups * blocks
    lines = out_ref.shape[1]
    held[...] = jnp.zeros(held.shape, jnp.float32)
    owned = grows[0].shape[0] // width
    ranks = ranks_ref[group * groups].astype(jnp.float32)
    for other in range(1, groups):
        ranks = ranks + ranks_ref[group * groups + other].astype(jnp.float32)
    get = (total_ref.shape[0], ranks.shape[0])
    draft = parts_of(as_gathered, sizes, iota(get, 0))[2]
    get = slots_ref[:, 3:4] * drafts + draft == iota(get, 1)
    ranks = dot(jnp.where(get, 1.0, 0.0).astype(jnp.bfloat16), ranks.astype(jnp.bfloat16))
    place = slots_ref[:, 0:1] - group * owned
    wide = spread_ranks(ranks.astype(jnp.bfloat16), place, width, owned, len(grows))
    arranged = reorder(sizes, by_draft, as_gathered)
    start, column = 0, 0
    for index, grow in enumerate(grows):
        deep, cols = grow.shape
        if column < total_ref.shape[1]:
            full = total_ref[:, column : column + cols]
        else:
            full = dot(rows_ref[...], value_ref[...])
        full = full + dot(wide[:, index * deep : (index + 1) * deep], grow[...])
        column += cols
        full = dot(arranged, full.astype(jnp.bfloat16))
        for head in range(cols // 128):
            for draft in range(drafts):
                held[pl.ds(start + draft, requests, stride=lines), :] = full[
                    draft * requests : (draft + 1) * requests, head * 128 : (head + 1) * 128
                ]
            start += drafts
    for row in range(requests):
        out_ref[row] = held[row * lines : (row + 1) * lines, :].astype(jnp.bfloat16)


def attend_kernel(
    sizes, arrived_ref, keys_ref, values_ref, length_ref, cosine_ref, sine_ref, out_ref, *scratch
):
    groups, blocks, drafts = sizes
    (fresh_s,) = scratch
    cache_size, head_size = keys_ref.shape[2:]
    count = out_ref.shape[1]
    scale = 1.0 / math.sqrt(head_size)
    fresh_s[...] = jnp.zeros(fresh_s.shape, jnp.float32)
    for block in range(blocks):
        joined = arrived_ref[block * groups].astype(jnp.float32)
        for other in range(1, groups):
            joined = joined + arrived_ref[block * groups + other].astype(jnp.float32)
        joined = joined.astype(jnp.bfloat16).astype(jnp.float32)
        rotated = joined * cosine_ref[...] + pltpu.roll(joined, head_size // 2, 1) * sine_ref[...]
        fresh_s[2 * block, 0:drafts, :] = rotated[count : count + drafts]
        fresh_s[2 * block + 1, 0:drafts, :] = joined[count + drafts : count + 2 * drafts]
        query = rotated[0:count].astype(jnp.bfloat16)
        old = dot_nt(query, keys_ref[0, block]) * scale
        new = dot_nt(query, fresh_s[2 * block].astype(jnp.bfloat16)) * scale
        old = jnp.where(iota(old.shape, 1) < length_ref[0], old, -jnp.inf)
        seen = iota(new.shape, 1) <= lax.rem(iota(new.shape, 0), drafts)
        new = jnp.where(seen, new, -jnp.inf)
        peak = jnp.maximum(jnp.max(old, 1, keepdims=True), jnp.max(new, 1, keepdims=True))
        old = jnp.exp(old - peak)
        new = jnp.exp(new - peak)
        below = jnp.sum(old, 1, keepdims=True) + jnp.sum(new, 1, keepdims=True)
        mixed = dot((old / below).astype(jnp.bfloat16), values_ref[0, block]) + dot(
            (new / below).astype(jnp.bfloat16), fresh_s[2 * block + 1].astype(jnp.bfloat16)
        )
        mixed = mixed.astype(jnp.bfloat16)
        for target in range(groups):
            out_ref[block * groups + target] = mixed


def packing(rows, width, lanes):
    parts = lanes // width
    return parts, rows // parts


def out_rank_kernel(sizes, owned, got_ref, shrink_ref, slots_ref, rows_ref, rank_ref, wide):
    drafts = sizes[2]
    requests, lines, head_size = got_ref.shape
    for row in range(requests):
        wide[row * lines : (row + 1) * lines, :] = got_ref[row].astype(jnp.float32)
    for head in range(lines // drafts):
        for draft in range(drafts):
            rows_ref[
                draft * requests : (draft + 1) * requests,
                head * head_size : (head + 1) * head_size,
            ] = wide[pl.ds(head * drafts + draft, requests, stride=lines), :].astype(jnp.bfloat16)
    rows = rows_ref[...]
    place = slots_ref[:, 1:2] - group_of() * owned
    width = shrink_ref.shape[0] // owned
    _, held, lanes = rank_ref.shape
    parts, span = packing(rows.shape[0], width, lanes)
    ranks = dot_nt(rows, shrink_ref[...])
    kept = jnp.where(over(iota(ranks.shape, 1), width) == place, ranks, 0.0).astype(jnp.bfloat16)
    fold = (ranks.shape[1], lanes)
    fold = rest_of(iota(fold, 0), width) == rest_of(iota(fold, 1), width)
    ranks = dot(kept, jnp.where(fold, 1.0, 0.0).astype(jnp.bfloat16))
    mine = over(iota(ranks.shape, 1), width) == over(iota(ranks.shape, 0), span)
    ranks = jnp.where(mine, ranks, 0.0).astype(jnp.bfloat16)
    put = (held, rows.shape[0])
    put = iota(put, 0) == rest_of(iota(put, 1), span)
    ranks = dot(jnp.where(put, 1.0, 0.0).astype(jnp.bfloat16), ranks).astype(jnp.bfloat16)
    for target in range(rank_ref.shape[0]):
        rank_ref[target] = ranks


def out_grow_kernel(sizes, width, total_ref, slots_ref, ranks_ref, grow_ref, *outs):
    groups, blocks, drafts = sizes
    owned = grow_ref.shape[0] // width
    me = lax.axis_index("tensor")
    ranks = ranks_ref[me].astype(jnp.float32)
    for source in range(1, blocks):
        ranks = ranks + ranks_ref[source * groups + me].astype(jnp.float32)
    count = total_ref.shape[0]
    held, lanes = ranks.shape
    parts, span = packing(count, width, lanes)
    put = rest_of(iota((count, held), 0), span) == iota((count, held), 1)
    ranks = dot(jnp.where(put, 1.0, 0.0).astype(jnp.bfloat16), ranks.astype(jnp.bfloat16))
    mine = over(iota(ranks.shape, 1), width) == over(iota(ranks.shape, 0), span)
    ranks = jnp.where(mine, ranks, 0.0).astype(jnp.bfloat16)
    tile = (lanes, owned * width)
    tile = rest_of(iota(tile, 0), width) == rest_of(iota(tile, 1), width)
    ranks = dot(ranks, jnp.where(tile, 1.0, 0.0).astype(jnp.bfloat16))
    place = slots_ref[:, 1:2] - me * owned
    wide = jnp.where(over(iota(ranks.shape, 1), width) == place, ranks, 0.0).astype(jnp.bfloat16)
    full = (total_ref[...] + dot(wide, grow_ref[...])).astype(jnp.bfloat16)
    full = dot(reorder(sizes, as_gathered, by_draft), full).astype(jnp.bfloat16)
    for block in range(blocks):
        for draft in range(drafts):
            start = (block * drafts + draft) * groups
            outs[block][draft] = full[start : start + groups]


def by_kernels(
    tokens,
    w_query,
    w_key,
    w_value,
    w_out,
    shrink_qkv,
    grow_query,
    grow_key,
    grow_value,
    shrink_out,
    grow_out,
    cache_keys,
    cache_values,
    cache_lengths,
    adapter_ids,
    adapter_slots,
):
    blocks = lax.axis_size("tensor")
    groups = lax.axis_size(GROUP)
    _, drafts, features = tokens.shape
    sizes = (groups, blocks, drafts)
    owned = shrink_qkv.shape[0]
    width = grow_out.shape[1]
    head_size = cache_keys.shape[3]
    span = blocks * drafts
    count = groups * span
    lanes = -(-shrink_qkv.shape[2] // 128) * 128

    def over_tensor(value, shift):
        route = [(t, (t + shift) % blocks) for t in range(blocks)]
        return lax.ppermute(value, "tensor", route)

    def exchange(value):
        return lax.all_to_all(value, EVERY, split_axis=0, concat_axis=0, tiled=True)

    mine = jnp.transpose(tokens, (1, 0, 2))
    pieces = [mine] + [over_tensor(mine, shift) for shift in range(1, blocks)]

    lines = (w_query.shape[1] // head_size + 2) * drafts
    lines = -(-lines // 8) * 8
    slots, cosine, sine = prepare(
        sizes, owned, adapter_ids, adapter_slots, cache_lengths, (lines, head_size), w_out
    )
    packed = -(-2 * blocks * drafts // 16) * 16
    shrink_in = jnp.transpose(shrink_qkv, (0, 2, 1)).reshape(-1, features)
    rows, rank_part = call(
        functools.partial(rank_kernel, sizes, owned),
        [shape((count, features)), shape((blocks * groups, packed, lanes))],
        [VMEM] * (blocks + 2),
        [pltpu.VMEM((count, features), jnp.float32)],
        2 * count * shrink_qkv.size,
        2 * shrink_qkv.size + 4 * count * features,
    )(*pieces, shrink_in, slots)
    ranks = exchange(rank_part)
    total = stream(rows, w_query, 8, [w_key], [w_out] * 3)
    cols = total.shape[1] + w_value.shape[1]
    head_cols = w_query.shape[1]
    query_lines = head_cols // head_size * drafts
    sent = call(
        functools.partial(grow_kernel, sizes, width),
        shape((blocks * groups, lines, head_size)),
        [VMEM] * 8 + [HBM] * 2,
        [pltpu.VMEM((blocks * groups * lines, head_size), jnp.float32)],
        limit=40 * MIB,
    )(
        total,
        rows,
        w_value,
        slots,
        ranks,
        *[grow.reshape(owned * width, -1) for grow in (grow_query, grow_key, grow_value)],
        *[w_out] * 2,
    )
    mixed = call(
        functools.partial(attend_kernel, sizes),
        shape((blocks * groups, query_lines, head_size)),
        [VMEM] * 3 + [pl.BlockSpec(memory_space=pltpu.SMEM)] + [VMEM] * 2,
        [pltpu.VMEM((2 * blocks, 128, head_size), jnp.float32)],
    )(exchange(sent), cache_keys, cache_values, cache_lengths, cosine, sine)
    gathered = exchange(mixed)
    held = -(-packing(count, width, 128)[1] // 16) * 16
    out_rows, out_part = call(
        functools.partial(out_rank_kernel, sizes, owned),
        [shape((count, head_cols)), shape((blocks * groups, held, 128))],
        [VMEM] * 3,
        [pltpu.VMEM((blocks * groups * query_lines, head_size), jnp.float32)],
    )(gathered, jnp.transpose(shrink_out, (0, 2, 1)).reshape(-1, head_cols), slots)
    out_ranks = exchange(out_part)
    out_total = stream(out_rows, w_out, 8)
    out_cols = out_total.shape[1]
    leaving = call(
        functools.partial(out_grow_kernel, sizes, width),
        [shape((drafts, groups, out_cols))] * blocks,
        [VMEM] * 4,
        [],
        2 * count * owned * width * out_cols,
        8 * count * out_cols + 2 * owned * width * out_cols,
    )(out_total, slots, out_ranks, grow_out.reshape(owned * width, -1))
    result = leaving[0].astype(jnp.float32)
    for shift in range(1, blocks):
        result = result + over_tensor(leaving[shift], -shift).astype(jnp.float32)
    return jnp.transpose(result.astype(jnp.bfloat16), (1, 0, 2))


def rotate(vectors, positions):
    half_size = vectors.shape[-1] // 2
    frequency = rope_base ** (-2.0 * jnp.arange(half_size, dtype=jnp.float32) / vectors.shape[-1])
    angles = positions[:, None, None] * frequency
    cosine = jnp.cos(angles)
    sine_value = jnp.sin(angles)
    first_half = vectors[..., :half_size]
    second = vectors[..., half_size:]
    return jnp.concatenate(
        [first_half * cosine - second * sine_value, second * cosine + first_half * sine_value], -1
    )


def to_growers(partial, splits):
    total = None
    for shift in range(splits):
        route = [
            (t * splits + g, ((g + shift) % splits) * splits + t)
            for t in range(splits)
            for g in range(splits)
        ]
        got = lax.ppermute(partial, EVERY, route).astype(jnp.float32)
        total = got if total is None else total + got
    return total


def to_out_growers(partial, splits):
    total = None
    for shift in range(splits):
        route = [
            (t * splits + g, g * splits + (t + shift) % splits)
            for t in range(splits)
            for g in range(splits)
        ]
        got = lax.ppermute(partial, EVERY, route).astype(jnp.float32)
        total = got if total is None else total + got
    return total


def slot_table(adapter_ids, adapter_slots):
    matches = adapter_ids[:, None] == jnp.arange(adapter_slots.shape[0], dtype=jnp.int32)[None, :]
    return jnp.sum(jnp.where(matches, adapter_slots[None, :], 0), axis=1)


def attend(query_heads, key_new, value_new, cache_keys, cache_values, length):
    drafts, head_count, head_size = query_heads.shape
    kv_heads, cache_size, _ = cache_keys.shape
    positions = (length + jnp.arange(drafts, dtype=jnp.int32)).astype(jnp.float32)
    query_rot = rotate(query_heads.astype(jnp.float32), positions).astype(jnp.bfloat16)
    key_rot = rotate(key_new.astype(jnp.float32), positions).astype(jnp.bfloat16)
    grouped = query_rot.reshape(drafts, kv_heads, head_count // kv_heads, head_size)
    score_scale = 1.0 / math.sqrt(head_size)
    cached = (
        jnp.einsum("skgd,kld->skgl", grouped, cache_keys, preferred_element_type=jnp.float32)
        * score_scale
    )
    fresh_scores = (
        jnp.einsum("skgd,tkd->skgt", grouped, key_rot, preferred_element_type=jnp.float32)
        * score_scale
    )
    cache_mask = jnp.arange(cache_size, dtype=jnp.int32) < length
    draft_mask = jnp.arange(drafts)[None, :] <= jnp.arange(drafts)[:, None]
    cached = jnp.where(cache_mask[None, None, None, :], cached, -jnp.inf)
    fresh_scores = jnp.where(draft_mask[:, None, None, :], fresh_scores, -jnp.inf)
    row_peak = jnp.maximum(jnp.max(cached, -1), jnp.max(fresh_scores, -1))
    cached_exp = jnp.exp(cached - row_peak[..., None])
    fresh_exp = jnp.exp(fresh_scores - row_peak[..., None])
    denominator = jnp.sum(cached_exp, -1) + jnp.sum(fresh_exp, -1)
    cached_prob = (cached_exp / denominator[..., None]).astype(jnp.bfloat16)
    fresh_prob = (fresh_exp / denominator[..., None]).astype(jnp.bfloat16)
    mixed = jnp.einsum(
        "skgl,kld->skgd", cached_prob, cache_values, preferred_element_type=jnp.float32
    )
    mixed = mixed + jnp.einsum(
        "skgt,tkd->skgd", fresh_prob, value_new, preferred_element_type=jnp.float32
    )
    return mixed.astype(jnp.bfloat16)


def by_row(
    tokens,
    w_query,
    w_key,
    w_value,
    w_out,
    shrink_qkv,
    grow_query,
    grow_key,
    grow_value,
    shrink_out,
    grow_out,
    cache_keys,
    cache_values,
    cache_lengths,
    adapter_ids,
    adapter_slots,
):
    splits = lax.axis_size("tensor")
    groups = lax.axis_size(("dp", "pipe"))
    tensor_index = lax.axis_index("tensor")
    group_index = lax.axis_index(("dp", "pipe"))
    local_rows, drafts, feature_width = tokens.shape
    per_owner = shrink_qkv.shape[0]
    rank_size = grow_out.shape[1]
    query_cols = w_query.shape[1]
    key_cols = w_key.shape[1]
    kv_heads = cache_keys.shape[1]
    head_size = cache_keys.shape[3]
    rows = splits * groups
    row_slots = jnp.repeat(slot_table(adapter_ids, adapter_slots), drafts)
    within = jnp.arange(per_owner, dtype=jnp.int32)[None, :]
    width_hot = (row_slots[:, None] == within + tensor_index * per_owner)[:, :, None]
    column_hot = (row_slots[:, None] == within + group_index * per_owner)[:, :, None]

    def spread_ranks(ranks, hot):
        return jnp.where(hot, ranks[:, None, :], 0.0).reshape(rows * drafts, -1).astype(jnp.bfloat16)

    flat_tokens = lax.all_gather(tokens, "tensor", axis=0, tiled=True).reshape(
        rows * drafts, feature_width
    )
    rank_part = jnp.einsum(
        "nd,adr->nar", flat_tokens, shrink_qkv, preferred_element_type=jnp.float32
    )
    rank_part = jnp.sum(jnp.where(width_hot, rank_part, 0.0), 1)
    rank_all = to_growers(rank_part.astype(jnp.bfloat16), splits)

    def grown(index, grow):
        ranks = spread_ranks(rank_all[:, index * rank_size : (index + 1) * rank_size], column_hot)
        return jnp.dot(
            ranks, grow.reshape(per_owner * rank_size, -1), preferred_element_type=jnp.float32
        )

    bases = [
        jnp.dot(flat_tokens, weight, preferred_element_type=jnp.float32)
        for weight in (w_query, w_key, w_value)
    ]

    def product(index, grow):
        return (bases[index] + grown(index, grow)).astype(jnp.bfloat16).reshape(rows, drafts, -1)

    partial = jnp.concatenate(
        [
            product(0, grow_query),
            product(1, grow_key),
            product(2, grow_value),
        ],
        2,
    )
    arrived = lax.all_to_all(partial, EVERY, split_axis=0, concat_axis=0, tiled=True)
    joined = jnp.sum(
        arrived.reshape(splits, groups, drafts, -1).astype(jnp.float32), 1
    ).astype(jnp.bfloat16)
    joined = jnp.transpose(joined, (1, 0, 2))
    query_heads = joined[:, :, :query_cols].reshape(drafts, -1, head_size)
    key_new = joined[:, :, query_cols : query_cols + key_cols].reshape(drafts, kv_heads, head_size)
    value_new = joined[:, :, query_cols + key_cols :].reshape(drafts, kv_heads, head_size)
    mixed = attend(
        query_heads, key_new, value_new, cache_keys[0], cache_values[0], cache_lengths[0]
    )
    mixed = jnp.transpose(mixed.reshape(drafts, splits, -1), (1, 0, 2))
    outgoing = jnp.repeat(mixed, groups, axis=0)
    flat_heads = lax.all_to_all(
        outgoing, EVERY, split_axis=0, concat_axis=0, tiled=True
    ).reshape(rows * drafts, -1)
    out_part = jnp.einsum(
        "nw,awr->nar", flat_heads, shrink_out, preferred_element_type=jnp.float32
    )
    out_part = jnp.sum(jnp.where(column_hot, out_part, 0.0), 1)
    out_rank = to_out_growers(out_part.astype(jnp.bfloat16), splits)
    out = jnp.dot(flat_heads, w_out, preferred_element_type=jnp.float32)
    out = out + jnp.dot(
        spread_ranks(out_rank, width_hot),
        grow_out.reshape(per_owner * rank_size, -1),
        preferred_element_type=jnp.float32,
    )
    blocks = lax.all_to_all(
        out.astype(jnp.bfloat16).reshape(splits, local_rows, drafts, feature_width),
        "tensor",
        split_axis=0,
        concat_axis=0,
        tiled=True,
    )
    return jnp.sum(blocks.astype(jnp.float32), 0).astype(jnp.bfloat16)


def local(*arrays):
    heads = arrays[11].shape[1]
    if heads == lax.axis_size("tensor") == lax.axis_size(GROUP):
        return by_kernels(*arrays)
    return by_row(*arrays)


def solution(mesh):
    placed = (
        P(("parts", "tensor"), None, ("dp", "pipe")),
        P(("dp", "pipe"), "tensor"),
        P(("dp", "pipe"), "tensor"),
        P(("dp", "pipe"), "tensor"),
        P("tensor", ("dp", "pipe")),
        P("tensor", ("dp", "pipe"), None),
        P(("dp", "pipe"), None, "tensor"),
        P(("dp", "pipe"), None, "tensor"),
        P(("dp", "pipe"), None, "tensor"),
        P(("dp", "pipe"), "tensor", None),
        P("tensor", None, ("dp", "pipe")),
        P(("parts", "tensor", "dp", "pipe"), None, None, None),
        P(("parts", "tensor", "dp", "pipe"), None, None, None),
        P(("parts", "tensor", "dp", "pipe")),
        P(),
        P(),
    )
    return jax.shard_map(
        local,
        mesh=mesh,
        in_specs=placed,
        out_specs=P(("parts", "tensor"), None, ("dp", "pipe")),
        check_vma=False,
    )
```

```python
import functools
import math

import jax
import jax.numpy as jnp
import numpy as np
from jax import lax
from jax.experimental import pallas as pl
from jax.experimental.pallas import tpu as pltpu
from jax.sharding import PartitionSpec as P

rope_base = 500000.0
EVERY = ("tensor", "dp", "pipe")
GROUP = ("dp", "pipe")
VMEM = pl.BlockSpec(memory_space=pltpu.VMEM)
HBM = pl.BlockSpec(memory_space=pltpu.HBM)
MIB = 1 << 20


def dot(left, right):
    return jnp.dot(left, right, preferred_element_type=jnp.float32)


def dot_nt(left, right):
    return lax.dot_general(
        left, right, (((1,), (1,)), ((), ())), preferred_element_type=jnp.float32
    )


def iota(shape, axis):
    return lax.broadcasted_iota(jnp.int32, shape, axis)


def call(kernel, outs, ins, scratch=(), flops=0, moved=0, limit=24 * MIB):
    return pl.pallas_call(
        kernel,
        out_shape=outs,
        in_specs=ins,
        out_specs=jax.tree.map(lambda _: VMEM, outs),
        scratch_shapes=list(scratch),
        cost_estimate=pl.CostEstimate(flops=flops, bytes_accessed=moved, transcendentals=0),
        compiler_params=pltpu.CompilerParams(vmem_limit_bytes=limit),
    )


def shape(dims, kind=jnp.bfloat16):
    return jax.ShapeDtypeStruct(tuple(dims), kind)


def over(value, size):
    return value >> (size.bit_length() - 1) if size & (size - 1) == 0 else lax.div(value, size)


def rest_of(value, size):
    return value & (size - 1) if size & (size - 1) == 0 else lax.rem(value, size)


def as_gathered(sizes, group, block, draft):
    groups, blocks, drafts = sizes
    return (block * drafts + draft) * groups + group


def by_draft(sizes, group, block, draft):
    groups, blocks, drafts = sizes
    return (draft * blocks + block) * groups + group


def parts_of(order, sizes, index):
    groups, blocks, drafts = sizes
    group, left = rest_of(index, groups), over(index, groups)
    if order is as_gathered:
        return group, over(left, drafts), rest_of(left, drafts)
    return group, rest_of(left, blocks), over(left, blocks)


def turned(block, blocks):
    return rest_of(lax.axis_index("tensor") - block + blocks, blocks)


def reorder(sizes, after, before):
    groups, blocks, drafts = sizes
    rows = groups * blocks * drafts
    group, block, draft = parts_of(after, sizes, iota((rows, rows), 0))
    wanted = before(sizes, group, turned(block, blocks), draft)
    return jnp.where(wanted == iota((rows, rows), 1), 1.0, 0.0).astype(jnp.bfloat16)


def group_of():
    return lax.axis_index("dp") * lax.axis_size("pipe") + lax.axis_index("pipe")


def rank_kernel(sizes, owned, *refs):
    groups, blocks, drafts = sizes
    pieces = refs[:blocks]
    shrink_ref, slots_ref = refs[blocks : blocks + 2]
    rows_ref, rank_ref, wide = refs[-3:]
    for block in range(blocks):
        for draft in range(drafts):
            start = (block * drafts + draft) * groups
            wide[start : start + groups, :] = pieces[block][draft].astype(jnp.float32)
    rows = wide[...].astype(jnp.bfloat16)
    rows_ref[...] = rows
    place = slots_ref[:, 0:1] - lax.axis_index("tensor") * owned
    ranks = owned_ranks(
        rows, shrink_ref[...], place, shrink_ref.shape[0] // owned, rank_ref.shape[1]
    )
    put = (rank_ref.shape[0], rows.shape[0])
    draft = parts_of(as_gathered, sizes, iota((rows.shape[0], put[0]), 0))[2]
    line = slots_ref[:, 2:3] * drafts + draft
    put = jnp.where(line == iota((rows.shape[0], put[0]), 1), 1.0, 0.0).astype(jnp.bfloat16)
    ranks = lax.dot_general(
        put, ranks, (((0,), (0,)), ((), ())), preferred_element_type=jnp.float32
    )
    rank_ref[...] = ranks.astype(jnp.bfloat16)


def owned_ranks(rows, shrink, place, width, lanes):
    ranks = dot_nt(rows, shrink)
    kept = jnp.where(over(iota(ranks.shape, 1), width) == place, ranks, 0.0).astype(jnp.bfloat16)
    fold = (ranks.shape[1], lanes)
    fold = rest_of(iota(fold, 0), width) == iota(fold, 1)
    return dot(kept, jnp.where(fold, 1.0, 0.0).astype(jnp.bfloat16)).astype(jnp.bfloat16)


def spread_ranks(ranks, place, width, owned, parts):
    span = owned * width
    row = iota((ranks.shape[1], parts * span), 0)
    column = iota((ranks.shape[1], parts * span), 1)
    tile = (over(row, width) == over(column, span)) & (
        rest_of(row, width) == rest_of(column, width)
    )
    wide = dot(ranks, jnp.where(tile, 1.0, 0.0).astype(jnp.bfloat16))
    slot = over(rest_of(iota(wide.shape, 1), span), width)
    return jnp.where(slot == place, wide, 0.0).astype(jnp.bfloat16)


def product_kernel(rows_ref, *refs):
    *weights, total_ref = refs
    start = 0
    for weight in weights:
        width = weight.shape[1]
        step = width if width % 1024 else 1024
        for first in range(0, width, step):
            total_ref[:, start : start + step] = dot(
                rows_ref[...], weight[:, first : first + step]
            )
            start += step


def product(rows, *weights):
    width = sum(weight.shape[1] for weight in weights)
    return call(
        product_kernel,
        shape((rows.shape[0], width), jnp.float32),
        [VMEM] * (1 + len(weights)),
    )(rows, *weights)


def prepare_kernel(sizes, owned, ids_ref, pool_ref, length_ref, *refs):
    slots_ref, cosine_ref, sine_ref = refs[-3:]
    groups, blocks, drafts = sizes
    width = cosine_ref.shape[1]
    lane = iota(cosine_ref.shape, 1)
    half = (lane & (width // 2 - 1)).astype(jnp.float32)
    positions = (lax.rem(iota(cosine_ref.shape, 0), drafts) + length_ref[0]).astype(jnp.float32)
    angles = positions * jnp.exp(half * (-2.0 * math.log(rope_base) / width))
    cosine_ref[...] = jnp.cos(angles)
    sine_ref[...] = jnp.sin(angles) * jnp.where(lane < width // 2, -1.0, 1.0)
    index = iota(slots_ref.shape, 0)
    column = iota(slots_ref.shape, 1)
    near = parts_of(as_gathered, sizes, index)
    far = parts_of(by_draft, sizes, index)
    row_group = jnp.where(column == 1, far[0], near[0])
    row_block = jnp.where(column == 1, far[1], turned(near[1], blocks))
    place = row_block * groups + row_group
    slots = jnp.zeros(slots_ref.shape, jnp.int32)
    sent, taken = 0, 0
    for row in range(blocks * groups):
        slot = pool_ref[ids_ref[row]]
        owner = over(slot, owned)
        sends = jnp.where(owner == lax.axis_index("tensor"), 1, 0)
        takes = jnp.where(owner == group_of(), 1, 0)
        line = jnp.where(column == 2, sent - 64 * (1 - sends), taken - 64 * (1 - takes))
        slots = jnp.where(place == row, jnp.where(column < 2, slot, line), slots)
        sent, taken = sent + sends, taken + takes
    slots_ref[...] = slots


def prepare(sizes, owned, ids, pool, lengths, table, later):
    groups, blocks, drafts = sizes
    smem = pl.BlockSpec(memory_space=pltpu.SMEM)
    table = shape(table, jnp.float32)
    return call(
        functools.partial(prepare_kernel, sizes, owned),
        [shape((groups * blocks * drafts, 128), jnp.int32), table, table],
        [smem, smem, smem] + [HBM] * 3,
        limit=40 * MIB,
    )(ids, pool, lengths, *[later] * 3)


def grow_kernel(sizes, width, total_ref, slots_ref, *refs):
    groups, blocks, drafts = sizes
    ranks_in, grows, (out_ref, held) = refs[:groups], refs[groups : groups + 3], refs[-2:]
    group = group_of()
    requests = groups * blocks
    lines = out_ref.shape[1]
    held[...] = jnp.zeros(held.shape, jnp.float32)
    owned = grows[0].shape[0] // width
    ranks = ranks_in[0][...].astype(jnp.float32)
    for other in ranks_in[1:]:
        ranks = ranks + other[...].astype(jnp.float32)
    get = (total_ref.shape[0], ranks.shape[0])
    draft = parts_of(as_gathered, sizes, iota(get, 0))[2]
    get = slots_ref[:, 3:4] * drafts + draft == iota(get, 1)
    ranks = dot(jnp.where(get, 1.0, 0.0).astype(jnp.bfloat16), ranks.astype(jnp.bfloat16))
    place = slots_ref[:, 0:1] - group * owned
    wide = spread_ranks(ranks.astype(jnp.bfloat16), place, width, owned, len(grows))
    arranged = reorder(sizes, by_draft, as_gathered)
    start, column = 0, 0
    for index, grow in enumerate(grows):
        deep, cols = grow.shape
        full = total_ref[:, column : column + cols] + dot(
            wide[:, index * deep : (index + 1) * deep], grow[...]
        )
        column += cols
        full = dot(arranged, full.astype(jnp.bfloat16))
        for head in range(cols // 128):
            for draft in range(drafts):
                held[pl.ds(start + draft, requests, stride=lines), :] = full[
                    draft * requests : (draft + 1) * requests, head * 128 : (head + 1) * 128
                ]
            start += drafts
    for row in range(requests):
        out_ref[row] = held[row * lines : (row + 1) * lines, :].astype(jnp.bfloat16)


def attend_kernel(
    sizes, arrived_ref, keys_ref, values_ref, length_ref, cosine_ref, sine_ref, out_ref, *scratch
):
    groups, blocks, drafts = sizes
    (fresh_s,) = scratch
    cache_size, head_size = keys_ref.shape[2:]
    count = out_ref.shape[1]
    scale = 1.0 / math.sqrt(head_size)
    fresh_s[...] = jnp.zeros(fresh_s.shape, jnp.float32)
    for block in range(blocks):
        joined = arrived_ref[block * groups].astype(jnp.float32)
        for other in range(1, groups):
            joined = joined + arrived_ref[block * groups + other].astype(jnp.float32)
        joined = joined.astype(jnp.bfloat16).astype(jnp.float32)
        rotated = joined * cosine_ref[...] + pltpu.roll(joined, head_size // 2, 1) * sine_ref[...]
        fresh_s[2 * block, 0:drafts, :] = rotated[count : count + drafts]
        fresh_s[2 * block + 1, 0:drafts, :] = joined[count + drafts : count + 2 * drafts]
        query = rotated[0:count].astype(jnp.bfloat16)
        old = dot_nt(query, keys_ref[0, block]) * scale
        new = dot_nt(query, fresh_s[2 * block].astype(jnp.bfloat16)) * scale
        old = jnp.where(iota(old.shape, 1) < length_ref[0], old, -jnp.inf)
        seen = iota(new.shape, 1) <= lax.rem(iota(new.shape, 0), drafts)
        new = jnp.where(seen, new, -jnp.inf)
        peak = jnp.maximum(jnp.max(old, 1, keepdims=True), jnp.max(new, 1, keepdims=True))
        old = jnp.exp(old - peak)
        new = jnp.exp(new - peak)
        below = jnp.sum(old, 1, keepdims=True) + jnp.sum(new, 1, keepdims=True)
        mixed = dot((old / below).astype(jnp.bfloat16), values_ref[0, block]) + dot(
            (new / below).astype(jnp.bfloat16), fresh_s[2 * block + 1].astype(jnp.bfloat16)
        )
        mixed = mixed.astype(jnp.bfloat16)
        for target in range(groups):
            out_ref[block * groups + target] = mixed


def packing(rows, width, lanes):
    parts = lanes // width
    return parts, rows // parts


def out_rank_kernel(sizes, owned, got_ref, shrink_ref, slots_ref, *refs):
    rows_ref, rank_ref, wide = refs[-3:]
    drafts = sizes[2]
    requests, lines, head_size = got_ref.shape
    for row in range(requests):
        wide[row * lines : (row + 1) * lines, :] = got_ref[row].astype(jnp.float32)
    for head in range(lines // drafts):
        for draft in range(drafts):
            rows_ref[
                draft * requests : (draft + 1) * requests,
                head * head_size : (head + 1) * head_size,
            ] = wide[pl.ds(head * drafts + draft, requests, stride=lines), :].astype(jnp.bfloat16)
    rows = rows_ref[...]
    place = slots_ref[:, 1:2] - group_of() * owned
    width = shrink_ref.shape[0] // owned
    held, lanes = rank_ref.shape
    parts, span = packing(rows.shape[0], width, lanes)
    ranks = dot_nt(rows, shrink_ref[...])
    kept = jnp.where(over(iota(ranks.shape, 1), width) == place, ranks, 0.0).astype(jnp.bfloat16)
    fold = (ranks.shape[1], lanes)
    fold = rest_of(iota(fold, 0), width) == rest_of(iota(fold, 1), width)
    ranks = dot(kept, jnp.where(fold, 1.0, 0.0).astype(jnp.bfloat16))
    mine = over(iota(ranks.shape, 1), width) == over(iota(ranks.shape, 0), span)
    ranks = jnp.where(mine, ranks, 0.0).astype(jnp.bfloat16)
    put = (held, rows.shape[0])
    put = iota(put, 0) == rest_of(iota(put, 1), span)
    ranks = dot(jnp.where(put, 1.0, 0.0).astype(jnp.bfloat16), ranks)
    rank_ref[...] = ranks.astype(jnp.bfloat16)


def out_grow_kernel(sizes, width, total_ref, slots_ref, grow_ref, *refs):
    groups, blocks, drafts = sizes
    ranks_in, outs = refs[:blocks], refs[blocks:]
    owned = grow_ref.shape[0] // width
    me = lax.axis_index("tensor")
    ranks = ranks_in[0][...].astype(jnp.float32)
    for other in ranks_in[1:]:
        ranks = ranks + other[...].astype(jnp.float32)
    count = total_ref.shape[0]
    held, lanes = ranks.shape
    parts, span = packing(count, width, lanes)
    put = rest_of(iota((count, held), 0), span) == iota((count, held), 1)
    ranks = dot(jnp.where(put, 1.0, 0.0).astype(jnp.bfloat16), ranks.astype(jnp.bfloat16))
    mine = over(iota(ranks.shape, 1), width) == over(iota(ranks.shape, 0), span)
    ranks = jnp.where(mine, ranks, 0.0).astype(jnp.bfloat16)
    tile = (lanes, owned * width)
    tile = rest_of(iota(tile, 0), width) == rest_of(iota(tile, 1), width)
    ranks = dot(ranks, jnp.where(tile, 1.0, 0.0).astype(jnp.bfloat16))
    place = slots_ref[:, 1:2] - me * owned
    wide = jnp.where(over(iota(ranks.shape, 1), width) == place, ranks, 0.0).astype(jnp.bfloat16)
    full = (total_ref[...] + dot(wide, grow_ref[...])).astype(jnp.bfloat16)
    full = dot(reorder(sizes, as_gathered, by_draft), full).astype(jnp.bfloat16)
    for block in range(blocks):
        for draft in range(drafts):
            start = (block * drafts + draft) * groups
            outs[block][draft] = full[start : start + groups]


def by_kernels(
    tokens,
    w_query,
    w_key,
    w_value,
    w_out,
    shrink_qkv,
    grow_query,
    grow_key,
    grow_value,
    shrink_out,
    grow_out,
    cache_keys,
    cache_values,
    cache_lengths,
    adapter_ids,
    adapter_slots,
):
    blocks = lax.axis_size("tensor")
    groups = lax.axis_size(GROUP)
    _, drafts, features = tokens.shape
    sizes = (groups, blocks, drafts)
    owned = shrink_qkv.shape[0]
    width = grow_out.shape[1]
    head_size = cache_keys.shape[3]
    span = blocks * drafts
    count = groups * span
    lanes = -(-shrink_qkv.shape[2] // 128) * 128

    def over_tensor(value, shift):
        route = [(t, (t + shift) % blocks) for t in range(blocks)]
        return lax.ppermute(value, "tensor", route)

    def to_growers(value, shift):
        route = [
            (t * groups + g, ((g + shift) % blocks) * groups + t)
            for t in range(blocks)
            for g in range(groups)
        ]
        return lax.ppermute(value, EVERY, route)

    def to_out_growers(value, shift):
        route = [
            (t * groups + g, g * groups + (t + shift) % groups)
            for t in range(blocks)
            for g in range(groups)
        ]
        return lax.ppermute(value, EVERY, route)

    def exchange(value):
        return lax.all_to_all(value, EVERY, split_axis=0, concat_axis=0, tiled=True)

    mine = jnp.transpose(tokens, (1, 0, 2))
    pieces = [mine] + [over_tensor(mine, shift) for shift in range(1, blocks)]

    lines = (w_query.shape[1] // head_size + 2) * drafts
    lines = -(-lines // 8) * 8
    slots, cosine, sine = prepare(
        sizes, owned, adapter_ids, adapter_slots, cache_lengths, (lines, head_size), w_out
    )
    packed = -(-2 * blocks * drafts // 16) * 16
    shrink_in = jnp.transpose(shrink_qkv, (0, 2, 1)).reshape(-1, features)
    rows, rank_part = call(
        functools.partial(rank_kernel, sizes, owned),
        [shape((count, features)), shape((packed, lanes))],
        [VMEM] * (blocks + 2),
        [pltpu.VMEM((count, features), jnp.float32)],
        2 * count * shrink_qkv.size,
        2 * shrink_qkv.size + 4 * count * features,
    )(*pieces, shrink_in, slots)
    ranks = [to_growers(rank_part, shift) for shift in range(blocks)]
    total = product(rows, w_query, w_key, w_value)
    cols = total.shape[1]
    head_cols = w_query.shape[1]
    query_lines = head_cols // head_size * drafts
    sent = call(
        functools.partial(grow_kernel, sizes, width),
        shape((blocks * groups, lines, head_size)),
        [VMEM] * (5 + groups) + [HBM] * 2,
        [pltpu.VMEM((blocks * groups * lines, head_size), jnp.float32)],
        limit=40 * MIB,
    )(
        total,
        slots,
        *ranks,
        *[grow.reshape(owned * width, -1) for grow in (grow_query, grow_key, grow_value)],
        *[w_out] * 2,
    )
    mixed = call(
        functools.partial(attend_kernel, sizes),
        shape((blocks * groups, query_lines, head_size)),
        [VMEM] * 3 + [pl.BlockSpec(memory_space=pltpu.SMEM)] + [VMEM] * 2,
        [pltpu.VMEM((2 * blocks, 128, head_size), jnp.float32)],
    )(exchange(sent), cache_keys, cache_values, cache_lengths, cosine, sine)
    gathered = exchange(mixed)
    held = -(-packing(count, width, 128)[1] // 16) * 16
    out_rows, out_part = call(
        functools.partial(out_rank_kernel, sizes, owned),
        [shape((count, head_cols)), shape((held, 128))],
        [VMEM] * 3 + [HBM] * 4,
        [pltpu.VMEM((blocks * groups * query_lines, head_size), jnp.float32)],
        limit=40 * MIB,
    )(gathered, jnp.transpose(shrink_out, (0, 2, 1)).reshape(-1, head_cols), slots, *[w_query] * 4)
    out_ranks = [to_out_growers(out_part, shift) for shift in range(blocks)]
    out_total = product(out_rows, w_out)
    out_cols = out_total.shape[1]
    leaving = call(
        functools.partial(out_grow_kernel, sizes, width),
        [shape((drafts, groups, out_cols))] * blocks,
        [VMEM] * (3 + blocks),
        [],
        2 * count * owned * width * out_cols,
        8 * count * out_cols + 2 * owned * width * out_cols,
    )(out_total, slots, grow_out.reshape(owned * width, -1), *out_ranks)
    result = leaving[0].astype(jnp.float32)
    for shift in range(1, blocks):
        result = result + over_tensor(leaving[shift], -shift).astype(jnp.float32)
    return jnp.transpose(result.astype(jnp.bfloat16), (1, 0, 2))


def rotate(vectors, positions):
    half_size = vectors.shape[-1] // 2
    frequency = rope_base ** (-2.0 * jnp.arange(half_size, dtype=jnp.float32) / vectors.shape[-1])
    angles = positions[:, None, None] * frequency
    cosine = jnp.cos(angles)
    sine_value = jnp.sin(angles)
    first_half = vectors[..., :half_size]
    second = vectors[..., half_size:]
    return jnp.concatenate(
        [first_half * cosine - second * sine_value, second * cosine + first_half * sine_value], -1
    )


def to_growers(partial, splits):
    total = None
    for shift in range(splits):
        route = [
            (t * splits + g, ((g + shift) % splits) * splits + t)
            for t in range(splits)
            for g in range(splits)
        ]
        got = lax.ppermute(partial, EVERY, route).astype(jnp.float32)
        total = got if total is None else total + got
    return total


def to_out_growers(partial, splits):
    total = None
    for shift in range(splits):
        route = [
            (t * splits + g, g * splits + (t + shift) % splits)
            for t in range(splits)
            for g in range(splits)
        ]
        got = lax.ppermute(partial, EVERY, route).astype(jnp.float32)
        total = got if total is None else total + got
    return total


def slot_table(adapter_ids, adapter_slots):
    matches = adapter_ids[:, None] == jnp.arange(adapter_slots.shape[0], dtype=jnp.int32)[None, :]
    return jnp.sum(jnp.where(matches, adapter_slots[None, :], 0), axis=1)


def attend(query_heads, key_new, value_new, cache_keys, cache_values, length):
    drafts, head_count, head_size = query_heads.shape
    kv_heads, cache_size, _ = cache_keys.shape
    positions = (length + jnp.arange(drafts, dtype=jnp.int32)).astype(jnp.float32)
    query_rot = rotate(query_heads.astype(jnp.float32), positions).astype(jnp.bfloat16)
    key_rot = rotate(key_new.astype(jnp.float32), positions).astype(jnp.bfloat16)
    grouped = query_rot.reshape(drafts, kv_heads, head_count // kv_heads, head_size)
    score_scale = 1.0 / math.sqrt(head_size)
    cached = (
        jnp.einsum("skgd,kld->skgl", grouped, cache_keys, preferred_element_type=jnp.float32)
        * score_scale
    )
    fresh_scores = (
        jnp.einsum("skgd,tkd->skgt", grouped, key_rot, preferred_element_type=jnp.float32)
        * score_scale
    )
    cache_mask = jnp.arange(cache_size, dtype=jnp.int32) < length
    draft_mask = jnp.arange(drafts)[None, :] <= jnp.arange(drafts)[:, None]
    cached = jnp.where(cache_mask[None, None, None, :], cached, -jnp.inf)
    fresh_scores = jnp.where(draft_mask[:, None, None, :], fresh_scores, -jnp.inf)
    row_peak = jnp.maximum(jnp.max(cached, -1), jnp.max(fresh_scores, -1))
    cached_exp = jnp.exp(cached - row_peak[..., None])
    fresh_exp = jnp.exp(fresh_scores - row_peak[..., None])
    denominator = jnp.sum(cached_exp, -1) + jnp.sum(fresh_exp, -1)
    cached_prob = (cached_exp / denominator[..., None]).astype(jnp.bfloat16)
    fresh_prob = (fresh_exp / denominator[..., None]).astype(jnp.bfloat16)
    mixed = jnp.einsum(
        "skgl,kld->skgd", cached_prob, cache_values, preferred_element_type=jnp.float32
    )
    mixed = mixed + jnp.einsum(
        "skgt,tkd->skgd", fresh_prob, value_new, preferred_element_type=jnp.float32
    )
    return mixed.astype(jnp.bfloat16)


def by_row(
    tokens,
    w_query,
    w_key,
    w_value,
    w_out,
    shrink_qkv,
    grow_query,
    grow_key,
    grow_value,
    shrink_out,
    grow_out,
    cache_keys,
    cache_values,
    cache_lengths,
    adapter_ids,
    adapter_slots,
):
    splits = lax.axis_size("tensor")
    groups = lax.axis_size(("dp", "pipe"))
    tensor_index = lax.axis_index("tensor")
    group_index = lax.axis_index(("dp", "pipe"))
    local_rows, drafts, feature_width = tokens.shape
    per_owner = shrink_qkv.shape[0]
    rank_size = grow_out.shape[1]
    query_cols = w_query.shape[1]
    key_cols = w_key.shape[1]
    kv_heads = cache_keys.shape[1]
    head_size = cache_keys.shape[3]
    rows = splits * groups
    row_slots = jnp.repeat(slot_table(adapter_ids, adapter_slots), drafts)
    within = jnp.arange(per_owner, dtype=jnp.int32)[None, :]
    width_hot = (row_slots[:, None] == within + tensor_index * per_owner)[:, :, None]
    column_hot = (row_slots[:, None] == within + group_index * per_owner)[:, :, None]

    def spread_ranks(ranks, hot):
        return jnp.where(hot, ranks[:, None, :], 0.0).reshape(rows * drafts, -1).astype(jnp.bfloat16)

    flat_tokens = lax.all_gather(tokens, "tensor", axis=0, tiled=True).reshape(
        rows * drafts, feature_width
    )
    rank_part = jnp.einsum(
        "nd,adr->nar", flat_tokens, shrink_qkv, preferred_element_type=jnp.float32
    )
    rank_part = jnp.sum(jnp.where(width_hot, rank_part, 0.0), 1)
    rank_all = to_growers(rank_part.astype(jnp.bfloat16), splits)

    def grown(index, grow):
        ranks = spread_ranks(rank_all[:, index * rank_size : (index + 1) * rank_size], column_hot)
        return jnp.dot(
            ranks, grow.reshape(per_owner * rank_size, -1), preferred_element_type=jnp.float32
        )

    bases = [
        jnp.dot(flat_tokens, weight, preferred_element_type=jnp.float32)
        for weight in (w_query, w_key, w_value)
    ]

    def product(index, grow):
        return (bases[index] + grown(index, grow)).astype(jnp.bfloat16).reshape(rows, drafts, -1)

    partial = jnp.concatenate(
        [
            product(0, grow_query),
            product(1, grow_key),
            product(2, grow_value),
        ],
        2,
    )
    arrived = lax.all_to_all(partial, EVERY, split_axis=0, concat_axis=0, tiled=True)
    joined = jnp.sum(
        arrived.reshape(splits, groups, drafts, -1).astype(jnp.float32), 1
    ).astype(jnp.bfloat16)
    joined = jnp.transpose(joined, (1, 0, 2))
    query_heads = joined[:, :, :query_cols].reshape(drafts, -1, head_size)
    key_new = joined[:, :, query_cols : query_cols + key_cols].reshape(drafts, kv_heads, head_size)
    value_new = joined[:, :, query_cols + key_cols :].reshape(drafts, kv_heads, head_size)
    mixed = attend(
        query_heads, key_new, value_new, cache_keys[0], cache_values[0], cache_lengths[0]
    )
    mixed = jnp.transpose(mixed.reshape(drafts, splits, -1), (1, 0, 2))
    outgoing = jnp.repeat(mixed, groups, axis=0)
    flat_heads = lax.all_to_all(
        outgoing, EVERY, split_axis=0, concat_axis=0, tiled=True
    ).reshape(rows * drafts, -1)
    out_part = jnp.einsum(
        "nw,awr->nar", flat_heads, shrink_out, preferred_element_type=jnp.float32
    )
    out_part = jnp.sum(jnp.where(column_hot, out_part, 0.0), 1)
    out_rank = to_out_growers(out_part.astype(jnp.bfloat16), splits)
    out = jnp.dot(flat_heads, w_out, preferred_element_type=jnp.float32)
    out = out + jnp.dot(
        spread_ranks(out_rank, width_hot),
        grow_out.reshape(per_owner * rank_size, -1),
        preferred_element_type=jnp.float32,
    )
    blocks = lax.all_to_all(
        out.astype(jnp.bfloat16).reshape(splits, local_rows, drafts, feature_width),
        "tensor",
        split_axis=0,
        concat_axis=0,
        tiled=True,
    )
    return jnp.sum(blocks.astype(jnp.float32), 0).astype(jnp.bfloat16)


def local(*arrays):
    heads = arrays[11].shape[1]
    if heads == lax.axis_size("tensor") == lax.axis_size(GROUP):
        return by_kernels(*arrays)
    return by_row(*arrays)


def solution(mesh):
    placed = (
        P(("parts", "tensor"), None, ("dp", "pipe")),
        P(("dp", "pipe"), "tensor"),
        P(("dp", "pipe"), "tensor"),
        P(("dp", "pipe"), "tensor"),
        P("tensor", ("dp", "pipe")),
        P("tensor", ("dp", "pipe"), None),
        P(("dp", "pipe"), None, "tensor"),
        P(("dp", "pipe"), None, "tensor"),
        P(("dp", "pipe"), None, "tensor"),
        P(("dp", "pipe"), "tensor", None),
        P("tensor", None, ("dp", "pipe")),
        P(("parts", "tensor", "dp", "pipe"), None, None, None),
        P(("parts", "tensor", "dp", "pipe"), None, None, None),
        P(("parts", "tensor", "dp", "pipe")),
        P(),
        P(),
    )
    return jax.shard_map(
        local,
        mesh=mesh,
        in_specs=placed,
        out_specs=P(("parts", "tensor"), None, ("dp", "pipe")),
        check_vma=False,
    )
```

```python
import functools
import math

import jax
import jax.numpy as jnp
import numpy as np
from jax import lax
from jax.experimental import pallas as pl
from jax.experimental.pallas import tpu as pltpu
from jax.sharding import PartitionSpec as P

rope_base = 500000.0
EVERY = ("tensor", "dp", "pipe")
GROUP = ("dp", "pipe")
VMEM = pl.BlockSpec(memory_space=pltpu.VMEM)
HBM = pl.BlockSpec(memory_space=pltpu.HBM)
MIB = 1 << 20


def dot(left, right):
    return jnp.dot(left, right, preferred_element_type=jnp.float32)


def dot_nt(left, right):
    return lax.dot_general(
        left, right, (((1,), (1,)), ((), ())), preferred_element_type=jnp.float32
    )


def iota(shape, axis):
    return lax.broadcasted_iota(jnp.int32, shape, axis)


def call(kernel, outs, ins, scratch=(), flops=0, moved=0, limit=24 * MIB):
    return pl.pallas_call(
        kernel,
        out_shape=outs,
        in_specs=ins,
        out_specs=jax.tree.map(lambda _: VMEM, outs),
        scratch_shapes=list(scratch),
        cost_estimate=pl.CostEstimate(flops=flops, bytes_accessed=moved, transcendentals=0),
        compiler_params=pltpu.CompilerParams(vmem_limit_bytes=limit),
    )


def shape(dims, kind=jnp.bfloat16):
    return jax.ShapeDtypeStruct(tuple(dims), kind)


def over(value, size):
    return value >> (size.bit_length() - 1) if size & (size - 1) == 0 else lax.div(value, size)


def rest_of(value, size):
    return value & (size - 1) if size & (size - 1) == 0 else lax.rem(value, size)


def as_gathered(sizes, group, block, draft):
    groups, blocks, drafts = sizes
    return (block * drafts + draft) * groups + group


def by_draft(sizes, group, block, draft):
    groups, blocks, drafts = sizes
    return (draft * blocks + block) * groups + group


def parts_of(order, sizes, index):
    groups, blocks, drafts = sizes
    group, left = rest_of(index, groups), over(index, groups)
    if order is as_gathered:
        return group, over(left, drafts), rest_of(left, drafts)
    return group, rest_of(left, blocks), over(left, blocks)


def turned(block):
    return lax.axis_index("tensor") ^ block


def reorder(sizes, after, before):
    groups, blocks, drafts = sizes
    rows = groups * blocks * drafts
    group, block, draft = parts_of(after, sizes, iota((rows, rows), 0))
    wanted = before(sizes, group, turned(block), draft)
    return jnp.where(wanted == iota((rows, rows), 1), 1.0, 0.0).astype(jnp.bfloat16)


def group_of():
    return lax.axis_index("dp") * lax.axis_size("pipe") + lax.axis_index("pipe")


def rank_kernel(sizes, owned, *refs):
    groups, blocks, drafts = sizes
    pieces = refs[:blocks]
    shrink_ref, slots_ref = refs[blocks : blocks + 2]
    rows_ref, rank_ref, wide = refs[-3:]
    for block in range(blocks):
        for draft in range(drafts):
            start = (block * drafts + draft) * groups
            wide[start : start + groups, :] = pieces[block][draft].astype(jnp.float32)
    rows = wide[...].astype(jnp.bfloat16)
    rows_ref[...] = rows
    place = slots_ref[:, 0:1] - lax.axis_index("tensor") * owned
    ranks = owned_ranks(
        rows, shrink_ref[...], place, shrink_ref.shape[0] // owned, rank_ref.shape[1]
    )
    put = (rank_ref.shape[0], rows.shape[0])
    draft = parts_of(as_gathered, sizes, iota((rows.shape[0], put[0]), 0))[2]
    line = slots_ref[:, 2:3] * drafts + draft
    put = jnp.where(line == iota((rows.shape[0], put[0]), 1), 1.0, 0.0).astype(jnp.bfloat16)
    ranks = lax.dot_general(
        put, ranks, (((0,), (0,)), ((), ())), preferred_element_type=jnp.float32
    )
    rank_ref[...] = ranks.astype(jnp.bfloat16)


def owned_ranks(rows, shrink, place, width, lanes):
    ranks = dot_nt(rows, shrink)
    kept = jnp.where(over(iota(ranks.shape, 1), width) == place, ranks, 0.0).astype(jnp.bfloat16)
    fold = (ranks.shape[1], lanes)
    fold = rest_of(iota(fold, 0), width) == iota(fold, 1)
    return dot(kept, jnp.where(fold, 1.0, 0.0).astype(jnp.bfloat16)).astype(jnp.bfloat16)


def spread_ranks(ranks, place, width, owned, parts):
    span = owned * width
    row = iota((ranks.shape[1], parts * span), 0)
    column = iota((ranks.shape[1], parts * span), 1)
    tile = (over(row, width) == over(column, span)) & (
        rest_of(row, width) == rest_of(column, width)
    )
    wide = dot(ranks, jnp.where(tile, 1.0, 0.0).astype(jnp.bfloat16))
    slot = over(rest_of(iota(wide.shape, 1), span), width)
    return jnp.where(slot == place, wide, 0.0).astype(jnp.bfloat16)


def product_kernel(rows_ref, *refs):
    *weights, total_ref = refs
    start = 0
    for weight in weights:
        width = weight.shape[1]
        step = width if width % 1024 else 1024
        for first in range(0, width, step):
            total_ref[:, start : start + step] = dot(
                rows_ref[...], weight[:, first : first + step]
            )
            start += step


def product(rows, *weights):
    width = sum(weight.shape[1] for weight in weights)
    return call(
        product_kernel,
        shape((rows.shape[0], width), jnp.float32),
        [VMEM] * (1 + len(weights)),
    )(rows, *weights)


def prepare_kernel(sizes, owned, ids_ref, pool_ref, length_ref, *refs):
    slots_ref, cosine_ref, sine_ref = refs[-3:]
    groups, blocks, drafts = sizes
    width = cosine_ref.shape[1]
    lane = iota(cosine_ref.shape, 1)
    half = (lane & (width // 2 - 1)).astype(jnp.float32)
    positions = (lax.rem(iota(cosine_ref.shape, 0), drafts) + length_ref[0]).astype(jnp.float32)
    angles = positions * jnp.exp(half * (-2.0 * math.log(rope_base) / width))
    cosine_ref[...] = jnp.cos(angles)
    sine_ref[...] = jnp.sin(angles) * jnp.where(lane < width // 2, -1.0, 1.0)
    index = iota(slots_ref.shape, 0)
    column = iota(slots_ref.shape, 1)
    near = parts_of(as_gathered, sizes, index)
    far = parts_of(by_draft, sizes, index)
    row_group = jnp.where(column == 1, far[0], near[0])
    row_block = jnp.where(column == 1, far[1], turned(near[1]))
    place = row_block * groups + row_group
    slots = jnp.zeros(slots_ref.shape, jnp.int32)
    sent, taken = 0, 0
    for row in range(blocks * groups):
        slot = pool_ref[ids_ref[row]]
        owner = over(slot, owned)
        sends = jnp.where(owner == lax.axis_index("tensor"), 1, 0)
        takes = jnp.where(owner == group_of(), 1, 0)
        line = jnp.where(column == 2, sent - 64 * (1 - sends), taken - 64 * (1 - takes))
        slots = jnp.where(place == row, jnp.where(column < 2, slot, line), slots)
        sent, taken = sent + sends, taken + takes
    slots_ref[...] = slots


def prepare(sizes, owned, ids, pool, lengths, table, later):
    groups, blocks, drafts = sizes
    smem = pl.BlockSpec(memory_space=pltpu.SMEM)
    table = shape(table, jnp.float32)
    return call(
        functools.partial(prepare_kernel, sizes, owned),
        [shape((groups * blocks * drafts, 128), jnp.int32), table, table],
        [smem, smem, smem] + [HBM] * 3,
        limit=40 * MIB,
    )(ids, pool, lengths, *[later] * 3)


def grow_kernel(sizes, width, total_ref, slots_ref, *refs):
    groups, blocks, drafts = sizes
    ranks_in, grows, (out_ref, held) = refs[:groups], refs[groups : groups + 3], refs[-2:]
    group = group_of()
    requests = groups * blocks
    lines = out_ref.shape[1]
    held[...] = jnp.zeros(held.shape, jnp.float32)
    owned = grows[0].shape[0] // width
    ranks = ranks_in[0][...].astype(jnp.float32)
    for other in ranks_in[1:]:
        ranks = ranks + other[...].astype(jnp.float32)
    get = (total_ref.shape[0], ranks.shape[0])
    draft = parts_of(as_gathered, sizes, iota(get, 0))[2]
    get = slots_ref[:, 3:4] * drafts + draft == iota(get, 1)
    ranks = dot(jnp.where(get, 1.0, 0.0).astype(jnp.bfloat16), ranks.astype(jnp.bfloat16))
    place = slots_ref[:, 0:1] - group * owned
    wide = spread_ranks(ranks.astype(jnp.bfloat16), place, width, owned, len(grows))
    arranged = reorder(sizes, by_draft, as_gathered)
    start, column = 0, 0
    for index, grow in enumerate(grows):
        deep, cols = grow.shape
        full = total_ref[:, column : column + cols] + dot(
            wide[:, index * deep : (index + 1) * deep], grow[...]
        )
        column += cols
        full = dot(arranged, full.astype(jnp.bfloat16))
        for head in range(cols // 128):
            for draft in range(drafts):
                held[pl.ds(start + draft, requests, stride=lines), :] = full[
                    draft * requests : (draft + 1) * requests, head * 128 : (head + 1) * 128
                ]
            start += drafts
    for row in range(requests):
        out_ref[row] = held[row * lines : (row + 1) * lines, :].astype(jnp.bfloat16)


def attend_kernel(
    sizes, arrived_ref, keys_ref, values_ref, length_ref, cosine_ref, sine_ref, out_ref, *scratch
):
    groups, blocks, drafts = sizes
    (fresh_s,) = scratch
    cache_size, head_size = keys_ref.shape[2:]
    count = out_ref.shape[1]
    scale = 1.0 / math.sqrt(head_size)
    fresh_s[...] = jnp.zeros(fresh_s.shape, jnp.float32)
    for block in range(blocks):
        joined = arrived_ref[block * groups].astype(jnp.float32)
        for other in range(1, groups):
            joined = joined + arrived_ref[block * groups + other].astype(jnp.float32)
        joined = joined.astype(jnp.bfloat16).astype(jnp.float32)
        rotated = joined * cosine_ref[...] + pltpu.roll(joined, head_size // 2, 1) * sine_ref[...]
        fresh_s[2 * block, 0:drafts, :] = rotated[count : count + drafts]
        fresh_s[2 * block + 1, 0:drafts, :] = joined[count + drafts : count + 2 * drafts]
        query = rotated[0:count].astype(jnp.bfloat16)
        old = dot_nt(query, keys_ref[0, block]) * scale
        new = dot_nt(query, fresh_s[2 * block].astype(jnp.bfloat16)) * scale
        old = jnp.where(iota(old.shape, 1) < length_ref[0], old, -jnp.inf)
        seen = iota(new.shape, 1) <= lax.rem(iota(new.shape, 0), drafts)
        new = jnp.where(seen, new, -jnp.inf)
        peak = jnp.maximum(jnp.max(old, 1, keepdims=True), jnp.max(new, 1, keepdims=True))
        old = jnp.exp(old - peak)
        new = jnp.exp(new - peak)
        below = jnp.sum(old, 1, keepdims=True) + jnp.sum(new, 1, keepdims=True)
        mixed = dot((old / below).astype(jnp.bfloat16), values_ref[0, block]) + dot(
            (new / below).astype(jnp.bfloat16), fresh_s[2 * block + 1].astype(jnp.bfloat16)
        )
        mixed = mixed.astype(jnp.bfloat16)
        for target in range(groups):
            out_ref[block * groups + target] = mixed


def packing(rows, width, lanes):
    parts = lanes // width
    return parts, rows // parts


def out_rank_kernel(sizes, owned, got_ref, shrink_ref, slots_ref, *refs):
    rows_ref, rank_ref, wide = refs[-3:]
    drafts = sizes[2]
    requests, lines, head_size = got_ref.shape
    for row in range(requests):
        wide[row * lines : (row + 1) * lines, :] = got_ref[row].astype(jnp.float32)
    for head in range(lines // drafts):
        for draft in range(drafts):
            rows_ref[
                draft * requests : (draft + 1) * requests,
                head * head_size : (head + 1) * head_size,
            ] = wide[pl.ds(head * drafts + draft, requests, stride=lines), :].astype(jnp.bfloat16)
    rows = rows_ref[...]
    place = slots_ref[:, 1:2] - group_of() * owned
    width = shrink_ref.shape[0] // owned
    held, lanes = rank_ref.shape
    parts, span = packing(rows.shape[0], width, lanes)
    ranks = dot_nt(rows, shrink_ref[...])
    kept = jnp.where(over(iota(ranks.shape, 1), width) == place, ranks, 0.0).astype(jnp.bfloat16)
    fold = (ranks.shape[1], lanes)
    fold = rest_of(iota(fold, 0), width) == rest_of(iota(fold, 1), width)
    ranks = dot(kept, jnp.where(fold, 1.0, 0.0).astype(jnp.bfloat16))
    mine = over(iota(ranks.shape, 1), width) == over(iota(ranks.shape, 0), span)
    ranks = jnp.where(mine, ranks, 0.0).astype(jnp.bfloat16)
    put = (held, rows.shape[0])
    put = iota(put, 0) == rest_of(iota(put, 1), span)
    ranks = dot(jnp.where(put, 1.0, 0.0).astype(jnp.bfloat16), ranks)
    rank_ref[...] = ranks.astype(jnp.bfloat16)


def out_grow_kernel(sizes, width, total_ref, slots_ref, grow_ref, *refs):
    groups, blocks, drafts = sizes
    ranks_in, outs = refs[:blocks], refs[blocks:]
    owned = grow_ref.shape[0] // width
    me = lax.axis_index("tensor")
    ranks = ranks_in[0][...].astype(jnp.float32)
    for other in ranks_in[1:]:
        ranks = ranks + other[...].astype(jnp.float32)
    count = total_ref.shape[0]
    held, lanes = ranks.shape
    parts, span = packing(count, width, lanes)
    put = rest_of(iota((count, held), 0), span) == iota((count, held), 1)
    ranks = dot(jnp.where(put, 1.0, 0.0).astype(jnp.bfloat16), ranks.astype(jnp.bfloat16))
    mine = over(iota(ranks.shape, 1), width) == over(iota(ranks.shape, 0), span)
    ranks = jnp.where(mine, ranks, 0.0).astype(jnp.bfloat16)
    tile = (lanes, owned * width)
    tile = rest_of(iota(tile, 0), width) == rest_of(iota(tile, 1), width)
    ranks = dot(ranks, jnp.where(tile, 1.0, 0.0).astype(jnp.bfloat16))
    place = slots_ref[:, 1:2] - me * owned
    wide = jnp.where(over(iota(ranks.shape, 1), width) == place, ranks, 0.0).astype(jnp.bfloat16)
    full = (total_ref[...] + dot(wide, grow_ref[...])).astype(jnp.bfloat16)
    full = dot(reorder(sizes, as_gathered, by_draft), full).astype(jnp.bfloat16)
    for block in range(blocks):
        for draft in range(drafts):
            start = (block * drafts + draft) * groups
            outs[block][draft] = full[start : start + groups]


def by_kernels(
    tokens,
    w_query,
    w_key,
    w_value,
    w_out,
    shrink_qkv,
    grow_query,
    grow_key,
    grow_value,
    shrink_out,
    grow_out,
    cache_keys,
    cache_values,
    cache_lengths,
    adapter_ids,
    adapter_slots,
):
    blocks = lax.axis_size("tensor")
    groups = lax.axis_size(GROUP)
    _, drafts, features = tokens.shape
    sizes = (groups, blocks, drafts)
    owned = shrink_qkv.shape[0]
    width = grow_out.shape[1]
    head_size = cache_keys.shape[3]
    span = blocks * drafts
    count = groups * span
    lanes = -(-shrink_qkv.shape[2] // 128) * 128

    def over_tensor(value, shift):
        route = [(t, t ^ shift) for t in range(blocks)]
        return lax.ppermute(value, "tensor", route)

    def to_growers(value, shift):
        route = [
            (t * groups + g, ((g + shift) % blocks) * groups + t)
            for t in range(blocks)
            for g in range(groups)
        ]
        return lax.ppermute(value, EVERY, route)

    def to_out_growers(value, shift):
        route = [
            (t * groups + g, g * groups + (t + shift) % groups)
            for t in range(blocks)
            for g in range(groups)
        ]
        return lax.ppermute(value, EVERY, route)

    def exchange(value):
        return lax.all_to_all(value, EVERY, split_axis=0, concat_axis=0, tiled=True)

    mine = jnp.transpose(tokens, (1, 0, 2))
    pieces = [mine] + [over_tensor(mine, shift) for shift in range(1, blocks)]

    lines = (w_query.shape[1] // head_size + 2) * drafts
    lines = -(-lines // 8) * 8
    slots, cosine, sine = prepare(
        sizes, owned, adapter_ids, adapter_slots, cache_lengths, (lines, head_size), w_out
    )
    packed = -(-2 * blocks * drafts // 16) * 16
    shrink_in = jnp.transpose(shrink_qkv, (0, 2, 1)).reshape(-1, features)
    rows, rank_part = call(
        functools.partial(rank_kernel, sizes, owned),
        [shape((count, features)), shape((packed, lanes))],
        [VMEM] * (blocks + 2),
        [pltpu.VMEM((count, features), jnp.float32)],
        2 * count * shrink_qkv.size,
        2 * shrink_qkv.size + 4 * count * features,
    )(*pieces, shrink_in, slots)
    ranks = [to_growers(rank_part, shift) for shift in range(blocks)]
    total = product(rows, w_query, w_key, w_value)
    cols = total.shape[1]
    head_cols = w_query.shape[1]
    query_lines = head_cols // head_size * drafts
    sent = call(
        functools.partial(grow_kernel, sizes, width),
        shape((blocks * groups, lines, head_size)),
        [VMEM] * (5 + groups) + [HBM] * 2,
        [pltpu.VMEM((blocks * groups * lines, head_size), jnp.float32)],
        limit=40 * MIB,
    )(
        total,
        slots,
        *ranks,
        *[grow.reshape(owned * width, -1) for grow in (grow_query, grow_key, grow_value)],
        *[w_out] * 2,
    )
    mixed = call(
        functools.partial(attend_kernel, sizes),
        shape((blocks * groups, query_lines, head_size)),
        [VMEM] * 3 + [pl.BlockSpec(memory_space=pltpu.SMEM)] + [VMEM] * 2,
        [pltpu.VMEM((2 * blocks, 128, head_size), jnp.float32)],
    )(exchange(sent), cache_keys, cache_values, cache_lengths, cosine, sine)
    gathered = exchange(mixed)
    held = -(-packing(count, width, 128)[1] // 16) * 16
    out_rows, out_part = call(
        functools.partial(out_rank_kernel, sizes, owned),
        [shape((count, head_cols)), shape((held, 128))],
        [VMEM] * 3 + [HBM] * 4,
        [pltpu.VMEM((blocks * groups * query_lines, head_size), jnp.float32)],
        limit=40 * MIB,
    )(gathered, jnp.transpose(shrink_out, (0, 2, 1)).reshape(-1, head_cols), slots, *[w_query] * 4)
    out_ranks = [to_out_growers(out_part, shift) for shift in range(blocks)]
    out_total = product(out_rows, w_out)
    out_cols = out_total.shape[1]
    leaving = call(
        functools.partial(out_grow_kernel, sizes, width),
        [shape((drafts, groups, out_cols))] * blocks,
        [VMEM] * (3 + blocks),
        [],
        2 * count * owned * width * out_cols,
        8 * count * out_cols + 2 * owned * width * out_cols,
    )(out_total, slots, grow_out.reshape(owned * width, -1), *out_ranks)
    result = leaving[0].astype(jnp.float32)
    for shift in range(1, blocks):
        result = result + over_tensor(leaving[shift], shift).astype(jnp.float32)
    return jnp.transpose(result.astype(jnp.bfloat16), (1, 0, 2))


def rotate(vectors, positions):
    half_size = vectors.shape[-1] // 2
    frequency = rope_base ** (-2.0 * jnp.arange(half_size, dtype=jnp.float32) / vectors.shape[-1])
    angles = positions[:, None, None] * frequency
    cosine = jnp.cos(angles)
    sine_value = jnp.sin(angles)
    first_half = vectors[..., :half_size]
    second = vectors[..., half_size:]
    return jnp.concatenate(
        [first_half * cosine - second * sine_value, second * cosine + first_half * sine_value], -1
    )


def to_growers(partial, splits):
    total = None
    for shift in range(splits):
        route = [
            (t * splits + g, ((g + shift) % splits) * splits + t)
            for t in range(splits)
            for g in range(splits)
        ]
        got = lax.ppermute(partial, EVERY, route).astype(jnp.float32)
        total = got if total is None else total + got
    return total


def to_out_growers(partial, splits):
    total = None
    for shift in range(splits):
        route = [
            (t * splits + g, g * splits + (t + shift) % splits)
            for t in range(splits)
            for g in range(splits)
        ]
        got = lax.ppermute(partial, EVERY, route).astype(jnp.float32)
        total = got if total is None else total + got
    return total


def slot_table(adapter_ids, adapter_slots):
    matches = adapter_ids[:, None] == jnp.arange(adapter_slots.shape[0], dtype=jnp.int32)[None, :]
    return jnp.sum(jnp.where(matches, adapter_slots[None, :], 0), axis=1)


def attend(query_heads, key_new, value_new, cache_keys, cache_values, length):
    drafts, head_count, head_size = query_heads.shape
    kv_heads, cache_size, _ = cache_keys.shape
    positions = (length + jnp.arange(drafts, dtype=jnp.int32)).astype(jnp.float32)
    query_rot = rotate(query_heads.astype(jnp.float32), positions).astype(jnp.bfloat16)
    key_rot = rotate(key_new.astype(jnp.float32), positions).astype(jnp.bfloat16)
    grouped = query_rot.reshape(drafts, kv_heads, head_count // kv_heads, head_size)
    score_scale = 1.0 / math.sqrt(head_size)
    cached = (
        jnp.einsum("skgd,kld->skgl", grouped, cache_keys, preferred_element_type=jnp.float32)
        * score_scale
    )
    fresh_scores = (
        jnp.einsum("skgd,tkd->skgt", grouped, key_rot, preferred_element_type=jnp.float32)
        * score_scale
    )
    cache_mask = jnp.arange(cache_size, dtype=jnp.int32) < length
    draft_mask = jnp.arange(drafts)[None, :] <= jnp.arange(drafts)[:, None]
    cached = jnp.where(cache_mask[None, None, None, :], cached, -jnp.inf)
    fresh_scores = jnp.where(draft_mask[:, None, None, :], fresh_scores, -jnp.inf)
    row_peak = jnp.maximum(jnp.max(cached, -1), jnp.max(fresh_scores, -1))
    cached_exp = jnp.exp(cached - row_peak[..., None])
    fresh_exp = jnp.exp(fresh_scores - row_peak[..., None])
    denominator = jnp.sum(cached_exp, -1) + jnp.sum(fresh_exp, -1)
    cached_prob = (cached_exp / denominator[..., None]).astype(jnp.bfloat16)
    fresh_prob = (fresh_exp / denominator[..., None]).astype(jnp.bfloat16)
    mixed = jnp.einsum(
        "skgl,kld->skgd", cached_prob, cache_values, preferred_element_type=jnp.float32
    )
    mixed = mixed + jnp.einsum(
        "skgt,tkd->skgd", fresh_prob, value_new, preferred_element_type=jnp.float32
    )
    return mixed.astype(jnp.bfloat16)


def by_row(
    tokens,
    w_query,
    w_key,
    w_value,
    w_out,
    shrink_qkv,
    grow_query,
    grow_key,
    grow_value,
    shrink_out,
    grow_out,
    cache_keys,
    cache_values,
    cache_lengths,
    adapter_ids,
    adapter_slots,
):
    splits = lax.axis_size("tensor")
    groups = lax.axis_size(("dp", "pipe"))
    tensor_index = lax.axis_index("tensor")
    group_index = lax.axis_index(("dp", "pipe"))
    local_rows, drafts, feature_width = tokens.shape
    per_owner = shrink_qkv.shape[0]
    rank_size = grow_out.shape[1]
    query_cols = w_query.shape[1]
    key_cols = w_key.shape[1]
    kv_heads = cache_keys.shape[1]
    head_size = cache_keys.shape[3]
    rows = splits * groups
    row_slots = jnp.repeat(slot_table(adapter_ids, adapter_slots), drafts)
    within = jnp.arange(per_owner, dtype=jnp.int32)[None, :]
    width_hot = (row_slots[:, None] == within + tensor_index * per_owner)[:, :, None]
    column_hot = (row_slots[:, None] == within + group_index * per_owner)[:, :, None]

    def spread_ranks(ranks, hot):
        return jnp.where(hot, ranks[:, None, :], 0.0).reshape(rows * drafts, -1).astype(jnp.bfloat16)

    flat_tokens = lax.all_gather(tokens, "tensor", axis=0, tiled=True).reshape(
        rows * drafts, feature_width
    )
    rank_part = jnp.einsum(
        "nd,adr->nar", flat_tokens, shrink_qkv, preferred_element_type=jnp.float32
    )
    rank_part = jnp.sum(jnp.where(width_hot, rank_part, 0.0), 1)
    rank_all = to_growers(rank_part.astype(jnp.bfloat16), splits)

    def grown(index, grow):
        ranks = spread_ranks(rank_all[:, index * rank_size : (index + 1) * rank_size], column_hot)
        return jnp.dot(
            ranks, grow.reshape(per_owner * rank_size, -1), preferred_element_type=jnp.float32
        )

    bases = [
        jnp.dot(flat_tokens, weight, preferred_element_type=jnp.float32)
        for weight in (w_query, w_key, w_value)
    ]

    def product(index, grow):
        return (bases[index] + grown(index, grow)).astype(jnp.bfloat16).reshape(rows, drafts, -1)

    partial = jnp.concatenate(
        [
            product(0, grow_query),
            product(1, grow_key),
            product(2, grow_value),
        ],
        2,
    )
    arrived = lax.all_to_all(partial, EVERY, split_axis=0, concat_axis=0, tiled=True)
    joined = jnp.sum(
        arrived.reshape(splits, groups, drafts, -1).astype(jnp.float32), 1
    ).astype(jnp.bfloat16)
    joined = jnp.transpose(joined, (1, 0, 2))
    query_heads = joined[:, :, :query_cols].reshape(drafts, -1, head_size)
    key_new = joined[:, :, query_cols : query_cols + key_cols].reshape(drafts, kv_heads, head_size)
    value_new = joined[:, :, query_cols + key_cols :].reshape(drafts, kv_heads, head_size)
    mixed = attend(
        query_heads, key_new, value_new, cache_keys[0], cache_values[0], cache_lengths[0]
    )
    mixed = jnp.transpose(mixed.reshape(drafts, splits, -1), (1, 0, 2))
    outgoing = jnp.repeat(mixed, groups, axis=0)
    flat_heads = lax.all_to_all(
        outgoing, EVERY, split_axis=0, concat_axis=0, tiled=True
    ).reshape(rows * drafts, -1)
    out_part = jnp.einsum(
        "nw,awr->nar", flat_heads, shrink_out, preferred_element_type=jnp.float32
    )
    out_part = jnp.sum(jnp.where(column_hot, out_part, 0.0), 1)
    out_rank = to_out_growers(out_part.astype(jnp.bfloat16), splits)
    out = jnp.dot(flat_heads, w_out, preferred_element_type=jnp.float32)
    out = out + jnp.dot(
        spread_ranks(out_rank, width_hot),
        grow_out.reshape(per_owner * rank_size, -1),
        preferred_element_type=jnp.float32,
    )
    blocks = lax.all_to_all(
        out.astype(jnp.bfloat16).reshape(splits, local_rows, drafts, feature_width),
        "tensor",
        split_axis=0,
        concat_axis=0,
        tiled=True,
    )
    return jnp.sum(blocks.astype(jnp.float32), 0).astype(jnp.bfloat16)


def local(*arrays):
    heads = arrays[11].shape[1]
    paired = heads & (heads - 1) == 0
    if paired and heads == lax.axis_size("tensor") == lax.axis_size(GROUP):
        return by_kernels(*arrays)
    return by_row(*arrays)


def solution(mesh):
    placed = (
        P(("parts", "tensor"), None, ("dp", "pipe")),
        P(("dp", "pipe"), "tensor"),
        P(("dp", "pipe"), "tensor"),
        P(("dp", "pipe"), "tensor"),
        P("tensor", ("dp", "pipe")),
        P("tensor", ("dp", "pipe"), None),
        P(("dp", "pipe"), None, "tensor"),
        P(("dp", "pipe"), None, "tensor"),
        P(("dp", "pipe"), None, "tensor"),
        P(("dp", "pipe"), "tensor", None),
        P("tensor", None, ("dp", "pipe")),
        P(("parts", "tensor", "dp", "pipe"), None, None, None),
        P(("parts", "tensor", "dp", "pipe"), None, None, None),
        P(("parts", "tensor", "dp", "pipe")),
        P(),
        P(),
    )
    return jax.shard_map(
        local,
        mesh=mesh,
        in_specs=placed,
        out_specs=P(("parts", "tensor"), None, ("dp", "pipe")),
        check_vma=False,
    )
```

```python
import functools
import math

import jax
import jax.numpy as jnp
import numpy as np
from jax import lax
from jax.experimental import pallas as pl
from jax.experimental.pallas import tpu as pltpu
from jax.sharding import PartitionSpec as P

rope_base = 500000.0
EVERY = ("tensor", "dp", "pipe")
GROUP = ("dp", "pipe")
VMEM = pl.BlockSpec(memory_space=pltpu.VMEM)
HBM = pl.BlockSpec(memory_space=pltpu.HBM)
MIB = 1 << 20


def dot(left, right):
    return jnp.dot(left, right, preferred_element_type=jnp.float32)


def dot_nt(left, right):
    return lax.dot_general(
        left, right, (((1,), (1,)), ((), ())), preferred_element_type=jnp.float32
    )


def iota(shape, axis):
    return lax.broadcasted_iota(jnp.int32, shape, axis)


def call(kernel, outs, ins, scratch=(), flops=0, moved=0, limit=24 * MIB):
    return pl.pallas_call(
        kernel,
        out_shape=outs,
        in_specs=ins,
        out_specs=jax.tree.map(lambda _: VMEM, outs),
        scratch_shapes=list(scratch),
        cost_estimate=pl.CostEstimate(flops=flops, bytes_accessed=moved, transcendentals=0),
        compiler_params=pltpu.CompilerParams(vmem_limit_bytes=limit),
    )


def shape(dims, kind=jnp.bfloat16):
    return jax.ShapeDtypeStruct(tuple(dims), kind)


def over(value, size):
    return value >> (size.bit_length() - 1) if size & (size - 1) == 0 else lax.div(value, size)


def rest_of(value, size):
    return value & (size - 1) if size & (size - 1) == 0 else lax.rem(value, size)


def as_gathered(sizes, group, block, draft):
    groups, blocks, drafts = sizes
    return (block * drafts + draft) * groups + group


def by_draft(sizes, group, block, draft):
    groups, blocks, drafts = sizes
    return (draft * blocks + block) * groups + group


def parts_of(order, sizes, index):
    groups, blocks, drafts = sizes
    group, left = rest_of(index, groups), over(index, groups)
    if order is as_gathered:
        return group, over(left, drafts), rest_of(left, drafts)
    return group, rest_of(left, blocks), over(left, blocks)


def turned(block):
    return lax.axis_index("tensor") ^ block


def reorder(sizes, after, before):
    groups, blocks, drafts = sizes
    rows = groups * blocks * drafts
    group, block, draft = parts_of(after, sizes, iota((rows, rows), 0))
    wanted = before(sizes, group, turned(block), draft)
    return jnp.where(wanted == iota((rows, rows), 1), 1.0, 0.0).astype(jnp.bfloat16)


def group_of():
    return lax.axis_index("dp") * lax.axis_size("pipe") + lax.axis_index("pipe")


def rank_kernel(sizes, owned, *refs):
    groups, blocks, drafts = sizes
    pieces = refs[:blocks]
    shrink_ref, slots_ref = refs[blocks : blocks + 2]
    rows_ref, rank_ref, wide = refs[-3:]
    for block in range(blocks):
        for draft in range(drafts):
            start = (block * drafts + draft) * groups
            wide[start : start + groups, :] = pieces[block][draft].astype(jnp.float32)
    rows = wide[...].astype(jnp.bfloat16)
    rows_ref[...] = rows
    place = slots_ref[:, 0:1] - lax.axis_index("tensor") * owned
    ranks = owned_ranks(
        rows, shrink_ref[...], place, shrink_ref.shape[0] // owned, rank_ref.shape[1]
    )
    put = (rank_ref.shape[0], rows.shape[0])
    draft = parts_of(as_gathered, sizes, iota((rows.shape[0], put[0]), 0))[2]
    line = slots_ref[:, 2:3] * drafts + draft
    put = jnp.where(line == iota((rows.shape[0], put[0]), 1), 1.0, 0.0).astype(jnp.bfloat16)
    ranks = lax.dot_general(
        put, ranks, (((0,), (0,)), ((), ())), preferred_element_type=jnp.float32
    )
    rank_ref[...] = ranks.astype(jnp.bfloat16)


def owned_ranks(rows, shrink, place, width, lanes):
    ranks = dot_nt(rows, shrink)
    kept = jnp.where(over(iota(ranks.shape, 1), width) == place, ranks, 0.0).astype(jnp.bfloat16)
    fold = (ranks.shape[1], lanes)
    fold = rest_of(iota(fold, 0), width) == iota(fold, 1)
    return dot(kept, jnp.where(fold, 1.0, 0.0).astype(jnp.bfloat16)).astype(jnp.bfloat16)


def spread_ranks(ranks, place, width, owned, parts):
    span = owned * width
    row = iota((ranks.shape[1], parts * span), 0)
    column = iota((ranks.shape[1], parts * span), 1)
    tile = (over(row, width) == over(column, span)) & (
        rest_of(row, width) == rest_of(column, width)
    )
    wide = dot(ranks, jnp.where(tile, 1.0, 0.0).astype(jnp.bfloat16))
    slot = over(rest_of(iota(wide.shape, 1), span), width)
    return jnp.where(slot == place, wide, 0.0).astype(jnp.bfloat16)


def product_kernel(rows_ref, *refs):
    *weights, total_ref = refs
    start = 0
    for weight in weights:
        width = weight.shape[1]
        step = width if width % 1024 else 1024
        for first in range(0, width, step):
            total_ref[:, start : start + step] = dot(
                rows_ref[...], weight[:, first : first + step]
            )
            start += step


def product(rows, *weights):
    width = sum(weight.shape[1] for weight in weights)
    return call(
        product_kernel,
        shape((rows.shape[0], width), jnp.float32),
        [VMEM] * (1 + len(weights)),
    )(rows, *weights)


def prepare_kernel(sizes, owned, ids_ref, pool_ref, length_ref, *refs):
    slots_ref, cosine_ref, sine_ref = refs[-3:]
    groups, blocks, drafts = sizes
    width = cosine_ref.shape[1]
    lane = iota(cosine_ref.shape, 1)
    half = (lane & (width // 2 - 1)).astype(jnp.float32)
    positions = (lax.rem(iota(cosine_ref.shape, 0), drafts) + length_ref[0]).astype(jnp.float32)
    angles = positions * jnp.exp(half * (-2.0 * math.log(rope_base) / width))
    cosine_ref[...] = jnp.cos(angles)
    sine_ref[...] = jnp.sin(angles) * jnp.where(lane < width // 2, -1.0, 1.0)
    index = iota(slots_ref.shape, 0)
    column = iota(slots_ref.shape, 1)
    near = parts_of(as_gathered, sizes, index)
    far = parts_of(by_draft, sizes, index)
    row_group = jnp.where(column == 1, far[0], near[0])
    row_block = jnp.where(column == 1, far[1], turned(near[1]))
    place = row_block * groups + row_group
    slots = jnp.zeros(slots_ref.shape, jnp.int32)
    sent, taken = 0, 0
    for row in range(blocks * groups):
        slot = pool_ref[ids_ref[row]]
        owner = over(slot, owned)
        sends = jnp.where(owner == lax.axis_index("tensor"), 1, 0)
        takes = jnp.where(owner == group_of(), 1, 0)
        line = jnp.where(column == 2, sent - 64 * (1 - sends), taken - 64 * (1 - takes))
        slots = jnp.where(place == row, jnp.where(column < 2, slot, line), slots)
        sent, taken = sent + sends, taken + takes
    slots_ref[...] = slots


def prepare(sizes, owned, ids, pool, lengths, table, later):
    groups, blocks, drafts = sizes
    smem = pl.BlockSpec(memory_space=pltpu.SMEM)
    table = shape(table, jnp.float32)
    return call(
        functools.partial(prepare_kernel, sizes, owned),
        [shape((groups * blocks * drafts, 128), jnp.int32), table, table],
        [smem, smem, smem] + [HBM] * 3,
        limit=40 * MIB,
    )(ids, pool, lengths, *[later] * 3)


def grow_kernel(sizes, width, total_ref, slots_ref, *refs):
    groups, blocks, drafts = sizes
    ranks_in, grows, (out_ref, held) = refs[:2], refs[2:5], refs[-2:]
    group = group_of()
    requests = groups * blocks
    lines = out_ref.shape[1]
    held[...] = jnp.zeros(held.shape, jnp.float32)
    owned = grows[0].shape[0] // width
    ranks = ranks_in[0][...].astype(jnp.float32)
    for other in ranks_in[1:]:
        ranks = ranks + other[...].astype(jnp.float32)
    get = (total_ref.shape[0], ranks.shape[0])
    draft = parts_of(as_gathered, sizes, iota(get, 0))[2]
    get = slots_ref[:, 3:4] * drafts + draft == iota(get, 1)
    ranks = dot(jnp.where(get, 1.0, 0.0).astype(jnp.bfloat16), ranks.astype(jnp.bfloat16))
    place = slots_ref[:, 0:1] - group * owned
    wide = spread_ranks(ranks.astype(jnp.bfloat16), place, width, owned, len(grows))
    arranged = reorder(sizes, by_draft, as_gathered)
    start, column = 0, 0
    for index, grow in enumerate(grows):
        deep, cols = grow.shape
        full = total_ref[:, column : column + cols] + dot(
            wide[:, index * deep : (index + 1) * deep], grow[...]
        )
        column += cols
        full = dot(arranged, full.astype(jnp.bfloat16))
        for head in range(cols // 128):
            for draft in range(drafts):
                held[pl.ds(start + draft, requests, stride=lines), :] = full[
                    draft * requests : (draft + 1) * requests, head * 128 : (head + 1) * 128
                ]
            start += drafts
    for row in range(requests):
        out_ref[row] = held[row * lines : (row + 1) * lines, :].astype(jnp.bfloat16)


def attend_kernel(
    sizes, arrived_ref, keys_ref, values_ref, length_ref, cosine_ref, sine_ref, out_ref, *scratch
):
    groups, blocks, drafts = sizes
    (fresh_s,) = scratch
    cache_size, head_size = keys_ref.shape[2:]
    count = out_ref.shape[1]
    scale = 1.0 / math.sqrt(head_size)
    fresh_s[...] = jnp.zeros(fresh_s.shape, jnp.float32)
    for block in range(blocks):
        joined = arrived_ref[block * groups].astype(jnp.float32)
        for other in range(1, groups):
            joined = joined + arrived_ref[block * groups + other].astype(jnp.float32)
        joined = joined.astype(jnp.bfloat16).astype(jnp.float32)
        rotated = joined * cosine_ref[...] + pltpu.roll(joined, head_size // 2, 1) * sine_ref[...]
        fresh_s[2 * block, 0:drafts, :] = rotated[count : count + drafts]
        fresh_s[2 * block + 1, 0:drafts, :] = joined[count + drafts : count + 2 * drafts]
        query = rotated[0:count].astype(jnp.bfloat16)
        old = dot_nt(query, keys_ref[0, block]) * scale
        new = dot_nt(query, fresh_s[2 * block].astype(jnp.bfloat16)) * scale
        old = jnp.where(iota(old.shape, 1) < length_ref[0], old, -jnp.inf)
        seen = iota(new.shape, 1) <= lax.rem(iota(new.shape, 0), drafts)
        new = jnp.where(seen, new, -jnp.inf)
        peak = jnp.maximum(jnp.max(old, 1, keepdims=True), jnp.max(new, 1, keepdims=True))
        old = jnp.exp(old - peak)
        new = jnp.exp(new - peak)
        below = jnp.sum(old, 1, keepdims=True) + jnp.sum(new, 1, keepdims=True)
        mixed = dot((old / below).astype(jnp.bfloat16), values_ref[0, block]) + dot(
            (new / below).astype(jnp.bfloat16), fresh_s[2 * block + 1].astype(jnp.bfloat16)
        )
        mixed = mixed.astype(jnp.bfloat16)
        for target in range(groups):
            out_ref[block * groups + target] = mixed


def add_kernel(left_ref, right_ref, out_ref):
    total = left_ref[...].astype(jnp.float32) + right_ref[...].astype(jnp.float32)
    out_ref[...] = total.astype(jnp.bfloat16)


def packing(rows, width, lanes):
    parts = lanes // width
    return parts, rows // parts


def out_rank_kernel(sizes, owned, got_ref, shrink_ref, slots_ref, *refs):
    rows_ref, rank_ref, wide = refs[-3:]
    drafts = sizes[2]
    requests, lines, head_size = got_ref.shape
    for row in range(requests):
        wide[row * lines : (row + 1) * lines, :] = got_ref[row].astype(jnp.float32)
    for head in range(lines // drafts):
        for draft in range(drafts):
            rows_ref[
                draft * requests : (draft + 1) * requests,
                head * head_size : (head + 1) * head_size,
            ] = wide[pl.ds(head * drafts + draft, requests, stride=lines), :].astype(jnp.bfloat16)
    rows = rows_ref[...]
    place = slots_ref[:, 1:2] - group_of() * owned
    width = shrink_ref.shape[0] // owned
    held, lanes = rank_ref.shape
    parts, span = packing(rows.shape[0], width, lanes)
    ranks = dot_nt(rows, shrink_ref[...])
    kept = jnp.where(over(iota(ranks.shape, 1), width) == place, ranks, 0.0).astype(jnp.bfloat16)
    fold = (ranks.shape[1], lanes)
    fold = rest_of(iota(fold, 0), width) == rest_of(iota(fold, 1), width)
    ranks = dot(kept, jnp.where(fold, 1.0, 0.0).astype(jnp.bfloat16))
    mine = over(iota(ranks.shape, 1), width) == over(iota(ranks.shape, 0), span)
    ranks = jnp.where(mine, ranks, 0.0).astype(jnp.bfloat16)
    put = (held, rows.shape[0])
    put = iota(put, 0) == rest_of(iota(put, 1), span)
    ranks = dot(jnp.where(put, 1.0, 0.0).astype(jnp.bfloat16), ranks)
    rank_ref[...] = ranks.astype(jnp.bfloat16)


def out_grow_kernel(sizes, width, total_ref, slots_ref, grow_ref, *refs):
    groups, blocks, drafts = sizes
    ranks_in, outs = refs[:2], refs[2:]
    owned = grow_ref.shape[0] // width
    me = lax.axis_index("tensor")
    ranks = ranks_in[0][...].astype(jnp.float32)
    for other in ranks_in[1:]:
        ranks = ranks + other[...].astype(jnp.float32)
    count = total_ref.shape[0]
    held, lanes = ranks.shape
    parts, span = packing(count, width, lanes)
    put = rest_of(iota((count, held), 0), span) == iota((count, held), 1)
    ranks = dot(jnp.where(put, 1.0, 0.0).astype(jnp.bfloat16), ranks.astype(jnp.bfloat16))
    mine = over(iota(ranks.shape, 1), width) == over(iota(ranks.shape, 0), span)
    ranks = jnp.where(mine, ranks, 0.0).astype(jnp.bfloat16)
    tile = (lanes, owned * width)
    tile = rest_of(iota(tile, 0), width) == rest_of(iota(tile, 1), width)
    ranks = dot(ranks, jnp.where(tile, 1.0, 0.0).astype(jnp.bfloat16))
    place = slots_ref[:, 1:2] - me * owned
    wide = jnp.where(over(iota(ranks.shape, 1), width) == place, ranks, 0.0).astype(jnp.bfloat16)
    full = (total_ref[...] + dot(wide, grow_ref[...])).astype(jnp.bfloat16)
    full = dot(reorder(sizes, as_gathered, by_draft), full).astype(jnp.bfloat16)
    for block in range(blocks):
        for draft in range(drafts):
            start = (block * drafts + draft) * groups
            outs[block][draft] = full[start : start + groups]


def by_kernels(
    tokens,
    w_query,
    w_key,
    w_value,
    w_out,
    shrink_qkv,
    grow_query,
    grow_key,
    grow_value,
    shrink_out,
    grow_out,
    cache_keys,
    cache_values,
    cache_lengths,
    adapter_ids,
    adapter_slots,
):
    blocks = lax.axis_size("tensor")
    groups = lax.axis_size(GROUP)
    _, drafts, features = tokens.shape
    sizes = (groups, blocks, drafts)
    owned = shrink_qkv.shape[0]
    width = grow_out.shape[1]
    head_size = cache_keys.shape[3]
    span = blocks * drafts
    count = groups * span
    lanes = -(-shrink_qkv.shape[2] // 128) * 128

    def over_tensor(value, shift):
        route = [(t, t ^ shift) for t in range(blocks)]
        return lax.ppermute(value, "tensor", route)

    def over_core(value):
        return lax.ppermute(value, "pipe", [(0, 1), (1, 0)])

    def to_growers(value, flip):
        route = [
            (t * groups + 2 * x + c, (2 * c + (x ^ flip)) * groups + t)
            for t in range(blocks)
            for x in range(2)
            for c in range(2)
        ]
        return lax.ppermute(value, EVERY, route)

    def to_out_growers(value, flip):
        route = [
            (t * groups + g, g * groups + 2 * ((t // 2) ^ flip) + t % 2)
            for t in range(blocks)
            for g in range(groups)
        ]
        return lax.ppermute(value, EVERY, route)

    def added(left, right):
        return call(add_kernel, shape(left.shape), [VMEM] * 2)(left, right)

    def exchange(value):
        return lax.all_to_all(value, EVERY, split_axis=0, concat_axis=0, tiled=True)

    mine = jnp.transpose(tokens, (1, 0, 2))
    pieces = [mine] + [over_tensor(mine, shift) for shift in range(1, blocks)]

    lines = (w_query.shape[1] // head_size + 2) * drafts
    lines = -(-lines // 8) * 8
    slots, cosine, sine = prepare(
        sizes, owned, adapter_ids, adapter_slots, cache_lengths, (lines, head_size), w_out
    )
    packed = -(-2 * blocks * drafts // 16) * 16
    shrink_in = jnp.transpose(shrink_qkv, (0, 2, 1)).reshape(-1, features)
    rows, rank_part = call(
        functools.partial(rank_kernel, sizes, owned),
        [shape((count, features)), shape((packed, lanes))],
        [VMEM] * (blocks + 2),
        [pltpu.VMEM((count, features), jnp.float32)],
        2 * count * shrink_qkv.size,
        2 * shrink_qkv.size + 4 * count * features,
    )(*pieces, shrink_in, slots)
    rank_part = added(rank_part, over_core(rank_part))
    ranks = [to_growers(rank_part, flip) for flip in range(2)]
    total = product(rows, w_query, w_key, w_value)
    cols = total.shape[1]
    head_cols = w_query.shape[1]
    query_lines = head_cols // head_size * drafts
    sent = call(
        functools.partial(grow_kernel, sizes, width),
        shape((blocks * groups, lines, head_size)),
        [VMEM] * 7 + [HBM] * 2,
        [pltpu.VMEM((blocks * groups * lines, head_size), jnp.float32)],
        limit=40 * MIB,
    )(
        total,
        slots,
        *ranks,
        *[grow.reshape(owned * width, -1) for grow in (grow_query, grow_key, grow_value)],
        *[w_out] * 2,
    )
    mixed = call(
        functools.partial(attend_kernel, sizes),
        shape((blocks * groups, query_lines, head_size)),
        [VMEM] * 3 + [pl.BlockSpec(memory_space=pltpu.SMEM)] + [VMEM] * 2,
        [pltpu.VMEM((2 * blocks, 128, head_size), jnp.float32)],
    )(exchange(sent), cache_keys, cache_values, cache_lengths, cosine, sine)
    gathered = exchange(mixed)
    held = -(-packing(count, width, 128)[1] // 16) * 16
    out_rows, out_part = call(
        functools.partial(out_rank_kernel, sizes, owned),
        [shape((count, head_cols)), shape((held, 128))],
        [VMEM] * 3 + [HBM] * 4,
        [pltpu.VMEM((blocks * groups * query_lines, head_size), jnp.float32)],
        limit=40 * MIB,
    )(gathered, jnp.transpose(shrink_out, (0, 2, 1)).reshape(-1, head_cols), slots, *[w_query] * 4)
    out_part = added(*[to_out_growers(out_part, flip) for flip in range(2)])
    out_ranks = [out_part, over_core(out_part)]
    out_total = product(out_rows, w_out)
    out_cols = out_total.shape[1]
    leaving = call(
        functools.partial(out_grow_kernel, sizes, width),
        [shape((drafts, groups, out_cols))] * blocks,
        [VMEM] * 5,
        [],
        2 * count * owned * width * out_cols,
        8 * count * out_cols + 2 * owned * width * out_cols,
    )(out_total, slots, grow_out.reshape(owned * width, -1), *out_ranks)
    result = leaving[0].astype(jnp.float32)
    for shift in range(1, blocks):
        result = result + over_tensor(leaving[shift], shift).astype(jnp.float32)
    return jnp.transpose(result.astype(jnp.bfloat16), (1, 0, 2))


def rotate(vectors, positions):
    half_size = vectors.shape[-1] // 2
    frequency = rope_base ** (-2.0 * jnp.arange(half_size, dtype=jnp.float32) / vectors.shape[-1])
    angles = positions[:, None, None] * frequency
    cosine = jnp.cos(angles)
    sine_value = jnp.sin(angles)
    first_half = vectors[..., :half_size]
    second = vectors[..., half_size:]
    return jnp.concatenate(
        [first_half * cosine - second * sine_value, second * cosine + first_half * sine_value], -1
    )


def to_growers(partial, splits):
    total = None
    for shift in range(splits):
        route = [
            (t * splits + g, ((g + shift) % splits) * splits + t)
            for t in range(splits)
            for g in range(splits)
        ]
        got = lax.ppermute(partial, EVERY, route).astype(jnp.float32)
        total = got if total is None else total + got
    return total


def to_out_growers(partial, splits):
    total = None
    for shift in range(splits):
        route = [
            (t * splits + g, g * splits + (t + shift) % splits)
            for t in range(splits)
            for g in range(splits)
        ]
        got = lax.ppermute(partial, EVERY, route).astype(jnp.float32)
        total = got if total is None else total + got
    return total


def slot_table(adapter_ids, adapter_slots):
    matches = adapter_ids[:, None] == jnp.arange(adapter_slots.shape[0], dtype=jnp.int32)[None, :]
    return jnp.sum(jnp.where(matches, adapter_slots[None, :], 0), axis=1)


def attend(query_heads, key_new, value_new, cache_keys, cache_values, length):
    drafts, head_count, head_size = query_heads.shape
    kv_heads, cache_size, _ = cache_keys.shape
    positions = (length + jnp.arange(drafts, dtype=jnp.int32)).astype(jnp.float32)
    query_rot = rotate(query_heads.astype(jnp.float32), positions).astype(jnp.bfloat16)
    key_rot = rotate(key_new.astype(jnp.float32), positions).astype(jnp.bfloat16)
    grouped = query_rot.reshape(drafts, kv_heads, head_count // kv_heads, head_size)
    score_scale = 1.0 / math.sqrt(head_size)
    cached = (
        jnp.einsum("skgd,kld->skgl", grouped, cache_keys, preferred_element_type=jnp.float32)
        * score_scale
    )
    fresh_scores = (
        jnp.einsum("skgd,tkd->skgt", grouped, key_rot, preferred_element_type=jnp.float32)
        * score_scale
    )
    cache_mask = jnp.arange(cache_size, dtype=jnp.int32) < length
    draft_mask = jnp.arange(drafts)[None, :] <= jnp.arange(drafts)[:, None]
    cached = jnp.where(cache_mask[None, None, None, :], cached, -jnp.inf)
    fresh_scores = jnp.where(draft_mask[:, None, None, :], fresh_scores, -jnp.inf)
    row_peak = jnp.maximum(jnp.max(cached, -1), jnp.max(fresh_scores, -1))
    cached_exp = jnp.exp(cached - row_peak[..., None])
    fresh_exp = jnp.exp(fresh_scores - row_peak[..., None])
    denominator = jnp.sum(cached_exp, -1) + jnp.sum(fresh_exp, -1)
    cached_prob = (cached_exp / denominator[..., None]).astype(jnp.bfloat16)
    fresh_prob = (fresh_exp / denominator[..., None]).astype(jnp.bfloat16)
    mixed = jnp.einsum(
        "skgl,kld->skgd", cached_prob, cache_values, preferred_element_type=jnp.float32
    )
    mixed = mixed + jnp.einsum(
        "skgt,tkd->skgd", fresh_prob, value_new, preferred_element_type=jnp.float32
    )
    return mixed.astype(jnp.bfloat16)


def by_row(
    tokens,
    w_query,
    w_key,
    w_value,
    w_out,
    shrink_qkv,
    grow_query,
    grow_key,
    grow_value,
    shrink_out,
    grow_out,
    cache_keys,
    cache_values,
    cache_lengths,
    adapter_ids,
    adapter_slots,
):
    splits = lax.axis_size("tensor")
    groups = lax.axis_size(("dp", "pipe"))
    tensor_index = lax.axis_index("tensor")
    group_index = lax.axis_index(("dp", "pipe"))
    local_rows, drafts, feature_width = tokens.shape
    per_owner = shrink_qkv.shape[0]
    rank_size = grow_out.shape[1]
    query_cols = w_query.shape[1]
    key_cols = w_key.shape[1]
    kv_heads = cache_keys.shape[1]
    head_size = cache_keys.shape[3]
    rows = splits * groups
    row_slots = jnp.repeat(slot_table(adapter_ids, adapter_slots), drafts)
    within = jnp.arange(per_owner, dtype=jnp.int32)[None, :]
    width_hot = (row_slots[:, None] == within + tensor_index * per_owner)[:, :, None]
    column_hot = (row_slots[:, None] == within + group_index * per_owner)[:, :, None]

    def spread_ranks(ranks, hot):
        return jnp.where(hot, ranks[:, None, :], 0.0).reshape(rows * drafts, -1).astype(jnp.bfloat16)

    flat_tokens = lax.all_gather(tokens, "tensor", axis=0, tiled=True).reshape(
        rows * drafts, feature_width
    )
    rank_part = jnp.einsum(
        "nd,adr->nar", flat_tokens, shrink_qkv, preferred_element_type=jnp.float32
    )
    rank_part = jnp.sum(jnp.where(width_hot, rank_part, 0.0), 1)
    rank_all = to_growers(rank_part.astype(jnp.bfloat16), splits)

    def grown(index, grow):
        ranks = spread_ranks(rank_all[:, index * rank_size : (index + 1) * rank_size], column_hot)
        return jnp.dot(
            ranks, grow.reshape(per_owner * rank_size, -1), preferred_element_type=jnp.float32
        )

    bases = [
        jnp.dot(flat_tokens, weight, preferred_element_type=jnp.float32)
        for weight in (w_query, w_key, w_value)
    ]

    def product(index, grow):
        return (bases[index] + grown(index, grow)).astype(jnp.bfloat16).reshape(rows, drafts, -1)

    partial = jnp.concatenate(
        [
            product(0, grow_query),
            product(1, grow_key),
            product(2, grow_value),
        ],
        2,
    )
    arrived = lax.all_to_all(partial, EVERY, split_axis=0, concat_axis=0, tiled=True)
    joined = jnp.sum(
        arrived.reshape(splits, groups, drafts, -1).astype(jnp.float32), 1
    ).astype(jnp.bfloat16)
    joined = jnp.transpose(joined, (1, 0, 2))
    query_heads = joined[:, :, :query_cols].reshape(drafts, -1, head_size)
    key_new = joined[:, :, query_cols : query_cols + key_cols].reshape(drafts, kv_heads, head_size)
    value_new = joined[:, :, query_cols + key_cols :].reshape(drafts, kv_heads, head_size)
    mixed = attend(
        query_heads, key_new, value_new, cache_keys[0], cache_values[0], cache_lengths[0]
    )
    mixed = jnp.transpose(mixed.reshape(drafts, splits, -1), (1, 0, 2))
    outgoing = jnp.repeat(mixed, groups, axis=0)
    flat_heads = lax.all_to_all(
        outgoing, EVERY, split_axis=0, concat_axis=0, tiled=True
    ).reshape(rows * drafts, -1)
    out_part = jnp.einsum(
        "nw,awr->nar", flat_heads, shrink_out, preferred_element_type=jnp.float32
    )
    out_part = jnp.sum(jnp.where(column_hot, out_part, 0.0), 1)
    out_rank = to_out_growers(out_part.astype(jnp.bfloat16), splits)
    out = jnp.dot(flat_heads, w_out, preferred_element_type=jnp.float32)
    out = out + jnp.dot(
        spread_ranks(out_rank, width_hot),
        grow_out.reshape(per_owner * rank_size, -1),
        preferred_element_type=jnp.float32,
    )
    blocks = lax.all_to_all(
        out.astype(jnp.bfloat16).reshape(splits, local_rows, drafts, feature_width),
        "tensor",
        split_axis=0,
        concat_axis=0,
        tiled=True,
    )
    return jnp.sum(blocks.astype(jnp.float32), 0).astype(jnp.bfloat16)


def local(*arrays):
    heads = arrays[11].shape[1]
    sizes = [lax.axis_size(name) for name in EVERY]
    if heads == 4 and sizes == [4, 2, 2]:
        return by_kernels(*arrays)
    return by_row(*arrays)


def solution(mesh):
    placed = (
        P(("parts", "tensor"), None, ("dp", "pipe")),
        P(("dp", "pipe"), "tensor"),
        P(("dp", "pipe"), "tensor"),
        P(("dp", "pipe"), "tensor"),
        P("tensor", ("dp", "pipe")),
        P("tensor", ("dp", "pipe"), None),
        P(("dp", "pipe"), None, "tensor"),
        P(("dp", "pipe"), None, "tensor"),
        P(("dp", "pipe"), None, "tensor"),
        P(("dp", "pipe"), "tensor", None),
        P("tensor", None, ("dp", "pipe")),
        P(("parts", "tensor", "dp", "pipe"), None, None, None),
        P(("parts", "tensor", "dp", "pipe"), None, None, None),
        P(("parts", "tensor", "dp", "pipe")),
        P(),
        P(),
    )
    return jax.shard_map(
        local,
        mesh=mesh,
        in_specs=placed,
        out_specs=P(("parts", "tensor"), None, ("dp", "pipe")),
        check_vma=False,
    )
```

```python
import functools
import math

import jax
import jax.numpy as jnp
import numpy as np
from jax import lax
from jax.experimental import pallas as pl
from jax.experimental.pallas import tpu as pltpu
from jax.sharding import PartitionSpec as P

rope_base = 500000.0
EVERY = ("tensor", "dp", "pipe")
GROUP = ("dp", "pipe")
VMEM = pl.BlockSpec(memory_space=pltpu.VMEM)
HBM = pl.BlockSpec(memory_space=pltpu.HBM)
MIB = 1 << 20


def dot(left, right):
    return jnp.dot(left, right, preferred_element_type=jnp.float32)


def dot_nt(left, right):
    return lax.dot_general(
        left, right, (((1,), (1,)), ((), ())), preferred_element_type=jnp.float32
    )


def iota(shape, axis):
    return lax.broadcasted_iota(jnp.int32, shape, axis)


def call(kernel, outs, ins, scratch=(), flops=0, moved=0, limit=24 * MIB):
    return pl.pallas_call(
        kernel,
        out_shape=outs,
        in_specs=ins,
        out_specs=jax.tree.map(lambda _: VMEM, outs),
        scratch_shapes=list(scratch),
        cost_estimate=pl.CostEstimate(flops=flops, bytes_accessed=moved, transcendentals=0),
        compiler_params=pltpu.CompilerParams(vmem_limit_bytes=limit),
    )


def shape(dims, kind=jnp.bfloat16):
    return jax.ShapeDtypeStruct(tuple(dims), kind)


def over(value, size):
    return value >> (size.bit_length() - 1) if size & (size - 1) == 0 else lax.div(value, size)


def rest_of(value, size):
    return value & (size - 1) if size & (size - 1) == 0 else lax.rem(value, size)


def as_gathered(sizes, group, block, draft):
    groups, blocks, drafts = sizes
    return (block * drafts + draft) * groups + group


def by_draft(sizes, group, block, draft):
    groups, blocks, drafts = sizes
    return (draft * blocks + block) * groups + group


def parts_of(order, sizes, index):
    groups, blocks, drafts = sizes
    group, left = rest_of(index, groups), over(index, groups)
    if order is as_gathered:
        return group, over(left, drafts), rest_of(left, drafts)
    return group, rest_of(left, blocks), over(left, blocks)


def turned(block):
    return lax.axis_index("tensor") ^ block


def reorder(sizes, after, before):
    groups, blocks, drafts = sizes
    rows = groups * blocks * drafts
    group, block, draft = parts_of(after, sizes, iota((rows, rows), 0))
    wanted = before(sizes, group, turned(block), draft)
    return jnp.where(wanted == iota((rows, rows), 1), 1.0, 0.0).astype(jnp.bfloat16)


def group_of():
    return lax.axis_index("dp") * lax.axis_size("pipe") + lax.axis_index("pipe")


def rank_kernel(sizes, owned, *refs):
    groups, blocks, drafts = sizes
    pieces = refs[:blocks]
    shrink_ref, slots_ref = refs[blocks : blocks + 2]
    rows_ref, rank_ref, wide = refs[-3:]
    for block in range(blocks):
        for draft in range(drafts):
            start = (block * drafts + draft) * groups
            wide[start : start + groups, :] = pieces[block][draft].astype(jnp.float32)
    rows = wide[...].astype(jnp.bfloat16)
    rows_ref[...] = rows
    place = slots_ref[:, 0:1] - lax.axis_index("tensor") * owned
    ranks = owned_ranks(
        rows, shrink_ref[...], place, shrink_ref.shape[0] // owned, rank_ref.shape[1]
    )
    put = (rank_ref.shape[0], rows.shape[0])
    draft = parts_of(as_gathered, sizes, iota((rows.shape[0], put[0]), 0))[2]
    line = slots_ref[:, 2:3] * drafts + draft
    put = jnp.where(line == iota((rows.shape[0], put[0]), 1), 1.0, 0.0).astype(jnp.bfloat16)
    ranks = lax.dot_general(
        put, ranks, (((0,), (0,)), ((), ())), preferred_element_type=jnp.float32
    )
    rank_ref[...] = ranks.astype(jnp.bfloat16)


def owned_ranks(rows, shrink, place, width, lanes):
    ranks = dot_nt(rows, shrink)
    kept = jnp.where(over(iota(ranks.shape, 1), width) == place, ranks, 0.0).astype(jnp.bfloat16)
    fold = (ranks.shape[1], lanes)
    fold = rest_of(iota(fold, 0), width) == iota(fold, 1)
    return dot(kept, jnp.where(fold, 1.0, 0.0).astype(jnp.bfloat16)).astype(jnp.bfloat16)


def spread_ranks(ranks, place, width, owned, parts):
    span = owned * width
    row = iota((ranks.shape[1], parts * span), 0)
    column = iota((ranks.shape[1], parts * span), 1)
    tile = (over(row, width) == over(column, span)) & (
        rest_of(row, width) == rest_of(column, width)
    )
    wide = dot(ranks, jnp.where(tile, 1.0, 0.0).astype(jnp.bfloat16))
    slot = over(rest_of(iota(wide.shape, 1), span), width)
    return jnp.where(slot == place, wide, 0.0).astype(jnp.bfloat16)


def product_kernel(rows_ref, *refs):
    *weights, total_ref = refs
    start = 0
    for weight in weights:
        width = weight.shape[1]
        step = width if width % 1024 else 1024
        for first in range(0, width, step):
            total_ref[:, start : start + step] = dot(
                rows_ref[...], weight[:, first : first + step]
            )
            start += step


def product(rows, *weights):
    width = sum(weight.shape[1] for weight in weights)
    return call(
        product_kernel,
        shape((rows.shape[0], width), jnp.float32),
        [VMEM] * (1 + len(weights)),
    )(rows, *weights)


def prepare_kernel(sizes, owned, ids_ref, pool_ref, length_ref, *refs):
    slots_ref, cosine_ref, sine_ref = refs[-3:]
    groups, blocks, drafts = sizes
    width = cosine_ref.shape[1]
    lane = iota(cosine_ref.shape, 1)
    half = (lane & (width // 2 - 1)).astype(jnp.float32)
    positions = (lax.rem(iota(cosine_ref.shape, 0), drafts) + length_ref[0]).astype(jnp.float32)
    angles = positions * jnp.exp(half * (-2.0 * math.log(rope_base) / width))
    cosine_ref[...] = jnp.cos(angles)
    sine_ref[...] = jnp.sin(angles) * jnp.where(lane < width // 2, -1.0, 1.0)
    index = iota(slots_ref.shape, 0)
    column = iota(slots_ref.shape, 1)
    near = parts_of(as_gathered, sizes, index)
    far = parts_of(by_draft, sizes, index)
    row_group = jnp.where(column == 1, far[0], near[0])
    row_block = jnp.where(column == 1, far[1], turned(near[1]))
    place = row_block * groups + row_group
    slots = jnp.zeros(slots_ref.shape, jnp.int32)
    sent, taken = 0, 0
    for row in range(blocks * groups):
        slot = pool_ref[ids_ref[row]]
        owner = over(slot, owned)
        sends = jnp.where(owner == lax.axis_index("tensor"), 1, 0)
        takes = jnp.where(owner == group_of(), 1, 0)
        line = jnp.where(column == 2, sent - 64 * (1 - sends), taken - 64 * (1 - takes))
        slots = jnp.where(place == row, jnp.where(column < 2, slot, line), slots)
        sent, taken = sent + sends, taken + takes
    slots_ref[...] = slots


def prepare(sizes, owned, ids, pool, lengths, table, later):
    groups, blocks, drafts = sizes
    smem = pl.BlockSpec(memory_space=pltpu.SMEM)
    table = shape(table, jnp.float32)
    return call(
        functools.partial(prepare_kernel, sizes, owned),
        [shape((groups * blocks * drafts, 128), jnp.int32), table, table],
        [smem, smem, smem] + [HBM] * 3,
        limit=40 * MIB,
    )(ids, pool, lengths, *[later] * 3)


def grow_kernel(sizes, width, total_ref, slots_ref, *refs):
    groups, blocks, drafts = sizes
    ranks_in, grows, (out_ref, held) = refs[:2], refs[2:5], refs[-2:]
    group = group_of()
    requests = groups * blocks
    lines = out_ref.shape[1]
    held[...] = jnp.zeros(held.shape, jnp.float32)
    owned = grows[0].shape[0] // width
    ranks = ranks_in[0][...].astype(jnp.float32)
    for other in ranks_in[1:]:
        ranks = ranks + other[...].astype(jnp.float32)
    get = (total_ref.shape[0], ranks.shape[0])
    draft = parts_of(as_gathered, sizes, iota(get, 0))[2]
    get = slots_ref[:, 3:4] * drafts + draft == iota(get, 1)
    ranks = dot(jnp.where(get, 1.0, 0.0).astype(jnp.bfloat16), ranks.astype(jnp.bfloat16))
    place = slots_ref[:, 0:1] - group * owned
    wide = spread_ranks(ranks.astype(jnp.bfloat16), place, width, owned, len(grows))
    arranged = reorder(sizes, by_draft, as_gathered)
    start, column = 0, 0
    for index, grow in enumerate(grows):
        deep, cols = grow.shape
        full = total_ref[:, column : column + cols] + dot(
            wide[:, index * deep : (index + 1) * deep], grow[...]
        )
        column += cols
        full = dot(arranged, full.astype(jnp.bfloat16))
        for head in range(cols // 128):
            for draft in range(drafts):
                held[pl.ds(start + draft, requests, stride=lines), :] = full[
                    draft * requests : (draft + 1) * requests, head * 128 : (head + 1) * 128
                ]
            start += drafts
    for row in range(requests):
        out_ref[row] = held[row * lines : (row + 1) * lines, :].astype(jnp.bfloat16)


def attend_kernel(
    sizes, arrived_ref, keys_ref, values_ref, length_ref, cosine_ref, sine_ref, out_ref, *scratch
):
    groups, blocks, drafts = sizes
    (fresh_s,) = scratch
    cache_size, head_size = keys_ref.shape[2:]
    count = out_ref.shape[1]
    scale = 1.0 / math.sqrt(head_size)
    fresh_s[...] = jnp.zeros(fresh_s.shape, jnp.float32)
    for block in range(blocks):
        joined = arrived_ref[block * groups].astype(jnp.float32)
        for other in range(1, groups):
            joined = joined + arrived_ref[block * groups + other].astype(jnp.float32)
        joined = joined.astype(jnp.bfloat16).astype(jnp.float32)
        rotated = joined * cosine_ref[...] + pltpu.roll(joined, head_size // 2, 1) * sine_ref[...]
        fresh_s[2 * block, 0:drafts, :] = rotated[count : count + drafts]
        fresh_s[2 * block + 1, 0:drafts, :] = joined[count + drafts : count + 2 * drafts]
        query = rotated[0:count].astype(jnp.bfloat16)
        old = dot_nt(query, keys_ref[0, block]) * scale
        new = dot_nt(query, fresh_s[2 * block].astype(jnp.bfloat16)) * scale
        old = jnp.where(iota(old.shape, 1) < length_ref[0], old, -jnp.inf)
        seen = iota(new.shape, 1) <= lax.rem(iota(new.shape, 0), drafts)
        new = jnp.where(seen, new, -jnp.inf)
        peak = jnp.maximum(jnp.max(old, 1, keepdims=True), jnp.max(new, 1, keepdims=True))
        old = jnp.exp(old - peak)
        new = jnp.exp(new - peak)
        below = jnp.sum(old, 1, keepdims=True) + jnp.sum(new, 1, keepdims=True)
        mixed = dot((old / below).astype(jnp.bfloat16), values_ref[0, block]) + dot(
            (new / below).astype(jnp.bfloat16), fresh_s[2 * block + 1].astype(jnp.bfloat16)
        )
        mixed = mixed.astype(jnp.bfloat16)
        for target in range(groups):
            out_ref[block * groups + target] = mixed


def add_kernel(left_ref, right_ref, out_ref):
    total = left_ref[...].astype(jnp.float32) + right_ref[...].astype(jnp.float32)
    out_ref[...] = total.astype(jnp.bfloat16)


def packing(rows, width, lanes):
    parts = lanes // width
    return parts, rows // parts


def out_rank_kernel(sizes, owned, got_ref, shrink_ref, slots_ref, *refs):
    rows_ref, rank_ref, wide = refs[-3:]
    drafts = sizes[2]
    requests, lines, head_size = got_ref.shape
    for row in range(requests):
        wide[row * lines : (row + 1) * lines, :] = got_ref[row].astype(jnp.float32)
    for head in range(lines // drafts):
        for draft in range(drafts):
            rows_ref[
                draft * requests : (draft + 1) * requests,
                head * head_size : (head + 1) * head_size,
            ] = wide[pl.ds(head * drafts + draft, requests, stride=lines), :].astype(jnp.bfloat16)
    rows = rows_ref[...]
    place = slots_ref[:, 1:2] - group_of() * owned
    width = shrink_ref.shape[0] // owned
    held, lanes = rank_ref.shape
    parts, span = packing(rows.shape[0], width, lanes)
    ranks = dot_nt(rows, shrink_ref[...])
    kept = jnp.where(over(iota(ranks.shape, 1), width) == place, ranks, 0.0).astype(jnp.bfloat16)
    fold = (ranks.shape[1], lanes)
    fold = rest_of(iota(fold, 0), width) == rest_of(iota(fold, 1), width)
    ranks = dot(kept, jnp.where(fold, 1.0, 0.0).astype(jnp.bfloat16))
    mine = over(iota(ranks.shape, 1), width) == over(iota(ranks.shape, 0), span)
    ranks = jnp.where(mine, ranks, 0.0).astype(jnp.bfloat16)
    put = (held, rows.shape[0])
    put = iota(put, 0) == rest_of(iota(put, 1), span)
    ranks = dot(jnp.where(put, 1.0, 0.0).astype(jnp.bfloat16), ranks)
    rank_ref[...] = ranks.astype(jnp.bfloat16)


def out_grow_kernel(sizes, width, total_ref, slots_ref, grow_ref, *refs):
    groups, blocks, drafts = sizes
    ranks_in, outs = refs[:blocks], refs[blocks:]
    owned = grow_ref.shape[0] // width
    me = lax.axis_index("tensor")
    ranks = ranks_in[0][...].astype(jnp.float32)
    for other in ranks_in[1:]:
        ranks = ranks + other[...].astype(jnp.float32)
    count = total_ref.shape[0]
    held, lanes = ranks.shape
    parts, span = packing(count, width, lanes)
    put = rest_of(iota((count, held), 0), span) == iota((count, held), 1)
    ranks = dot(jnp.where(put, 1.0, 0.0).astype(jnp.bfloat16), ranks.astype(jnp.bfloat16))
    mine = over(iota(ranks.shape, 1), width) == over(iota(ranks.shape, 0), span)
    ranks = jnp.where(mine, ranks, 0.0).astype(jnp.bfloat16)
    tile = (lanes, owned * width)
    tile = rest_of(iota(tile, 0), width) == rest_of(iota(tile, 1), width)
    ranks = dot(ranks, jnp.where(tile, 1.0, 0.0).astype(jnp.bfloat16))
    place = slots_ref[:, 1:2] - me * owned
    wide = jnp.where(over(iota(ranks.shape, 1), width) == place, ranks, 0.0).astype(jnp.bfloat16)
    full = (total_ref[...] + dot(wide, grow_ref[...])).astype(jnp.bfloat16)
    full = dot(reorder(sizes, as_gathered, by_draft), full).astype(jnp.bfloat16)
    for block in range(blocks):
        for draft in range(drafts):
            start = (block * drafts + draft) * groups
            outs[block][draft] = full[start : start + groups]


def by_kernels(
    tokens,
    w_query,
    w_key,
    w_value,
    w_out,
    shrink_qkv,
    grow_query,
    grow_key,
    grow_value,
    shrink_out,
    grow_out,
    cache_keys,
    cache_values,
    cache_lengths,
    adapter_ids,
    adapter_slots,
):
    blocks = lax.axis_size("tensor")
    groups = lax.axis_size(GROUP)
    _, drafts, features = tokens.shape
    sizes = (groups, blocks, drafts)
    owned = shrink_qkv.shape[0]
    width = grow_out.shape[1]
    head_size = cache_keys.shape[3]
    span = blocks * drafts
    count = groups * span
    lanes = -(-shrink_qkv.shape[2] // 128) * 128

    def over_tensor(value, shift):
        route = [(t, t ^ shift) for t in range(blocks)]
        return lax.ppermute(value, "tensor", route)

    def over_core(value):
        return lax.ppermute(value, "pipe", [(0, 1), (1, 0)])

    def to_growers(value, flip):
        route = [
            (t * groups + 2 * x + c, (2 * c + (x ^ flip)) * groups + t)
            for t in range(blocks)
            for x in range(2)
            for c in range(2)
        ]
        return lax.ppermute(value, EVERY, route)

    def to_out_growers(value, shift):
        route = [
            (t * groups + g, g * groups + (t + shift) % groups)
            for t in range(blocks)
            for g in range(groups)
        ]
        return lax.ppermute(value, EVERY, route)

    def added(left, right):
        return call(add_kernel, shape(left.shape), [VMEM] * 2)(left, right)

    def exchange(value):
        return lax.all_to_all(value, EVERY, split_axis=0, concat_axis=0, tiled=True)

    mine = jnp.transpose(tokens, (1, 0, 2))
    pieces = [mine] + [over_tensor(mine, shift) for shift in range(1, blocks)]

    lines = (w_query.shape[1] // head_size + 2) * drafts
    lines = -(-lines // 8) * 8
    slots, cosine, sine = prepare(
        sizes, owned, adapter_ids, adapter_slots, cache_lengths, (lines, head_size), w_out
    )
    packed = -(-2 * blocks * drafts // 16) * 16
    shrink_in = jnp.transpose(shrink_qkv, (0, 2, 1)).reshape(-1, features)
    rows, rank_part = call(
        functools.partial(rank_kernel, sizes, owned),
        [shape((count, features)), shape((packed, lanes))],
        [VMEM] * (blocks + 2),
        [pltpu.VMEM((count, features), jnp.float32)],
        2 * count * shrink_qkv.size,
        2 * shrink_qkv.size + 4 * count * features,
    )(*pieces, shrink_in, slots)
    rank_part = added(rank_part, over_core(rank_part))
    ranks = [to_growers(rank_part, flip) for flip in range(2)]
    total = product(rows, w_query, w_key, w_value)
    cols = total.shape[1]
    head_cols = w_query.shape[1]
    query_lines = head_cols // head_size * drafts
    sent = call(
        functools.partial(grow_kernel, sizes, width),
        shape((blocks * groups, lines, head_size)),
        [VMEM] * 7 + [HBM] * 2,
        [pltpu.VMEM((blocks * groups * lines, head_size), jnp.float32)],
        limit=40 * MIB,
    )(
        total,
        slots,
        *ranks,
        *[grow.reshape(owned * width, -1) for grow in (grow_query, grow_key, grow_value)],
        *[w_out] * 2,
    )
    mixed = call(
        functools.partial(attend_kernel, sizes),
        shape((blocks * groups, query_lines, head_size)),
        [VMEM] * 3 + [pl.BlockSpec(memory_space=pltpu.SMEM)] + [VMEM] * 2,
        [pltpu.VMEM((2 * blocks, 128, head_size), jnp.float32)],
    )(exchange(sent), cache_keys, cache_values, cache_lengths, cosine, sine)
    gathered = exchange(mixed)
    held = -(-packing(count, width, 128)[1] // 16) * 16
    out_rows, out_part = call(
        functools.partial(out_rank_kernel, sizes, owned),
        [shape((count, head_cols)), shape((held, 128))],
        [VMEM] * 3 + [HBM] * 4,
        [pltpu.VMEM((blocks * groups * query_lines, head_size), jnp.float32)],
        limit=40 * MIB,
    )(gathered, jnp.transpose(shrink_out, (0, 2, 1)).reshape(-1, head_cols), slots, *[w_query] * 4)
    out_ranks = [to_out_growers(out_part, shift) for shift in range(blocks)]
    out_total = product(out_rows, w_out)
    out_cols = out_total.shape[1]
    leaving = call(
        functools.partial(out_grow_kernel, sizes, width),
        [shape((drafts, groups, out_cols))] * blocks,
        [VMEM] * (3 + blocks),
        [],
        2 * count * owned * width * out_cols,
        8 * count * out_cols + 2 * owned * width * out_cols,
    )(out_total, slots, grow_out.reshape(owned * width, -1), *out_ranks)
    result = leaving[0].astype(jnp.float32)
    for shift in range(1, blocks):
        result = result + over_tensor(leaving[shift], shift).astype(jnp.float32)
    return jnp.transpose(result.astype(jnp.bfloat16), (1, 0, 2))


def rotate(vectors, positions):
    half_size = vectors.shape[-1] // 2
    frequency = rope_base ** (-2.0 * jnp.arange(half_size, dtype=jnp.float32) / vectors.shape[-1])
    angles = positions[:, None, None] * frequency
    cosine = jnp.cos(angles)
    sine_value = jnp.sin(angles)
    first_half = vectors[..., :half_size]
    second = vectors[..., half_size:]
    return jnp.concatenate(
        [first_half * cosine - second * sine_value, second * cosine + first_half * sine_value], -1
    )


def to_growers(partial, splits):
    total = None
    for shift in range(splits):
        route = [
            (t * splits + g, ((g + shift) % splits) * splits + t)
            for t in range(splits)
            for g in range(splits)
        ]
        got = lax.ppermute(partial, EVERY, route).astype(jnp.float32)
        total = got if total is None else total + got
    return total


def to_out_growers(partial, splits):
    total = None
    for shift in range(splits):
        route = [
            (t * splits + g, g * splits + (t + shift) % splits)
            for t in range(splits)
            for g in range(splits)
        ]
        got = lax.ppermute(partial, EVERY, route).astype(jnp.float32)
        total = got if total is None else total + got
    return total


def slot_table(adapter_ids, adapter_slots):
    matches = adapter_ids[:, None] == jnp.arange(adapter_slots.shape[0], dtype=jnp.int32)[None, :]
    return jnp.sum(jnp.where(matches, adapter_slots[None, :], 0), axis=1)


def attend(query_heads, key_new, value_new, cache_keys, cache_values, length):
    drafts, head_count, head_size = query_heads.shape
    kv_heads, cache_size, _ = cache_keys.shape
    positions = (length + jnp.arange(drafts, dtype=jnp.int32)).astype(jnp.float32)
    query_rot = rotate(query_heads.astype(jnp.float32), positions).astype(jnp.bfloat16)
    key_rot = rotate(key_new.astype(jnp.float32), positions).astype(jnp.bfloat16)
    grouped = query_rot.reshape(drafts, kv_heads, head_count // kv_heads, head_size)
    score_scale = 1.0 / math.sqrt(head_size)
    cached = (
        jnp.einsum("skgd,kld->skgl", grouped, cache_keys, preferred_element_type=jnp.float32)
        * score_scale
    )
    fresh_scores = (
        jnp.einsum("skgd,tkd->skgt", grouped, key_rot, preferred_element_type=jnp.float32)
        * score_scale
    )
    cache_mask = jnp.arange(cache_size, dtype=jnp.int32) < length
    draft_mask = jnp.arange(drafts)[None, :] <= jnp.arange(drafts)[:, None]
    cached = jnp.where(cache_mask[None, None, None, :], cached, -jnp.inf)
    fresh_scores = jnp.where(draft_mask[:, None, None, :], fresh_scores, -jnp.inf)
    row_peak = jnp.maximum(jnp.max(cached, -1), jnp.max(fresh_scores, -1))
    cached_exp = jnp.exp(cached - row_peak[..., None])
    fresh_exp = jnp.exp(fresh_scores - row_peak[..., None])
    denominator = jnp.sum(cached_exp, -1) + jnp.sum(fresh_exp, -1)
    cached_prob = (cached_exp / denominator[..., None]).astype(jnp.bfloat16)
    fresh_prob = (fresh_exp / denominator[..., None]).astype(jnp.bfloat16)
    mixed = jnp.einsum(
        "skgl,kld->skgd", cached_prob, cache_values, preferred_element_type=jnp.float32
    )
    mixed = mixed + jnp.einsum(
        "skgt,tkd->skgd", fresh_prob, value_new, preferred_element_type=jnp.float32
    )
    return mixed.astype(jnp.bfloat16)


def by_row(
    tokens,
    w_query,
    w_key,
    w_value,
    w_out,
    shrink_qkv,
    grow_query,
    grow_key,
    grow_value,
    shrink_out,
    grow_out,
    cache_keys,
    cache_values,
    cache_lengths,
    adapter_ids,
    adapter_slots,
):
    splits = lax.axis_size("tensor")
    groups = lax.axis_size(("dp", "pipe"))
    tensor_index = lax.axis_index("tensor")
    group_index = lax.axis_index(("dp", "pipe"))
    local_rows, drafts, feature_width = tokens.shape
    per_owner = shrink_qkv.shape[0]
    rank_size = grow_out.shape[1]
    query_cols = w_query.shape[1]
    key_cols = w_key.shape[1]
    kv_heads = cache_keys.shape[1]
    head_size = cache_keys.shape[3]
    rows = splits * groups
    row_slots = jnp.repeat(slot_table(adapter_ids, adapter_slots), drafts)
    within = jnp.arange(per_owner, dtype=jnp.int32)[None, :]
    width_hot = (row_slots[:, None] == within + tensor_index * per_owner)[:, :, None]
    column_hot = (row_slots[:, None] == within + group_index * per_owner)[:, :, None]

    def spread_ranks(ranks, hot):
        return jnp.where(hot, ranks[:, None, :], 0.0).reshape(rows * drafts, -1).astype(jnp.bfloat16)

    flat_tokens = lax.all_gather(tokens, "tensor", axis=0, tiled=True).reshape(
        rows * drafts, feature_width
    )
    rank_part = jnp.einsum(
        "nd,adr->nar", flat_tokens, shrink_qkv, preferred_element_type=jnp.float32
    )
    rank_part = jnp.sum(jnp.where(width_hot, rank_part, 0.0), 1)
    rank_all = to_growers(rank_part.astype(jnp.bfloat16), splits)

    def grown(index, grow):
        ranks = spread_ranks(rank_all[:, index * rank_size : (index + 1) * rank_size], column_hot)
        return jnp.dot(
            ranks, grow.reshape(per_owner * rank_size, -1), preferred_element_type=jnp.float32
        )

    bases = [
        jnp.dot(flat_tokens, weight, preferred_element_type=jnp.float32)
        for weight in (w_query, w_key, w_value)
    ]

    def product(index, grow):
        return (bases[index] + grown(index, grow)).astype(jnp.bfloat16).reshape(rows, drafts, -1)

    partial = jnp.concatenate(
        [
            product(0, grow_query),
            product(1, grow_key),
            product(2, grow_value),
        ],
        2,
    )
    arrived = lax.all_to_all(partial, EVERY, split_axis=0, concat_axis=0, tiled=True)
    joined = jnp.sum(
        arrived.reshape(splits, groups, drafts, -1).astype(jnp.float32), 1
    ).astype(jnp.bfloat16)
    joined = jnp.transpose(joined, (1, 0, 2))
    query_heads = joined[:, :, :query_cols].reshape(drafts, -1, head_size)
    key_new = joined[:, :, query_cols : query_cols + key_cols].reshape(drafts, kv_heads, head_size)
    value_new = joined[:, :, query_cols + key_cols :].reshape(drafts, kv_heads, head_size)
    mixed = attend(
        query_heads, key_new, value_new, cache_keys[0], cache_values[0], cache_lengths[0]
    )
    mixed = jnp.transpose(mixed.reshape(drafts, splits, -1), (1, 0, 2))
    outgoing = jnp.repeat(mixed, groups, axis=0)
    flat_heads = lax.all_to_all(
        outgoing, EVERY, split_axis=0, concat_axis=0, tiled=True
    ).reshape(rows * drafts, -1)
    out_part = jnp.einsum(
        "nw,awr->nar", flat_heads, shrink_out, preferred_element_type=jnp.float32
    )
    out_part = jnp.sum(jnp.where(column_hot, out_part, 0.0), 1)
    out_rank = to_out_growers(out_part.astype(jnp.bfloat16), splits)
    out = jnp.dot(flat_heads, w_out, preferred_element_type=jnp.float32)
    out = out + jnp.dot(
        spread_ranks(out_rank, width_hot),
        grow_out.reshape(per_owner * rank_size, -1),
        preferred_element_type=jnp.float32,
    )
    blocks = lax.all_to_all(
        out.astype(jnp.bfloat16).reshape(splits, local_rows, drafts, feature_width),
        "tensor",
        split_axis=0,
        concat_axis=0,
        tiled=True,
    )
    return jnp.sum(blocks.astype(jnp.float32), 0).astype(jnp.bfloat16)


def local(*arrays):
    heads = arrays[11].shape[1]
    sizes = [lax.axis_size(name) for name in EVERY]
    if heads == 4 and sizes == [4, 2, 2]:
        return by_kernels(*arrays)
    return by_row(*arrays)


def solution(mesh):
    placed = (
        P(("parts", "tensor"), None, ("dp", "pipe")),
        P(("dp", "pipe"), "tensor"),
        P(("dp", "pipe"), "tensor"),
        P(("dp", "pipe"), "tensor"),
        P("tensor", ("dp", "pipe")),
        P("tensor", ("dp", "pipe"), None),
        P(("dp", "pipe"), None, "tensor"),
        P(("dp", "pipe"), None, "tensor"),
        P(("dp", "pipe"), None, "tensor"),
        P(("dp", "pipe"), "tensor", None),
        P("tensor", None, ("dp", "pipe")),
        P(("parts", "tensor", "dp", "pipe"), None, None, None),
        P(("parts", "tensor", "dp", "pipe"), None, None, None),
        P(("parts", "tensor", "dp", "pipe")),
        P(),
        P(),
    )
    return jax.shard_map(
        local,
        mesh=mesh,
        in_specs=placed,
        out_specs=P(("parts", "tensor"), None, ("dp", "pipe")),
        check_vma=False,
    )
```

```python
import functools
import math

import jax
import jax.numpy as jnp
import numpy as np
from jax import lax
from jax.experimental import pallas as pl
from jax.experimental.pallas import tpu as pltpu
from jax.sharding import PartitionSpec as P

rope_base = 500000.0
EVERY = ("tensor", "dp", "pipe")
GROUP = ("dp", "pipe")
VMEM = pl.BlockSpec(memory_space=pltpu.VMEM)
HBM = pl.BlockSpec(memory_space=pltpu.HBM)
MIB = 1 << 20


def dot(left, right):
    return jnp.dot(left, right, preferred_element_type=jnp.float32)


def dot_nt(left, right):
    return lax.dot_general(
        left, right, (((1,), (1,)), ((), ())), preferred_element_type=jnp.float32
    )


def iota(shape, axis):
    return lax.broadcasted_iota(jnp.int32, shape, axis)


def call(kernel, outs, ins, scratch=(), flops=0, moved=0, limit=24 * MIB):
    return pl.pallas_call(
        kernel,
        out_shape=outs,
        in_specs=ins,
        out_specs=jax.tree.map(lambda _: VMEM, outs),
        scratch_shapes=list(scratch),
        cost_estimate=pl.CostEstimate(flops=flops, bytes_accessed=moved, transcendentals=0),
        compiler_params=pltpu.CompilerParams(vmem_limit_bytes=limit),
    )


def shape(dims, kind=jnp.bfloat16):
    return jax.ShapeDtypeStruct(tuple(dims), kind)


def over(value, size):
    return value >> (size.bit_length() - 1) if size & (size - 1) == 0 else lax.div(value, size)


def rest_of(value, size):
    return value & (size - 1) if size & (size - 1) == 0 else lax.rem(value, size)


def as_gathered(sizes, group, block, draft):
    groups, blocks, drafts = sizes
    return (block * drafts + draft) * groups + group


def by_draft(sizes, group, block, draft):
    groups, blocks, drafts = sizes
    return (draft * blocks + block) * groups + group


def parts_of(order, sizes, index):
    groups, blocks, drafts = sizes
    group, left = rest_of(index, groups), over(index, groups)
    if order is as_gathered:
        return group, over(left, drafts), rest_of(left, drafts)
    return group, rest_of(left, blocks), over(left, blocks)


def turned(block):
    return lax.axis_index("tensor") ^ block


def reorder(sizes, after, before):
    groups, blocks, drafts = sizes
    rows = groups * blocks * drafts
    group, block, draft = parts_of(after, sizes, iota((rows, rows), 0))
    wanted = before(sizes, group, turned(block), draft)
    return jnp.where(wanted == iota((rows, rows), 1), 1.0, 0.0).astype(jnp.bfloat16)


def group_of():
    return lax.axis_index("dp") * lax.axis_size("pipe") + lax.axis_index("pipe")


def rank_kernel(sizes, owned, *refs):
    groups, blocks, drafts = sizes
    pieces = refs[:blocks]
    shrink_ref, slots_ref = refs[blocks : blocks + 2]
    rows_ref, rank_ref, wide = refs[-3:]
    for block in range(blocks):
        for draft in range(drafts):
            start = (block * drafts + draft) * groups
            wide[start : start + groups, :] = pieces[block][draft].astype(jnp.float32)
    rows = wide[...].astype(jnp.bfloat16)
    rows_ref[...] = rows
    place = slots_ref[:, 0:1] - lax.axis_index("tensor") * owned
    ranks = owned_ranks(
        rows, shrink_ref[...], place, shrink_ref.shape[0] // owned, rank_ref.shape[1]
    )
    put = (rank_ref.shape[0], rows.shape[0])
    draft = parts_of(as_gathered, sizes, iota((rows.shape[0], put[0]), 0))[2]
    line = slots_ref[:, 2:3] * drafts + draft
    put = jnp.where(line == iota((rows.shape[0], put[0]), 1), 1.0, 0.0).astype(jnp.bfloat16)
    ranks = lax.dot_general(
        put, ranks, (((0,), (0,)), ((), ())), preferred_element_type=jnp.float32
    )
    rank_ref[...] = ranks.astype(jnp.bfloat16)


def owned_ranks(rows, shrink, place, width, lanes):
    ranks = dot_nt(rows, shrink)
    kept = jnp.where(over(iota(ranks.shape, 1), width) == place, ranks, 0.0).astype(jnp.bfloat16)
    fold = (ranks.shape[1], lanes)
    fold = rest_of(iota(fold, 0), width) == iota(fold, 1)
    return dot(kept, jnp.where(fold, 1.0, 0.0).astype(jnp.bfloat16)).astype(jnp.bfloat16)


def spread_ranks(ranks, place, width, owned, parts):
    span = owned * width
    row = iota((ranks.shape[1], parts * span), 0)
    column = iota((ranks.shape[1], parts * span), 1)
    tile = (over(row, width) == over(column, span)) & (
        rest_of(row, width) == rest_of(column, width)
    )
    wide = dot(ranks, jnp.where(tile, 1.0, 0.0).astype(jnp.bfloat16))
    slot = over(rest_of(iota(wide.shape, 1), span), width)
    return jnp.where(slot == place, wide, 0.0).astype(jnp.bfloat16)


def product_kernel(rows_ref, *refs):
    *weights, total_ref = refs
    start = 0
    for weight in weights:
        width = weight.shape[1]
        step = width if width % 1024 else 1024
        for first in range(0, width, step):
            total_ref[:, start : start + step] = dot(
                rows_ref[...], weight[:, first : first + step]
            )
            start += step


def product(rows, *weights):
    width = sum(weight.shape[1] for weight in weights)
    return call(
        product_kernel,
        shape((rows.shape[0], width), jnp.float32),
        [VMEM] * (1 + len(weights)),
    )(rows, *weights)


def prepare_kernel(sizes, owned, ids_ref, pool_ref, length_ref, *refs):
    slots_ref, cosine_ref, sine_ref = refs[-3:]
    groups, blocks, drafts = sizes
    width = cosine_ref.shape[1]
    lane = iota(cosine_ref.shape, 1)
    half = (lane & (width // 2 - 1)).astype(jnp.float32)
    positions = (lax.rem(iota(cosine_ref.shape, 0), drafts) + length_ref[0]).astype(jnp.float32)
    angles = positions * jnp.exp(half * (-2.0 * math.log(rope_base) / width))
    cosine_ref[...] = jnp.cos(angles)
    sine_ref[...] = jnp.sin(angles) * jnp.where(lane < width // 2, -1.0, 1.0)
    index = iota(slots_ref.shape, 0)
    column = iota(slots_ref.shape, 1)
    near = parts_of(as_gathered, sizes, index)
    far = parts_of(by_draft, sizes, index)
    row_group = jnp.where(column == 1, far[0] ^ group_of(), near[0])
    row_block = jnp.where(column == 1, turned(far[1]), turned(near[1]))
    place = row_block * groups + row_group
    slots = jnp.zeros(slots_ref.shape, jnp.int32)
    sent, taken = 0, 0
    for row in range(blocks * groups):
        slot = pool_ref[ids_ref[row]]
        owner = over(slot, owned)
        sends = jnp.where(owner == lax.axis_index("tensor"), 1, 0)
        takes = jnp.where(owner == group_of(), 1, 0)
        line = jnp.where(column == 2, sent - 64 * (1 - sends), taken - 64 * (1 - takes))
        slots = jnp.where(place == row, jnp.where(column < 2, slot, line), slots)
        sent, taken = sent + sends, taken + takes
    slots_ref[...] = slots


def prepare(sizes, owned, ids, pool, lengths, table, later):
    groups, blocks, drafts = sizes
    smem = pl.BlockSpec(memory_space=pltpu.SMEM)
    table = shape(table, jnp.float32)
    return call(
        functools.partial(prepare_kernel, sizes, owned),
        [shape((groups * blocks * drafts, 128), jnp.int32), table, table],
        [smem, smem, smem] + [HBM] * 3,
        limit=40 * MIB,
    )(ids, pool, lengths, *[later] * 3)


def grow_kernel(sizes, width, total_ref, slots_ref, *refs):
    groups, blocks, drafts = sizes
    ranks_in, grows, (out_ref, held) = refs[:2], refs[2:5], refs[-2:]
    group = group_of()
    requests = groups * blocks
    lines = out_ref.shape[1]
    held[...] = jnp.zeros(held.shape, jnp.float32)
    owned = grows[0].shape[0] // width
    ranks = ranks_in[0][...].astype(jnp.float32)
    for other in ranks_in[1:]:
        ranks = ranks + other[...].astype(jnp.float32)
    get = (total_ref.shape[0], ranks.shape[0])
    draft = parts_of(as_gathered, sizes, iota(get, 0))[2]
    get = slots_ref[:, 3:4] * drafts + draft == iota(get, 1)
    ranks = dot(jnp.where(get, 1.0, 0.0).astype(jnp.bfloat16), ranks.astype(jnp.bfloat16))
    place = slots_ref[:, 0:1] - group * owned
    wide = spread_ranks(ranks.astype(jnp.bfloat16), place, width, owned, len(grows))
    arranged = reorder(sizes, by_draft, as_gathered)
    start, column = 0, 0
    for index, grow in enumerate(grows):
        deep, cols = grow.shape
        full = total_ref[:, column : column + cols] + dot(
            wide[:, index * deep : (index + 1) * deep], grow[...]
        )
        column += cols
        full = dot(arranged, full.astype(jnp.bfloat16))
        for head in range(cols // 128):
            for draft in range(drafts):
                held[pl.ds(start + draft, requests, stride=lines), :] = full[
                    draft * requests : (draft + 1) * requests, head * 128 : (head + 1) * 128
                ]
            start += drafts
    for row in range(requests):
        out_ref[row] = held[row * lines : (row + 1) * lines, :].astype(jnp.bfloat16)


def attend_kernel(
    sizes, arrived_ref, keys_ref, values_ref, length_ref, cosine_ref, sine_ref, *refs
):
    groups, blocks, drafts = sizes
    outs, fresh_s = refs[:blocks], refs[blocks]
    cache_size, head_size = keys_ref.shape[2:]
    count = outs[0].shape[0]
    scale = 1.0 / math.sqrt(head_size)
    fresh_s[...] = jnp.zeros(fresh_s.shape, jnp.float32)
    for block in range(blocks):
        head = turned(block)
        joined = arrived_ref[head * groups].astype(jnp.float32)
        for other in range(1, groups):
            joined = joined + arrived_ref[head * groups + other].astype(jnp.float32)
        joined = joined.astype(jnp.bfloat16).astype(jnp.float32)
        rotated = joined * cosine_ref[...] + pltpu.roll(joined, head_size // 2, 1) * sine_ref[...]
        fresh_s[2 * block, 0:drafts, :] = rotated[count : count + drafts]
        fresh_s[2 * block + 1, 0:drafts, :] = joined[count + drafts : count + 2 * drafts]
        query = rotated[0:count].astype(jnp.bfloat16)
        old = dot_nt(query, keys_ref[0, head]) * scale
        new = dot_nt(query, fresh_s[2 * block].astype(jnp.bfloat16)) * scale
        old = jnp.where(iota(old.shape, 1) < length_ref[0], old, -jnp.inf)
        seen = iota(new.shape, 1) <= lax.rem(iota(new.shape, 0), drafts)
        new = jnp.where(seen, new, -jnp.inf)
        peak = jnp.maximum(jnp.max(old, 1, keepdims=True), jnp.max(new, 1, keepdims=True))
        old = jnp.exp(old - peak)
        new = jnp.exp(new - peak)
        below = jnp.sum(old, 1, keepdims=True) + jnp.sum(new, 1, keepdims=True)
        mixed = dot((old / below).astype(jnp.bfloat16), values_ref[0, head]) + dot(
            (new / below).astype(jnp.bfloat16), fresh_s[2 * block + 1].astype(jnp.bfloat16)
        )
        outs[block][...] = mixed.astype(jnp.bfloat16)


def add_kernel(left_ref, right_ref, out_ref):
    total = left_ref[...].astype(jnp.float32) + right_ref[...].astype(jnp.float32)
    out_ref[...] = total.astype(jnp.bfloat16)


def absolute(sizes, index):
    group, block, draft = parts_of(by_draft, sizes, index)
    return by_draft(sizes, group ^ group_of(), turned(block), draft)


def stack_kernel(*refs):
    for index, ref in enumerate(refs[:-1]):
        refs[-1][index] = ref[...]


def packing(rows, width, lanes):
    parts = lanes // width
    return parts, rows // parts


def out_rank_kernel(sizes, owned, *refs):
    groups, blocks, drafts = sizes
    shrink_ref, slots_ref = refs[groups : groups + 2]
    rows_ref, rank_ref, wide = refs[-3:]
    lines, head_size = refs[0].shape[1:]
    requests = blocks * groups
    for block in range(blocks):
        for group in range(groups):
            start = (block * groups + group) * lines
            wide[start : start + lines, :] = refs[group][block].astype(jnp.float32)
    for head in range(lines // drafts):
        for draft in range(drafts):
            rows_ref[
                draft * requests : (draft + 1) * requests,
                head * head_size : (head + 1) * head_size,
            ] = wide[pl.ds(head * drafts + draft, requests, stride=lines), :].astype(jnp.bfloat16)
    rows = rows_ref[...]
    place = slots_ref[:, 1:2] - group_of() * owned
    width = shrink_ref.shape[0] // owned
    held, lanes = rank_ref.shape
    parts, span = packing(rows.shape[0], width, lanes)
    ranks = dot_nt(rows, shrink_ref[...])
    kept = jnp.where(over(iota(ranks.shape, 1), width) == place, ranks, 0.0).astype(jnp.bfloat16)
    fold = (ranks.shape[1], lanes)
    fold = rest_of(iota(fold, 0), width) == rest_of(iota(fold, 1), width)
    ranks = dot(kept, jnp.where(fold, 1.0, 0.0).astype(jnp.bfloat16))
    mine = over(iota(ranks.shape, 1), width) == over(absolute(sizes, iota(ranks.shape, 0)), span)
    ranks = jnp.where(mine, ranks, 0.0).astype(jnp.bfloat16)
    put = (held, rows.shape[0])
    put = iota(put, 0) == rest_of(absolute(sizes, iota(put, 1)), span)
    ranks = dot(jnp.where(put, 1.0, 0.0).astype(jnp.bfloat16), ranks)
    rank_ref[...] = ranks.astype(jnp.bfloat16)


def out_grow_kernel(sizes, width, total_ref, slots_ref, grow_ref, *refs):
    groups, blocks, drafts = sizes
    ranks_in, outs = refs[:blocks], refs[blocks:]
    owned = grow_ref.shape[0] // width
    me = lax.axis_index("tensor")
    ranks = ranks_in[0][...].astype(jnp.float32)
    for other in ranks_in[1:]:
        ranks = ranks + other[...].astype(jnp.float32)
    count = total_ref.shape[0]
    held, lanes = ranks.shape
    parts, span = packing(count, width, lanes)
    put = rest_of(absolute(sizes, iota((count, held), 0)), span) == iota((count, held), 1)
    ranks = dot(jnp.where(put, 1.0, 0.0).astype(jnp.bfloat16), ranks.astype(jnp.bfloat16))
    mine = over(iota(ranks.shape, 1), width) == over(absolute(sizes, iota(ranks.shape, 0)), span)
    ranks = jnp.where(mine, ranks, 0.0).astype(jnp.bfloat16)
    tile = (lanes, owned * width)
    tile = rest_of(iota(tile, 0), width) == rest_of(iota(tile, 1), width)
    ranks = dot(ranks, jnp.where(tile, 1.0, 0.0).astype(jnp.bfloat16))
    place = slots_ref[:, 1:2] - me * owned
    wide = jnp.where(over(iota(ranks.shape, 1), width) == place, ranks, 0.0).astype(jnp.bfloat16)
    full = (total_ref[...] + dot(wide, grow_ref[...])).astype(jnp.bfloat16)
    group, block, draft = parts_of(as_gathered, sizes, iota((count, count), 0))
    wanted = by_draft(sizes, group ^ group_of(), block, draft) == iota((count, count), 1)
    full = dot(jnp.where(wanted, 1.0, 0.0).astype(jnp.bfloat16), full).astype(jnp.bfloat16)
    for block in range(blocks):
        for draft in range(drafts):
            start = (block * drafts + draft) * groups
            outs[block][draft] = full[start : start + groups]


def by_kernels(
    tokens,
    w_query,
    w_key,
    w_value,
    w_out,
    shrink_qkv,
    grow_query,
    grow_key,
    grow_value,
    shrink_out,
    grow_out,
    cache_keys,
    cache_values,
    cache_lengths,
    adapter_ids,
    adapter_slots,
):
    blocks = lax.axis_size("tensor")
    groups = lax.axis_size(GROUP)
    _, drafts, features = tokens.shape
    sizes = (groups, blocks, drafts)
    owned = shrink_qkv.shape[0]
    width = grow_out.shape[1]
    head_size = cache_keys.shape[3]
    span = blocks * drafts
    count = groups * span
    lanes = -(-shrink_qkv.shape[2] // 128) * 128

    def over_tensor(value, shift):
        route = [(t, t ^ shift) for t in range(blocks)]
        return lax.ppermute(value, "tensor", route)

    def over_group(value, shift):
        return lax.ppermute(value, GROUP, [(g, g ^ shift) for g in range(groups)])

    def over_core(value):
        return lax.ppermute(value, "pipe", [(0, 1), (1, 0)])

    def to_growers(value, flip):
        route = [
            (t * groups + 2 * x + c, (2 * c + (x ^ flip)) * groups + t)
            for t in range(blocks)
            for x in range(2)
            for c in range(2)
        ]
        return lax.ppermute(value, EVERY, route)

    def to_out_growers(value, shift):
        route = [
            (t * groups + g, g * groups + (t ^ shift))
            for t in range(blocks)
            for g in range(groups)
        ]
        return lax.ppermute(value, EVERY, route)

    def added(left, right):
        return call(add_kernel, shape(left.shape), [VMEM] * 2)(left, right)

    def exchange(value):
        return lax.all_to_all(value, EVERY, split_axis=0, concat_axis=0, tiled=True)

    mine = jnp.transpose(tokens, (1, 0, 2))
    pieces = [mine] + [over_tensor(mine, shift) for shift in range(1, blocks)]

    lines = (w_query.shape[1] // head_size + 2) * drafts
    lines = -(-lines // 8) * 8
    slots, cosine, sine = prepare(
        sizes, owned, adapter_ids, adapter_slots, cache_lengths, (lines, head_size), w_out
    )
    packed = -(-2 * blocks * drafts // 16) * 16
    shrink_in = jnp.transpose(shrink_qkv, (0, 2, 1)).reshape(-1, features)
    rows, rank_part = call(
        functools.partial(rank_kernel, sizes, owned),
        [shape((count, features)), shape((packed, lanes))],
        [VMEM] * (blocks + 2),
        [pltpu.VMEM((count, features), jnp.float32)],
        2 * count * shrink_qkv.size,
        2 * shrink_qkv.size + 4 * count * features,
    )(*pieces, shrink_in, slots)
    rank_part = added(rank_part, over_core(rank_part))
    ranks = [to_growers(rank_part, flip) for flip in range(2)]
    total = product(rows, w_query, w_key, w_value)
    cols = total.shape[1]
    head_cols = w_query.shape[1]
    query_lines = head_cols // head_size * drafts
    sent = call(
        functools.partial(grow_kernel, sizes, width),
        shape((blocks * groups, lines, head_size)),
        [VMEM] * 7 + [HBM] * 2,
        [pltpu.VMEM((blocks * groups * lines, head_size), jnp.float32)],
        limit=40 * MIB,
    )(
        total,
        slots,
        *ranks,
        *[grow.reshape(owned * width, -1) for grow in (grow_query, grow_key, grow_value)],
        *[w_out] * 2,
    )
    mixed = call(
        functools.partial(attend_kernel, sizes),
        [shape((query_lines, head_size))] * blocks,
        [VMEM] * 3 + [pl.BlockSpec(memory_space=pltpu.SMEM)] + [VMEM] * 2,
        [pltpu.VMEM((2 * blocks, 128, head_size), jnp.float32)],
    )(exchange(sent), cache_keys, cache_values, cache_lengths, cosine, sine)
    stacked = call(
        stack_kernel, shape((blocks, query_lines, head_size)), [VMEM] * blocks
    )(mixed[0], *[over_tensor(mixed[shift], shift) for shift in range(1, blocks)])
    gathered = [stacked] + [over_group(stacked, shift) for shift in range(1, groups)]
    held = -(-packing(count, width, 128)[1] // 16) * 16
    out_rows, out_part = call(
        functools.partial(out_rank_kernel, sizes, owned),
        [shape((count, head_cols)), shape((held, 128))],
        [VMEM] * (groups + 2) + [HBM] * 4,
        [pltpu.VMEM((blocks * groups * query_lines, head_size), jnp.float32)],
        limit=40 * MIB,
    )(*gathered, jnp.transpose(shrink_out, (0, 2, 1)).reshape(-1, head_cols), slots, *[w_query] * 4)
    out_ranks = [to_out_growers(out_part, shift) for shift in range(blocks)]
    out_total = product(out_rows, w_out)
    out_cols = out_total.shape[1]
    leaving = call(
        functools.partial(out_grow_kernel, sizes, width),
        [shape((drafts, groups, out_cols))] * blocks,
        [VMEM] * (3 + blocks),
        [],
        2 * count * owned * width * out_cols,
        8 * count * out_cols + 2 * owned * width * out_cols,
    )(out_total, slots, grow_out.reshape(owned * width, -1), *out_ranks)
    result = leaving[0].astype(jnp.float32)
    for shift in range(1, blocks):
        result = result + over_tensor(leaving[shift], shift).astype(jnp.float32)
    return jnp.transpose(result.astype(jnp.bfloat16), (1, 0, 2))


def rotate(vectors, positions):
    half_size = vectors.shape[-1] // 2
    frequency = rope_base ** (-2.0 * jnp.arange(half_size, dtype=jnp.float32) / vectors.shape[-1])
    angles = positions[:, None, None] * frequency
    cosine = jnp.cos(angles)
    sine_value = jnp.sin(angles)
    first_half = vectors[..., :half_size]
    second = vectors[..., half_size:]
    return jnp.concatenate(
        [first_half * cosine - second * sine_value, second * cosine + first_half * sine_value], -1
    )


def to_growers(partial, splits):
    total = None
    for shift in range(splits):
        route = [
            (t * splits + g, ((g + shift) % splits) * splits + t)
            for t in range(splits)
            for g in range(splits)
        ]
        got = lax.ppermute(partial, EVERY, route).astype(jnp.float32)
        total = got if total is None else total + got
    return total


def to_out_growers(partial, splits):
    total = None
    for shift in range(splits):
        route = [
            (t * splits + g, g * splits + (t + shift) % splits)
            for t in range(splits)
            for g in range(splits)
        ]
        got = lax.ppermute(partial, EVERY, route).astype(jnp.float32)
        total = got if total is None else total + got
    return total


def slot_table(adapter_ids, adapter_slots):
    matches = adapter_ids[:, None] == jnp.arange(adapter_slots.shape[0], dtype=jnp.int32)[None, :]
    return jnp.sum(jnp.where(matches, adapter_slots[None, :], 0), axis=1)


def attend(query_heads, key_new, value_new, cache_keys, cache_values, length):
    drafts, head_count, head_size = query_heads.shape
    kv_heads, cache_size, _ = cache_keys.shape
    positions = (length + jnp.arange(drafts, dtype=jnp.int32)).astype(jnp.float32)
    query_rot = rotate(query_heads.astype(jnp.float32), positions).astype(jnp.bfloat16)
    key_rot = rotate(key_new.astype(jnp.float32), positions).astype(jnp.bfloat16)
    grouped = query_rot.reshape(drafts, kv_heads, head_count // kv_heads, head_size)
    score_scale = 1.0 / math.sqrt(head_size)
    cached = (
        jnp.einsum("skgd,kld->skgl", grouped, cache_keys, preferred_element_type=jnp.float32)
        * score_scale
    )
    fresh_scores = (
        jnp.einsum("skgd,tkd->skgt", grouped, key_rot, preferred_element_type=jnp.float32)
        * score_scale
    )
    cache_mask = jnp.arange(cache_size, dtype=jnp.int32) < length
    draft_mask = jnp.arange(drafts)[None, :] <= jnp.arange(drafts)[:, None]
    cached = jnp.where(cache_mask[None, None, None, :], cached, -jnp.inf)
    fresh_scores = jnp.where(draft_mask[:, None, None, :], fresh_scores, -jnp.inf)
    row_peak = jnp.maximum(jnp.max(cached, -1), jnp.max(fresh_scores, -1))
    cached_exp = jnp.exp(cached - row_peak[..., None])
    fresh_exp = jnp.exp(fresh_scores - row_peak[..., None])
    denominator = jnp.sum(cached_exp, -1) + jnp.sum(fresh_exp, -1)
    cached_prob = (cached_exp / denominator[..., None]).astype(jnp.bfloat16)
    fresh_prob = (fresh_exp / denominator[..., None]).astype(jnp.bfloat16)
    mixed = jnp.einsum(
        "skgl,kld->skgd", cached_prob, cache_values, preferred_element_type=jnp.float32
    )
    mixed = mixed + jnp.einsum(
        "skgt,tkd->skgd", fresh_prob, value_new, preferred_element_type=jnp.float32
    )
    return mixed.astype(jnp.bfloat16)


def by_row(
    tokens,
    w_query,
    w_key,
    w_value,
    w_out,
    shrink_qkv,
    grow_query,
    grow_key,
    grow_value,
    shrink_out,
    grow_out,
    cache_keys,
    cache_values,
    cache_lengths,
    adapter_ids,
    adapter_slots,
):
    splits = lax.axis_size("tensor")
    groups = lax.axis_size(("dp", "pipe"))
    tensor_index = lax.axis_index("tensor")
    group_index = lax.axis_index(("dp", "pipe"))
    local_rows, drafts, feature_width = tokens.shape
    per_owner = shrink_qkv.shape[0]
    rank_size = grow_out.shape[1]
    query_cols = w_query.shape[1]
    key_cols = w_key.shape[1]
    kv_heads = cache_keys.shape[1]
    head_size = cache_keys.shape[3]
    rows = splits * groups
    row_slots = jnp.repeat(slot_table(adapter_ids, adapter_slots), drafts)
    within = jnp.arange(per_owner, dtype=jnp.int32)[None, :]
    width_hot = (row_slots[:, None] == within + tensor_index * per_owner)[:, :, None]
    column_hot = (row_slots[:, None] == within + group_index * per_owner)[:, :, None]

    def spread_ranks(ranks, hot):
        return jnp.where(hot, ranks[:, None, :], 0.0).reshape(rows * drafts, -1).astype(jnp.bfloat16)

    flat_tokens = lax.all_gather(tokens, "tensor", axis=0, tiled=True).reshape(
        rows * drafts, feature_width
    )
    rank_part = jnp.einsum(
        "nd,adr->nar", flat_tokens, shrink_qkv, preferred_element_type=jnp.float32
    )
    rank_part = jnp.sum(jnp.where(width_hot, rank_part, 0.0), 1)
    rank_all = to_growers(rank_part.astype(jnp.bfloat16), splits)

    def grown(index, grow):
        ranks = spread_ranks(rank_all[:, index * rank_size : (index + 1) * rank_size], column_hot)
        return jnp.dot(
            ranks, grow.reshape(per_owner * rank_size, -1), preferred_element_type=jnp.float32
        )

    bases = [
        jnp.dot(flat_tokens, weight, preferred_element_type=jnp.float32)
        for weight in (w_query, w_key, w_value)
    ]

    def product(index, grow):
        return (bases[index] + grown(index, grow)).astype(jnp.bfloat16).reshape(rows, drafts, -1)

    partial = jnp.concatenate(
        [
            product(0, grow_query),
            product(1, grow_key),
            product(2, grow_value),
        ],
        2,
    )
    arrived = lax.all_to_all(partial, EVERY, split_axis=0, concat_axis=0, tiled=True)
    joined = jnp.sum(
        arrived.reshape(splits, groups, drafts, -1).astype(jnp.float32), 1
    ).astype(jnp.bfloat16)
    joined = jnp.transpose(joined, (1, 0, 2))
    query_heads = joined[:, :, :query_cols].reshape(drafts, -1, head_size)
    key_new = joined[:, :, query_cols : query_cols + key_cols].reshape(drafts, kv_heads, head_size)
    value_new = joined[:, :, query_cols + key_cols :].reshape(drafts, kv_heads, head_size)
    mixed = attend(
        query_heads, key_new, value_new, cache_keys[0], cache_values[0], cache_lengths[0]
    )
    mixed = jnp.transpose(mixed.reshape(drafts, splits, -1), (1, 0, 2))
    outgoing = jnp.repeat(mixed, groups, axis=0)
    flat_heads = lax.all_to_all(
        outgoing, EVERY, split_axis=0, concat_axis=0, tiled=True
    ).reshape(rows * drafts, -1)
    out_part = jnp.einsum(
        "nw,awr->nar", flat_heads, shrink_out, preferred_element_type=jnp.float32
    )
    out_part = jnp.sum(jnp.where(column_hot, out_part, 0.0), 1)
    out_rank = to_out_growers(out_part.astype(jnp.bfloat16), splits)
    out = jnp.dot(flat_heads, w_out, preferred_element_type=jnp.float32)
    out = out + jnp.dot(
        spread_ranks(out_rank, width_hot),
        grow_out.reshape(per_owner * rank_size, -1),
        preferred_element_type=jnp.float32,
    )
    blocks = lax.all_to_all(
        out.astype(jnp.bfloat16).reshape(splits, local_rows, drafts, feature_width),
        "tensor",
        split_axis=0,
        concat_axis=0,
        tiled=True,
    )
    return jnp.sum(blocks.astype(jnp.float32), 0).astype(jnp.bfloat16)


def local(*arrays):
    heads = arrays[11].shape[1]
    sizes = [lax.axis_size(name) for name in EVERY]
    if heads == 4 and sizes == [4, 2, 2]:
        return by_kernels(*arrays)
    return by_row(*arrays)


def solution(mesh):
    placed = (
        P(("parts", "tensor"), None, ("dp", "pipe")),
        P(("dp", "pipe"), "tensor"),
        P(("dp", "pipe"), "tensor"),
        P(("dp", "pipe"), "tensor"),
        P("tensor", ("dp", "pipe")),
        P("tensor", ("dp", "pipe"), None),
        P(("dp", "pipe"), None, "tensor"),
        P(("dp", "pipe"), None, "tensor"),
        P(("dp", "pipe"), None, "tensor"),
        P(("dp", "pipe"), "tensor", None),
        P("tensor", None, ("dp", "pipe")),
        P(("parts", "tensor", "dp", "pipe"), None, None, None),
        P(("parts", "tensor", "dp", "pipe"), None, None, None),
        P(("parts", "tensor", "dp", "pipe")),
        P(),
        P(),
    )
    return jax.shard_map(
        local,
        mesh=mesh,
        in_specs=placed,
        out_specs=P(("parts", "tensor"), None, ("dp", "pipe")),
        check_vma=False,
    )
```

```python
import functools
import math

import jax
import jax.numpy as jnp
import numpy as np
from jax import lax
from jax.experimental import pallas as pl
from jax.experimental.pallas import tpu as pltpu
from jax.sharding import PartitionSpec as P

rope_base = 500000.0
EVERY = ("tensor", "dp", "pipe")
GROUP = ("dp", "pipe")
VMEM = pl.BlockSpec(memory_space=pltpu.VMEM)
HBM = pl.BlockSpec(memory_space=pltpu.HBM)
MIB = 1 << 20


def dot(left, right):
    return jnp.dot(left, right, preferred_element_type=jnp.float32)


def dot_nt(left, right):
    return lax.dot_general(
        left, right, (((1,), (1,)), ((), ())), preferred_element_type=jnp.float32
    )


def iota(shape, axis):
    return lax.broadcasted_iota(jnp.int32, shape, axis)


def call(kernel, outs, ins, scratch=(), flops=0, moved=0, limit=24 * MIB):
    return pl.pallas_call(
        kernel,
        out_shape=outs,
        in_specs=ins,
        out_specs=jax.tree.map(lambda _: VMEM, outs),
        scratch_shapes=list(scratch),
        cost_estimate=pl.CostEstimate(flops=flops, bytes_accessed=moved, transcendentals=0),
        compiler_params=pltpu.CompilerParams(vmem_limit_bytes=limit),
    )


def shape(dims, kind=jnp.bfloat16):
    return jax.ShapeDtypeStruct(tuple(dims), kind)


def over(value, size):
    return value >> (size.bit_length() - 1) if size & (size - 1) == 0 else lax.div(value, size)


def rest_of(value, size):
    return value & (size - 1) if size & (size - 1) == 0 else lax.rem(value, size)


def as_gathered(sizes, group, block, draft):
    groups, blocks, drafts = sizes
    return (block * drafts + draft) * groups + group


def by_draft(sizes, group, block, draft):
    groups, blocks, drafts = sizes
    return (draft * blocks + block) * groups + group


def parts_of(order, sizes, index):
    groups, blocks, drafts = sizes
    group, left = rest_of(index, groups), over(index, groups)
    if order is as_gathered:
        return group, over(left, drafts), rest_of(left, drafts)
    return group, rest_of(left, blocks), over(left, blocks)


def turned(block):
    return lax.axis_index("tensor") ^ block


def reorder(sizes, after, before):
    groups, blocks, drafts = sizes
    rows = groups * blocks * drafts
    group, block, draft = parts_of(after, sizes, iota((rows, rows), 0))
    wanted = before(sizes, group, turned(block), draft)
    return jnp.where(wanted == iota((rows, rows), 1), 1.0, 0.0).astype(jnp.bfloat16)


def group_of():
    return lax.axis_index("dp") * lax.axis_size("pipe") + lax.axis_index("pipe")


def rank_kernel(sizes, owned, *refs):
    groups, blocks, drafts = sizes
    pieces = refs[:blocks]
    shrink_ref, slots_ref = refs[blocks : blocks + 2]
    rows_ref, rank_ref, wide = refs[-3:]
    for block in range(blocks):
        for draft in range(drafts):
            start = (block * drafts + draft) * groups
            wide[start : start + groups, :] = pieces[block][draft].astype(jnp.float32)
    rows = wide[...].astype(jnp.bfloat16)
    rows_ref[...] = rows
    place = slots_ref[:, 0:1] - lax.axis_index("tensor") * owned
    ranks = owned_ranks(
        rows, shrink_ref[...], place, shrink_ref.shape[0] // owned, rank_ref.shape[1]
    )
    put = (rank_ref.shape[0], rows.shape[0])
    draft = parts_of(as_gathered, sizes, iota((rows.shape[0], put[0]), 0))[2]
    line = slots_ref[:, 2:3] * drafts + draft
    put = jnp.where(line == iota((rows.shape[0], put[0]), 1), 1.0, 0.0).astype(jnp.bfloat16)
    ranks = lax.dot_general(
        put, ranks, (((0,), (0,)), ((), ())), preferred_element_type=jnp.float32
    )
    rank_ref[...] = ranks.astype(jnp.bfloat16)


def owned_ranks(rows, shrink, place, width, lanes):
    ranks = dot_nt(rows, shrink)
    kept = jnp.where(over(iota(ranks.shape, 1), width) == place, ranks, 0.0).astype(jnp.bfloat16)
    fold = (ranks.shape[1], lanes)
    fold = rest_of(iota(fold, 0), width) == iota(fold, 1)
    return dot(kept, jnp.where(fold, 1.0, 0.0).astype(jnp.bfloat16)).astype(jnp.bfloat16)


def spread_ranks(ranks, place, width, owned, parts):
    span = owned * width
    row = iota((ranks.shape[1], parts * span), 0)
    column = iota((ranks.shape[1], parts * span), 1)
    tile = (over(row, width) == over(column, span)) & (
        rest_of(row, width) == rest_of(column, width)
    )
    wide = dot(ranks, jnp.where(tile, 1.0, 0.0).astype(jnp.bfloat16))
    slot = over(rest_of(iota(wide.shape, 1), span), width)
    return jnp.where(slot == place, wide, 0.0).astype(jnp.bfloat16)


def product_kernel(rows_ref, *refs):
    *weights, total_ref = refs
    start = 0
    for weight in weights:
        width = weight.shape[1]
        step = width if width % 1024 else 1024
        for first in range(0, width, step):
            total_ref[:, start : start + step] = dot(
                rows_ref[...], weight[:, first : first + step]
            )
            start += step


def product(rows, *weights):
    width = sum(weight.shape[1] for weight in weights)
    return call(
        product_kernel,
        shape((rows.shape[0], width), jnp.float32),
        [VMEM] * (1 + len(weights)),
    )(rows, *weights)


def prepare_kernel(sizes, owned, ids_ref, pool_ref, length_ref, *refs):
    slots_ref, cosine_ref, sine_ref = refs[-3:]
    groups, blocks, drafts = sizes
    width = cosine_ref.shape[1]
    lane = iota(cosine_ref.shape, 1)
    half = (lane & (width // 2 - 1)).astype(jnp.float32)
    positions = (lax.rem(iota(cosine_ref.shape, 0), drafts) + length_ref[0]).astype(jnp.float32)
    angles = positions * jnp.exp(half * (-2.0 * math.log(rope_base) / width))
    cosine_ref[...] = jnp.cos(angles)
    sine_ref[...] = jnp.sin(angles) * jnp.where(lane < width // 2, -1.0, 1.0)
    index = iota(slots_ref.shape, 0)
    column = iota(slots_ref.shape, 1)
    near = parts_of(as_gathered, sizes, index)
    far = parts_of(by_draft, sizes, index)
    row_group = jnp.where(column == 1, far[0], near[0])
    row_block = jnp.where(column == 1, far[1], turned(near[1]))
    place = row_block * groups + row_group
    slots = jnp.zeros(slots_ref.shape, jnp.int32)
    sent, taken = 0, 0
    for row in range(blocks * groups):
        slot = pool_ref[ids_ref[row]]
        owner = over(slot, owned)
        sends = jnp.where(owner == lax.axis_index("tensor"), 1, 0)
        takes = jnp.where(owner == group_of(), 1, 0)
        line = jnp.where(column == 2, sent - 64 * (1 - sends), taken - 64 * (1 - takes))
        slots = jnp.where(place == row, jnp.where(column < 2, slot, line), slots)
        sent, taken = sent + sends, taken + takes
    slots_ref[...] = slots


def prepare(sizes, owned, ids, pool, lengths, table, later):
    groups, blocks, drafts = sizes
    smem = pl.BlockSpec(memory_space=pltpu.SMEM)
    table = shape(table, jnp.float32)
    return call(
        functools.partial(prepare_kernel, sizes, owned),
        [shape((groups * blocks * drafts, 128), jnp.int32), table, table],
        [smem, smem, smem] + [HBM] * 3,
        limit=40 * MIB,
    )(ids, pool, lengths, *[later] * 3)


def grow_kernel(sizes, width, total_ref, slots_ref, *refs):
    groups, blocks, drafts = sizes
    ranks_in, grows, (out_ref, held) = refs[:2], refs[2:5], refs[-2:]
    group = group_of()
    requests = groups * blocks
    lines = out_ref.shape[1]
    held[...] = jnp.zeros(held.shape, jnp.float32)
    owned = grows[0].shape[0] // width
    ranks = ranks_in[0][...].astype(jnp.float32)
    for other in ranks_in[1:]:
        ranks = ranks + other[...].astype(jnp.float32)
    get = (total_ref.shape[0], ranks.shape[0])
    draft = parts_of(as_gathered, sizes, iota(get, 0))[2]
    get = slots_ref[:, 3:4] * drafts + draft == iota(get, 1)
    ranks = dot(jnp.where(get, 1.0, 0.0).astype(jnp.bfloat16), ranks.astype(jnp.bfloat16))
    place = slots_ref[:, 0:1] - group * owned
    wide = spread_ranks(ranks.astype(jnp.bfloat16), place, width, owned, len(grows))
    arranged = reorder(sizes, by_draft, as_gathered)
    start, column = 0, 0
    for index, grow in enumerate(grows):
        deep, cols = grow.shape
        full = total_ref[:, column : column + cols] + dot(
            wide[:, index * deep : (index + 1) * deep], grow[...]
        )
        column += cols
        full = dot(arranged, full.astype(jnp.bfloat16))
        for head in range(cols // 128):
            for draft in range(drafts):
                held[pl.ds(start + draft, requests, stride=lines), :] = full[
                    draft * requests : (draft + 1) * requests, head * 128 : (head + 1) * 128
                ]
            start += drafts
    for row in range(requests):
        out_ref[row] = held[row * lines : (row + 1) * lines, :].astype(jnp.bfloat16)


def attend_kernel(
    sizes, arrived_ref, keys_ref, values_ref, length_ref, cosine_ref, sine_ref, out_ref, *scratch
):
    groups, blocks, drafts = sizes
    (fresh_s,) = scratch
    cache_size, head_size = keys_ref.shape[2:]
    count = out_ref.shape[1]
    scale = 1.0 / math.sqrt(head_size)
    fresh_s[...] = jnp.zeros(fresh_s.shape, jnp.float32)
    scores = []
    for block in range(blocks):
        joined = arrived_ref[block * groups].astype(jnp.float32)
        for other in range(1, groups):
            joined = joined + arrived_ref[block * groups + other].astype(jnp.float32)
        joined = joined.astype(jnp.bfloat16).astype(jnp.float32)
        rotated = joined * cosine_ref[...] + pltpu.roll(joined, head_size // 2, 1) * sine_ref[...]
        fresh_s[2 * block, 0:drafts, :] = rotated[count : count + drafts]
        fresh_s[2 * block + 1, 0:drafts, :] = joined[count + drafts : count + 2 * drafts]
        query = rotated[0:count].astype(jnp.bfloat16)
        old = dot_nt(query, keys_ref[0, block])
        new = dot_nt(query, fresh_s[2 * block].astype(jnp.bfloat16))
        scores.append(jnp.concatenate([old, new], 1))
    scores = jnp.concatenate(scores, 0) * scale
    column = iota(scores.shape, 1)
    limit = cache_size + lax.rem(iota((scores.shape[0], 1), 0), drafts)
    seen = (column < length_ref[0]) | ((column >= cache_size) & (column <= limit))
    scores = jnp.where(seen, scores, -jnp.inf)
    scores = jnp.exp(scores - jnp.max(scores, 1, keepdims=True))
    below = 1.0 / jnp.sum(scores, 1, keepdims=True)
    probs = (scores * below).astype(jnp.bfloat16)
    for block in range(blocks):
        mine = probs[block * count : (block + 1) * count]
        mixed = dot(mine[:, :cache_size], values_ref[0, block]) + dot(
            mine[:, cache_size:], fresh_s[2 * block + 1].astype(jnp.bfloat16)
        )
        mixed = mixed.astype(jnp.bfloat16)
        for target in range(groups):
            out_ref[block * groups + target] = mixed


def add_kernel(left_ref, right_ref, out_ref):
    total = left_ref[...].astype(jnp.float32) + right_ref[...].astype(jnp.float32)
    out_ref[...] = total.astype(jnp.bfloat16)


def packing(rows, width, lanes):
    parts = lanes // width
    return parts, rows // parts


def out_rank_kernel(sizes, owned, got_ref, shrink_ref, slots_ref, *refs):
    rows_ref, rank_ref, wide = refs[-3:]
    drafts = sizes[2]
    requests, lines, head_size = got_ref.shape
    for row in range(requests):
        wide[row * lines : (row + 1) * lines, :] = got_ref[row].astype(jnp.float32)
    for head in range(lines // drafts):
        for draft in range(drafts):
            rows_ref[
                draft * requests : (draft + 1) * requests,
                head * head_size : (head + 1) * head_size,
            ] = wide[pl.ds(head * drafts + draft, requests, stride=lines), :].astype(jnp.bfloat16)
    rows = rows_ref[...]
    place = slots_ref[:, 1:2] - group_of() * owned
    width = shrink_ref.shape[0] // owned
    held, lanes = rank_ref.shape
    parts, span = packing(rows.shape[0], width, lanes)
    ranks = dot_nt(rows, shrink_ref[...])
    kept = jnp.where(over(iota(ranks.shape, 1), width) == place, ranks, 0.0).astype(jnp.bfloat16)
    fold = (ranks.shape[1], lanes)
    fold = rest_of(iota(fold, 0), width) == rest_of(iota(fold, 1), width)
    ranks = dot(kept, jnp.where(fold, 1.0, 0.0).astype(jnp.bfloat16))
    mine = over(iota(ranks.shape, 1), width) == over(iota(ranks.shape, 0), span)
    ranks = jnp.where(mine, ranks, 0.0).astype(jnp.bfloat16)
    put = (held, rows.shape[0])
    put = iota(put, 0) == rest_of(iota(put, 1), span)
    ranks = dot(jnp.where(put, 1.0, 0.0).astype(jnp.bfloat16), ranks)
    rank_ref[...] = ranks.astype(jnp.bfloat16)


def out_grow_kernel(sizes, width, total_ref, slots_ref, grow_ref, *refs):
    groups, blocks, drafts = sizes
    ranks_in, outs = refs[:blocks], refs[blocks:]
    owned = grow_ref.shape[0] // width
    me = lax.axis_index("tensor")
    ranks = ranks_in[0][...].astype(jnp.float32)
    for other in ranks_in[1:]:
        ranks = ranks + other[...].astype(jnp.float32)
    count = total_ref.shape[0]
    held, lanes = ranks.shape
    parts, span = packing(count, width, lanes)
    put = rest_of(iota((count, held), 0), span) == iota((count, held), 1)
    ranks = dot(jnp.where(put, 1.0, 0.0).astype(jnp.bfloat16), ranks.astype(jnp.bfloat16))
    mine = over(iota(ranks.shape, 1), width) == over(iota(ranks.shape, 0), span)
    ranks = jnp.where(mine, ranks, 0.0).astype(jnp.bfloat16)
    tile = (lanes, owned * width)
    tile = rest_of(iota(tile, 0), width) == rest_of(iota(tile, 1), width)
    ranks = dot(ranks, jnp.where(tile, 1.0, 0.0).astype(jnp.bfloat16))
    place = slots_ref[:, 1:2] - me * owned
    wide = jnp.where(over(iota(ranks.shape, 1), width) == place, ranks, 0.0).astype(jnp.bfloat16)
    full = (total_ref[...] + dot(wide, grow_ref[...])).astype(jnp.bfloat16)
    full = dot(reorder(sizes, as_gathered, by_draft), full).astype(jnp.bfloat16)
    for block in range(blocks):
        for draft in range(drafts):
            start = (block * drafts + draft) * groups
            outs[block][draft] = full[start : start + groups]


def by_kernels(
    tokens,
    w_query,
    w_key,
    w_value,
    w_out,
    shrink_qkv,
    grow_query,
    grow_key,
    grow_value,
    shrink_out,
    grow_out,
    cache_keys,
    cache_values,
    cache_lengths,
    adapter_ids,
    adapter_slots,
):
    blocks = lax.axis_size("tensor")
    groups = lax.axis_size(GROUP)
    _, drafts, features = tokens.shape
    sizes = (groups, blocks, drafts)
    owned = shrink_qkv.shape[0]
    width = grow_out.shape[1]
    head_size = cache_keys.shape[3]
    span = blocks * drafts
    count = groups * span
    lanes = -(-shrink_qkv.shape[2] // 128) * 128

    def over_tensor(value, shift):
        route = [(t, t ^ shift) for t in range(blocks)]
        return lax.ppermute(value, "tensor", route)

    def over_core(value):
        return lax.ppermute(value, "pipe", [(0, 1), (1, 0)])

    def to_growers(value, flip):
        route = [
            (t * groups + 2 * x + c, (2 * c + (x ^ flip)) * groups + t)
            for t in range(blocks)
            for x in range(2)
            for c in range(2)
        ]
        return lax.ppermute(value, EVERY, route)

    def to_out_growers(value, shift):
        route = [
            (t * groups + g, g * groups + (t ^ shift))
            for t in range(blocks)
            for g in range(groups)
        ]
        return lax.ppermute(value, EVERY, route)

    def added(left, right):
        return call(add_kernel, shape(left.shape), [VMEM] * 2)(left, right)

    def exchange(value):
        return lax.all_to_all(value, EVERY, split_axis=0, concat_axis=0, tiled=True)

    mine = jnp.transpose(tokens, (1, 0, 2))
    pieces = [mine] + [over_tensor(mine, shift) for shift in range(1, blocks)]

    lines = (w_query.shape[1] // head_size + 2) * drafts
    lines = -(-lines // 8) * 8
    slots, cosine, sine = prepare(
        sizes, owned, adapter_ids, adapter_slots, cache_lengths, (lines, head_size), w_out
    )
    packed = -(-2 * blocks * drafts // 16) * 16
    shrink_in = jnp.transpose(shrink_qkv, (0, 2, 1)).reshape(-1, features)
    rows, rank_part = call(
        functools.partial(rank_kernel, sizes, owned),
        [shape((count, features)), shape((packed, lanes))],
        [VMEM] * (blocks + 2),
        [pltpu.VMEM((count, features), jnp.float32)],
        2 * count * shrink_qkv.size,
        2 * shrink_qkv.size + 4 * count * features,
    )(*pieces, shrink_in, slots)
    rank_part = added(rank_part, over_core(rank_part))
    ranks = [to_growers(rank_part, flip) for flip in range(2)]
    total = product(rows, w_query, w_key, w_value)
    cols = total.shape[1]
    head_cols = w_query.shape[1]
    query_lines = head_cols // head_size * drafts
    sent = call(
        functools.partial(grow_kernel, sizes, width),
        shape((blocks * groups, lines, head_size)),
        [VMEM] * 7 + [HBM] * 2,
        [pltpu.VMEM((blocks * groups * lines, head_size), jnp.float32)],
        limit=40 * MIB,
    )(
        total,
        slots,
        *ranks,
        *[grow.reshape(owned * width, -1) for grow in (grow_query, grow_key, grow_value)],
        *[w_out] * 2,
    )
    mixed = call(
        functools.partial(attend_kernel, sizes),
        shape((blocks * groups, query_lines, head_size)),
        [VMEM] * 3 + [pl.BlockSpec(memory_space=pltpu.SMEM)] + [VMEM] * 2,
        [pltpu.VMEM((2 * blocks, 128, head_size), jnp.float32)],
    )(exchange(sent), cache_keys, cache_values, cache_lengths, cosine, sine)
    gathered = exchange(mixed)
    held = -(-packing(count, width, 128)[1] // 16) * 16
    out_rows, out_part = call(
        functools.partial(out_rank_kernel, sizes, owned),
        [shape((count, head_cols)), shape((held, 128))],
        [VMEM] * 3 + [HBM] * 4,
        [pltpu.VMEM((blocks * groups * query_lines, head_size), jnp.float32)],
        limit=40 * MIB,
    )(gathered, jnp.transpose(shrink_out, (0, 2, 1)).reshape(-1, head_cols), slots, *[w_query] * 4)
    out_ranks = [to_out_growers(out_part, shift) for shift in range(blocks)]
    out_total = product(out_rows, w_out)
    out_cols = out_total.shape[1]
    leaving = call(
        functools.partial(out_grow_kernel, sizes, width),
        [shape((drafts, groups, out_cols))] * blocks,
        [VMEM] * (3 + blocks),
        [],
        2 * count * owned * width * out_cols,
        8 * count * out_cols + 2 * owned * width * out_cols,
    )(out_total, slots, grow_out.reshape(owned * width, -1), *out_ranks)
    result = leaving[0].astype(jnp.float32)
    for shift in sorted(range(1, blocks), key=lambda shift: shift < blocks // 2):
        result = result + over_tensor(leaving[shift], shift).astype(jnp.float32)
    return jnp.transpose(result.astype(jnp.bfloat16), (1, 0, 2))


def rotate(vectors, positions):
    half_size = vectors.shape[-1] // 2
    frequency = rope_base ** (-2.0 * jnp.arange(half_size, dtype=jnp.float32) / vectors.shape[-1])
    angles = positions[:, None, None] * frequency
    cosine = jnp.cos(angles)
    sine_value = jnp.sin(angles)
    first_half = vectors[..., :half_size]
    second = vectors[..., half_size:]
    return jnp.concatenate(
        [first_half * cosine - second * sine_value, second * cosine + first_half * sine_value], -1
    )


def to_growers(partial, splits):
    total = None
    for shift in range(splits):
        route = [
            (t * splits + g, ((g + shift) % splits) * splits + t)
            for t in range(splits)
            for g in range(splits)
        ]
        got = lax.ppermute(partial, EVERY, route).astype(jnp.float32)
        total = got if total is None else total + got
    return total


def to_out_growers(partial, splits):
    total = None
    for shift in range(splits):
        route = [
            (t * splits + g, g * splits + (t + shift) % splits)
            for t in range(splits)
            for g in range(splits)
        ]
        got = lax.ppermute(partial, EVERY, route).astype(jnp.float32)
        total = got if total is None else total + got
    return total


def slot_table(adapter_ids, adapter_slots):
    matches = adapter_ids[:, None] == jnp.arange(adapter_slots.shape[0], dtype=jnp.int32)[None, :]
    return jnp.sum(jnp.where(matches, adapter_slots[None, :], 0), axis=1)


def attend(query_heads, key_new, value_new, cache_keys, cache_values, length):
    drafts, head_count, head_size = query_heads.shape
    kv_heads, cache_size, _ = cache_keys.shape
    positions = (length + jnp.arange(drafts, dtype=jnp.int32)).astype(jnp.float32)
    query_rot = rotate(query_heads.astype(jnp.float32), positions).astype(jnp.bfloat16)
    key_rot = rotate(key_new.astype(jnp.float32), positions).astype(jnp.bfloat16)
    grouped = query_rot.reshape(drafts, kv_heads, head_count // kv_heads, head_size)
    score_scale = 1.0 / math.sqrt(head_size)
    cached = (
        jnp.einsum("skgd,kld->skgl", grouped, cache_keys, preferred_element_type=jnp.float32)
        * score_scale
    )
    fresh_scores = (
        jnp.einsum("skgd,tkd->skgt", grouped, key_rot, preferred_element_type=jnp.float32)
        * score_scale
    )
    cache_mask = jnp.arange(cache_size, dtype=jnp.int32) < length
    draft_mask = jnp.arange(drafts)[None, :] <= jnp.arange(drafts)[:, None]
    cached = jnp.where(cache_mask[None, None, None, :], cached, -jnp.inf)
    fresh_scores = jnp.where(draft_mask[:, None, None, :], fresh_scores, -jnp.inf)
    row_peak = jnp.maximum(jnp.max(cached, -1), jnp.max(fresh_scores, -1))
    cached_exp = jnp.exp(cached - row_peak[..., None])
    fresh_exp = jnp.exp(fresh_scores - row_peak[..., None])
    denominator = jnp.sum(cached_exp, -1) + jnp.sum(fresh_exp, -1)
    cached_prob = (cached_exp / denominator[..., None]).astype(jnp.bfloat16)
    fresh_prob = (fresh_exp / denominator[..., None]).astype(jnp.bfloat16)
    mixed = jnp.einsum(
        "skgl,kld->skgd", cached_prob, cache_values, preferred_element_type=jnp.float32
    )
    mixed = mixed + jnp.einsum(
        "skgt,tkd->skgd", fresh_prob, value_new, preferred_element_type=jnp.float32
    )
    return mixed.astype(jnp.bfloat16)


def by_row(
    tokens,
    w_query,
    w_key,
    w_value,
    w_out,
    shrink_qkv,
    grow_query,
    grow_key,
    grow_value,
    shrink_out,
    grow_out,
    cache_keys,
    cache_values,
    cache_lengths,
    adapter_ids,
    adapter_slots,
):
    splits = lax.axis_size("tensor")
    groups = lax.axis_size(("dp", "pipe"))
    tensor_index = lax.axis_index("tensor")
    group_index = lax.axis_index(("dp", "pipe"))
    local_rows, drafts, feature_width = tokens.shape
    per_owner = shrink_qkv.shape[0]
    rank_size = grow_out.shape[1]
    query_cols = w_query.shape[1]
    key_cols = w_key.shape[1]
    kv_heads = cache_keys.shape[1]
    head_size = cache_keys.shape[3]
    rows = splits * groups
    row_slots = jnp.repeat(slot_table(adapter_ids, adapter_slots), drafts)
    within = jnp.arange(per_owner, dtype=jnp.int32)[None, :]
    width_hot = (row_slots[:, None] == within + tensor_index * per_owner)[:, :, None]
    column_hot = (row_slots[:, None] == within + group_index * per_owner)[:, :, None]

    def spread_ranks(ranks, hot):
        return jnp.where(hot, ranks[:, None, :], 0.0).reshape(rows * drafts, -1).astype(jnp.bfloat16)

    flat_tokens = lax.all_gather(tokens, "tensor", axis=0, tiled=True).reshape(
        rows * drafts, feature_width
    )
    rank_part = jnp.einsum(
        "nd,adr->nar", flat_tokens, shrink_qkv, preferred_element_type=jnp.float32
    )
    rank_part = jnp.sum(jnp.where(width_hot, rank_part, 0.0), 1)
    rank_all = to_growers(rank_part.astype(jnp.bfloat16), splits)

    def grown(index, grow):
        ranks = spread_ranks(rank_all[:, index * rank_size : (index + 1) * rank_size], column_hot)
        return jnp.dot(
            ranks, grow.reshape(per_owner * rank_size, -1), preferred_element_type=jnp.float32
        )

    bases = [
        jnp.dot(flat_tokens, weight, preferred_element_type=jnp.float32)
        for weight in (w_query, w_key, w_value)
    ]

    def product(index, grow):
        return (bases[index] + grown(index, grow)).astype(jnp.bfloat16).reshape(rows, drafts, -1)

    partial = jnp.concatenate(
        [
            product(0, grow_query),
            product(1, grow_key),
            product(2, grow_value),
        ],
        2,
    )
    arrived = lax.all_to_all(partial, EVERY, split_axis=0, concat_axis=0, tiled=True)
    joined = jnp.sum(
        arrived.reshape(splits, groups, drafts, -1).astype(jnp.float32), 1
    ).astype(jnp.bfloat16)
    joined = jnp.transpose(joined, (1, 0, 2))
    query_heads = joined[:, :, :query_cols].reshape(drafts, -1, head_size)
    key_new = joined[:, :, query_cols : query_cols + key_cols].reshape(drafts, kv_heads, head_size)
    value_new = joined[:, :, query_cols + key_cols :].reshape(drafts, kv_heads, head_size)
    mixed = attend(
        query_heads, key_new, value_new, cache_keys[0], cache_values[0], cache_lengths[0]
    )
    mixed = jnp.transpose(mixed.reshape(drafts, splits, -1), (1, 0, 2))
    outgoing = jnp.repeat(mixed, groups, axis=0)
    flat_heads = lax.all_to_all(
        outgoing, EVERY, split_axis=0, concat_axis=0, tiled=True
    ).reshape(rows * drafts, -1)
    out_part = jnp.einsum(
        "nw,awr->nar", flat_heads, shrink_out, preferred_element_type=jnp.float32
    )
    out_part = jnp.sum(jnp.where(column_hot, out_part, 0.0), 1)
    out_rank = to_out_growers(out_part.astype(jnp.bfloat16), splits)
    out = jnp.dot(flat_heads, w_out, preferred_element_type=jnp.float32)
    out = out + jnp.dot(
        spread_ranks(out_rank, width_hot),
        grow_out.reshape(per_owner * rank_size, -1),
        preferred_element_type=jnp.float32,
    )
    blocks = lax.all_to_all(
        out.astype(jnp.bfloat16).reshape(splits, local_rows, drafts, feature_width),
        "tensor",
        split_axis=0,
        concat_axis=0,
        tiled=True,
    )
    return jnp.sum(blocks.astype(jnp.float32), 0).astype(jnp.bfloat16)


def local(*arrays):
    heads = arrays[11].shape[1]
    sizes = [lax.axis_size(name) for name in EVERY]
    if heads == 4 and sizes == [4, 2, 2]:
        return by_kernels(*arrays)
    return by_row(*arrays)


def solution(mesh):
    placed = (
        P(("parts", "tensor"), None, ("dp", "pipe")),
        P(("dp", "pipe"), "tensor"),
        P(("dp", "pipe"), "tensor"),
        P(("dp", "pipe"), "tensor"),
        P("tensor", ("dp", "pipe")),
        P("tensor", ("dp", "pipe"), None),
        P(("dp", "pipe"), None, "tensor"),
        P(("dp", "pipe"), None, "tensor"),
        P(("dp", "pipe"), None, "tensor"),
        P(("dp", "pipe"), "tensor", None),
        P("tensor", None, ("dp", "pipe")),
        P(("parts", "tensor", "dp", "pipe"), None, None, None),
        P(("parts", "tensor", "dp", "pipe"), None, None, None),
        P(("parts", "tensor", "dp", "pipe")),
        P(),
        P(),
    )
    return jax.shard_map(
        local,
        mesh=mesh,
        in_specs=placed,
        out_specs=P(("parts", "tensor"), None, ("dp", "pipe")),
        check_vma=False,
    )
```

```python
import functools
import math

import jax
import jax.numpy as jnp
import numpy as np
from jax import lax
from jax.experimental import pallas as pl
from jax.experimental.pallas import tpu as pltpu
from jax.sharding import PartitionSpec as P

rope_base = 500000.0
EVERY = ("tensor", "dp", "pipe")
GROUP = ("dp", "pipe")
VMEM = pl.BlockSpec(memory_space=pltpu.VMEM)
HBM = pl.BlockSpec(memory_space=pltpu.HBM)
MIB = 1 << 20


def dot(left, right):
    return jnp.dot(left, right, preferred_element_type=jnp.float32)


def dot_nt(left, right):
    return lax.dot_general(
        left, right, (((1,), (1,)), ((), ())), preferred_element_type=jnp.float32
    )


def iota(shape, axis):
    return lax.broadcasted_iota(jnp.int32, shape, axis)


def call(kernel, outs, ins, scratch=(), flops=0, moved=0, limit=24 * MIB):
    return pl.pallas_call(
        kernel,
        out_shape=outs,
        in_specs=ins,
        out_specs=jax.tree.map(lambda _: VMEM, outs),
        scratch_shapes=list(scratch),
        cost_estimate=pl.CostEstimate(flops=flops, bytes_accessed=moved, transcendentals=0),
        compiler_params=pltpu.CompilerParams(vmem_limit_bytes=limit),
    )


def shape(dims, kind=jnp.bfloat16):
    return jax.ShapeDtypeStruct(tuple(dims), kind)


def over(value, size):
    return value >> (size.bit_length() - 1) if size & (size - 1) == 0 else lax.div(value, size)


def rest_of(value, size):
    return value & (size - 1) if size & (size - 1) == 0 else lax.rem(value, size)


def as_gathered(sizes, group, block, draft):
    groups, blocks, drafts = sizes
    return (block * drafts + draft) * groups + group


def by_draft(sizes, group, block, draft):
    groups, blocks, drafts = sizes
    return (draft * blocks + block) * groups + group


def parts_of(order, sizes, index):
    groups, blocks, drafts = sizes
    group, left = rest_of(index, groups), over(index, groups)
    if order is as_gathered:
        return group, over(left, drafts), rest_of(left, drafts)
    return group, rest_of(left, blocks), over(left, blocks)


def turned(block):
    return lax.axis_index("tensor") ^ block


def reorder(sizes, after, before):
    groups, blocks, drafts = sizes
    rows = groups * blocks * drafts
    group, block, draft = parts_of(after, sizes, iota((rows, rows), 0))
    wanted = before(sizes, group, turned(block), draft)
    return jnp.where(wanted == iota((rows, rows), 1), 1.0, 0.0).astype(jnp.bfloat16)


def group_of():
    return lax.axis_index("dp") * lax.axis_size("pipe") + lax.axis_index("pipe")


def rank_kernel(sizes, owned, *refs):
    groups, blocks, drafts = sizes
    pieces = refs[:blocks]
    shrink_ref, slots_ref = refs[blocks : blocks + 2]
    rows_ref, rank_ref, wide = refs[-3:]
    for block in range(blocks):
        for draft in range(drafts):
            start = (block * drafts + draft) * groups
            wide[start : start + groups, :] = pieces[block][draft].astype(jnp.float32)
    rows = wide[...].astype(jnp.bfloat16)
    rows_ref[...] = rows
    place = slots_ref[:, 0:1] - lax.axis_index("tensor") * owned
    ranks = owned_ranks(
        rows, shrink_ref[...], place, shrink_ref.shape[0] // owned, rank_ref.shape[1]
    )
    put = (rank_ref.shape[0], rows.shape[0])
    draft = parts_of(as_gathered, sizes, iota((rows.shape[0], put[0]), 0))[2]
    line = slots_ref[:, 2:3] * drafts + draft
    put = jnp.where(line == iota((rows.shape[0], put[0]), 1), 1.0, 0.0).astype(jnp.bfloat16)
    ranks = lax.dot_general(
        put, ranks, (((0,), (0,)), ((), ())), preferred_element_type=jnp.float32
    )
    rank_ref[...] = ranks.astype(jnp.bfloat16)


def owned_ranks(rows, shrink, place, width, lanes):
    ranks = dot_nt(rows, shrink)
    kept = jnp.where(over(iota(ranks.shape, 1), width) == place, ranks, 0.0).astype(jnp.bfloat16)
    fold = (ranks.shape[1], lanes)
    fold = rest_of(iota(fold, 0), width) == iota(fold, 1)
    return dot(kept, jnp.where(fold, 1.0, 0.0).astype(jnp.bfloat16)).astype(jnp.bfloat16)


def spread_ranks(ranks, place, width, owned, parts):
    span = owned * width
    row = iota((ranks.shape[1], parts * span), 0)
    column = iota((ranks.shape[1], parts * span), 1)
    tile = (over(row, width) == over(column, span)) & (
        rest_of(row, width) == rest_of(column, width)
    )
    wide = dot(ranks, jnp.where(tile, 1.0, 0.0).astype(jnp.bfloat16))
    slot = over(rest_of(iota(wide.shape, 1), span), width)
    return jnp.where(slot == place, wide, 0.0).astype(jnp.bfloat16)


def product_kernel(rows_ref, *refs):
    *weights, total_ref = refs
    start = 0
    for weight in weights:
        width = weight.shape[1]
        step = width if width % 1024 else 1024
        for first in range(0, width, step):
            total_ref[:, start : start + step] = dot(
                rows_ref[...], weight[:, first : first + step]
            )
            start += step


def product(rows, *weights):
    width = sum(weight.shape[1] for weight in weights)
    return call(
        product_kernel,
        shape((rows.shape[0], width), jnp.float32),
        [VMEM] * (1 + len(weights)),
    )(rows, *weights)


def prepare_kernel(sizes, owned, ids_ref, pool_ref, length_ref, *refs):
    slots_ref, cosine_ref, sine_ref = refs[-3:]
    groups, blocks, drafts = sizes
    width = cosine_ref.shape[1]
    lane = iota(cosine_ref.shape, 1)
    half = (lane & (width // 2 - 1)).astype(jnp.float32)
    positions = (lax.rem(iota(cosine_ref.shape, 0), drafts) + length_ref[0]).astype(jnp.float32)
    angles = positions * jnp.exp(half * (-2.0 * math.log(rope_base) / width))
    cosine_ref[...] = jnp.cos(angles)
    sine_ref[...] = jnp.sin(angles) * jnp.where(lane < width // 2, -1.0, 1.0)
    index = iota(slots_ref.shape, 0)
    column = iota(slots_ref.shape, 1)
    near = parts_of(as_gathered, sizes, index)
    far = parts_of(by_draft, sizes, index)
    row_group = jnp.where(column == 1, far[0], near[0])
    row_block = jnp.where(column == 1, far[1], turned(near[1]))
    place = row_block * groups + row_group
    slots = jnp.zeros(slots_ref.shape, jnp.int32)
    sent, taken = 0, 0
    for row in range(blocks * groups):
        slot = pool_ref[ids_ref[row]]
        owner = over(slot, owned)
        sends = jnp.where(owner == lax.axis_index("tensor"), 1, 0)
        takes = jnp.where(owner == group_of(), 1, 0)
        line = jnp.where(column == 2, sent - 64 * (1 - sends), taken - 64 * (1 - takes))
        slots = jnp.where(place == row, jnp.where(column < 2, slot, line), slots)
        sent, taken = sent + sends, taken + takes
    slots_ref[...] = slots


def prepare(sizes, owned, ids, pool, lengths, table, later):
    groups, blocks, drafts = sizes
    smem = pl.BlockSpec(memory_space=pltpu.SMEM)
    table = shape(table, jnp.float32)
    return call(
        functools.partial(prepare_kernel, sizes, owned),
        [shape((groups * blocks * drafts, 128), jnp.int32), table, table],
        [smem, smem, smem] + [HBM] * 3,
        limit=40 * MIB,
    )(ids, pool, lengths, *[later] * 3)


def grow_kernel(sizes, width, total_ref, slots_ref, *refs):
    groups, blocks, drafts = sizes
    ranks_in, grows, (out_ref, held) = refs[:2], refs[2:5], refs[-2:]
    group = group_of()
    requests = groups * blocks
    lines = out_ref.shape[1]
    held[...] = jnp.zeros(held.shape, jnp.float32)
    owned = grows[0].shape[0] // width
    ranks = ranks_in[0][...].astype(jnp.float32)
    for other in ranks_in[1:]:
        ranks = ranks + other[...].astype(jnp.float32)
    get = (total_ref.shape[0], ranks.shape[0])
    draft = parts_of(as_gathered, sizes, iota(get, 0))[2]
    get = slots_ref[:, 3:4] * drafts + draft == iota(get, 1)
    ranks = dot(jnp.where(get, 1.0, 0.0).astype(jnp.bfloat16), ranks.astype(jnp.bfloat16))
    place = slots_ref[:, 0:1] - group * owned
    wide = spread_ranks(ranks.astype(jnp.bfloat16), place, width, owned, len(grows))
    arranged = reorder(sizes, by_draft, as_gathered)
    start, column = 0, 0
    for index, grow in enumerate(grows):
        deep, cols = grow.shape
        full = total_ref[:, column : column + cols] + dot(
            wide[:, index * deep : (index + 1) * deep], grow[...]
        )
        column += cols
        full = dot(arranged, full.astype(jnp.bfloat16))
        for head in range(cols // 128):
            for draft in range(drafts):
                held[pl.ds(start + draft, requests, stride=lines), :] = full[
                    draft * requests : (draft + 1) * requests, head * 128 : (head + 1) * 128
                ]
            start += drafts
    for row in range(requests):
        out_ref[row] = held[row * lines : (row + 1) * lines, :].astype(jnp.bfloat16)


def attend_kernel(
    sizes, arrived_ref, keys_ref, values_ref, length_ref, cosine_ref, sine_ref, out_ref, *scratch
):
    groups, blocks, drafts = sizes
    (fresh_s,) = scratch
    cache_size, head_size = keys_ref.shape[2:]
    count = out_ref.shape[1]
    scale = 1.0 / math.sqrt(head_size)
    fresh_s[...] = jnp.zeros(fresh_s.shape, jnp.float32)
    scores = []
    for block in range(blocks):
        joined = arrived_ref[block * groups].astype(jnp.float32)
        for other in range(1, groups):
            joined = joined + arrived_ref[block * groups + other].astype(jnp.float32)
        joined = joined.astype(jnp.bfloat16).astype(jnp.float32)
        rotated = joined * cosine_ref[...] + pltpu.roll(joined, head_size // 2, 1) * sine_ref[...]
        fresh_s[2 * block, 0:drafts, :] = rotated[count : count + drafts]
        fresh_s[2 * block + 1, 0:drafts, :] = joined[count + drafts : count + 2 * drafts]
        query = rotated[0:count].astype(jnp.bfloat16)
        old = dot_nt(query, keys_ref[0, block])
        new = dot_nt(query, fresh_s[2 * block].astype(jnp.bfloat16))
        scores.append(jnp.concatenate([old, new], 1))
    scores = jnp.concatenate(scores, 0) * scale
    column = iota(scores.shape, 1)
    limit = cache_size + lax.rem(iota((scores.shape[0], 1), 0), drafts)
    seen = (column < length_ref[0]) | ((column >= cache_size) & (column <= limit))
    scores = jnp.where(seen, scores, -jnp.inf)
    scores = jnp.exp(scores - jnp.max(scores, 1, keepdims=True))
    below = 1.0 / jnp.sum(scores, 1, keepdims=True)
    probs = (scores * below).astype(jnp.bfloat16)
    for block in range(blocks):
        mine = probs[block * count : (block + 1) * count]
        mixed = dot(mine[:, :cache_size], values_ref[0, block]) + dot(
            mine[:, cache_size:], fresh_s[2 * block + 1].astype(jnp.bfloat16)
        )
        mixed = mixed.astype(jnp.bfloat16)
        for target in range(groups):
            out_ref[block * groups + target] = mixed


def add_kernel(left_ref, right_ref, out_ref):
    total = left_ref[...].astype(jnp.float32) + right_ref[...].astype(jnp.float32)
    out_ref[...] = total.astype(jnp.bfloat16)


def packing(rows, width, lanes):
    parts = lanes // width
    return parts, rows // parts


def out_rank_kernel(sizes, owned, got_ref, shrink_ref, slots_ref, *refs):
    rows_ref, rank_ref, wide = refs[-3:]
    drafts = sizes[2]
    requests, lines, head_size = got_ref.shape
    for row in range(requests):
        wide[row * lines : (row + 1) * lines, :] = got_ref[row].astype(jnp.float32)
    for head in range(lines // drafts):
        for draft in range(drafts):
            rows_ref[
                draft * requests : (draft + 1) * requests,
                head * head_size : (head + 1) * head_size,
            ] = wide[pl.ds(head * drafts + draft, requests, stride=lines), :].astype(jnp.bfloat16)
    rows = rows_ref[...]
    place = slots_ref[:, 1:2] - group_of() * owned
    width = shrink_ref.shape[0] // owned
    held, lanes = rank_ref.shape
    parts, span = packing(rows.shape[0], width, lanes)
    ranks = dot_nt(rows, shrink_ref[...])
    kept = jnp.where(over(iota(ranks.shape, 1), width) == place, ranks, 0.0).astype(jnp.bfloat16)
    fold = (ranks.shape[1], lanes)
    fold = rest_of(iota(fold, 0), width) == rest_of(iota(fold, 1), width)
    ranks = dot(kept, jnp.where(fold, 1.0, 0.0).astype(jnp.bfloat16))
    mine = over(iota(ranks.shape, 1), width) == over(iota(ranks.shape, 0), span)
    ranks = jnp.where(mine, ranks, 0.0).astype(jnp.bfloat16)
    put = (held, rows.shape[0])
    put = iota(put, 0) == rest_of(iota(put, 1), span)
    ranks = dot(jnp.where(put, 1.0, 0.0).astype(jnp.bfloat16), ranks)
    rank_ref[...] = ranks.astype(jnp.bfloat16)


def out_grow_kernel(sizes, width, total_ref, slots_ref, grow_ref, *refs):
    groups, blocks, drafts = sizes
    ranks_in, outs = refs[:2], refs[2:]
    owned = grow_ref.shape[0] // width
    me = lax.axis_index("tensor")
    ranks = ranks_in[0][...].astype(jnp.float32)
    for other in ranks_in[1:]:
        ranks = ranks + other[...].astype(jnp.float32)
    count = total_ref.shape[0]
    held, lanes = ranks.shape
    parts, span = packing(count, width, lanes)
    put = rest_of(iota((count, held), 0), span) == iota((count, held), 1)
    ranks = dot(jnp.where(put, 1.0, 0.0).astype(jnp.bfloat16), ranks.astype(jnp.bfloat16))
    mine = over(iota(ranks.shape, 1), width) == over(iota(ranks.shape, 0), span)
    ranks = jnp.where(mine, ranks, 0.0).astype(jnp.bfloat16)
    tile = (lanes, owned * width)
    tile = rest_of(iota(tile, 0), width) == rest_of(iota(tile, 1), width)
    ranks = dot(ranks, jnp.where(tile, 1.0, 0.0).astype(jnp.bfloat16))
    place = slots_ref[:, 1:2] - me * owned
    wide = jnp.where(over(iota(ranks.shape, 1), width) == place, ranks, 0.0).astype(jnp.bfloat16)
    full = (total_ref[...] + dot(wide, grow_ref[...])).astype(jnp.bfloat16)
    full = dot(reorder(sizes, as_gathered, by_draft), full).astype(jnp.bfloat16)
    for block in range(blocks):
        for draft in range(drafts):
            start = (block * drafts + draft) * groups
            outs[block][draft] = full[start : start + groups]


def by_kernels(
    tokens,
    w_query,
    w_key,
    w_value,
    w_out,
    shrink_qkv,
    grow_query,
    grow_key,
    grow_value,
    shrink_out,
    grow_out,
    cache_keys,
    cache_values,
    cache_lengths,
    adapter_ids,
    adapter_slots,
):
    blocks = lax.axis_size("tensor")
    groups = lax.axis_size(GROUP)
    _, drafts, features = tokens.shape
    sizes = (groups, blocks, drafts)
    owned = shrink_qkv.shape[0]
    width = grow_out.shape[1]
    head_size = cache_keys.shape[3]
    span = blocks * drafts
    count = groups * span
    lanes = -(-shrink_qkv.shape[2] // 128) * 128

    def over_tensor(value, shift):
        route = [(t, t ^ shift) for t in range(blocks)]
        return lax.ppermute(value, "tensor", route)

    def over_core(value):
        return lax.ppermute(value, "pipe", [(0, 1), (1, 0)])

    def to_growers(value, flip):
        route = [
            (t * groups + 2 * x + c, (2 * c + (x ^ flip)) * groups + t)
            for t in range(blocks)
            for x in range(2)
            for c in range(2)
        ]
        return lax.ppermute(value, EVERY, route)

    def to_out_growers(value, flip):
        route = [
            (t * groups + g, g * groups + 2 * (t % 2) + ((t // 2) ^ flip))
            for t in range(blocks)
            for g in range(groups)
        ]
        return lax.ppermute(value, EVERY, route)

    def added(left, right):
        return call(add_kernel, shape(left.shape), [VMEM] * 2)(left, right)

    def exchange(value):
        return lax.all_to_all(value, EVERY, split_axis=0, concat_axis=0, tiled=True)

    mine = jnp.transpose(tokens, (1, 0, 2))
    pieces = [mine] + [over_tensor(mine, shift) for shift in range(1, blocks)]

    lines = (w_query.shape[1] // head_size + 2) * drafts
    lines = -(-lines // 8) * 8
    slots, cosine, sine = prepare(
        sizes, owned, adapter_ids, adapter_slots, cache_lengths, (lines, head_size), w_out
    )
    packed = -(-2 * blocks * drafts // 16) * 16
    shrink_in = jnp.transpose(shrink_qkv, (0, 2, 1)).reshape(-1, features)
    rows, rank_part = call(
        functools.partial(rank_kernel, sizes, owned),
        [shape((count, features)), shape((packed, lanes))],
        [VMEM] * (blocks + 2),
        [pltpu.VMEM((count, features), jnp.float32)],
        2 * count * shrink_qkv.size,
        2 * shrink_qkv.size + 4 * count * features,
    )(*pieces, shrink_in, slots)
    rank_part = added(rank_part, over_core(rank_part))
    ranks = [to_growers(rank_part, flip) for flip in range(2)]
    total = product(rows, w_query, w_key, w_value)
    cols = total.shape[1]
    head_cols = w_query.shape[1]
    query_lines = head_cols // head_size * drafts
    sent = call(
        functools.partial(grow_kernel, sizes, width),
        shape((blocks * groups, lines, head_size)),
        [VMEM] * 7 + [HBM] * 2,
        [pltpu.VMEM((blocks * groups * lines, head_size), jnp.float32)],
        limit=40 * MIB,
    )(
        total,
        slots,
        *ranks,
        *[grow.reshape(owned * width, -1) for grow in (grow_query, grow_key, grow_value)],
        *[w_out] * 2,
    )
    mixed = call(
        functools.partial(attend_kernel, sizes),
        shape((blocks * groups, query_lines, head_size)),
        [VMEM] * 3 + [pl.BlockSpec(memory_space=pltpu.SMEM)] + [VMEM] * 2,
        [pltpu.VMEM((2 * blocks, 128, head_size), jnp.float32)],
    )(exchange(sent), cache_keys, cache_values, cache_lengths, cosine, sine)
    gathered = exchange(mixed)
    held = -(-packing(count, width, 128)[1] // 16) * 16
    out_rows, out_part = call(
        functools.partial(out_rank_kernel, sizes, owned),
        [shape((count, head_cols)), shape((held, 128))],
        [VMEM] * 3 + [HBM] * 4,
        [pltpu.VMEM((blocks * groups * query_lines, head_size), jnp.float32)],
        limit=40 * MIB,
    )(gathered, jnp.transpose(shrink_out, (0, 2, 1)).reshape(-1, head_cols), slots, *[w_query] * 4)
    out_part = added(out_part, over_tensor(out_part, 1))
    out_ranks = [to_out_growers(out_part, flip) for flip in range(2)]
    out_total = product(out_rows, w_out)
    out_cols = out_total.shape[1]
    leaving = call(
        functools.partial(out_grow_kernel, sizes, width),
        [shape((drafts, groups, out_cols))] * blocks,
        [VMEM] * 5,
        [],
        2 * count * owned * width * out_cols,
        8 * count * out_cols + 2 * owned * width * out_cols,
    )(out_total, slots, grow_out.reshape(owned * width, -1), *out_ranks)
    result = leaving[0].astype(jnp.float32)
    for shift in sorted(range(1, blocks), key=lambda shift: shift < blocks // 2):
        result = result + over_tensor(leaving[shift], shift).astype(jnp.float32)
    return jnp.transpose(result.astype(jnp.bfloat16), (1, 0, 2))


def rotate(vectors, positions):
    half_size = vectors.shape[-1] // 2
    frequency = rope_base ** (-2.0 * jnp.arange(half_size, dtype=jnp.float32) / vectors.shape[-1])
    angles = positions[:, None, None] * frequency
    cosine = jnp.cos(angles)
    sine_value = jnp.sin(angles)
    first_half = vectors[..., :half_size]
    second = vectors[..., half_size:]
    return jnp.concatenate(
        [first_half * cosine - second * sine_value, second * cosine + first_half * sine_value], -1
    )


def to_growers(partial, splits):
    total = None
    for shift in range(splits):
        route = [
            (t * splits + g, ((g + shift) % splits) * splits + t)
            for t in range(splits)
            for g in range(splits)
        ]
        got = lax.ppermute(partial, EVERY, route).astype(jnp.float32)
        total = got if total is None else total + got
    return total


def to_out_growers(partial, splits):
    total = None
    for shift in range(splits):
        route = [
            (t * splits + g, g * splits + (t + shift) % splits)
            for t in range(splits)
            for g in range(splits)
        ]
        got = lax.ppermute(partial, EVERY, route).astype(jnp.float32)
        total = got if total is None else total + got
    return total


def slot_table(adapter_ids, adapter_slots):
    matches = adapter_ids[:, None] == jnp.arange(adapter_slots.shape[0], dtype=jnp.int32)[None, :]
    return jnp.sum(jnp.where(matches, adapter_slots[None, :], 0), axis=1)


def attend(query_heads, key_new, value_new, cache_keys, cache_values, length):
    drafts, head_count, head_size = query_heads.shape
    kv_heads, cache_size, _ = cache_keys.shape
    positions = (length + jnp.arange(drafts, dtype=jnp.int32)).astype(jnp.float32)
    query_rot = rotate(query_heads.astype(jnp.float32), positions).astype(jnp.bfloat16)
    key_rot = rotate(key_new.astype(jnp.float32), positions).astype(jnp.bfloat16)
    grouped = query_rot.reshape(drafts, kv_heads, head_count // kv_heads, head_size)
    score_scale = 1.0 / math.sqrt(head_size)
    cached = (
        jnp.einsum("skgd,kld->skgl", grouped, cache_keys, preferred_element_type=jnp.float32)
        * score_scale
    )
    fresh_scores = (
        jnp.einsum("skgd,tkd->skgt", grouped, key_rot, preferred_element_type=jnp.float32)
        * score_scale
    )
    cache_mask = jnp.arange(cache_size, dtype=jnp.int32) < length
    draft_mask = jnp.arange(drafts)[None, :] <= jnp.arange(drafts)[:, None]
    cached = jnp.where(cache_mask[None, None, None, :], cached, -jnp.inf)
    fresh_scores = jnp.where(draft_mask[:, None, None, :], fresh_scores, -jnp.inf)
    row_peak = jnp.maximum(jnp.max(cached, -1), jnp.max(fresh_scores, -1))
    cached_exp = jnp.exp(cached - row_peak[..., None])
    fresh_exp = jnp.exp(fresh_scores - row_peak[..., None])
    denominator = jnp.sum(cached_exp, -1) + jnp.sum(fresh_exp, -1)
    cached_prob = (cached_exp / denominator[..., None]).astype(jnp.bfloat16)
    fresh_prob = (fresh_exp / denominator[..., None]).astype(jnp.bfloat16)
    mixed = jnp.einsum(
        "skgl,kld->skgd", cached_prob, cache_values, preferred_element_type=jnp.float32
    )
    mixed = mixed + jnp.einsum(
        "skgt,tkd->skgd", fresh_prob, value_new, preferred_element_type=jnp.float32
    )
    return mixed.astype(jnp.bfloat16)


def by_row(
    tokens,
    w_query,
    w_key,
    w_value,
    w_out,
    shrink_qkv,
    grow_query,
    grow_key,
    grow_value,
    shrink_out,
    grow_out,
    cache_keys,
    cache_values,
    cache_lengths,
    adapter_ids,
    adapter_slots,
):
    splits = lax.axis_size("tensor")
    groups = lax.axis_size(("dp", "pipe"))
    tensor_index = lax.axis_index("tensor")
    group_index = lax.axis_index(("dp", "pipe"))
    local_rows, drafts, feature_width = tokens.shape
    per_owner = shrink_qkv.shape[0]
    rank_size = grow_out.shape[1]
    query_cols = w_query.shape[1]
    key_cols = w_key.shape[1]
    kv_heads = cache_keys.shape[1]
    head_size = cache_keys.shape[3]
    rows = splits * groups
    row_slots = jnp.repeat(slot_table(adapter_ids, adapter_slots), drafts)
    within = jnp.arange(per_owner, dtype=jnp.int32)[None, :]
    width_hot = (row_slots[:, None] == within + tensor_index * per_owner)[:, :, None]
    column_hot = (row_slots[:, None] == within + group_index * per_owner)[:, :, None]

    def spread_ranks(ranks, hot):
        return jnp.where(hot, ranks[:, None, :], 0.0).reshape(rows * drafts, -1).astype(jnp.bfloat16)

    flat_tokens = lax.all_gather(tokens, "tensor", axis=0, tiled=True).reshape(
        rows * drafts, feature_width
    )
    rank_part = jnp.einsum(
        "nd,adr->nar", flat_tokens, shrink_qkv, preferred_element_type=jnp.float32
    )
    rank_part = jnp.sum(jnp.where(width_hot, rank_part, 0.0), 1)
    rank_all = to_growers(rank_part.astype(jnp.bfloat16), splits)

    def grown(index, grow):
        ranks = spread_ranks(rank_all[:, index * rank_size : (index + 1) * rank_size], column_hot)
        return jnp.dot(
            ranks, grow.reshape(per_owner * rank_size, -1), preferred_element_type=jnp.float32
        )

    bases = [
        jnp.dot(flat_tokens, weight, preferred_element_type=jnp.float32)
        for weight in (w_query, w_key, w_value)
    ]

    def product(index, grow):
        return (bases[index] + grown(index, grow)).astype(jnp.bfloat16).reshape(rows, drafts, -1)

    partial = jnp.concatenate(
        [
            product(0, grow_query),
            product(1, grow_key),
            product(2, grow_value),
        ],
        2,
    )
    arrived = lax.all_to_all(partial, EVERY, split_axis=0, concat_axis=0, tiled=True)
    joined = jnp.sum(
        arrived.reshape(splits, groups, drafts, -1).astype(jnp.float32), 1
    ).astype(jnp.bfloat16)
    joined = jnp.transpose(joined, (1, 0, 2))
    query_heads = joined[:, :, :query_cols].reshape(drafts, -1, head_size)
    key_new = joined[:, :, query_cols : query_cols + key_cols].reshape(drafts, kv_heads, head_size)
    value_new = joined[:, :, query_cols + key_cols :].reshape(drafts, kv_heads, head_size)
    mixed = attend(
        query_heads, key_new, value_new, cache_keys[0], cache_values[0], cache_lengths[0]
    )
    mixed = jnp.transpose(mixed.reshape(drafts, splits, -1), (1, 0, 2))
    outgoing = jnp.repeat(mixed, groups, axis=0)
    flat_heads = lax.all_to_all(
        outgoing, EVERY, split_axis=0, concat_axis=0, tiled=True
    ).reshape(rows * drafts, -1)
    out_part = jnp.einsum(
        "nw,awr->nar", flat_heads, shrink_out, preferred_element_type=jnp.float32
    )
    out_part = jnp.sum(jnp.where(column_hot, out_part, 0.0), 1)
    out_rank = to_out_growers(out_part.astype(jnp.bfloat16), splits)
    out = jnp.dot(flat_heads, w_out, preferred_element_type=jnp.float32)
    out = out + jnp.dot(
        spread_ranks(out_rank, width_hot),
        grow_out.reshape(per_owner * rank_size, -1),
        preferred_element_type=jnp.float32,
    )
    blocks = lax.all_to_all(
        out.astype(jnp.bfloat16).reshape(splits, local_rows, drafts, feature_width),
        "tensor",
        split_axis=0,
        concat_axis=0,
        tiled=True,
    )
    return jnp.sum(blocks.astype(jnp.float32), 0).astype(jnp.bfloat16)


def local(*arrays):
    heads = arrays[11].shape[1]
    sizes = [lax.axis_size(name) for name in EVERY]
    if heads == 4 and sizes == [4, 2, 2]:
        return by_kernels(*arrays)
    return by_row(*arrays)


def solution(mesh):
    placed = (
        P(("parts", "tensor"), None, ("dp", "pipe")),
        P(("dp", "pipe"), "tensor"),
        P(("dp", "pipe"), "tensor"),
        P(("dp", "pipe"), "tensor"),
        P("tensor", ("dp", "pipe")),
        P("tensor", ("dp", "pipe"), None),
        P(("dp", "pipe"), None, "tensor"),
        P(("dp", "pipe"), None, "tensor"),
        P(("dp", "pipe"), None, "tensor"),
        P(("dp", "pipe"), "tensor", None),
        P("tensor", None, ("dp", "pipe")),
        P(("parts", "tensor", "dp", "pipe"), None, None, None),
        P(("parts", "tensor", "dp", "pipe"), None, None, None),
        P(("parts", "tensor", "dp", "pipe")),
        P(),
        P(),
    )
    return jax.shard_map(
        local,
        mesh=mesh,
        in_specs=placed,
        out_specs=P(("parts", "tensor"), None, ("dp", "pipe")),
        check_vma=False,
    )
```

```python
import functools
import math

import jax
import jax.numpy as jnp
import numpy as np
from jax import lax
from jax.experimental import pallas as pl
from jax.experimental.pallas import tpu as pltpu
from jax.sharding import PartitionSpec as P

rope_base = 500000.0
EVERY = ("tensor", "dp", "pipe")
GROUP = ("dp", "pipe")
VMEM = pl.BlockSpec(memory_space=pltpu.VMEM)
HBM = pl.BlockSpec(memory_space=pltpu.HBM)
MIB = 1 << 20


def dot(left, right):
    return jnp.dot(left, right, preferred_element_type=jnp.float32)


def dot_nt(left, right):
    return lax.dot_general(
        left, right, (((1,), (1,)), ((), ())), preferred_element_type=jnp.float32
    )


def iota(shape, axis):
    return lax.broadcasted_iota(jnp.int32, shape, axis)


def call(kernel, outs, ins, scratch=(), flops=0, moved=0, limit=24 * MIB):
    return pl.pallas_call(
        kernel,
        out_shape=outs,
        in_specs=ins,
        out_specs=jax.tree.map(lambda _: VMEM, outs),
        scratch_shapes=list(scratch),
        cost_estimate=pl.CostEstimate(flops=flops, bytes_accessed=moved, transcendentals=0),
        compiler_params=pltpu.CompilerParams(vmem_limit_bytes=limit),
    )


def shape(dims, kind=jnp.bfloat16):
    return jax.ShapeDtypeStruct(tuple(dims), kind)


def over(value, size):
    return value >> (size.bit_length() - 1) if size & (size - 1) == 0 else lax.div(value, size)


def rest_of(value, size):
    return value & (size - 1) if size & (size - 1) == 0 else lax.rem(value, size)


def as_gathered(sizes, group, block, draft):
    groups, blocks, drafts = sizes
    return (block * drafts + draft) * groups + group


def by_draft(sizes, group, block, draft):
    groups, blocks, drafts = sizes
    return (draft * blocks + block) * groups + group


def parts_of(order, sizes, index):
    groups, blocks, drafts = sizes
    group, left = rest_of(index, groups), over(index, groups)
    if order is as_gathered:
        return group, over(left, drafts), rest_of(left, drafts)
    return group, rest_of(left, blocks), over(left, blocks)


def turned(block):
    return lax.axis_index("tensor") ^ block


def reorder(sizes, after, before):
    groups, blocks, drafts = sizes
    rows = groups * blocks * drafts
    group, block, draft = parts_of(after, sizes, iota((rows, rows), 0))
    wanted = before(sizes, group, turned(block), draft)
    return jnp.where(wanted == iota((rows, rows), 1), 1.0, 0.0).astype(jnp.bfloat16)


def group_of():
    return lax.axis_index("dp") * lax.axis_size("pipe") + lax.axis_index("pipe")


def rank_kernel(sizes, owned, *refs):
    groups, blocks, drafts = sizes
    pieces = refs[:blocks]
    shrink_ref, slots_ref = refs[blocks : blocks + 2]
    rows_ref, rank_ref, wide = refs[-3:]
    for block in range(blocks):
        for draft in range(drafts):
            start = (block * drafts + draft) * groups
            wide[start : start + groups, :] = pieces[block][draft].astype(jnp.float32)
    rows = wide[...].astype(jnp.bfloat16)
    rows_ref[...] = rows
    place = slots_ref[:, 0:1] - lax.axis_index("tensor") * owned
    ranks = owned_ranks(
        rows, shrink_ref[...], place, shrink_ref.shape[0] // owned, rank_ref.shape[1]
    )
    put = (rank_ref.shape[0], rows.shape[0])
    draft = parts_of(as_gathered, sizes, iota((rows.shape[0], put[0]), 0))[2]
    line = slots_ref[:, 2:3] * drafts + draft
    put = jnp.where(line == iota((rows.shape[0], put[0]), 1), 1.0, 0.0).astype(jnp.bfloat16)
    ranks = lax.dot_general(
        put, ranks, (((0,), (0,)), ((), ())), preferred_element_type=jnp.float32
    )
    rank_ref[...] = ranks.astype(jnp.bfloat16)


def owned_ranks(rows, shrink, place, width, lanes):
    ranks = dot_nt(rows, shrink)
    kept = jnp.where(over(iota(ranks.shape, 1), width) == place, ranks, 0.0).astype(jnp.bfloat16)
    fold = (ranks.shape[1], lanes)
    fold = rest_of(iota(fold, 0), width) == iota(fold, 1)
    return dot(kept, jnp.where(fold, 1.0, 0.0).astype(jnp.bfloat16)).astype(jnp.bfloat16)


def spread_ranks(ranks, place, width, owned, parts):
    span = owned * width
    row = iota((ranks.shape[1], parts * span), 0)
    column = iota((ranks.shape[1], parts * span), 1)
    tile = (over(row, width) == over(column, span)) & (
        rest_of(row, width) == rest_of(column, width)
    )
    wide = dot(ranks, jnp.where(tile, 1.0, 0.0).astype(jnp.bfloat16))
    slot = over(rest_of(iota(wide.shape, 1), span), width)
    return jnp.where(slot == place, wide, 0.0).astype(jnp.bfloat16)


def product_kernel(rows_ref, *refs):
    *weights, total_ref = refs
    start = 0
    for weight in weights:
        width = weight.shape[1]
        step = width if width % 1024 else 1024
        for first in range(0, width, step):
            total_ref[:, start : start + step] = dot(
                rows_ref[...], weight[:, first : first + step]
            )
            start += step


def product(rows, *weights):
    width = sum(weight.shape[1] for weight in weights)
    return call(
        product_kernel,
        shape((rows.shape[0], width), jnp.float32),
        [VMEM] * (1 + len(weights)),
    )(rows, *weights)


def prepare_kernel(sizes, owned, ids_ref, pool_ref, length_ref, *refs):
    slots_ref, cosine_ref, sine_ref = refs[-3:]
    groups, blocks, drafts = sizes
    width = cosine_ref.shape[1]
    lane = iota(cosine_ref.shape, 1)
    half = (lane & (width // 2 - 1)).astype(jnp.float32)
    positions = (lax.rem(iota(cosine_ref.shape, 0), drafts) + length_ref[0]).astype(jnp.float32)
    angles = positions * jnp.exp(half * (-2.0 * math.log(rope_base) / width))
    cosine_ref[...] = jnp.cos(angles)
    sine_ref[...] = jnp.sin(angles) * jnp.where(lane < width // 2, -1.0, 1.0)
    index = iota(slots_ref.shape, 0)
    column = iota(slots_ref.shape, 1)
    near = parts_of(as_gathered, sizes, index)
    far = parts_of(by_draft, sizes, index)
    row_group = jnp.where(column == 1, far[0], near[0])
    row_block = jnp.where(column == 1, far[1], turned(near[1]))
    place = row_block * groups + row_group
    slots = jnp.zeros(slots_ref.shape, jnp.int32)
    sent, taken = 0, 0
    for row in range(blocks * groups):
        slot = pool_ref[ids_ref[row]]
        owner = over(slot, owned)
        sends = jnp.where(owner == lax.axis_index("tensor"), 1, 0)
        takes = jnp.where(owner == group_of(), 1, 0)
        line = jnp.where(column == 2, sent - 64 * (1 - sends), taken - 64 * (1 - takes))
        slots = jnp.where(place == row, jnp.where(column < 2, slot, line), slots)
        sent, taken = sent + sends, taken + takes
    slots_ref[...] = slots


def prepare(sizes, owned, ids, pool, lengths, table, later):
    groups, blocks, drafts = sizes
    smem = pl.BlockSpec(memory_space=pltpu.SMEM)
    table = shape(table, jnp.float32)
    return call(
        functools.partial(prepare_kernel, sizes, owned),
        [shape((groups * blocks * drafts, 128), jnp.int32), table, table],
        [smem, smem, smem] + [HBM] * 3,
        limit=40 * MIB,
    )(ids, pool, lengths, *[later] * 3)


def grow_kernel(sizes, width, total_ref, slots_ref, *refs):
    groups, blocks, drafts = sizes
    ranks_in, grows, (out_ref, held) = refs[:2], refs[2:5], refs[-2:]
    group = group_of()
    requests = groups * blocks
    lines = out_ref.shape[1]
    held[...] = jnp.zeros(held.shape, jnp.float32)
    owned = grows[0].shape[0] // width
    ranks = ranks_in[0][...].astype(jnp.float32)
    for other in ranks_in[1:]:
        ranks = ranks + other[...].astype(jnp.float32)
    get = (total_ref.shape[0], ranks.shape[0])
    draft = parts_of(as_gathered, sizes, iota(get, 0))[2]
    get = slots_ref[:, 3:4] * drafts + draft == iota(get, 1)
    ranks = dot(jnp.where(get, 1.0, 0.0).astype(jnp.bfloat16), ranks.astype(jnp.bfloat16))
    place = slots_ref[:, 0:1] - group * owned
    wide = spread_ranks(ranks.astype(jnp.bfloat16), place, width, owned, len(grows))
    arranged = reorder(sizes, by_draft, as_gathered)
    start, column = 0, 0
    for index, grow in enumerate(grows):
        deep, cols = grow.shape
        full = total_ref[:, column : column + cols] + dot(
            wide[:, index * deep : (index + 1) * deep], grow[...]
        )
        column += cols
        full = dot(arranged, full.astype(jnp.bfloat16))
        for head in range(cols // 128):
            for draft in range(drafts):
                held[pl.ds(start + draft, requests, stride=lines), :] = full[
                    draft * requests : (draft + 1) * requests, head * 128 : (head + 1) * 128
                ]
            start += drafts
    for row in range(requests):
        out_ref[row] = held[row * lines : (row + 1) * lines, :].astype(jnp.bfloat16)


def attend_kernel(
    sizes, arrived_ref, keys_ref, values_ref, length_ref, cosine_ref, sine_ref, out_ref, *scratch
):
    groups, blocks, drafts = sizes
    (fresh_s,) = scratch
    cache_size, head_size = keys_ref.shape[2:]
    count = out_ref.shape[1]
    scale = 1.0 / math.sqrt(head_size)
    fresh_s[...] = jnp.zeros(fresh_s.shape, jnp.float32)
    scores = []
    for block in range(blocks):
        joined = arrived_ref[block * groups].astype(jnp.float32)
        for other in range(1, groups):
            joined = joined + arrived_ref[block * groups + other].astype(jnp.float32)
        joined = joined.astype(jnp.bfloat16).astype(jnp.float32)
        rotated = joined * cosine_ref[...] + pltpu.roll(joined, head_size // 2, 1) * sine_ref[...]
        fresh_s[2 * block, 0:drafts, :] = rotated[count : count + drafts]
        fresh_s[2 * block + 1, 0:drafts, :] = joined[count + drafts : count + 2 * drafts]
        query = rotated[0:count].astype(jnp.bfloat16)
        old = dot_nt(query, keys_ref[0, block])
        new = dot_nt(query, fresh_s[2 * block].astype(jnp.bfloat16))
        scores.append(jnp.concatenate([old, new], 1))
    scores = jnp.concatenate(scores, 0) * scale
    column = iota(scores.shape, 1)
    limit = cache_size + lax.rem(iota((scores.shape[0], 1), 0), drafts)
    seen = (column < length_ref[0]) | ((column >= cache_size) & (column <= limit))
    scores = jnp.where(seen, scores, -jnp.inf)
    scores = jnp.exp(scores - jnp.max(scores, 1, keepdims=True))
    below = 1.0 / jnp.sum(scores, 1, keepdims=True)
    probs = (scores * below).astype(jnp.bfloat16)
    for block in range(blocks):
        mine = probs[block * count : (block + 1) * count]
        mixed = dot(mine[:, :cache_size], values_ref[0, block]) + dot(
            mine[:, cache_size:], fresh_s[2 * block + 1].astype(jnp.bfloat16)
        )
        mixed = mixed.astype(jnp.bfloat16)
        for target in range(groups):
            out_ref[block * groups + target] = mixed


def add_kernel(left_ref, right_ref, out_ref):
    total = left_ref[...].astype(jnp.float32) + right_ref[...].astype(jnp.float32)
    out_ref[...] = total.astype(jnp.bfloat16)


def packing(rows, width, lanes):
    parts = lanes // width
    return parts, rows // parts


def out_rank_kernel(sizes, owned, got_ref, shrink_ref, slots_ref, *refs):
    rows_ref, rank_ref, wide = refs[-3:]
    drafts = sizes[2]
    requests, lines, head_size = got_ref.shape
    for row in range(requests):
        wide[row * lines : (row + 1) * lines, :] = got_ref[row].astype(jnp.float32)
    for head in range(lines // drafts):
        for draft in range(drafts):
            rows_ref[
                draft * requests : (draft + 1) * requests,
                head * head_size : (head + 1) * head_size,
            ] = wide[pl.ds(head * drafts + draft, requests, stride=lines), :].astype(jnp.bfloat16)
    rows = rows_ref[...]
    place = slots_ref[:, 1:2] - group_of() * owned
    width = shrink_ref.shape[0] // owned
    held, lanes = rank_ref.shape
    parts, span = packing(rows.shape[0], width, lanes)
    ranks = dot_nt(rows, shrink_ref[...])
    kept = jnp.where(over(iota(ranks.shape, 1), width) == place, ranks, 0.0).astype(jnp.bfloat16)
    fold = (ranks.shape[1], lanes)
    fold = rest_of(iota(fold, 0), width) == rest_of(iota(fold, 1), width)
    ranks = dot(kept, jnp.where(fold, 1.0, 0.0).astype(jnp.bfloat16))
    mine = over(iota(ranks.shape, 1), width) == over(iota(ranks.shape, 0), span)
    ranks = jnp.where(mine, ranks, 0.0).astype(jnp.bfloat16)
    put = (held, rows.shape[0])
    put = iota(put, 0) == rest_of(iota(put, 1), span)
    ranks = dot(jnp.where(put, 1.0, 0.0).astype(jnp.bfloat16), ranks)
    rank_ref[...] = ranks.astype(jnp.bfloat16)


def out_grow_kernel(sizes, width, total_ref, slots_ref, grow_ref, *refs):
    groups, blocks, drafts = sizes
    ranks_in, outs = refs[:blocks], refs[blocks:]
    owned = grow_ref.shape[0] // width
    me = lax.axis_index("tensor")
    ranks = ranks_in[0][...].astype(jnp.float32)
    for other in ranks_in[1:]:
        ranks = ranks + other[...].astype(jnp.float32)
    count = total_ref.shape[0]
    held, lanes = ranks.shape
    parts, span = packing(count, width, lanes)
    put = rest_of(iota((count, held), 0), span) == iota((count, held), 1)
    ranks = dot(jnp.where(put, 1.0, 0.0).astype(jnp.bfloat16), ranks.astype(jnp.bfloat16))
    mine = over(iota(ranks.shape, 1), width) == over(iota(ranks.shape, 0), span)
    ranks = jnp.where(mine, ranks, 0.0).astype(jnp.bfloat16)
    tile = (lanes, owned * width)
    tile = rest_of(iota(tile, 0), width) == rest_of(iota(tile, 1), width)
    ranks = dot(ranks, jnp.where(tile, 1.0, 0.0).astype(jnp.bfloat16))
    place = slots_ref[:, 1:2] - me * owned
    wide = jnp.where(over(iota(ranks.shape, 1), width) == place, ranks, 0.0).astype(jnp.bfloat16)
    full = (total_ref[...] + dot(wide, grow_ref[...])).astype(jnp.bfloat16)
    full = dot(reorder(sizes, as_gathered, by_draft), full).astype(jnp.bfloat16)
    for block in range(blocks):
        for draft in range(drafts):
            start = (block * drafts + draft) * groups
            outs[block][draft] = full[start : start + groups]


def by_kernels(
    tokens,
    w_query,
    w_key,
    w_value,
    w_out,
    shrink_qkv,
    grow_query,
    grow_key,
    grow_value,
    shrink_out,
    grow_out,
    cache_keys,
    cache_values,
    cache_lengths,
    adapter_ids,
    adapter_slots,
):
    blocks = lax.axis_size("tensor")
    groups = lax.axis_size(GROUP)
    _, drafts, features = tokens.shape
    sizes = (groups, blocks, drafts)
    owned = shrink_qkv.shape[0]
    width = grow_out.shape[1]
    head_size = cache_keys.shape[3]
    span = blocks * drafts
    count = groups * span
    lanes = -(-shrink_qkv.shape[2] // 128) * 128

    def over_tensor(value, shift):
        route = [(t, t ^ shift) for t in range(blocks)]
        return lax.ppermute(value, "tensor", route)

    def over_core(value):
        return lax.ppermute(value, "pipe", [(0, 1), (1, 0)])

    def to_growers(value, flip):
        route = [
            (t * groups + 2 * x + c, (3 - c if x ^ flip else c) * groups + t)
            for t in range(blocks)
            for x in range(2)
            for c in range(2)
        ]
        return lax.ppermute(value, EVERY, route)

    def to_out_growers(value, shift):
        route = [
            (t * groups + g, g * groups + (t ^ shift))
            for t in range(blocks)
            for g in range(groups)
        ]
        return lax.ppermute(value, EVERY, route)

    def added(left, right):
        return call(add_kernel, shape(left.shape), [VMEM] * 2)(left, right)

    def exchange(value):
        return lax.all_to_all(value, EVERY, split_axis=0, concat_axis=0, tiled=True)

    mine = jnp.transpose(tokens, (1, 0, 2))
    pieces = [mine] + [over_tensor(mine, shift) for shift in range(1, blocks)]

    lines = (w_query.shape[1] // head_size + 2) * drafts
    lines = -(-lines // 8) * 8
    slots, cosine, sine = prepare(
        sizes, owned, adapter_ids, adapter_slots, cache_lengths, (lines, head_size), w_out
    )
    packed = -(-2 * blocks * drafts // 16) * 16
    shrink_in = jnp.transpose(shrink_qkv, (0, 2, 1)).reshape(-1, features)
    rows, rank_part = call(
        functools.partial(rank_kernel, sizes, owned),
        [shape((count, features)), shape((packed, lanes))],
        [VMEM] * (blocks + 2),
        [pltpu.VMEM((count, features), jnp.float32)],
        2 * count * shrink_qkv.size,
        2 * shrink_qkv.size + 4 * count * features,
    )(*pieces, shrink_in, slots)
    rank_part = added(rank_part, over_core(rank_part))
    ranks = [to_growers(rank_part, flip) for flip in range(2)]
    total = product(rows, w_query, w_key, w_value)
    cols = total.shape[1]
    head_cols = w_query.shape[1]
    query_lines = head_cols // head_size * drafts
    sent = call(
        functools.partial(grow_kernel, sizes, width),
        shape((blocks * groups, lines, head_size)),
        [VMEM] * 7 + [HBM] * 2,
        [pltpu.VMEM((blocks * groups * lines, head_size), jnp.float32)],
        limit=40 * MIB,
    )(
        total,
        slots,
        *ranks,
        *[grow.reshape(owned * width, -1) for grow in (grow_query, grow_key, grow_value)],
        *[w_out] * 2,
    )
    mixed = call(
        functools.partial(attend_kernel, sizes),
        shape((blocks * groups, query_lines, head_size)),
        [VMEM] * 3 + [pl.BlockSpec(memory_space=pltpu.SMEM)] + [VMEM] * 2,
        [pltpu.VMEM((2 * blocks, 128, head_size), jnp.float32)],
    )(exchange(sent), cache_keys, cache_values, cache_lengths, cosine, sine)
    gathered = exchange(mixed)
    held = -(-packing(count, width, 128)[1] // 16) * 16
    out_rows, out_part = call(
        functools.partial(out_rank_kernel, sizes, owned),
        [shape((count, head_cols)), shape((held, 128))],
        [VMEM] * 3 + [HBM] * 4,
        [pltpu.VMEM((blocks * groups * query_lines, head_size), jnp.float32)],
        limit=40 * MIB,
    )(gathered, jnp.transpose(shrink_out, (0, 2, 1)).reshape(-1, head_cols), slots, *[w_query] * 4)
    out_ranks = [to_out_growers(out_part, shift) for shift in range(blocks)]
    out_total = product(out_rows, w_out)
    out_cols = out_total.shape[1]
    leaving = call(
        functools.partial(out_grow_kernel, sizes, width),
        [shape((drafts, groups, out_cols))] * blocks,
        [VMEM] * (3 + blocks),
        [],
        2 * count * owned * width * out_cols,
        8 * count * out_cols + 2 * owned * width * out_cols,
    )(out_total, slots, grow_out.reshape(owned * width, -1), *out_ranks)
    result = leaving[0].astype(jnp.float32)
    for shift in sorted(range(1, blocks), key=lambda shift: shift < blocks // 2):
        result = result + over_tensor(leaving[shift], shift).astype(jnp.float32)
    return jnp.transpose(result.astype(jnp.bfloat16), (1, 0, 2))


def rotate(vectors, positions):
    half_size = vectors.shape[-1] // 2
    frequency = rope_base ** (-2.0 * jnp.arange(half_size, dtype=jnp.float32) / vectors.shape[-1])
    angles = positions[:, None, None] * frequency
    cosine = jnp.cos(angles)
    sine_value = jnp.sin(angles)
    first_half = vectors[..., :half_size]
    second = vectors[..., half_size:]
    return jnp.concatenate(
        [first_half * cosine - second * sine_value, second * cosine + first_half * sine_value], -1
    )


def to_growers(partial, splits):
    total = None
    for shift in range(splits):
        route = [
            (t * splits + g, ((g + shift) % splits) * splits + t)
            for t in range(splits)
            for g in range(splits)
        ]
        got = lax.ppermute(partial, EVERY, route).astype(jnp.float32)
        total = got if total is None else total + got
    return total


def to_out_growers(partial, splits):
    total = None
    for shift in range(splits):
        route = [
            (t * splits + g, g * splits + (t + shift) % splits)
            for t in range(splits)
            for g in range(splits)
        ]
        got = lax.ppermute(partial, EVERY, route).astype(jnp.float32)
        total = got if total is None else total + got
    return total


def slot_table(adapter_ids, adapter_slots):
    matches = adapter_ids[:, None] == jnp.arange(adapter_slots.shape[0], dtype=jnp.int32)[None, :]
    return jnp.sum(jnp.where(matches, adapter_slots[None, :], 0), axis=1)


def attend(query_heads, key_new, value_new, cache_keys, cache_values, length):
    drafts, head_count, head_size = query_heads.shape
    kv_heads, cache_size, _ = cache_keys.shape
    positions = (length + jnp.arange(drafts, dtype=jnp.int32)).astype(jnp.float32)
    query_rot = rotate(query_heads.astype(jnp.float32), positions).astype(jnp.bfloat16)
    key_rot = rotate(key_new.astype(jnp.float32), positions).astype(jnp.bfloat16)
    grouped = query_rot.reshape(drafts, kv_heads, head_count // kv_heads, head_size)
    score_scale = 1.0 / math.sqrt(head_size)
    cached = (
        jnp.einsum("skgd,kld->skgl", grouped, cache_keys, preferred_element_type=jnp.float32)
        * score_scale
    )
    fresh_scores = (
        jnp.einsum("skgd,tkd->skgt", grouped, key_rot, preferred_element_type=jnp.float32)
        * score_scale
    )
    cache_mask = jnp.arange(cache_size, dtype=jnp.int32) < length
    draft_mask = jnp.arange(drafts)[None, :] <= jnp.arange(drafts)[:, None]
    cached = jnp.where(cache_mask[None, None, None, :], cached, -jnp.inf)
    fresh_scores = jnp.where(draft_mask[:, None, None, :], fresh_scores, -jnp.inf)
    row_peak = jnp.maximum(jnp.max(cached, -1), jnp.max(fresh_scores, -1))
    cached_exp = jnp.exp(cached - row_peak[..., None])
    fresh_exp = jnp.exp(fresh_scores - row_peak[..., None])
    denominator = jnp.sum(cached_exp, -1) + jnp.sum(fresh_exp, -1)
    cached_prob = (cached_exp / denominator[..., None]).astype(jnp.bfloat16)
    fresh_prob = (fresh_exp / denominator[..., None]).astype(jnp.bfloat16)
    mixed = jnp.einsum(
        "skgl,kld->skgd", cached_prob, cache_values, preferred_element_type=jnp.float32
    )
    mixed = mixed + jnp.einsum(
        "skgt,tkd->skgd", fresh_prob, value_new, preferred_element_type=jnp.float32
    )
    return mixed.astype(jnp.bfloat16)


def by_row(
    tokens,
    w_query,
    w_key,
    w_value,
    w_out,
    shrink_qkv,
    grow_query,
    grow_key,
    grow_value,
    shrink_out,
    grow_out,
    cache_keys,
    cache_values,
    cache_lengths,
    adapter_ids,
    adapter_slots,
):
    splits = lax.axis_size("tensor")
    groups = lax.axis_size(("dp", "pipe"))
    tensor_index = lax.axis_index("tensor")
    group_index = lax.axis_index(("dp", "pipe"))
    local_rows, drafts, feature_width = tokens.shape
    per_owner = shrink_qkv.shape[0]
    rank_size = grow_out.shape[1]
    query_cols = w_query.shape[1]
    key_cols = w_key.shape[1]
    kv_heads = cache_keys.shape[1]
    head_size = cache_keys.shape[3]
    rows = splits * groups
    row_slots = jnp.repeat(slot_table(adapter_ids, adapter_slots), drafts)
    within = jnp.arange(per_owner, dtype=jnp.int32)[None, :]
    width_hot = (row_slots[:, None] == within + tensor_index * per_owner)[:, :, None]
    column_hot = (row_slots[:, None] == within + group_index * per_owner)[:, :, None]

    def spread_ranks(ranks, hot):
        return jnp.where(hot, ranks[:, None, :], 0.0).reshape(rows * drafts, -1).astype(jnp.bfloat16)

    flat_tokens = lax.all_gather(tokens, "tensor", axis=0, tiled=True).reshape(
        rows * drafts, feature_width
    )
    rank_part = jnp.einsum(
        "nd,adr->nar", flat_tokens, shrink_qkv, preferred_element_type=jnp.float32
    )
    rank_part = jnp.sum(jnp.where(width_hot, rank_part, 0.0), 1)
    rank_all = to_growers(rank_part.astype(jnp.bfloat16), splits)

    def grown(index, grow):
        ranks = spread_ranks(rank_all[:, index * rank_size : (index + 1) * rank_size], column_hot)
        return jnp.dot(
            ranks, grow.reshape(per_owner * rank_size, -1), preferred_element_type=jnp.float32
        )

    bases = [
        jnp.dot(flat_tokens, weight, preferred_element_type=jnp.float32)
        for weight in (w_query, w_key, w_value)
    ]

    def product(index, grow):
        return (bases[index] + grown(index, grow)).astype(jnp.bfloat16).reshape(rows, drafts, -1)

    partial = jnp.concatenate(
        [
            product(0, grow_query),
            product(1, grow_key),
            product(2, grow_value),
        ],
        2,
    )
    arrived = lax.all_to_all(partial, EVERY, split_axis=0, concat_axis=0, tiled=True)
    joined = jnp.sum(
        arrived.reshape(splits, groups, drafts, -1).astype(jnp.float32), 1
    ).astype(jnp.bfloat16)
    joined = jnp.transpose(joined, (1, 0, 2))
    query_heads = joined[:, :, :query_cols].reshape(drafts, -1, head_size)
    key_new = joined[:, :, query_cols : query_cols + key_cols].reshape(drafts, kv_heads, head_size)
    value_new = joined[:, :, query_cols + key_cols :].reshape(drafts, kv_heads, head_size)
    mixed = attend(
        query_heads, key_new, value_new, cache_keys[0], cache_values[0], cache_lengths[0]
    )
    mixed = jnp.transpose(mixed.reshape(drafts, splits, -1), (1, 0, 2))
    outgoing = jnp.repeat(mixed, groups, axis=0)
    flat_heads = lax.all_to_all(
        outgoing, EVERY, split_axis=0, concat_axis=0, tiled=True
    ).reshape(rows * drafts, -1)
    out_part = jnp.einsum(
        "nw,awr->nar", flat_heads, shrink_out, preferred_element_type=jnp.float32
    )
    out_part = jnp.sum(jnp.where(column_hot, out_part, 0.0), 1)
    out_rank = to_out_growers(out_part.astype(jnp.bfloat16), splits)
    out = jnp.dot(flat_heads, w_out, preferred_element_type=jnp.float32)
    out = out + jnp.dot(
        spread_ranks(out_rank, width_hot),
        grow_out.reshape(per_owner * rank_size, -1),
        preferred_element_type=jnp.float32,
    )
    blocks = lax.all_to_all(
        out.astype(jnp.bfloat16).reshape(splits, local_rows, drafts, feature_width),
        "tensor",
        split_axis=0,
        concat_axis=0,
        tiled=True,
    )
    return jnp.sum(blocks.astype(jnp.float32), 0).astype(jnp.bfloat16)


def local(*arrays):
    heads = arrays[11].shape[1]
    sizes = [lax.axis_size(name) for name in EVERY]
    if heads == 4 and sizes == [4, 2, 2]:
        return by_kernels(*arrays)
    return by_row(*arrays)


def solution(mesh):
    placed = (
        P(("parts", "tensor"), None, ("dp", "pipe")),
        P(("dp", "pipe"), "tensor"),
        P(("dp", "pipe"), "tensor"),
        P(("dp", "pipe"), "tensor"),
        P("tensor", ("dp", "pipe")),
        P("tensor", ("dp", "pipe"), None),
        P(("dp", "pipe"), None, "tensor"),
        P(("dp", "pipe"), None, "tensor"),
        P(("dp", "pipe"), None, "tensor"),
        P(("dp", "pipe"), "tensor", None),
        P("tensor", None, ("dp", "pipe")),
        P(("parts", "tensor", "dp", "pipe"), None, None, None),
        P(("parts", "tensor", "dp", "pipe"), None, None, None),
        P(("parts", "tensor", "dp", "pipe")),
        P(),
        P(),
    )
    return jax.shard_map(
        local,
        mesh=mesh,
        in_specs=placed,
        out_specs=P(("parts", "tensor"), None, ("dp", "pipe")),
        check_vma=False,
    )
```

```python
import functools
import math

import jax
import jax.numpy as jnp
import numpy as np
from jax import lax
from jax.experimental import pallas as pl
from jax.experimental.pallas import tpu as pltpu
from jax.sharding import PartitionSpec as P

rope_base = 500000.0
EVERY = ("tensor", "dp", "pipe")
GROUP = ("dp", "pipe")
VMEM = pl.BlockSpec(memory_space=pltpu.VMEM)
HBM = pl.BlockSpec(memory_space=pltpu.HBM)
MIB = 1 << 20


def dot(left, right):
    return jnp.dot(left, right, preferred_element_type=jnp.float32)


def dot_nt(left, right):
    return lax.dot_general(
        left, right, (((1,), (1,)), ((), ())), preferred_element_type=jnp.float32
    )


def iota(shape, axis):
    return lax.broadcasted_iota(jnp.int32, shape, axis)


def call(kernel, outs, ins, scratch=(), flops=0, moved=0, limit=24 * MIB):
    return pl.pallas_call(
        kernel,
        out_shape=outs,
        in_specs=ins,
        out_specs=jax.tree.map(lambda _: VMEM, outs),
        scratch_shapes=list(scratch),
        cost_estimate=pl.CostEstimate(flops=flops, bytes_accessed=moved, transcendentals=0),
        compiler_params=pltpu.CompilerParams(vmem_limit_bytes=limit),
    )


def shape(dims, kind=jnp.bfloat16):
    return jax.ShapeDtypeStruct(tuple(dims), kind)


def over(value, size):
    return value >> (size.bit_length() - 1) if size & (size - 1) == 0 else lax.div(value, size)


def rest_of(value, size):
    return value & (size - 1) if size & (size - 1) == 0 else lax.rem(value, size)


def as_gathered(sizes, group, block, draft):
    groups, blocks, drafts = sizes
    return (block * drafts + draft) * groups + group


def by_draft(sizes, group, block, draft):
    groups, blocks, drafts = sizes
    return (draft * blocks + block) * groups + group


def parts_of(order, sizes, index):
    groups, blocks, drafts = sizes
    group, left = rest_of(index, groups), over(index, groups)
    if order is as_gathered:
        return group, over(left, drafts), rest_of(left, drafts)
    return group, rest_of(left, blocks), over(left, blocks)


def turned(block):
    return lax.axis_index("tensor") ^ block


def reorder(sizes, after, before):
    groups, blocks, drafts = sizes
    rows = groups * blocks * drafts
    group, block, draft = parts_of(after, sizes, iota((rows, rows), 0))
    wanted = before(sizes, group, turned(block), draft)
    return jnp.where(wanted == iota((rows, rows), 1), 1.0, 0.0).astype(jnp.bfloat16)


def group_of():
    return lax.axis_index("dp") * lax.axis_size("pipe") + lax.axis_index("pipe")


def rank_kernel(sizes, owned, *refs):
    groups, blocks, drafts = sizes
    pieces = refs[:blocks]
    shrink_ref, slots_ref = refs[blocks : blocks + 2]
    rows_ref, rank_ref, wide = refs[-3:]
    for block in range(blocks):
        for draft in range(drafts):
            start = (block * drafts + draft) * groups
            wide[start : start + groups, :] = pieces[block][draft].astype(jnp.float32)
    rows = wide[...].astype(jnp.bfloat16)
    rows_ref[...] = rows
    place = slots_ref[:, 0:1] - lax.axis_index("tensor") * owned
    ranks = owned_ranks(
        rows, shrink_ref[...], place, shrink_ref.shape[0] // owned, rank_ref.shape[1]
    )
    put = (rank_ref.shape[0], rows.shape[0])
    draft = parts_of(as_gathered, sizes, iota((rows.shape[0], put[0]), 0))[2]
    line = slots_ref[:, 2:3] * drafts + draft
    put = jnp.where(line == iota((rows.shape[0], put[0]), 1), 1.0, 0.0).astype(jnp.bfloat16)
    ranks = lax.dot_general(
        put, ranks, (((0,), (0,)), ((), ())), preferred_element_type=jnp.float32
    )
    rank_ref[...] = ranks.astype(jnp.bfloat16)


def owned_ranks(rows, shrink, place, width, lanes):
    ranks = dot_nt(rows, shrink)
    kept = jnp.where(over(iota(ranks.shape, 1), width) == place, ranks, 0.0).astype(jnp.bfloat16)
    fold = (ranks.shape[1], lanes)
    fold = rest_of(iota(fold, 0), width) == iota(fold, 1)
    return dot(kept, jnp.where(fold, 1.0, 0.0).astype(jnp.bfloat16)).astype(jnp.bfloat16)


def spread_ranks(ranks, place, width, owned, parts):
    span = owned * width
    row = iota((ranks.shape[1], parts * span), 0)
    column = iota((ranks.shape[1], parts * span), 1)
    tile = (over(row, width) == over(column, span)) & (
        rest_of(row, width) == rest_of(column, width)
    )
    wide = dot(ranks, jnp.where(tile, 1.0, 0.0).astype(jnp.bfloat16))
    slot = over(rest_of(iota(wide.shape, 1), span), width)
    return jnp.where(slot == place, wide, 0.0).astype(jnp.bfloat16)


def product_kernel(rows_ref, *refs):
    *weights, total_ref = refs
    start = 0
    for weight in weights:
        width = weight.shape[1]
        step = width if width % 1024 else 1024
        for first in range(0, width, step):
            total_ref[:, start : start + step] = dot(
                rows_ref[...], weight[:, first : first + step]
            )
            start += step


def product(rows, *weights):
    width = sum(weight.shape[1] for weight in weights)
    return call(
        product_kernel,
        shape((rows.shape[0], width), jnp.float32),
        [VMEM] * (1 + len(weights)),
    )(rows, *weights)


def prepare_kernel(sizes, owned, ids_ref, pool_ref, length_ref, *refs):
    slots_ref, cosine_ref, sine_ref = refs[-3:]
    groups, blocks, drafts = sizes
    width = cosine_ref.shape[1]
    lane = iota(cosine_ref.shape, 1)
    half = (lane & (width // 2 - 1)).astype(jnp.float32)
    positions = (lax.rem(iota(cosine_ref.shape, 0), drafts) + length_ref[0]).astype(jnp.float32)
    angles = positions * jnp.exp(half * (-2.0 * math.log(rope_base) / width))
    cosine_ref[...] = jnp.cos(angles)
    sine_ref[...] = jnp.sin(angles) * jnp.where(lane < width // 2, -1.0, 1.0)
    index = iota(slots_ref.shape, 0)
    column = iota(slots_ref.shape, 1)
    near = parts_of(as_gathered, sizes, index)
    far = parts_of(by_draft, sizes, index)
    row_group = jnp.where(column == 1, far[0], near[0])
    row_block = jnp.where(column == 1, far[1], turned(near[1]))
    place = row_block * groups + row_group
    slots = jnp.zeros(slots_ref.shape, jnp.int32)
    sent, taken = 0, 0
    for row in range(blocks * groups):
        slot = pool_ref[ids_ref[row]]
        owner = over(slot, owned)
        sends = jnp.where(owner == lax.axis_index("tensor"), 1, 0)
        takes = jnp.where(owner == group_of(), 1, 0)
        line = jnp.where(column == 2, sent - 64 * (1 - sends), taken - 64 * (1 - takes))
        slots = jnp.where(place == row, jnp.where(column < 2, slot, line), slots)
        sent, taken = sent + sends, taken + takes
    slots_ref[...] = slots


def prepare(sizes, owned, ids, pool, lengths, table, later):
    groups, blocks, drafts = sizes
    smem = pl.BlockSpec(memory_space=pltpu.SMEM)
    table = shape(table, jnp.float32)
    return call(
        functools.partial(prepare_kernel, sizes, owned),
        [shape((groups * blocks * drafts, 128), jnp.int32), table, table],
        [smem, smem, smem] + [HBM] * 3,
        limit=40 * MIB,
    )(ids, pool, lengths, *[later] * 3)


def grow_kernel(sizes, width, total_ref, slots_ref, *refs):
    groups, blocks, drafts = sizes
    ranks_in, grows, (out_ref, held) = refs[:2], refs[2:5], refs[-2:]
    group = group_of()
    requests = groups * blocks
    lines = out_ref.shape[1]
    held[...] = jnp.zeros(held.shape, jnp.float32)
    owned = grows[0].shape[0] // width
    ranks = ranks_in[0][...].astype(jnp.float32)
    for other in ranks_in[1:]:
        ranks = ranks + other[...].astype(jnp.float32)
    get = (total_ref.shape[0], ranks.shape[0])
    draft = parts_of(as_gathered, sizes, iota(get, 0))[2]
    get = slots_ref[:, 3:4] * drafts + draft == iota(get, 1)
    ranks = dot(jnp.where(get, 1.0, 0.0).astype(jnp.bfloat16), ranks.astype(jnp.bfloat16))
    place = slots_ref[:, 0:1] - group * owned
    wide = spread_ranks(ranks.astype(jnp.bfloat16), place, width, owned, len(grows))
    arranged = reorder(sizes, by_draft, as_gathered)
    start, column = 0, 0
    for index, grow in enumerate(grows):
        deep, cols = grow.shape
        full = total_ref[:, column : column + cols] + dot(
            wide[:, index * deep : (index + 1) * deep], grow[...]
        )
        column += cols
        full = dot(arranged, full.astype(jnp.bfloat16))
        for head in range(cols // 128):
            for draft in range(drafts):
                held[pl.ds(start + draft, requests, stride=lines), :] = full[
                    draft * requests : (draft + 1) * requests, head * 128 : (head + 1) * 128
                ]
            start += drafts
    for row in range(requests):
        out_ref[row] = held[row * lines : (row + 1) * lines, :].astype(jnp.bfloat16)


def attend_kernel(
    sizes, arrived_ref, keys_ref, values_ref, length_ref, cosine_ref, sine_ref, out_ref, *scratch
):
    groups, blocks, drafts = sizes
    (fresh_s,) = scratch
    cache_size, head_size = keys_ref.shape[2:]
    count = out_ref.shape[1]
    scale = 1.0 / math.sqrt(head_size)
    fresh_s[...] = jnp.zeros(fresh_s.shape, jnp.float32)
    scores = []
    for block in range(blocks):
        joined = arrived_ref[block * groups].astype(jnp.float32)
        for other in range(1, groups):
            joined = joined + arrived_ref[block * groups + other].astype(jnp.float32)
        joined = joined.astype(jnp.bfloat16).astype(jnp.float32)
        rotated = joined * cosine_ref[...] + pltpu.roll(joined, head_size // 2, 1) * sine_ref[...]
        fresh_s[2 * block, 0:drafts, :] = rotated[count : count + drafts]
        fresh_s[2 * block + 1, 0:drafts, :] = joined[count + drafts : count + 2 * drafts]
        query = rotated[0:count].astype(jnp.bfloat16)
        old = dot_nt(query, keys_ref[0, block])
        new = dot_nt(query, fresh_s[2 * block].astype(jnp.bfloat16))
        scores.append(jnp.concatenate([old, new], 1))
    scores = jnp.concatenate(scores, 0) * scale
    column = iota(scores.shape, 1)
    limit = cache_size + lax.rem(iota((scores.shape[0], 1), 0), drafts)
    seen = (column < length_ref[0]) | ((column >= cache_size) & (column <= limit))
    scores = jnp.where(seen, scores, -jnp.inf)
    scores = jnp.exp(scores - jnp.max(scores, 1, keepdims=True))
    below = 1.0 / jnp.sum(scores, 1, keepdims=True)
    probs = (scores * below).astype(jnp.bfloat16)
    for block in range(blocks):
        mine = probs[block * count : (block + 1) * count]
        mixed = dot(mine[:, :cache_size], values_ref[0, block]) + dot(
            mine[:, cache_size:], fresh_s[2 * block + 1].astype(jnp.bfloat16)
        )
        mixed = mixed.astype(jnp.bfloat16)
        for target in range(groups):
            out_ref[block * groups + target] = mixed


def add_kernel(left_ref, right_ref, out_ref):
    total = left_ref[...].astype(jnp.float32) + right_ref[...].astype(jnp.float32)
    out_ref[...] = total.astype(jnp.bfloat16)


def packing(rows, width, lanes):
    parts = lanes // width
    return parts, rows // parts


def out_rank_kernel(sizes, owned, got_ref, shrink_ref, slots_ref, *refs):
    rows_ref, rank_ref, wide = refs[-3:]
    drafts = sizes[2]
    requests, lines, head_size = got_ref.shape
    for row in range(requests):
        wide[row * lines : (row + 1) * lines, :] = got_ref[row].astype(jnp.float32)
    for head in range(lines // drafts):
        for draft in range(drafts):
            rows_ref[
                draft * requests : (draft + 1) * requests,
                head * head_size : (head + 1) * head_size,
            ] = wide[pl.ds(head * drafts + draft, requests, stride=lines), :].astype(jnp.bfloat16)
    rows = rows_ref[...]
    place = slots_ref[:, 1:2] - group_of() * owned
    width = shrink_ref.shape[0] // owned
    held, lanes = rank_ref.shape
    parts, span = packing(rows.shape[0], width, lanes)
    ranks = dot_nt(rows, shrink_ref[...])
    kept = jnp.where(over(iota(ranks.shape, 1), width) == place, ranks, 0.0).astype(jnp.bfloat16)
    fold = (ranks.shape[1], lanes)
    fold = rest_of(iota(fold, 0), width) == rest_of(iota(fold, 1), width)
    ranks = dot(kept, jnp.where(fold, 1.0, 0.0).astype(jnp.bfloat16))
    mine = over(iota(ranks.shape, 1), width) == over(iota(ranks.shape, 0), span)
    ranks = jnp.where(mine, ranks, 0.0).astype(jnp.bfloat16)
    put = (held, rows.shape[0])
    put = iota(put, 0) == rest_of(iota(put, 1), span)
    ranks = dot(jnp.where(put, 1.0, 0.0).astype(jnp.bfloat16), ranks)
    rank_ref[...] = ranks.astype(jnp.bfloat16)


def out_grow_kernel(sizes, width, total_ref, slots_ref, grow_ref, *refs):
    groups, blocks, drafts = sizes
    ranks_in, outs = refs[:blocks], refs[blocks:]
    owned = grow_ref.shape[0] // width
    me = lax.axis_index("tensor")
    ranks = ranks_in[0][...].astype(jnp.float32)
    for other in ranks_in[1:]:
        ranks = ranks + other[...].astype(jnp.float32)
    count = total_ref.shape[0]
    held, lanes = ranks.shape
    parts, span = packing(count, width, lanes)
    put = rest_of(iota((count, held), 0), span) == iota((count, held), 1)
    ranks = dot(jnp.where(put, 1.0, 0.0).astype(jnp.bfloat16), ranks.astype(jnp.bfloat16))
    mine = over(iota(ranks.shape, 1), width) == over(iota(ranks.shape, 0), span)
    ranks = jnp.where(mine, ranks, 0.0).astype(jnp.bfloat16)
    tile = (lanes, owned * width)
    tile = rest_of(iota(tile, 0), width) == rest_of(iota(tile, 1), width)
    ranks = dot(ranks, jnp.where(tile, 1.0, 0.0).astype(jnp.bfloat16))
    place = slots_ref[:, 1:2] - me * owned
    wide = jnp.where(over(iota(ranks.shape, 1), width) == place, ranks, 0.0).astype(jnp.bfloat16)
    full = (total_ref[...] + dot(wide, grow_ref[...])).astype(jnp.bfloat16)
    full = dot(reorder(sizes, as_gathered, by_draft), full).astype(jnp.bfloat16)
    for block in range(blocks):
        for draft in range(drafts):
            start = (block * drafts + draft) * groups
            outs[block][draft] = full[start : start + groups]


def by_kernels(
    tokens,
    w_query,
    w_key,
    w_value,
    w_out,
    shrink_qkv,
    grow_query,
    grow_key,
    grow_value,
    shrink_out,
    grow_out,
    cache_keys,
    cache_values,
    cache_lengths,
    adapter_ids,
    adapter_slots,
):
    blocks = lax.axis_size("tensor")
    groups = lax.axis_size(GROUP)
    _, drafts, features = tokens.shape
    sizes = (groups, blocks, drafts)
    owned = shrink_qkv.shape[0]
    width = grow_out.shape[1]
    head_size = cache_keys.shape[3]
    span = blocks * drafts
    count = groups * span
    lanes = -(-shrink_qkv.shape[2] // 128) * 128

    def over_tensor(value, shift):
        route = [(t, t ^ shift) for t in range(blocks)]
        return lax.ppermute(value, "tensor", route)

    def over_core(value):
        return lax.ppermute(value, "pipe", [(0, 1), (1, 0)])

    def to_growers(value, flip):
        route = [
            (t * groups + 2 * x + c, (2 * c + (x ^ flip)) * groups + t)
            for t in range(blocks)
            for x in range(2)
            for c in range(2)
        ]
        return lax.ppermute(value, EVERY, route)

    def to_out_growers(value, shift):
        route = [
            (t * groups + g, g * groups + (t ^ shift))
            for t in range(blocks)
            for g in range(groups)
        ]
        return lax.ppermute(value, EVERY, route)

    def added(left, right):
        return call(add_kernel, shape(left.shape), [VMEM] * 2)(left, right)

    def exchange(value):
        return lax.all_to_all(value, EVERY, split_axis=0, concat_axis=0, tiled=True)

    mine = jnp.transpose(tokens, (1, 0, 2))
    pieces = [mine] + [over_tensor(mine, shift) for shift in range(1, blocks)]

    lines = (w_query.shape[1] // head_size + 2) * drafts
    lines = -(-lines // 8) * 8
    slots, cosine, sine = prepare(
        sizes, owned, adapter_ids, adapter_slots, cache_lengths, (lines, head_size), w_out
    )
    packed = -(-2 * blocks * drafts // 16) * 16
    shrink_in = jnp.transpose(shrink_qkv, (0, 2, 1)).reshape(-1, features)
    rows, rank_part = call(
        functools.partial(rank_kernel, sizes, owned),
        [shape((count, features)), shape((packed, lanes))],
        [VMEM] * (blocks + 2),
        [pltpu.VMEM((count, features), jnp.float32)],
        2 * count * shrink_qkv.size,
        2 * shrink_qkv.size + 4 * count * features,
    )(*pieces, shrink_in, slots)
    rank_part = added(rank_part, over_core(rank_part))
    ranks = [to_growers(rank_part, flip) for flip in range(2)]
    total = product(rows, w_query, w_key, w_value)
    cols = total.shape[1]
    head_cols = w_query.shape[1]
    query_lines = head_cols // head_size * drafts
    sent = call(
        functools.partial(grow_kernel, sizes, width),
        shape((blocks * groups, lines, head_size)),
        [VMEM] * 7 + [HBM] * 2,
        [pltpu.VMEM((blocks * groups * lines, head_size), jnp.float32)],
        limit=40 * MIB,
    )(
        total,
        slots,
        *ranks,
        *[grow.reshape(owned * width, -1) for grow in (grow_query, grow_key, grow_value)],
        *[w_out] * 2,
    )
    mixed = call(
        functools.partial(attend_kernel, sizes),
        shape((blocks * groups, query_lines, head_size)),
        [VMEM] * 3 + [pl.BlockSpec(memory_space=pltpu.SMEM)] + [VMEM] * 2,
        [pltpu.VMEM((2 * blocks, 128, head_size), jnp.float32)],
    )(exchange(sent), cache_keys, cache_values, cache_lengths, cosine, sine)
    gathered = exchange(mixed)
    held = -(-packing(count, width, 128)[1] // 16) * 16
    out_rows, out_part = call(
        functools.partial(out_rank_kernel, sizes, owned),
        [shape((count, head_cols)), shape((held, 128))],
        [VMEM] * 3 + [HBM] * 4,
        [pltpu.VMEM((blocks * groups * query_lines, head_size), jnp.float32)],
        limit=40 * MIB,
    )(gathered, jnp.transpose(shrink_out, (0, 2, 1)).reshape(-1, head_cols), slots, *[w_query] * 4)
    out_ranks = [to_out_growers(out_part, shift) for shift in range(blocks)]
    out_total = product(out_rows, w_out)
    out_cols = out_total.shape[1]
    leaving = call(
        functools.partial(out_grow_kernel, sizes, width),
        [shape((drafts, groups, out_cols))] * blocks,
        [VMEM] * (3 + blocks),
        [],
        2 * count * owned * width * out_cols,
        8 * count * out_cols + 2 * owned * width * out_cols,
    )(out_total, slots, grow_out.reshape(owned * width, -1), *out_ranks)
    result = leaving[0].astype(jnp.float32)
    for shift in range(1, blocks):
        result = result + over_tensor(leaving[shift], shift).astype(jnp.float32)
    return jnp.transpose(result.astype(jnp.bfloat16), (1, 0, 2))


def rotate(vectors, positions):
    half_size = vectors.shape[-1] // 2
    frequency = rope_base ** (-2.0 * jnp.arange(half_size, dtype=jnp.float32) / vectors.shape[-1])
    angles = positions[:, None, None] * frequency
    cosine = jnp.cos(angles)
    sine_value = jnp.sin(angles)
    first_half = vectors[..., :half_size]
    second = vectors[..., half_size:]
    return jnp.concatenate(
        [first_half * cosine - second * sine_value, second * cosine + first_half * sine_value], -1
    )


def to_growers(partial, splits):
    total = None
    for shift in range(splits):
        route = [
            (t * splits + g, ((g + shift) % splits) * splits + t)
            for t in range(splits)
            for g in range(splits)
        ]
        got = lax.ppermute(partial, EVERY, route).astype(jnp.float32)
        total = got if total is None else total + got
    return total


def to_out_growers(partial, splits):
    total = None
    for shift in range(splits):
        route = [
            (t * splits + g, g * splits + (t + shift) % splits)
            for t in range(splits)
            for g in range(splits)
        ]
        got = lax.ppermute(partial, EVERY, route).astype(jnp.float32)
        total = got if total is None else total + got
    return total


def slot_table(adapter_ids, adapter_slots):
    matches = adapter_ids[:, None] == jnp.arange(adapter_slots.shape[0], dtype=jnp.int32)[None, :]
    return jnp.sum(jnp.where(matches, adapter_slots[None, :], 0), axis=1)


def attend(query_heads, key_new, value_new, cache_keys, cache_values, length):
    drafts, head_count, head_size = query_heads.shape
    kv_heads, cache_size, _ = cache_keys.shape
    positions = (length + jnp.arange(drafts, dtype=jnp.int32)).astype(jnp.float32)
    query_rot = rotate(query_heads.astype(jnp.float32), positions).astype(jnp.bfloat16)
    key_rot = rotate(key_new.astype(jnp.float32), positions).astype(jnp.bfloat16)
    grouped = query_rot.reshape(drafts, kv_heads, head_count // kv_heads, head_size)
    score_scale = 1.0 / math.sqrt(head_size)
    cached = (
        jnp.einsum("skgd,kld->skgl", grouped, cache_keys, preferred_element_type=jnp.float32)
        * score_scale
    )
    fresh_scores = (
        jnp.einsum("skgd,tkd->skgt", grouped, key_rot, preferred_element_type=jnp.float32)
        * score_scale
    )
    cache_mask = jnp.arange(cache_size, dtype=jnp.int32) < length
    draft_mask = jnp.arange(drafts)[None, :] <= jnp.arange(drafts)[:, None]
    cached = jnp.where(cache_mask[None, None, None, :], cached, -jnp.inf)
    fresh_scores = jnp.where(draft_mask[:, None, None, :], fresh_scores, -jnp.inf)
    row_peak = jnp.maximum(jnp.max(cached, -1), jnp.max(fresh_scores, -1))
    cached_exp = jnp.exp(cached - row_peak[..., None])
    fresh_exp = jnp.exp(fresh_scores - row_peak[..., None])
    denominator = jnp.sum(cached_exp, -1) + jnp.sum(fresh_exp, -1)
    cached_prob = (cached_exp / denominator[..., None]).astype(jnp.bfloat16)
    fresh_prob = (fresh_exp / denominator[..., None]).astype(jnp.bfloat16)
    mixed = jnp.einsum(
        "skgl,kld->skgd", cached_prob, cache_values, preferred_element_type=jnp.float32
    )
    mixed = mixed + jnp.einsum(
        "skgt,tkd->skgd", fresh_prob, value_new, preferred_element_type=jnp.float32
    )
    return mixed.astype(jnp.bfloat16)


def by_row(
    tokens,
    w_query,
    w_key,
    w_value,
    w_out,
    shrink_qkv,
    grow_query,
    grow_key,
    grow_value,
    shrink_out,
    grow_out,
    cache_keys,
    cache_values,
    cache_lengths,
    adapter_ids,
    adapter_slots,
):
    splits = lax.axis_size("tensor")
    groups = lax.axis_size(("dp", "pipe"))
    tensor_index = lax.axis_index("tensor")
    group_index = lax.axis_index(("dp", "pipe"))
    local_rows, drafts, feature_width = tokens.shape
    per_owner = shrink_qkv.shape[0]
    rank_size = grow_out.shape[1]
    query_cols = w_query.shape[1]
    key_cols = w_key.shape[1]
    kv_heads = cache_keys.shape[1]
    head_size = cache_keys.shape[3]
    rows = splits * groups
    row_slots = jnp.repeat(slot_table(adapter_ids, adapter_slots), drafts)
    within = jnp.arange(per_owner, dtype=jnp.int32)[None, :]
    width_hot = (row_slots[:, None] == within + tensor_index * per_owner)[:, :, None]
    column_hot = (row_slots[:, None] == within + group_index * per_owner)[:, :, None]

    def spread_ranks(ranks, hot):
        return jnp.where(hot, ranks[:, None, :], 0.0).reshape(rows * drafts, -1).astype(jnp.bfloat16)

    flat_tokens = lax.all_gather(tokens, "tensor", axis=0, tiled=True).reshape(
        rows * drafts, feature_width
    )
    rank_part = jnp.einsum(
        "nd,adr->nar", flat_tokens, shrink_qkv, preferred_element_type=jnp.float32
    )
    rank_part = jnp.sum(jnp.where(width_hot, rank_part, 0.0), 1)
    rank_all = to_growers(rank_part.astype(jnp.bfloat16), splits)

    def grown(index, grow):
        ranks = spread_ranks(rank_all[:, index * rank_size : (index + 1) * rank_size], column_hot)
        return jnp.dot(
            ranks, grow.reshape(per_owner * rank_size, -1), preferred_element_type=jnp.float32
        )

    bases = [
        jnp.dot(flat_tokens, weight, preferred_element_type=jnp.float32)
        for weight in (w_query, w_key, w_value)
    ]

    def product(index, grow):
        return (bases[index] + grown(index, grow)).astype(jnp.bfloat16).reshape(rows, drafts, -1)

    partial = jnp.concatenate(
        [
            product(0, grow_query),
            product(1, grow_key),
            product(2, grow_value),
        ],
        2,
    )
    arrived = lax.all_to_all(partial, EVERY, split_axis=0, concat_axis=0, tiled=True)
    joined = jnp.sum(
        arrived.reshape(splits, groups, drafts, -1).astype(jnp.float32), 1
    ).astype(jnp.bfloat16)
    joined = jnp.transpose(joined, (1, 0, 2))
    query_heads = joined[:, :, :query_cols].reshape(drafts, -1, head_size)
    key_new = joined[:, :, query_cols : query_cols + key_cols].reshape(drafts, kv_heads, head_size)
    value_new = joined[:, :, query_cols + key_cols :].reshape(drafts, kv_heads, head_size)
    mixed = attend(
        query_heads, key_new, value_new, cache_keys[0], cache_values[0], cache_lengths[0]
    )
    mixed = jnp.transpose(mixed.reshape(drafts, splits, -1), (1, 0, 2))
    outgoing = jnp.repeat(mixed, groups, axis=0)
    flat_heads = lax.all_to_all(
        outgoing, EVERY, split_axis=0, concat_axis=0, tiled=True
    ).reshape(rows * drafts, -1)
    out_part = jnp.einsum(
        "nw,awr->nar", flat_heads, shrink_out, preferred_element_type=jnp.float32
    )
    out_part = jnp.sum(jnp.where(column_hot, out_part, 0.0), 1)
    out_rank = to_out_growers(out_part.astype(jnp.bfloat16), splits)
    out = jnp.dot(flat_heads, w_out, preferred_element_type=jnp.float32)
    out = out + jnp.dot(
        spread_ranks(out_rank, width_hot),
        grow_out.reshape(per_owner * rank_size, -1),
        preferred_element_type=jnp.float32,
    )
    blocks = lax.all_to_all(
        out.astype(jnp.bfloat16).reshape(splits, local_rows, drafts, feature_width),
        "tensor",
        split_axis=0,
        concat_axis=0,
        tiled=True,
    )
    return jnp.sum(blocks.astype(jnp.float32), 0).astype(jnp.bfloat16)


def local(*arrays):
    heads = arrays[11].shape[1]
    sizes = [lax.axis_size(name) for name in EVERY]
    if heads == 4 and sizes == [4, 2, 2]:
        return by_kernels(*arrays)
    return by_row(*arrays)


def solution(mesh):
    placed = (
        P(("parts", "tensor"), None, ("dp", "pipe")),
        P(("dp", "pipe"), "tensor"),
        P(("dp", "pipe"), "tensor"),
        P(("dp", "pipe"), "tensor"),
        P("tensor", ("dp", "pipe")),
        P("tensor", ("dp", "pipe"), None),
        P(("dp", "pipe"), None, "tensor"),
        P(("dp", "pipe"), None, "tensor"),
        P(("dp", "pipe"), None, "tensor"),
        P(("dp", "pipe"), "tensor", None),
        P("tensor", None, ("dp", "pipe")),
        P(("parts", "tensor", "dp", "pipe"), None, None, None),
        P(("parts", "tensor", "dp", "pipe"), None, None, None),
        P(("parts", "tensor", "dp", "pipe")),
        P(),
        P(),
    )
    return jax.shard_map(
        local,
        mesh=mesh,
        in_specs=placed,
        out_specs=P(("parts", "tensor"), None, ("dp", "pipe")),
        check_vma=False,
    )
```

```python
import functools
import math

import jax
import jax.numpy as jnp
import numpy as np
from jax import lax
from jax.experimental import pallas as pl
from jax.experimental.pallas import tpu as pltpu
from jax.sharding import PartitionSpec as P

rope_base = 500000.0
EVERY = ("tensor", "dp", "pipe")
GROUP = ("dp", "pipe")
VMEM = pl.BlockSpec(memory_space=pltpu.VMEM)
HBM = pl.BlockSpec(memory_space=pltpu.HBM)
MIB = 1 << 20


def dot(left, right):
    return jnp.dot(left, right, preferred_element_type=jnp.float32)


def dot_nt(left, right):
    return lax.dot_general(
        left, right, (((1,), (1,)), ((), ())), preferred_element_type=jnp.float32
    )


def iota(shape, axis):
    return lax.broadcasted_iota(jnp.int32, shape, axis)


def call(kernel, outs, ins, scratch=(), flops=0, moved=0, limit=24 * MIB):
    return pl.pallas_call(
        kernel,
        out_shape=outs,
        in_specs=ins,
        out_specs=jax.tree.map(lambda _: VMEM, outs),
        scratch_shapes=list(scratch),
        cost_estimate=pl.CostEstimate(flops=flops, bytes_accessed=moved, transcendentals=0),
        compiler_params=pltpu.CompilerParams(vmem_limit_bytes=limit),
    )


def shape(dims, kind=jnp.bfloat16):
    return jax.ShapeDtypeStruct(tuple(dims), kind)


def over(value, size):
    return value >> (size.bit_length() - 1) if size & (size - 1) == 0 else lax.div(value, size)


def rest_of(value, size):
    return value & (size - 1) if size & (size - 1) == 0 else lax.rem(value, size)


def as_gathered(sizes, group, block, draft):
    groups, blocks, drafts = sizes
    return (block * drafts + draft) * groups + group


def by_draft(sizes, group, block, draft):
    groups, blocks, drafts = sizes
    return (draft * blocks + block) * groups + group


def parts_of(order, sizes, index):
    groups, blocks, drafts = sizes
    group, left = rest_of(index, groups), over(index, groups)
    if order is as_gathered:
        return group, over(left, drafts), rest_of(left, drafts)
    return group, rest_of(left, blocks), over(left, blocks)


def turned(block):
    return lax.axis_index("tensor") ^ block


def reorder(sizes, after, before):
    groups, blocks, drafts = sizes
    rows = groups * blocks * drafts
    group, block, draft = parts_of(after, sizes, iota((rows, rows), 0))
    wanted = before(sizes, group, turned(block), draft)
    return jnp.where(wanted == iota((rows, rows), 1), 1.0, 0.0).astype(jnp.bfloat16)


def group_of():
    return lax.axis_index("dp") * lax.axis_size("pipe") + lax.axis_index("pipe")


def rank_kernel(sizes, owned, *refs):
    groups, blocks, drafts = sizes
    pieces = refs[:blocks]
    shrink_ref, slots_ref = refs[blocks : blocks + 2]
    rows_ref, rank_ref, wide = refs[-3:]
    for block in range(blocks):
        for draft in range(drafts):
            start = (block * drafts + draft) * groups
            wide[start : start + groups, :] = pieces[block][draft].astype(jnp.float32)
    rows = wide[...].astype(jnp.bfloat16)
    rows_ref[...] = rows
    place = slots_ref[:, 0:1] - lax.axis_index("tensor") * owned
    ranks = owned_ranks(
        rows, shrink_ref[...], place, shrink_ref.shape[0] // owned, rank_ref.shape[1]
    )
    put = (rank_ref.shape[0], rows.shape[0])
    draft = parts_of(as_gathered, sizes, iota((rows.shape[0], put[0]), 0))[2]
    line = slots_ref[:, 2:3] * drafts + draft
    put = jnp.where(line == iota((rows.shape[0], put[0]), 1), 1.0, 0.0).astype(jnp.bfloat16)
    ranks = lax.dot_general(
        put, ranks, (((0,), (0,)), ((), ())), preferred_element_type=jnp.float32
    )
    rank_ref[...] = ranks.astype(jnp.bfloat16)


def owned_ranks(rows, shrink, place, width, lanes):
    ranks = dot_nt(rows, shrink)
    kept = jnp.where(over(iota(ranks.shape, 1), width) == place, ranks, 0.0).astype(jnp.bfloat16)
    fold = (ranks.shape[1], lanes)
    fold = rest_of(iota(fold, 0), width) == iota(fold, 1)
    return dot(kept, jnp.where(fold, 1.0, 0.0).astype(jnp.bfloat16)).astype(jnp.bfloat16)


def spread_ranks(ranks, place, width, owned, parts):
    span = owned * width
    row = iota((ranks.shape[1], parts * span), 0)
    column = iota((ranks.shape[1], parts * span), 1)
    tile = (over(row, width) == over(column, span)) & (
        rest_of(row, width) == rest_of(column, width)
    )
    wide = dot(ranks, jnp.where(tile, 1.0, 0.0).astype(jnp.bfloat16))
    slot = over(rest_of(iota(wide.shape, 1), span), width)
    return jnp.where(slot == place, wide, 0.0).astype(jnp.bfloat16)


def product_kernel(rows_ref, *refs):
    *weights, total_ref = refs
    start = 0
    for weight in weights:
        width = weight.shape[1]
        step = width if width % 1024 else 1024
        for first in range(0, width, step):
            total_ref[:, start : start + step] = dot(
                rows_ref[...], weight[:, first : first + step]
            )
            start += step


def product(rows, *weights):
    width = sum(weight.shape[1] for weight in weights)
    return call(
        product_kernel,
        shape((rows.shape[0], width), jnp.float32),
        [VMEM] * (1 + len(weights)),
    )(rows, *weights)


def prepare_kernel(sizes, owned, ids_ref, pool_ref, length_ref, *refs):
    slots_ref, cosine_ref, sine_ref = refs[-3:]
    groups, blocks, drafts = sizes
    width = cosine_ref.shape[1]
    lane = iota(cosine_ref.shape, 1)
    half = (lane & (width // 2 - 1)).astype(jnp.float32)
    positions = (lax.rem(iota(cosine_ref.shape, 0), drafts) + length_ref[0]).astype(jnp.float32)
    angles = positions * jnp.exp(half * (-2.0 * math.log(rope_base) / width))
    cosine_ref[...] = jnp.cos(angles)
    sine_ref[...] = jnp.sin(angles) * jnp.where(lane < width // 2, -1.0, 1.0)
    index = iota(slots_ref.shape, 0)
    column = iota(slots_ref.shape, 1)
    near = parts_of(as_gathered, sizes, index)
    far = parts_of(by_draft, sizes, index)
    row_group = jnp.where(column == 1, far[0], near[0])
    row_block = jnp.where(column == 1, far[1], turned(near[1]))
    place = row_block * groups + row_group
    slots = jnp.zeros(slots_ref.shape, jnp.int32)
    sent, taken = 0, 0
    for row in range(blocks * groups):
        slot = pool_ref[ids_ref[row]]
        owner = over(slot, owned)
        sends = jnp.where(owner == lax.axis_index("tensor"), 1, 0)
        takes = jnp.where(owner == group_of(), 1, 0)
        line = jnp.where(column == 2, sent - 64 * (1 - sends), taken - 64 * (1 - takes))
        slots = jnp.where(place == row, jnp.where(column < 2, slot, line), slots)
        sent, taken = sent + sends, taken + takes
    slots_ref[...] = slots


def prepare(sizes, owned, ids, pool, lengths, table, later):
    groups, blocks, drafts = sizes
    smem = pl.BlockSpec(memory_space=pltpu.SMEM)
    table = shape(table, jnp.float32)
    return call(
        functools.partial(prepare_kernel, sizes, owned),
        [shape((groups * blocks * drafts, 128), jnp.int32), table, table],
        [smem, smem, smem] + [HBM] * 3,
        limit=40 * MIB,
    )(ids, pool, lengths, *[later] * 3)


def grow_kernel(sizes, width, total_ref, slots_ref, *refs):
    groups, blocks, drafts = sizes
    ranks_in, grows, (out_ref, held) = refs[:2], refs[2:5], refs[-2:]
    group = group_of()
    requests = groups * blocks
    lines = out_ref.shape[1]
    held[...] = jnp.zeros(held.shape, jnp.float32)
    owned = grows[0].shape[0] // width
    ranks = ranks_in[0][...].astype(jnp.float32)
    for other in ranks_in[1:]:
        ranks = ranks + other[...].astype(jnp.float32)
    get = (total_ref.shape[0], ranks.shape[0])
    draft = parts_of(as_gathered, sizes, iota(get, 0))[2]
    get = slots_ref[:, 3:4] * drafts + draft == iota(get, 1)
    ranks = dot(jnp.where(get, 1.0, 0.0).astype(jnp.bfloat16), ranks.astype(jnp.bfloat16))
    place = slots_ref[:, 0:1] - group * owned
    wide = spread_ranks(ranks.astype(jnp.bfloat16), place, width, owned, len(grows))
    arranged = reorder(sizes, by_draft, as_gathered)
    start, column = 0, 0
    for index, grow in enumerate(grows):
        deep, cols = grow.shape
        full = total_ref[:, column : column + cols] + dot(
            wide[:, index * deep : (index + 1) * deep], grow[...]
        )
        column += cols
        full = dot(arranged, full.astype(jnp.bfloat16))
        for head in range(cols // 128):
            for draft in range(drafts):
                held[pl.ds(start + draft, requests, stride=lines), :] = full[
                    draft * requests : (draft + 1) * requests, head * 128 : (head + 1) * 128
                ]
            start += drafts
    for row in range(requests):
        out_ref[row] = held[row * lines : (row + 1) * lines, :].astype(jnp.bfloat16)


def attend_kernel(
    sizes, arrived_ref, keys_ref, values_ref, length_ref, cosine_ref, sine_ref, out_ref, *scratch
):
    groups, blocks, drafts = sizes
    (fresh_s,) = scratch
    cache_size, head_size = keys_ref.shape[2:]
    count = out_ref.shape[1]
    scale = 1.0 / math.sqrt(head_size)
    fresh_s[...] = jnp.zeros(fresh_s.shape, jnp.float32)
    scores = []
    for block in range(blocks):
        joined = arrived_ref[block * groups].astype(jnp.float32)
        for other in range(1, groups):
            joined = joined + arrived_ref[block * groups + other].astype(jnp.float32)
        joined = joined.astype(jnp.bfloat16).astype(jnp.float32)
        rotated = joined * cosine_ref[...] + pltpu.roll(joined, head_size // 2, 1) * sine_ref[...]
        fresh_s[2 * block, 0:drafts, :] = rotated[count : count + drafts]
        fresh_s[2 * block + 1, 0:drafts, :] = joined[count + drafts : count + 2 * drafts]
        query = rotated[0:count].astype(jnp.bfloat16)
        old = dot_nt(query, keys_ref[0, block])
        new = dot_nt(query, fresh_s[2 * block].astype(jnp.bfloat16))
        scores.append(jnp.concatenate([old, new], 1))
    scores = jnp.concatenate(scores, 0) * scale
    column = iota(scores.shape, 1)
    limit = cache_size + lax.rem(iota((scores.shape[0], 1), 0), drafts)
    seen = (column < length_ref[0]) | ((column >= cache_size) & (column <= limit))
    scores = jnp.where(seen, scores, -jnp.inf)
    scores = jnp.exp(scores - jnp.max(scores, 1, keepdims=True))
    below = 1.0 / jnp.sum(scores, 1, keepdims=True)
    probs = (scores * below).astype(jnp.bfloat16)
    for block in range(blocks):
        mine = probs[block * count : (block + 1) * count]
        mixed = dot(mine[:, :cache_size], values_ref[0, block]) + dot(
            mine[:, cache_size:], fresh_s[2 * block + 1].astype(jnp.bfloat16)
        )
        mixed = mixed.astype(jnp.bfloat16)
        for target in range(groups):
            out_ref[block * groups + target] = mixed


def add_kernel(left_ref, right_ref, out_ref):
    total = left_ref[...].astype(jnp.float32) + right_ref[...].astype(jnp.float32)
    out_ref[...] = total.astype(jnp.bfloat16)


def packing(rows, width, lanes):
    parts = lanes // width
    return parts, rows // parts


def out_rank_kernel(sizes, owned, got_ref, shrink_ref, slots_ref, *refs):
    rows_ref, rank_ref, wide = refs[-3:]
    drafts = sizes[2]
    requests, lines, head_size = got_ref.shape
    for row in range(requests):
        wide[row * lines : (row + 1) * lines, :] = got_ref[row].astype(jnp.float32)
    for head in range(lines // drafts):
        for draft in range(drafts):
            rows_ref[
                draft * requests : (draft + 1) * requests,
                head * head_size : (head + 1) * head_size,
            ] = wide[pl.ds(head * drafts + draft, requests, stride=lines), :].astype(jnp.bfloat16)
    rows = rows_ref[...]
    place = slots_ref[:, 1:2] - group_of() * owned
    width = shrink_ref.shape[0] // owned
    held, lanes = rank_ref.shape
    parts, span = packing(rows.shape[0], width, lanes)
    ranks = dot_nt(rows, shrink_ref[...])
    kept = jnp.where(over(iota(ranks.shape, 1), width) == place, ranks, 0.0).astype(jnp.bfloat16)
    fold = (ranks.shape[1], lanes)
    fold = rest_of(iota(fold, 0), width) == rest_of(iota(fold, 1), width)
    ranks = dot(kept, jnp.where(fold, 1.0, 0.0).astype(jnp.bfloat16))
    mine = over(iota(ranks.shape, 1), width) == over(iota(ranks.shape, 0), span)
    ranks = jnp.where(mine, ranks, 0.0).astype(jnp.bfloat16)
    put = (held, rows.shape[0])
    put = iota(put, 0) == rest_of(iota(put, 1), span)
    ranks = dot(jnp.where(put, 1.0, 0.0).astype(jnp.bfloat16), ranks)
    rank_ref[...] = ranks.astype(jnp.bfloat16)


def out_grow_kernel(sizes, width, total_ref, slots_ref, grow_ref, *refs):
    groups, blocks, drafts = sizes
    ranks_in, outs = refs[:blocks], refs[blocks:]
    owned = grow_ref.shape[0] // width
    me = lax.axis_index("tensor")
    ranks = ranks_in[0][...].astype(jnp.float32)
    for other in ranks_in[1:]:
        ranks = ranks + other[...].astype(jnp.float32)
    count = total_ref.shape[0]
    held, lanes = ranks.shape
    parts, span = packing(count, width, lanes)
    put = rest_of(iota((count, held), 0), span) == iota((count, held), 1)
    ranks = dot(jnp.where(put, 1.0, 0.0).astype(jnp.bfloat16), ranks.astype(jnp.bfloat16))
    mine = over(iota(ranks.shape, 1), width) == over(iota(ranks.shape, 0), span)
    ranks = jnp.where(mine, ranks, 0.0).astype(jnp.bfloat16)
    tile = (lanes, owned * width)
    tile = rest_of(iota(tile, 0), width) == rest_of(iota(tile, 1), width)
    ranks = dot(ranks, jnp.where(tile, 1.0, 0.0).astype(jnp.bfloat16))
    place = slots_ref[:, 1:2] - me * owned
    wide = jnp.where(over(iota(ranks.shape, 1), width) == place, ranks, 0.0).astype(jnp.bfloat16)
    full = (total_ref[...] + dot(wide, grow_ref[...])).astype(jnp.bfloat16)
    full = dot(reorder(sizes, as_gathered, by_draft), full).astype(jnp.bfloat16)
    for block in range(blocks):
        for draft in range(drafts):
            start = (block * drafts + draft) * groups
            outs[block][draft] = full[start : start + groups]


def by_kernels(
    tokens,
    w_query,
    w_key,
    w_value,
    w_out,
    shrink_qkv,
    grow_query,
    grow_key,
    grow_value,
    shrink_out,
    grow_out,
    cache_keys,
    cache_values,
    cache_lengths,
    adapter_ids,
    adapter_slots,
):
    blocks = lax.axis_size("tensor")
    groups = lax.axis_size(GROUP)
    _, drafts, features = tokens.shape
    sizes = (groups, blocks, drafts)
    owned = shrink_qkv.shape[0]
    width = grow_out.shape[1]
    head_size = cache_keys.shape[3]
    span = blocks * drafts
    count = groups * span
    lanes = -(-shrink_qkv.shape[2] // 128) * 128

    def over_tensor(value, shift):
        route = [(t, t ^ shift) for t in range(blocks)]
        return lax.ppermute(value, "tensor", route)

    def over_core(value):
        return lax.ppermute(value, "pipe", [(0, 1), (1, 0)])

    def to_growers(value, flip):
        route = [
            (t * groups + 2 * x + c, (2 * c + (x ^ flip)) * groups + t)
            for t in range(blocks)
            for x in range(2)
            for c in range(2)
        ]
        return lax.ppermute(value, EVERY, route)

    def to_out_growers(value, shift):
        route = [
            (t * groups + g, g * groups + (t ^ shift))
            for t in range(blocks)
            for g in range(groups)
        ]
        return lax.ppermute(value, EVERY, route)

    def added(left, right):
        return call(add_kernel, shape(left.shape), [VMEM] * 2)(left, right)

    def exchange(value):
        return lax.all_to_all(value, EVERY, split_axis=0, concat_axis=0, tiled=True)

    mine = jnp.transpose(tokens, (1, 0, 2))
    pieces = [mine] + [over_tensor(mine, shift) for shift in range(1, blocks)]

    lines = (w_query.shape[1] // head_size + 2) * drafts
    lines = -(-lines // 8) * 8
    slots, cosine, sine = prepare(
        sizes, owned, adapter_ids, adapter_slots, cache_lengths, (lines, head_size), w_out
    )
    packed = -(-2 * blocks * drafts // 16) * 16
    shrink_in = jnp.transpose(shrink_qkv, (0, 2, 1)).reshape(-1, features)
    rows, rank_part = call(
        functools.partial(rank_kernel, sizes, owned),
        [shape((count, features)), shape((packed, lanes))],
        [VMEM] * (blocks + 2),
        [pltpu.VMEM((count, features), jnp.float32)],
        2 * count * shrink_qkv.size,
        2 * shrink_qkv.size + 4 * count * features,
    )(*pieces, shrink_in, slots)
    rank_part = added(rank_part, over_core(rank_part))
    ranks = [to_growers(rank_part, flip) for flip in range(2)]
    total = product(rows, w_query, w_key, w_value)
    cols = total.shape[1]
    head_cols = w_query.shape[1]
    query_lines = head_cols // head_size * drafts
    sent = call(
        functools.partial(grow_kernel, sizes, width),
        shape((blocks * groups, lines, head_size)),
        [VMEM] * 7 + [HBM] * 2,
        [pltpu.VMEM((blocks * groups * lines, head_size), jnp.float32)],
        limit=40 * MIB,
    )(
        total,
        slots,
        *ranks,
        *[grow.reshape(owned * width, -1) for grow in (grow_query, grow_key, grow_value)],
        *[w_out] * 2,
    )
    mixed = call(
        functools.partial(attend_kernel, sizes),
        shape((blocks * groups, query_lines, head_size)),
        [VMEM] * 3 + [pl.BlockSpec(memory_space=pltpu.SMEM)] + [VMEM] * 2,
        [pltpu.VMEM((2 * blocks, 128, head_size), jnp.float32)],
    )(exchange(sent), cache_keys, cache_values, cache_lengths, cosine, sine)
    gathered = exchange(mixed)
    held = -(-packing(count, width, 128)[1] // 16) * 16
    out_rows, out_part = call(
        functools.partial(out_rank_kernel, sizes, owned),
        [shape((count, head_cols)), shape((held, 128))],
        [VMEM] * 3 + [HBM] * 4,
        [pltpu.VMEM((blocks * groups * query_lines, head_size), jnp.float32)],
        limit=40 * MIB,
    )(gathered, jnp.transpose(shrink_out, (0, 2, 1)).reshape(-1, head_cols), slots, *[w_query] * 4)
    out_ranks = [to_out_growers(out_part, shift) for shift in range(blocks)]
    out_total = product(out_rows, w_out)
    out_cols = out_total.shape[1]
    leaving = call(
        functools.partial(out_grow_kernel, sizes, width),
        [shape((drafts, groups, out_cols))] * blocks,
        [VMEM] * (3 + blocks),
        [],
        2 * count * owned * width * out_cols,
        8 * count * out_cols + 2 * owned * width * out_cols,
    )(out_total, slots, grow_out.reshape(owned * width, -1), *out_ranks)
    result = leaving[0].astype(jnp.float32)
    for shift in reversed(range(1, blocks)):
        result = result + over_tensor(leaving[shift], shift).astype(jnp.float32)
    return jnp.transpose(result.astype(jnp.bfloat16), (1, 0, 2))


def rotate(vectors, positions):
    half_size = vectors.shape[-1] // 2
    frequency = rope_base ** (-2.0 * jnp.arange(half_size, dtype=jnp.float32) / vectors.shape[-1])
    angles = positions[:, None, None] * frequency
    cosine = jnp.cos(angles)
    sine_value = jnp.sin(angles)
    first_half = vectors[..., :half_size]
    second = vectors[..., half_size:]
    return jnp.concatenate(
        [first_half * cosine - second * sine_value, second * cosine + first_half * sine_value], -1
    )


def to_growers(partial, splits):
    total = None
    for shift in range(splits):
        route = [
            (t * splits + g, ((g + shift) % splits) * splits + t)
            for t in range(splits)
            for g in range(splits)
        ]
        got = lax.ppermute(partial, EVERY, route).astype(jnp.float32)
        total = got if total is None else total + got
    return total


def to_out_growers(partial, splits):
    total = None
    for shift in range(splits):
        route = [
            (t * splits + g, g * splits + (t + shift) % splits)
            for t in range(splits)
            for g in range(splits)
        ]
        got = lax.ppermute(partial, EVERY, route).astype(jnp.float32)
        total = got if total is None else total + got
    return total


def slot_table(adapter_ids, adapter_slots):
    matches = adapter_ids[:, None] == jnp.arange(adapter_slots.shape[0], dtype=jnp.int32)[None, :]
    return jnp.sum(jnp.where(matches, adapter_slots[None, :], 0), axis=1)


def attend(query_heads, key_new, value_new, cache_keys, cache_values, length):
    drafts, head_count, head_size = query_heads.shape
    kv_heads, cache_size, _ = cache_keys.shape
    positions = (length + jnp.arange(drafts, dtype=jnp.int32)).astype(jnp.float32)
    query_rot = rotate(query_heads.astype(jnp.float32), positions).astype(jnp.bfloat16)
    key_rot = rotate(key_new.astype(jnp.float32), positions).astype(jnp.bfloat16)
    grouped = query_rot.reshape(drafts, kv_heads, head_count // kv_heads, head_size)
    score_scale = 1.0 / math.sqrt(head_size)
    cached = (
        jnp.einsum("skgd,kld->skgl", grouped, cache_keys, preferred_element_type=jnp.float32)
        * score_scale
    )
    fresh_scores = (
        jnp.einsum("skgd,tkd->skgt", grouped, key_rot, preferred_element_type=jnp.float32)
        * score_scale
    )
    cache_mask = jnp.arange(cache_size, dtype=jnp.int32) < length
    draft_mask = jnp.arange(drafts)[None, :] <= jnp.arange(drafts)[:, None]
    cached = jnp.where(cache_mask[None, None, None, :], cached, -jnp.inf)
    fresh_scores = jnp.where(draft_mask[:, None, None, :], fresh_scores, -jnp.inf)
    row_peak = jnp.maximum(jnp.max(cached, -1), jnp.max(fresh_scores, -1))
    cached_exp = jnp.exp(cached - row_peak[..., None])
    fresh_exp = jnp.exp(fresh_scores - row_peak[..., None])
    denominator = jnp.sum(cached_exp, -1) + jnp.sum(fresh_exp, -1)
    cached_prob = (cached_exp / denominator[..., None]).astype(jnp.bfloat16)
    fresh_prob = (fresh_exp / denominator[..., None]).astype(jnp.bfloat16)
    mixed = jnp.einsum(
        "skgl,kld->skgd", cached_prob, cache_values, preferred_element_type=jnp.float32
    )
    mixed = mixed + jnp.einsum(
        "skgt,tkd->skgd", fresh_prob, value_new, preferred_element_type=jnp.float32
    )
    return mixed.astype(jnp.bfloat16)


def by_row(
    tokens,
    w_query,
    w_key,
    w_value,
    w_out,
    shrink_qkv,
    grow_query,
    grow_key,
    grow_value,
    shrink_out,
    grow_out,
    cache_keys,
    cache_values,
    cache_lengths,
    adapter_ids,
    adapter_slots,
):
    splits = lax.axis_size("tensor")
    groups = lax.axis_size(("dp", "pipe"))
    tensor_index = lax.axis_index("tensor")
    group_index = lax.axis_index(("dp", "pipe"))
    local_rows, drafts, feature_width = tokens.shape
    per_owner = shrink_qkv.shape[0]
    rank_size = grow_out.shape[1]
    query_cols = w_query.shape[1]
    key_cols = w_key.shape[1]
    kv_heads = cache_keys.shape[1]
    head_size = cache_keys.shape[3]
    rows = splits * groups
    row_slots = jnp.repeat(slot_table(adapter_ids, adapter_slots), drafts)
    within = jnp.arange(per_owner, dtype=jnp.int32)[None, :]
    width_hot = (row_slots[:, None] == within + tensor_index * per_owner)[:, :, None]
    column_hot = (row_slots[:, None] == within + group_index * per_owner)[:, :, None]

    def spread_ranks(ranks, hot):
        return jnp.where(hot, ranks[:, None, :], 0.0).reshape(rows * drafts, -1).astype(jnp.bfloat16)

    flat_tokens = lax.all_gather(tokens, "tensor", axis=0, tiled=True).reshape(
        rows * drafts, feature_width
    )
    rank_part = jnp.einsum(
        "nd,adr->nar", flat_tokens, shrink_qkv, preferred_element_type=jnp.float32
    )
    rank_part = jnp.sum(jnp.where(width_hot, rank_part, 0.0), 1)
    rank_all = to_growers(rank_part.astype(jnp.bfloat16), splits)

    def grown(index, grow):
        ranks = spread_ranks(rank_all[:, index * rank_size : (index + 1) * rank_size], column_hot)
        return jnp.dot(
            ranks, grow.reshape(per_owner * rank_size, -1), preferred_element_type=jnp.float32
        )

    bases = [
        jnp.dot(flat_tokens, weight, preferred_element_type=jnp.float32)
        for weight in (w_query, w_key, w_value)
    ]

    def product(index, grow):
        return (bases[index] + grown(index, grow)).astype(jnp.bfloat16).reshape(rows, drafts, -1)

    partial = jnp.concatenate(
        [
            product(0, grow_query),
            product(1, grow_key),
            product(2, grow_value),
        ],
        2,
    )
    arrived = lax.all_to_all(partial, EVERY, split_axis=0, concat_axis=0, tiled=True)
    joined = jnp.sum(
        arrived.reshape(splits, groups, drafts, -1).astype(jnp.float32), 1
    ).astype(jnp.bfloat16)
    joined = jnp.transpose(joined, (1, 0, 2))
    query_heads = joined[:, :, :query_cols].reshape(drafts, -1, head_size)
    key_new = joined[:, :, query_cols : query_cols + key_cols].reshape(drafts, kv_heads, head_size)
    value_new = joined[:, :, query_cols + key_cols :].reshape(drafts, kv_heads, head_size)
    mixed = attend(
        query_heads, key_new, value_new, cache_keys[0], cache_values[0], cache_lengths[0]
    )
    mixed = jnp.transpose(mixed.reshape(drafts, splits, -1), (1, 0, 2))
    outgoing = jnp.repeat(mixed, groups, axis=0)
    flat_heads = lax.all_to_all(
        outgoing, EVERY, split_axis=0, concat_axis=0, tiled=True
    ).reshape(rows * drafts, -1)
    out_part = jnp.einsum(
        "nw,awr->nar", flat_heads, shrink_out, preferred_element_type=jnp.float32
    )
    out_part = jnp.sum(jnp.where(column_hot, out_part, 0.0), 1)
    out_rank = to_out_growers(out_part.astype(jnp.bfloat16), splits)
    out = jnp.dot(flat_heads, w_out, preferred_element_type=jnp.float32)
    out = out + jnp.dot(
        spread_ranks(out_rank, width_hot),
        grow_out.reshape(per_owner * rank_size, -1),
        preferred_element_type=jnp.float32,
    )
    blocks = lax.all_to_all(
        out.astype(jnp.bfloat16).reshape(splits, local_rows, drafts, feature_width),
        "tensor",
        split_axis=0,
        concat_axis=0,
        tiled=True,
    )
    return jnp.sum(blocks.astype(jnp.float32), 0).astype(jnp.bfloat16)


def local(*arrays):
    heads = arrays[11].shape[1]
    sizes = [lax.axis_size(name) for name in EVERY]
    if heads == 4 and sizes == [4, 2, 2]:
        return by_kernels(*arrays)
    return by_row(*arrays)


def solution(mesh):
    placed = (
        P(("parts", "tensor"), None, ("dp", "pipe")),
        P(("dp", "pipe"), "tensor"),
        P(("dp", "pipe"), "tensor"),
        P(("dp", "pipe"), "tensor"),
        P("tensor", ("dp", "pipe")),
        P("tensor", ("dp", "pipe"), None),
        P(("dp", "pipe"), None, "tensor"),
        P(("dp", "pipe"), None, "tensor"),
        P(("dp", "pipe"), None, "tensor"),
        P(("dp", "pipe"), "tensor", None),
        P("tensor", None, ("dp", "pipe")),
        P(("parts", "tensor", "dp", "pipe"), None, None, None),
        P(("parts", "tensor", "dp", "pipe"), None, None, None),
        P(("parts", "tensor", "dp", "pipe")),
        P(),
        P(),
    )
    return jax.shard_map(
        local,
        mesh=mesh,
        in_specs=placed,
        out_specs=P(("parts", "tensor"), None, ("dp", "pipe")),
        check_vma=False,
    )
```

```python
import functools
import math

import jax
import jax.numpy as jnp
import numpy as np
from jax import lax
from jax.experimental import pallas as pl
from jax.experimental.pallas import tpu as pltpu
from jax.sharding import PartitionSpec as P

rope_base = 500000.0
EVERY = ("tensor", "dp", "pipe")
GROUP = ("dp", "pipe")
VMEM = pl.BlockSpec(memory_space=pltpu.VMEM)
HBM = pl.BlockSpec(memory_space=pltpu.HBM)
MIB = 1 << 20


def dot(left, right):
    return jnp.dot(left, right, preferred_element_type=jnp.float32)


def dot_nt(left, right):
    return lax.dot_general(
        left, right, (((1,), (1,)), ((), ())), preferred_element_type=jnp.float32
    )


def iota(shape, axis):
    return lax.broadcasted_iota(jnp.int32, shape, axis)


def call(kernel, outs, ins, scratch=(), flops=0, moved=0, limit=24 * MIB):
    return pl.pallas_call(
        kernel,
        out_shape=outs,
        in_specs=ins,
        out_specs=jax.tree.map(lambda _: VMEM, outs),
        scratch_shapes=list(scratch),
        cost_estimate=pl.CostEstimate(flops=flops, bytes_accessed=moved, transcendentals=0),
        compiler_params=pltpu.CompilerParams(vmem_limit_bytes=limit),
    )


def shape(dims, kind=jnp.bfloat16):
    return jax.ShapeDtypeStruct(tuple(dims), kind)


def over(value, size):
    return value >> (size.bit_length() - 1) if size & (size - 1) == 0 else lax.div(value, size)


def rest_of(value, size):
    return value & (size - 1) if size & (size - 1) == 0 else lax.rem(value, size)


def as_gathered(sizes, group, block, draft):
    groups, blocks, drafts = sizes
    return (block * drafts + draft) * groups + group


def by_draft(sizes, group, block, draft):
    groups, blocks, drafts = sizes
    return (draft * blocks + block) * groups + group


def parts_of(order, sizes, index):
    groups, blocks, drafts = sizes
    group, left = rest_of(index, groups), over(index, groups)
    if order is as_gathered:
        return group, over(left, drafts), rest_of(left, drafts)
    return group, rest_of(left, blocks), over(left, blocks)


def turned(block):
    return lax.axis_index("tensor") ^ block


def reorder(sizes, after, before):
    groups, blocks, drafts = sizes
    rows = groups * blocks * drafts
    group, block, draft = parts_of(after, sizes, iota((rows, rows), 0))
    wanted = before(sizes, group, turned(block), draft)
    return jnp.where(wanted == iota((rows, rows), 1), 1.0, 0.0).astype(jnp.bfloat16)


def group_of():
    return lax.axis_index("dp") * lax.axis_size("pipe") + lax.axis_index("pipe")


def rank_kernel(sizes, owned, *refs):
    groups, blocks, drafts = sizes
    pieces = refs[:blocks]
    shrink_ref, slots_ref = refs[blocks : blocks + 2]
    rows_ref, rank_ref, wide = refs[-3:]
    for block in range(blocks):
        for draft in range(drafts):
            start = (block * drafts + draft) * groups
            wide[start : start + groups, :] = pieces[block][draft].astype(jnp.float32)
    rows = wide[...].astype(jnp.bfloat16)
    rows_ref[...] = rows
    place = slots_ref[:, 0:1] - lax.axis_index("tensor") * owned
    ranks = owned_ranks(
        rows, shrink_ref[...], place, shrink_ref.shape[0] // owned, rank_ref.shape[1]
    )
    put = (rank_ref.shape[0], rows.shape[0])
    draft = parts_of(as_gathered, sizes, iota((rows.shape[0], put[0]), 0))[2]
    line = slots_ref[:, 2:3] * drafts + draft
    put = jnp.where(line == iota((rows.shape[0], put[0]), 1), 1.0, 0.0).astype(jnp.bfloat16)
    ranks = lax.dot_general(
        put, ranks, (((0,), (0,)), ((), ())), preferred_element_type=jnp.float32
    )
    rank_ref[...] = ranks.astype(jnp.bfloat16)


def owned_ranks(rows, shrink, place, width, lanes):
    ranks = dot_nt(rows, shrink)
    kept = jnp.where(over(iota(ranks.shape, 1), width) == place, ranks, 0.0).astype(jnp.bfloat16)
    fold = (ranks.shape[1], lanes)
    fold = rest_of(iota(fold, 0), width) == iota(fold, 1)
    return dot(kept, jnp.where(fold, 1.0, 0.0).astype(jnp.bfloat16)).astype(jnp.bfloat16)


def spread_ranks(ranks, place, width, owned, parts):
    span = owned * width
    row = iota((ranks.shape[1], parts * span), 0)
    column = iota((ranks.shape[1], parts * span), 1)
    tile = (over(row, width) == over(column, span)) & (
        rest_of(row, width) == rest_of(column, width)
    )
    wide = dot(ranks, jnp.where(tile, 1.0, 0.0).astype(jnp.bfloat16))
    slot = over(rest_of(iota(wide.shape, 1), span), width)
    return jnp.where(slot == place, wide, 0.0).astype(jnp.bfloat16)


def product_kernel(rows_ref, *refs):
    *weights, total_ref = refs
    start = 0
    for weight in weights:
        width = weight.shape[1]
        step = width if width % 1024 else 1024
        for first in range(0, width, step):
            total_ref[:, start : start + step] = dot(
                rows_ref[...], weight[:, first : first + step]
            )
            start += step


def product(rows, *weights):
    width = sum(weight.shape[1] for weight in weights)
    return call(
        product_kernel,
        shape((rows.shape[0], width), jnp.float32),
        [VMEM] * (1 + len(weights)),
    )(rows, *weights)


def prepare_kernel(sizes, owned, ids_ref, pool_ref, length_ref, *refs):
    slots_ref, cosine_ref, sine_ref = refs[-3:]
    groups, blocks, drafts = sizes
    width = cosine_ref.shape[1]
    lane = iota(cosine_ref.shape, 1)
    half = (lane & (width // 2 - 1)).astype(jnp.float32)
    positions = (lax.rem(iota(cosine_ref.shape, 0), drafts) + length_ref[0]).astype(jnp.float32)
    angles = positions * jnp.exp(half * (-2.0 * math.log(rope_base) / width))
    cosine_ref[...] = jnp.cos(angles)
    sine_ref[...] = jnp.sin(angles) * jnp.where(lane < width // 2, -1.0, 1.0)
    index = iota(slots_ref.shape, 0)
    column = iota(slots_ref.shape, 1)
    near = parts_of(as_gathered, sizes, index)
    far = parts_of(by_draft, sizes, index)
    row_group = jnp.where(column == 1, far[0], near[0])
    row_block = jnp.where(column == 1, far[1], turned(near[1]))
    place = row_block * groups + row_group
    slots = jnp.zeros(slots_ref.shape, jnp.int32)
    sent, taken = 0, 0
    for row in range(blocks * groups):
        slot = pool_ref[ids_ref[row]]
        owner = over(slot, owned)
        sends = jnp.where(owner == lax.axis_index("tensor"), 1, 0)
        takes = jnp.where(owner == group_of(), 1, 0)
        line = jnp.where(column == 2, sent - 64 * (1 - sends), taken - 64 * (1 - takes))
        slots = jnp.where(place == row, jnp.where(column < 2, slot, line), slots)
        sent, taken = sent + sends, taken + takes
    slots_ref[...] = slots


def prepare(sizes, owned, ids, pool, lengths, table, later):
    groups, blocks, drafts = sizes
    smem = pl.BlockSpec(memory_space=pltpu.SMEM)
    table = shape(table, jnp.float32)
    return call(
        functools.partial(prepare_kernel, sizes, owned),
        [shape((groups * blocks * drafts, 128), jnp.int32), table, table],
        [smem, smem, smem] + [HBM] * 3,
        limit=40 * MIB,
    )(ids, pool, lengths, *[later] * 3)


def grow_kernel(sizes, width, total_ref, slots_ref, *refs):
    groups, blocks, drafts = sizes
    ranks_in, grows, (out_ref, held) = refs[:2], refs[2:5], refs[-2:]
    group = group_of()
    requests = groups * blocks
    lines = out_ref.shape[1]
    held[...] = jnp.zeros(held.shape, jnp.float32)
    owned = grows[0].shape[0] // width
    ranks = ranks_in[0][...].astype(jnp.float32)
    for other in ranks_in[1:]:
        ranks = ranks + other[...].astype(jnp.float32)
    get = (total_ref.shape[0], ranks.shape[0])
    draft = parts_of(as_gathered, sizes, iota(get, 0))[2]
    get = slots_ref[:, 3:4] * drafts + draft == iota(get, 1)
    ranks = dot(jnp.where(get, 1.0, 0.0).astype(jnp.bfloat16), ranks.astype(jnp.bfloat16))
    place = slots_ref[:, 0:1] - group * owned
    wide = spread_ranks(ranks.astype(jnp.bfloat16), place, width, owned, len(grows))
    arranged = reorder(sizes, by_draft, as_gathered)
    start, column = 0, 0
    for index, grow in enumerate(grows):
        deep, cols = grow.shape
        full = total_ref[:, column : column + cols] + dot(
            wide[:, index * deep : (index + 1) * deep], grow[...]
        )
        column += cols
        full = dot(arranged, full.astype(jnp.bfloat16))
        for head in range(cols // 128):
            for draft in range(drafts):
                held[pl.ds(start + draft, requests, stride=lines), :] = full[
                    draft * requests : (draft + 1) * requests, head * 128 : (head + 1) * 128
                ]
            start += drafts
    for row in range(requests):
        out_ref[row] = held[row * lines : (row + 1) * lines, :].astype(jnp.bfloat16)


def attend_kernel(
    sizes, arrived_ref, keys_ref, values_ref, length_ref, cosine_ref, sine_ref, out_ref, *scratch
):
    groups, blocks, drafts = sizes
    (fresh_s,) = scratch
    cache_size, head_size = keys_ref.shape[2:]
    count = out_ref.shape[1]
    scale = 1.0 / math.sqrt(head_size)
    fresh_s[...] = jnp.zeros(fresh_s.shape, jnp.float32)
    scores = []
    for block in range(blocks):
        joined = arrived_ref[block * groups].astype(jnp.float32)
        for other in range(1, groups):
            joined = joined + arrived_ref[block * groups + other].astype(jnp.float32)
        joined = joined.astype(jnp.bfloat16).astype(jnp.float32)
        rotated = joined * cosine_ref[...] + pltpu.roll(joined, head_size // 2, 1) * sine_ref[...]
        fresh_s[2 * block, 0:drafts, :] = rotated[count : count + drafts]
        fresh_s[2 * block + 1, 0:drafts, :] = joined[count + drafts : count + 2 * drafts]
        query = rotated[0:count].astype(jnp.bfloat16)
        old = dot_nt(query, keys_ref[0, block])
        new = dot_nt(query, fresh_s[2 * block].astype(jnp.bfloat16))
        scores.append(jnp.concatenate([old, new], 1))
    scores = jnp.concatenate(scores, 0) * scale
    column = iota(scores.shape, 1)
    limit = cache_size + lax.rem(iota((scores.shape[0], 1), 0), drafts)
    seen = (column < length_ref[0]) | ((column >= cache_size) & (column <= limit))
    scores = jnp.where(seen, scores, -jnp.inf)
    scores = jnp.exp(scores - jnp.max(scores, 1, keepdims=True))
    below = 1.0 / jnp.sum(scores, 1, keepdims=True)
    probs = (scores * below).astype(jnp.bfloat16)
    for block in range(blocks):
        mine = probs[block * count : (block + 1) * count]
        mixed = dot(mine[:, :cache_size], values_ref[0, block]) + dot(
            mine[:, cache_size:], fresh_s[2 * block + 1].astype(jnp.bfloat16)
        )
        mixed = mixed.astype(jnp.bfloat16)
        for target in range(groups):
            out_ref[block * groups + target] = mixed


def sum_kernel(*refs):
    total = refs[0][...].astype(jnp.float32)
    for ref in refs[1:-1]:
        total = total + ref[...].astype(jnp.float32)
    refs[-1][...] = total.astype(jnp.bfloat16)


def add_kernel(left_ref, right_ref, out_ref):
    total = left_ref[...].astype(jnp.float32) + right_ref[...].astype(jnp.float32)
    out_ref[...] = total.astype(jnp.bfloat16)


def packing(rows, width, lanes):
    parts = lanes // width
    return parts, rows // parts


def out_rank_kernel(sizes, owned, got_ref, shrink_ref, slots_ref, *refs):
    rows_ref, rank_ref, wide = refs[-3:]
    drafts = sizes[2]
    requests, lines, head_size = got_ref.shape
    for row in range(requests):
        wide[row * lines : (row + 1) * lines, :] = got_ref[row].astype(jnp.float32)
    for head in range(lines // drafts):
        for draft in range(drafts):
            rows_ref[
                draft * requests : (draft + 1) * requests,
                head * head_size : (head + 1) * head_size,
            ] = wide[pl.ds(head * drafts + draft, requests, stride=lines), :].astype(jnp.bfloat16)
    rows = rows_ref[...]
    place = slots_ref[:, 1:2] - group_of() * owned
    width = shrink_ref.shape[0] // owned
    held, lanes = rank_ref.shape
    parts, span = packing(rows.shape[0], width, lanes)
    ranks = dot_nt(rows, shrink_ref[...])
    kept = jnp.where(over(iota(ranks.shape, 1), width) == place, ranks, 0.0).astype(jnp.bfloat16)
    fold = (ranks.shape[1], lanes)
    fold = rest_of(iota(fold, 0), width) == rest_of(iota(fold, 1), width)
    ranks = dot(kept, jnp.where(fold, 1.0, 0.0).astype(jnp.bfloat16))
    mine = over(iota(ranks.shape, 1), width) == over(iota(ranks.shape, 0), span)
    ranks = jnp.where(mine, ranks, 0.0).astype(jnp.bfloat16)
    put = (held, rows.shape[0])
    put = iota(put, 0) == rest_of(iota(put, 1), span)
    ranks = dot(jnp.where(put, 1.0, 0.0).astype(jnp.bfloat16), ranks)
    rank_ref[...] = ranks.astype(jnp.bfloat16)


def out_grow_kernel(sizes, width, total_ref, slots_ref, grow_ref, *refs):
    groups, blocks, drafts = sizes
    ranks_in, outs = refs[:blocks], refs[blocks:]
    owned = grow_ref.shape[0] // width
    me = lax.axis_index("tensor")
    ranks = ranks_in[0][...].astype(jnp.float32)
    for other in ranks_in[1:]:
        ranks = ranks + other[...].astype(jnp.float32)
    count = total_ref.shape[0]
    held, lanes = ranks.shape
    parts, span = packing(count, width, lanes)
    put = rest_of(iota((count, held), 0), span) == iota((count, held), 1)
    ranks = dot(jnp.where(put, 1.0, 0.0).astype(jnp.bfloat16), ranks.astype(jnp.bfloat16))
    mine = over(iota(ranks.shape, 1), width) == over(iota(ranks.shape, 0), span)
    ranks = jnp.where(mine, ranks, 0.0).astype(jnp.bfloat16)
    tile = (lanes, owned * width)
    tile = rest_of(iota(tile, 0), width) == rest_of(iota(tile, 1), width)
    ranks = dot(ranks, jnp.where(tile, 1.0, 0.0).astype(jnp.bfloat16))
    place = slots_ref[:, 1:2] - me * owned
    wide = jnp.where(over(iota(ranks.shape, 1), width) == place, ranks, 0.0).astype(jnp.bfloat16)
    full = (total_ref[...] + dot(wide, grow_ref[...])).astype(jnp.bfloat16)
    full = dot(reorder(sizes, as_gathered, by_draft), full).astype(jnp.bfloat16)
    for block in range(blocks):
        for draft in range(drafts):
            start = (block * drafts + draft) * groups
            outs[block][draft] = full[start : start + groups]


def by_kernels(
    tokens,
    w_query,
    w_key,
    w_value,
    w_out,
    shrink_qkv,
    grow_query,
    grow_key,
    grow_value,
    shrink_out,
    grow_out,
    cache_keys,
    cache_values,
    cache_lengths,
    adapter_ids,
    adapter_slots,
):
    blocks = lax.axis_size("tensor")
    groups = lax.axis_size(GROUP)
    _, drafts, features = tokens.shape
    sizes = (groups, blocks, drafts)
    owned = shrink_qkv.shape[0]
    width = grow_out.shape[1]
    head_size = cache_keys.shape[3]
    span = blocks * drafts
    count = groups * span
    lanes = -(-shrink_qkv.shape[2] // 128) * 128

    def over_tensor(value, shift):
        route = [(t, t ^ shift) for t in range(blocks)]
        return lax.ppermute(value, "tensor", route)

    def over_core(value):
        return lax.ppermute(value, "pipe", [(0, 1), (1, 0)])

    def to_growers(value, flip):
        route = [
            (t * groups + 2 * x + c, (2 * c + (x ^ flip)) * groups + t)
            for t in range(blocks)
            for x in range(2)
            for c in range(2)
        ]
        return lax.ppermute(value, EVERY, route)

    def to_out_growers(value, shift):
        route = [
            (t * groups + g, g * groups + (t ^ shift))
            for t in range(blocks)
            for g in range(groups)
        ]
        return lax.ppermute(value, EVERY, route)

    def added(left, right):
        return call(add_kernel, shape(left.shape), [VMEM] * 2)(left, right)

    def exchange(value):
        return lax.all_to_all(value, EVERY, split_axis=0, concat_axis=0, tiled=True)

    mine = jnp.transpose(tokens, (1, 0, 2))
    pieces = [mine] + [over_tensor(mine, shift) for shift in range(1, blocks)]

    lines = (w_query.shape[1] // head_size + 2) * drafts
    lines = -(-lines // 8) * 8
    slots, cosine, sine = prepare(
        sizes, owned, adapter_ids, adapter_slots, cache_lengths, (lines, head_size), w_out
    )
    packed = -(-2 * blocks * drafts // 16) * 16
    shrink_in = jnp.transpose(shrink_qkv, (0, 2, 1)).reshape(-1, features)
    rows, rank_part = call(
        functools.partial(rank_kernel, sizes, owned),
        [shape((count, features)), shape((packed, lanes))],
        [VMEM] * (blocks + 2),
        [pltpu.VMEM((count, features), jnp.float32)],
        2 * count * shrink_qkv.size,
        2 * shrink_qkv.size + 4 * count * features,
    )(*pieces, shrink_in, slots)
    rank_part = added(rank_part, over_core(rank_part))
    ranks = [to_growers(rank_part, flip) for flip in range(2)]
    total = product(rows, w_query, w_key, w_value)
    cols = total.shape[1]
    head_cols = w_query.shape[1]
    query_lines = head_cols // head_size * drafts
    sent = call(
        functools.partial(grow_kernel, sizes, width),
        shape((blocks * groups, lines, head_size)),
        [VMEM] * 7 + [HBM] * 2,
        [pltpu.VMEM((blocks * groups * lines, head_size), jnp.float32)],
        limit=40 * MIB,
    )(
        total,
        slots,
        *ranks,
        *[grow.reshape(owned * width, -1) for grow in (grow_query, grow_key, grow_value)],
        *[w_out] * 2,
    )
    mixed = call(
        functools.partial(attend_kernel, sizes),
        shape((blocks * groups, query_lines, head_size)),
        [VMEM] * 3 + [pl.BlockSpec(memory_space=pltpu.SMEM)] + [VMEM] * 2,
        [pltpu.VMEM((2 * blocks, 128, head_size), jnp.float32)],
    )(exchange(sent), cache_keys, cache_values, cache_lengths, cosine, sine)
    gathered = exchange(mixed)
    held = -(-packing(count, width, 128)[1] // 16) * 16
    out_rows, out_part = call(
        functools.partial(out_rank_kernel, sizes, owned),
        [shape((count, head_cols)), shape((held, 128))],
        [VMEM] * 3 + [HBM] * 4,
        [pltpu.VMEM((blocks * groups * query_lines, head_size), jnp.float32)],
        limit=40 * MIB,
    )(gathered, jnp.transpose(shrink_out, (0, 2, 1)).reshape(-1, head_cols), slots, *[w_query] * 4)
    out_ranks = [to_out_growers(out_part, shift) for shift in range(blocks)]
    out_total = product(out_rows, w_out)
    out_cols = out_total.shape[1]
    leaving = call(
        functools.partial(out_grow_kernel, sizes, width),
        [shape((drafts, groups, out_cols))] * blocks,
        [VMEM] * (3 + blocks),
        [],
        2 * count * owned * width * out_cols,
        8 * count * out_cols + 2 * owned * width * out_cols,
    )(out_total, slots, grow_out.reshape(owned * width, -1), *out_ranks)
    order = sorted(range(1, blocks), key=lambda shift: shift < blocks // 2)
    parts = [leaving[0]] + [over_tensor(leaving[shift], shift) for shift in order]
    result = call(sum_kernel, shape(parts[0].shape), [VMEM] * blocks)(*parts)
    return jnp.transpose(result, (1, 0, 2))


def rotate(vectors, positions):
    half_size = vectors.shape[-1] // 2
    frequency = rope_base ** (-2.0 * jnp.arange(half_size, dtype=jnp.float32) / vectors.shape[-1])
    angles = positions[:, None, None] * frequency
    cosine = jnp.cos(angles)
    sine_value = jnp.sin(angles)
    first_half = vectors[..., :half_size]
    second = vectors[..., half_size:]
    return jnp.concatenate(
        [first_half * cosine - second * sine_value, second * cosine + first_half * sine_value], -1
    )


def to_growers(partial, splits):
    total = None
    for shift in range(splits):
        route = [
            (t * splits + g, ((g + shift) % splits) * splits + t)
            for t in range(splits)
            for g in range(splits)
        ]
        got = lax.ppermute(partial, EVERY, route).astype(jnp.float32)
        total = got if total is None else total + got
    return total


def to_out_growers(partial, splits):
    total = None
    for shift in range(splits):
        route = [
            (t * splits + g, g * splits + (t + shift) % splits)
            for t in range(splits)
            for g in range(splits)
        ]
        got = lax.ppermute(partial, EVERY, route).astype(jnp.float32)
        total = got if total is None else total + got
    return total


def slot_table(adapter_ids, adapter_slots):
    matches = adapter_ids[:, None] == jnp.arange(adapter_slots.shape[0], dtype=jnp.int32)[None, :]
    return jnp.sum(jnp.where(matches, adapter_slots[None, :], 0), axis=1)


def attend(query_heads, key_new, value_new, cache_keys, cache_values, length):
    drafts, head_count, head_size = query_heads.shape
    kv_heads, cache_size, _ = cache_keys.shape
    positions = (length + jnp.arange(drafts, dtype=jnp.int32)).astype(jnp.float32)
    query_rot = rotate(query_heads.astype(jnp.float32), positions).astype(jnp.bfloat16)
    key_rot = rotate(key_new.astype(jnp.float32), positions).astype(jnp.bfloat16)
    grouped = query_rot.reshape(drafts, kv_heads, head_count // kv_heads, head_size)
    score_scale = 1.0 / math.sqrt(head_size)
    cached = (
        jnp.einsum("skgd,kld->skgl", grouped, cache_keys, preferred_element_type=jnp.float32)
        * score_scale
    )
    fresh_scores = (
        jnp.einsum("skgd,tkd->skgt", grouped, key_rot, preferred_element_type=jnp.float32)
        * score_scale
    )
    cache_mask = jnp.arange(cache_size, dtype=jnp.int32) < length
    draft_mask = jnp.arange(drafts)[None, :] <= jnp.arange(drafts)[:, None]
    cached = jnp.where(cache_mask[None, None, None, :], cached, -jnp.inf)
    fresh_scores = jnp.where(draft_mask[:, None, None, :], fresh_scores, -jnp.inf)
    row_peak = jnp.maximum(jnp.max(cached, -1), jnp.max(fresh_scores, -1))
    cached_exp = jnp.exp(cached - row_peak[..., None])
    fresh_exp = jnp.exp(fresh_scores - row_peak[..., None])
    denominator = jnp.sum(cached_exp, -1) + jnp.sum(fresh_exp, -1)
    cached_prob = (cached_exp / denominator[..., None]).astype(jnp.bfloat16)
    fresh_prob = (fresh_exp / denominator[..., None]).astype(jnp.bfloat16)
    mixed = jnp.einsum(
        "skgl,kld->skgd", cached_prob, cache_values, preferred_element_type=jnp.float32
    )
    mixed = mixed + jnp.einsum(
        "skgt,tkd->skgd", fresh_prob, value_new, preferred_element_type=jnp.float32
    )
    return mixed.astype(jnp.bfloat16)


def by_row(
    tokens,
    w_query,
    w_key,
    w_value,
    w_out,
    shrink_qkv,
    grow_query,
    grow_key,
    grow_value,
    shrink_out,
    grow_out,
    cache_keys,
    cache_values,
    cache_lengths,
    adapter_ids,
    adapter_slots,
):
    splits = lax.axis_size("tensor")
    groups = lax.axis_size(("dp", "pipe"))
    tensor_index = lax.axis_index("tensor")
    group_index = lax.axis_index(("dp", "pipe"))
    local_rows, drafts, feature_width = tokens.shape
    per_owner = shrink_qkv.shape[0]
    rank_size = grow_out.shape[1]
    query_cols = w_query.shape[1]
    key_cols = w_key.shape[1]
    kv_heads = cache_keys.shape[1]
    head_size = cache_keys.shape[3]
    rows = splits * groups
    row_slots = jnp.repeat(slot_table(adapter_ids, adapter_slots), drafts)
    within = jnp.arange(per_owner, dtype=jnp.int32)[None, :]
    width_hot = (row_slots[:, None] == within + tensor_index * per_owner)[:, :, None]
    column_hot = (row_slots[:, None] == within + group_index * per_owner)[:, :, None]

    def spread_ranks(ranks, hot):
        return jnp.where(hot, ranks[:, None, :], 0.0).reshape(rows * drafts, -1).astype(jnp.bfloat16)

    flat_tokens = lax.all_gather(tokens, "tensor", axis=0, tiled=True).reshape(
        rows * drafts, feature_width
    )
    rank_part = jnp.einsum(
        "nd,adr->nar", flat_tokens, shrink_qkv, preferred_element_type=jnp.float32
    )
    rank_part = jnp.sum(jnp.where(width_hot, rank_part, 0.0), 1)
    rank_all = to_growers(rank_part.astype(jnp.bfloat16), splits)

    def grown(index, grow):
        ranks = spread_ranks(rank_all[:, index * rank_size : (index + 1) * rank_size], column_hot)
        return jnp.dot(
            ranks, grow.reshape(per_owner * rank_size, -1), preferred_element_type=jnp.float32
        )

    bases = [
        jnp.dot(flat_tokens, weight, preferred_element_type=jnp.float32)
        for weight in (w_query, w_key, w_value)
    ]

    def product(index, grow):
        return (bases[index] + grown(index, grow)).astype(jnp.bfloat16).reshape(rows, drafts, -1)

    partial = jnp.concatenate(
        [
            product(0, grow_query),
            product(1, grow_key),
            product(2, grow_value),
        ],
        2,
    )
    arrived = lax.all_to_all(partial, EVERY, split_axis=0, concat_axis=0, tiled=True)
    joined = jnp.sum(
        arrived.reshape(splits, groups, drafts, -1).astype(jnp.float32), 1
    ).astype(jnp.bfloat16)
    joined = jnp.transpose(joined, (1, 0, 2))
    query_heads = joined[:, :, :query_cols].reshape(drafts, -1, head_size)
    key_new = joined[:, :, query_cols : query_cols + key_cols].reshape(drafts, kv_heads, head_size)
    value_new = joined[:, :, query_cols + key_cols :].reshape(drafts, kv_heads, head_size)
    mixed = attend(
        query_heads, key_new, value_new, cache_keys[0], cache_values[0], cache_lengths[0]
    )
    mixed = jnp.transpose(mixed.reshape(drafts, splits, -1), (1, 0, 2))
    outgoing = jnp.repeat(mixed, groups, axis=0)
    flat_heads = lax.all_to_all(
        outgoing, EVERY, split_axis=0, concat_axis=0, tiled=True
    ).reshape(rows * drafts, -1)
    out_part = jnp.einsum(
        "nw,awr->nar", flat_heads, shrink_out, preferred_element_type=jnp.float32
    )
    out_part = jnp.sum(jnp.where(column_hot, out_part, 0.0), 1)
    out_rank = to_out_growers(out_part.astype(jnp.bfloat16), splits)
    out = jnp.dot(flat_heads, w_out, preferred_element_type=jnp.float32)
    out = out + jnp.dot(
        spread_ranks(out_rank, width_hot),
        grow_out.reshape(per_owner * rank_size, -1),
        preferred_element_type=jnp.float32,
    )
    blocks = lax.all_to_all(
        out.astype(jnp.bfloat16).reshape(splits, local_rows, drafts, feature_width),
        "tensor",
        split_axis=0,
        concat_axis=0,
        tiled=True,
    )
    return jnp.sum(blocks.astype(jnp.float32), 0).astype(jnp.bfloat16)


def local(*arrays):
    heads = arrays[11].shape[1]
    sizes = [lax.axis_size(name) for name in EVERY]
    if heads == 4 and sizes == [4, 2, 2]:
        return by_kernels(*arrays)
    return by_row(*arrays)


def solution(mesh):
    placed = (
        P(("parts", "tensor"), None, ("dp", "pipe")),
        P(("dp", "pipe"), "tensor"),
        P(("dp", "pipe"), "tensor"),
        P(("dp", "pipe"), "tensor"),
        P("tensor", ("dp", "pipe")),
        P("tensor", ("dp", "pipe"), None),
        P(("dp", "pipe"), None, "tensor"),
        P(("dp", "pipe"), None, "tensor"),
        P(("dp", "pipe"), None, "tensor"),
        P(("dp", "pipe"), "tensor", None),
        P("tensor", None, ("dp", "pipe")),
        P(("parts", "tensor", "dp", "pipe"), None, None, None),
        P(("parts", "tensor", "dp", "pipe"), None, None, None),
        P(("parts", "tensor", "dp", "pipe")),
        P(),
        P(),
    )
    return jax.shard_map(
        local,
        mesh=mesh,
        in_specs=placed,
        out_specs=P(("parts", "tensor"), None, ("dp", "pipe")),
        check_vma=False,
    )
```
